32 devices in a mesh: section: 2 (over x), expert: 4 (over z), dp: 4 (over y, core).
Axes of the slice: x: 2, y: 2, z: 4, core: 2. Of those that a mesh axis runs over, the one named last changes fastest.
Arguments:
- frames: bfloat16 [4, 32, 48, 1280], P(None, ('expert', 'dp')), may hold values from -6 to 6
- norm_gain: float32 [2, 1280], P('section'), may hold values from 0.1 to 1.9
- router: bfloat16 [2, 1280, 4], P('section'), may hold values from -0.15625 to 0.15625
- w_in: bfloat16 [2, 4, 1280, 256], P('section', 'expert'), may hold values from -0.15625 to 0.15625
- w_out: bfloat16 [2, 4, 256, 1280], P('section', 'expert'), may hold values from -0.375 to 0.375
- routing: int32 [2, 4, 32, 48, 1], P('section', None, ('expert', 'dp')), may hold values from 0 to 3; in each aligned block of 96 rows (0 to 95, 96 to 191, ..., all dimensions but the last counted through in order) at most 27 rows name the same one
- head_gain: float32 [1280], replicated, may hold values from 0.1 to 1.9
- head_weight: bfloat16 [1280, 8000], P(None, 'expert'), may hold values from -6 to 6
- frame_lengths: int32 [4, 32], P(None, ('expert', 'dp')), may hold values from 24 to 48
- labels: int32 [4, 32, 12], P(None, ('expert', 'dp')), may hold values from 1 to 7999
- label_lengths: int32 [4, 32], P(None, ('expert', 'dp')), may hold values from 1 to 12
Outputs:
- losses: float32 [8, 16], P('section', ('expert', 'dp'))
- head_grad: bfloat16 [1280, 8000], P(None, 'expert')
The draws below stay inside these ranges and needn't reach their ends.
Inputs may be any that keep to these rules, and one draw needn't show every extreme that they name: `routing`: in each layer and micro-batch, within the frames of one device (aligned blocks of 96 frames), no expert is named by more than 27 frames.
All inputs are finite; a program needn't handle non-finite values.
Results may differ from the reference program's by a relative error of at most 0.015.
Values may be sent and summed in bfloat16 or wider, within the bound.
No kernel may reach another device: no remote copies, remote signals or barrier semaphores. Data moves between devices by JAX's collectives and lax.ppermute only.
A program may use at most 64 MiB of HBM per device.

```python
import math
import jax
import jax.numpy as jnp
import numpy as np
from jax import lax

D = 1280
EFF = 256
VOCAB = 8000
MICRO = 4
UTT_DEV = 2
FRAMES = 48
LMAX = 12
EXPERTS = 4
TOK_DEV = 96
CAP = 27
UTTS = 32
PAIRS = 8
EXT = 25
N_SECTION = 2


def draw_head_weight(key, part):
    key = jax.random.fold_in(key, 11)
    key_base = jax.random.fold_in(key, 0)
    weight = jax.random.normal(key_base, (D, VOCAB), jnp.float32) * (3.0 / math.sqrt(D))
    return jnp.clip(weight, -6.0, 6.0).astype(jnp.bfloat16)


def draw_frame_lengths(key, part):
    key = jax.random.fold_in(key, 21)
    key_value, key_spot = jax.random.split(key)
    counts = jax.random.randint(key_value, (MICRO * UTTS,), FRAMES // 2, FRAMES + 1)
    chosen = jax.random.randint(key_spot, (), 0, MICRO * UTTS)
    counts = jnp.where(jnp.arange(MICRO * UTTS) == chosen, FRAMES, counts)
    return counts.reshape(MICRO, UTTS).astype(jnp.int32)


def draw_label_lengths(key, part):
    key = jax.random.fold_in(key, 31)
    key_value, key_spot = jax.random.split(key)
    counts = jax.random.randint(key_value, (MICRO * UTTS,), 1, LMAX + 1)
    chosen = jax.random.randint(key_spot, (), 0, MICRO * UTTS)
    counts = jnp.where(jnp.arange(MICRO * UTTS) == chosen, LMAX, counts)
    return counts.reshape(MICRO, UTTS).astype(jnp.int32)


def plant(array, key, least, high):
    longest = array.shape.index(max(array.shape))
    spots = []
    for shift in (0, 1):
        where = [jax.random.randint(jax.random.fold_in(key, axis), (), 0, length) for axis, length in enumerate(array.shape)]
        where[longest] = (where[longest] + shift) % array.shape[longest]
        spots.append(tuple(where))
    return array.at[spots[0]].set(least).at[spots[1]].set(high)


def shard_levels(rng, dims, shards, smallest, high):
    level, own = 1.0, jax.random.fold_in(rng, 6)
    for axis_at, shards_of in shards:
        steps = jnp.exp(jax.random.uniform(jax.random.fold_in(own, axis_at), (shards_of,), jnp.float32, smallest / len(shards), high / len(shards)))
        level = level * jnp.repeat(steps, dims[axis_at] // shards_of).reshape([-1 if axis == axis_at else 1 for axis in range(len(dims))])
    return level


def routed_block(key, own, number, rows, count, top, reach, skew):
    ranking = jax.random.permutation(key, count)
    packed, usual = load_shares(count, rows * top, reach, skew, True), load_shares(count, rows * top, reach, skew, False)
    places = jnp.arange(count)

    def named(sizes, turn):
        used = int((sizes > 0).sum())
        fixed = max(1, used // 4)
        moved = fixed + (places - fixed + turn * (used - fixed)) % max(1, count - fixed)
        return jnp.zeros((count,), jnp.int32).at[ranking[jnp.where(places < fixed, places, moved)]].set(jnp.asarray(sizes, jnp.int32))

    sizes = jnp.where(number % 4 == 0, named(packed, number // 4), named(usual, number - number // 4 - 1))
    mixed = jax.random.permutation(jax.random.fold_in(own, 3), count)
    donor, sink = mixed[0:count // 2 * 2:2], mixed[1:count // 2 * 2:2]
    margin = jnp.minimum(sizes[donor] - 1, reach - sizes[sink]) // 2
    margin = jnp.where((donor == ranking[0]) | (sink == ranking[0]) | (sizes[sink] == 0), 0, jnp.maximum(margin, 0))
    moved = jax.random.randint(jax.random.fold_in(own, 4), (count // 2,), 0, 1 << 20) % (margin + 1)
    sizes = sizes.at[donor].add(-moved).at[sink].add(moved)
    items = jnp.searchsorted(jnp.cumsum(sizes), jnp.arange(rows * top), side="right").astype(jnp.int32)
    listing = items.reshape(top, rows).T
    listing = listing[jax.random.permutation(jax.random.fold_in(own, 1), rows)]
    turn = jax.random.randint(jax.random.fold_in(own, 2), (rows, 1), 0, top)
    return jnp.take_along_axis(listing, (jnp.arange(top)[None, :] + turn) % top, axis=1)


def load_shares(amount, total, limit, lean, full):
    loads = [(1 << 20) // math.isqrt(standing ** lean) + 1 for standing in range(1, amount + 1)]
    largest = limit if full else min(limit, max(-(-total // amount), total * loads[0] // sum(loads)))
    least = 1 if total - largest >= amount - 1 else 0
    given, rest = [largest] + [least] * (amount - 1), total - largest - least * (amount - 1)
    while rest > 0:
        free = [i for i in range(1, amount) if given[i] < largest] or [i for i in range(1, amount) if given[i] < limit]
        whole, remaining = sum([loads[i] for i in free]), rest
        for i in free:
            addition = min(limit - given[i], max(1, remaining * loads[i] // whole), rest)
            given[i] = given[i] + addition
            rest = rest - addition
    return np.array(given)


def normal_values(key, extent, scale, bound, cuts=(), kind=jnp.bfloat16):
    loudness = shard_levels(key, extent, cuts, -0.22, 0.18) if cuts else 1.0
    values = jax.random.normal(key, extent, jnp.float32) * scale * loudness
    return jnp.minimum(jnp.maximum(values, -bound), bound).astype(kind)


def setup_inputs(seed: int = 0) -> dict:
    key_of = jax.random.split(jax.random.key(seed), 12)
    frames = normal_values(key_of[0], (MICRO, UTTS, FRAMES, D), 1.0, 6.0, ((1, 16),))
    norm_gain = jnp.clip(1.0 + 0.18 * jax.random.normal(key_of[1], (N_SECTION, D), jnp.float32), 0.1, 1.9)
    router = normal_values(key_of[2], (N_SECTION, D, EXPERTS), D ** -0.5, 0.15625, ((0, 2),))
    w_in = normal_values(key_of[3], (N_SECTION, EXPERTS, D, EFF), D ** -0.5, 0.15625, ((0, 2), (1, 4)))
    w_out = normal_values(key_of[4], (N_SECTION, EXPERTS, EFF, D), EFF ** -0.5, 0.375, ((0, 2), (1, 4)))
    routing_keys = jax.random.split(jax.random.fold_in(key_of[5], 1), N_SECTION * MICRO * UTTS * FRAMES // TOK_DEV)
    routing_turns = jax.random.permutation(jax.random.fold_in(key_of[5], 3), N_SECTION * MICRO * UTTS * FRAMES // TOK_DEV)
    routing = jax.vmap(lambda own, number: routed_block(jax.random.fold_in(key_of[5], 2), own, number, TOK_DEV, EXPERTS, 1, CAP, 2))(routing_keys, routing_turns).reshape((N_SECTION, MICRO, UTTS, FRAMES, 1))
    head_gain = jnp.clip(1.0 + 0.18 * jax.random.normal(key_of[6], (D,), jnp.float32), 0.1, 1.9)
    head_weight = draw_head_weight(jax.random.fold_in(key_of[11], 71), 0)
    frame_lengths = draw_frame_lengths(jax.random.fold_in(key_of[11], 71), 0)
    labels = plant(jax.random.randint(key_of[9], (MICRO, UTTS, LMAX), 1, VOCAB), jax.random.fold_in(key_of[9], 1), 1, VOCAB - 1).astype(jnp.int32)
    label_lengths = draw_label_lengths(jax.random.fold_in(key_of[11], 71), 0)
    return {"frames": frames, "norm_gain": norm_gain, "router": router, "w_in": w_in, "w_out": w_out, "routing": routing, "head_gain": head_gain, "head_weight": head_weight, "frame_lengths": frame_lengths, "labels": labels, "label_lengths": label_lengths}


EPSILON = 1e-06
LOG_ZERO = -1e+30

def rms_scale(values, scaling):
    values = values.astype(jnp.float32)
    return values * lax.rsqrt(lax.optimization_barrier(jnp.mean(values * values, axis=-1, keepdims=True)) + EPSILON) * scaling

def slot_index(expert_ids, expert_count, capacity):
    one_hot = (expert_ids[:, None] == jnp.arange(expert_count, dtype=jnp.int32)[None, :]).astype(jnp.int32)
    slot_rank = lax.optimization_barrier(jnp.sum((jnp.cumsum(one_hot, axis=0) - 1) * one_hot, axis=1))
    return ((expert_ids * capacity + slot_rank).astype(jnp.int32), one_hot)

def extend_labels(label_rows):
    blanks = jnp.zeros_like(label_rows)
    paired = jnp.stack([blanks, label_rows], axis=-1).reshape(label_rows.shape[:-1] + (2 * label_rows.shape[-1],))
    return jnp.concatenate([paired, jnp.zeros(label_rows.shape[:-1] + (1,), jnp.int32)], axis=-1)

def ctc_single(emission, ext_labels, frame_count, label_count):
    state_count = ext_labels.shape[0]
    position = jnp.arange(state_count, dtype=jnp.int32)
    earlier = jnp.concatenate([jnp.full((2,), -1, jnp.int32), ext_labels[:-2]])
    skippable = (ext_labels != 0) & (ext_labels != earlier) & (position >= 2)
    lowest = jnp.full((state_count,), LOG_ZERO, emission.dtype)
    initial = jnp.where(position < 2, emission[0], lowest)

    def advance(forward_log, inputs):
        emit_row, time_step = inputs
        one_back = jnp.concatenate([lowest[:1], forward_log[:-1]])
        two_back = jnp.where(skippable, jnp.concatenate([lowest[:2], forward_log[:-2]]), lowest)
        moved = jnp.logaddexp(jnp.logaddexp(forward_log, one_back), two_back) + emit_row
        return (jnp.where(time_step < frame_count, moved, forward_log), None)
    time_steps = jnp.arange(1, emission.shape[0], dtype=jnp.int32)
    final_log, _ = lax.scan(advance, initial, (emission[1:], time_steps))
    last_state = 2 * label_count
    end_state = jnp.sum(jnp.where(position == last_state, final_log, 0.0))
    near_state = jnp.sum(jnp.where(position == last_state - 1, final_log, 0.0))
    return -jnp.logaddexp(end_state, near_state)

def ctc_terms(emission, ext_labels, frame_counts, label_counts):

    def summed_loss(values):
        losses = jax.vmap(ctc_single)(values, ext_labels, frame_counts, label_counts)
        return (jnp.sum(losses), losses)
    summed, pullback, losses = jax.vjp(summed_loss, emission, has_aux=True)
    occupancy = pullback(jnp.ones_like(summed))[0]
    return (losses, occupancy)

def moe_section(current_rows, layer_routes, scaling, router_w, weight_in, weight_out, capacity):
    expert_count = router_w.shape[1]
    block_count, tokens, width = current_rows.shape
    normed = rms_scale(current_rows, scaling).astype(jnp.bfloat16)
    logits = jnp.einsum('btd,de->bte', normed.astype(jnp.float32), router_w.astype(jnp.float32))
    target_slot, one_hot = jax.vmap(lambda routes: slot_index(routes, expert_count, capacity))(layer_routes)
    gate_value = jax.nn.sigmoid(lax.optimization_barrier(jnp.sum(jnp.where(one_hot > 0, logits, 0.0), axis=-1)))

    def place_rows(row_values, slots):
        return jnp.zeros((expert_count * capacity, width), jnp.bfloat16).at[slots].set(row_values)
    buffers = jax.vmap(place_rows)(normed, target_slot).reshape(block_count, expert_count, capacity, width)
    hidden = jnp.einsum('becd,edh->bech', buffers.astype(jnp.float32), weight_in.astype(jnp.float32))
    active = (hidden * jax.nn.sigmoid(hidden)).astype(jnp.bfloat16)
    outputs = jnp.einsum('bech,ehd->becd', active.astype(jnp.float32), weight_out.astype(jnp.float32)).astype(jnp.bfloat16)
    outputs = outputs.reshape(block_count, expert_count * capacity, width)
    picked = jax.vmap(lambda row_values, slots: row_values[slots])(outputs, target_slot)
    return (current_rows.astype(jnp.float32) + gate_value[..., None] * picked.astype(jnp.float32)).astype(jnp.bfloat16)

def reference(frames, norm_gain, router, w_in, w_out, routing, head_gain, head_weight, frame_lengths, labels, label_lengths):
    group_count = UTTS // UTT_DEV
    tokens = UTT_DEV * FRAMES
    hidden_state = frames.reshape(MICRO * group_count, tokens, D)
    for layer_index in range(N_SECTION):
        layer_routes = routing[layer_index, :, :, :, 0].reshape(MICRO * group_count, tokens)
        hidden_state = moe_section(hidden_state, layer_routes, norm_gain[layer_index], router[layer_index], w_in[layer_index], w_out[layer_index], CAP)
    final_rows = hidden_state.reshape(MICRO * UTTS, FRAMES, D)
    ext_all = extend_labels(labels.reshape(MICRO * UTTS, LMAX))
    frame_all = frame_lengths.reshape(MICRO * UTTS)
    label_all = label_lengths.reshape(MICRO * UTTS)
    block_size = 8
    block_total = MICRO * UTTS // block_size

    def head_block(grad_sum, inputs):
        hidden_rows, ext_rows, frame_rows, label_rows = inputs
        normed = rms_scale(hidden_rows, head_gain).astype(jnp.bfloat16)
        flat_rows = normed.reshape(block_size * FRAMES, D)
        logits = jnp.dot(flat_rows, head_weight, preferred_element_type=jnp.float32)
        highest = lax.optimization_barrier(jnp.max(logits, axis=1, keepdims=True))
        log_total = highest + jnp.log(lax.optimization_barrier(jnp.sum(jnp.exp(logits - highest), axis=1, keepdims=True)))
        logprob = (logits - log_total).reshape(block_size, FRAMES, VOCAB)
        selector = (ext_rows[:, :, None] == jnp.arange(VOCAB, dtype=jnp.int32)[None, None, :]).astype(jnp.float32)
        emission = jnp.einsum('btv,bsv->bts', logprob, selector, precision=lax.Precision.HIGHEST)
        losses, occupancy = ctc_terms(emission, ext_rows, frame_rows, label_rows)
        scattered = jnp.einsum('bts,bsv->btv', occupancy, selector, precision=lax.Precision.HIGHEST)
        grad_logits = (scattered - jnp.exp(logprob) * lax.optimization_barrier(jnp.sum(occupancy, axis=2, keepdims=True))).astype(jnp.bfloat16)
        grad_sum = grad_sum + lax.dot_general(flat_rows, grad_logits.reshape(block_size * FRAMES, VOCAB), (((0,), (0,)), ((), ())), preferred_element_type=jnp.float32)
        return (grad_sum, losses)
    grad_total, block_losses = lax.scan(head_block, jnp.zeros((D, VOCAB), jnp.float32), (final_rows.reshape(block_total, block_size, FRAMES, D), ext_all.reshape(block_total, block_size, EXT), frame_all.reshape(block_total, block_size), label_all.reshape(block_total, block_size)))
    loss_table = block_losses.reshape(MICRO, group_count, UTT_DEV).transpose(0, 2, 1).reshape(PAIRS, group_count)
    return (loss_table, grad_total.astype(jnp.bfloat16))
```

```python
import functools

import jax
import jax.numpy as jnp
from jax import lax
from jax.experimental import pallas as pl
from jax.experimental.pallas import tpu as pltpu
from jax.sharding import Mesh, PartitionSpec as P

EPSILON = 1e-06
LOG_ZERO = -1e30
VMEM_LIMIT = 48 * 1024 * 1024
COLS = 16
BLOCK_ROWS = 256
NT = (((1,), (1,)), ((), ()))
NN = (((1,), (0,)), ((), ()))


def round_up(value, unit):
    return -(-value // unit) * unit


def vmem_spec():
    return pl.BlockSpec(memory_space=pltpu.VMEM)


def smem_spec():
    return pl.BlockSpec(memory_space=pltpu.SMEM)


def call(kernel, out_shape, flops=0, moved=0, **options):
    return pl.pallas_call(
        kernel,
        out_shape=out_shape,
        compiler_params=pltpu.CompilerParams(vmem_limit_bytes=VMEM_LIMIT),
        cost_estimate=pl.CostEstimate(flops=flops, bytes_accessed=moved, transcendentals=0),
        **options,
    )


def rms_scale(values, gain):
    values = values.astype(jnp.float32)
    scale = lax.rsqrt(jnp.mean(values * values, axis=-1, keepdims=True) + EPSILON)
    return (values * scale * gain).astype(jnp.bfloat16)


def slots_in_row(ids_row, experts, capacity):
    count = ids_row.shape[1]
    height = round_up(experts, 8)
    named = lax.broadcasted_iota(jnp.int32, (height, count), 0) == ids_row
    one_hot = named.astype(jnp.float32)
    before = lax.broadcasted_iota(jnp.int32, (count, count), 0) <= lax.broadcasted_iota(
        jnp.int32, (count, count), 1
    )
    rank = lax.dot_general(
        one_hot.astype(jnp.bfloat16),
        before.astype(jnp.float32).astype(jnp.bfloat16),
        NN,
        preferred_element_type=jnp.float32,
    )
    start = (lax.broadcasted_iota(jnp.int32, (height, count), 0) * capacity - 1).astype(jnp.float32)
    return jnp.sum(one_hot * (rank + start), axis=0, keepdims=True).astype(jnp.int32)


def slots_in_column(ids_column, experts, capacity):
    count = ids_column.shape[0]
    named = lax.broadcasted_iota(jnp.int32, (count, 128), 1) == ids_column
    one_hot = named.astype(jnp.float32)
    before = lax.broadcasted_iota(jnp.int32, (count, count), 1) <= lax.broadcasted_iota(
        jnp.int32, (count, count), 0
    )
    rank = lax.dot_general(
        before.astype(jnp.float32).astype(jnp.bfloat16),
        one_hot.astype(jnp.bfloat16),
        NN,
        preferred_element_type=jnp.float32,
    )
    start = (lax.broadcasted_iota(jnp.int32, (count, 128), 1) * capacity - 1).astype(jnp.float32)
    return jnp.sum(one_hot * (rank + start), axis=1, keepdims=True).astype(jnp.int32), one_hot


def scatter_rows(rows, ids_row, experts, capacity):
    slots = slots_in_row(ids_row, experts, capacity)
    places = lax.broadcasted_iota(jnp.int32, (experts * capacity, rows.shape[0]), 0)
    pick = (places == slots).astype(jnp.float32).astype(jnp.bfloat16)
    return lax.dot_general(pick, rows, NN, preferred_element_type=jnp.float32).astype(jnp.bfloat16)


def combine_rows(rows, returned, ids_column, gain, router, experts, capacity):
    slots, one_hot = slots_in_column(ids_column, experts, capacity)
    normed = rms_scale(rows, gain)
    logits = lax.dot_general(normed, router, NT, preferred_element_type=jnp.float32)
    gate = jax.nn.sigmoid(jnp.sum(logits * one_hot, axis=1, keepdims=True))
    places = lax.broadcasted_iota(jnp.int32, (rows.shape[0], experts * capacity), 1)
    pick = (places == slots).astype(jnp.float32).astype(jnp.bfloat16)
    mixed = lax.dot_general(pick, returned, NN, preferred_element_type=jnp.float32)
    return (rows.astype(jnp.float32) + gate * mixed).astype(jnp.bfloat16)


def dispatch(rows, ids_row, experts, capacity):
    def kernel(rows_ref, ids_ref, out_ref):
        out_ref[...] = scatter_rows(rows_ref[...], ids_ref[...], experts, capacity)

    shape = jax.ShapeDtypeStruct((experts * capacity, rows.shape[1]), jnp.bfloat16)
    return call(
        kernel, shape, 1 << 27, 1 << 20, in_specs=[vmem_spec()] * 2, out_specs=vmem_spec()
    )(rows, ids_row)


def run_expert(received, gain, own_in, own_out, other_in, other_out, pick_own):
    def kernel(pick_ref, received_ref, gain_ref, in_a, out_a, in_b, out_b, out_ref):
        def work(weight_in, weight_out):
            normed = rms_scale(received_ref[...], gain_ref[...])
            hidden = lax.dot_general(normed, weight_in[...], NN, preferred_element_type=jnp.float32)
            active = (hidden / (1.0 + jnp.exp(-hidden))).astype(jnp.bfloat16)
            out_ref[...] = lax.dot_general(
                active, weight_out[...], NN, preferred_element_type=jnp.float32
            ).astype(jnp.bfloat16)

        @pl.when(pick_ref[0] == 1)
        def _():
            work(in_a, out_a)

        @pl.when(pick_ref[0] != 1)
        def _():
            work(in_b, out_b)

    shape = jax.ShapeDtypeStruct(received.shape, jnp.bfloat16)
    return call(
        kernel,
        shape,
        4 * received.size * own_in.shape[1],
        4 << 20,
        in_specs=[smem_spec()] + [vmem_spec()] * 6,
        out_specs=vmem_spec(),
    )(pick_own, received, gain, own_in, own_out, other_in, other_out)


def combine_and_dispatch(rows, returned, ids_column, gain, router, next_ids_row, experts, capacity):
    def kernel(rows_ref, returned_ref, ids_ref, gain_ref, router_ref, next_ref, x_ref, out_ref):
        mixed = combine_rows(
            rows_ref[...],
            returned_ref[...],
            ids_ref[...],
            gain_ref[...],
            router_ref[...],
            experts,
            capacity,
        )
        x_ref[...] = mixed
        out_ref[...] = scatter_rows(mixed, next_ref[...], experts, capacity)

    shapes = (
        jax.ShapeDtypeStruct(rows.shape, jnp.bfloat16),
        jax.ShapeDtypeStruct(returned.shape, jnp.bfloat16),
    )
    return call(
        kernel,
        shapes,
        1 << 28,
        2 << 20,
        in_specs=[vmem_spec()] * 6,
        out_specs=(vmem_spec(), vmem_spec()),
    )(rows, returned, ids_column, gain, router, next_ids_row)


def combine_and_norm(
    rows, returned, ids_column, gain, router, head_gain, experts, capacity, copies
):
    def kernel(rows_ref, returned_ref, ids_ref, gain_ref, router_ref, head_ref, out_ref):
        final = combine_rows(
            rows_ref[...],
            returned_ref[...],
            ids_ref[...],
            gain_ref[...],
            router_ref[...],
            experts,
            capacity,
        )
        normed = rms_scale(final, head_ref[...])
        for copy in range(copies):
            out_ref[copy] = normed

    shape = jax.ShapeDtypeStruct((copies,) + rows.shape, jnp.bfloat16)
    return call(
        kernel, shape, 1 << 28, 4 << 20, in_specs=[vmem_spec()] * 6, out_specs=vmem_spec()
    )(rows, returned, ids_column, gain, router, head_gain)


def head_logits(rows, weight, label_weight, frame_count, copies):
    row_count, width = rows.shape
    shard = weight.shape[0]
    blocks = -(-shard // BLOCK_ROWS)
    utterances = label_weight.shape[0] // COLS

    def kernel(rows_ref, weight_ref, label_ref, logits_ref, stats_ref, peak_ref, total_ref):
        step = pl.program_id(0)
        logits = lax.dot_general(
            weight_ref[...], rows_ref[...], NT, preferred_element_type=jnp.float32
        )
        entry = step * BLOCK_ROWS + lax.broadcasted_iota(jnp.int32, logits.shape, 0)
        logits = jnp.where(entry < shard, logits, LOG_ZERO)
        logits_ref[...] = logits

        @pl.when(step == 0)
        def _():
            peak_ref[...] = jnp.full(peak_ref.shape, LOG_ZERO, jnp.float32)
            total_ref[...] = jnp.zeros(total_ref.shape, jnp.float32)

        before = peak_ref[...]
        peak = jnp.maximum(before, jnp.max(logits, axis=0, keepdims=True))
        total_ref[...] = total_ref[...] * jnp.exp(before - peak) + jnp.sum(
            jnp.exp(logits - peak), axis=0, keepdims=True
        )
        peak_ref[...] = peak

        @pl.when(step == blocks - 1)
        def _():
            crossed = lax.dot_general(
                label_ref[...], rows_ref[...], NT, preferred_element_type=jnp.float32
            )
            owner = lax.broadcasted_iota(jnp.int32, (COLS, row_count), 1) // frame_count
            picked = jnp.zeros((COLS, row_count), jnp.float32)
            for utterance in range(utterances):
                part = crossed[utterance * COLS : (utterance + 1) * COLS]
                picked = picked + jnp.where(owner == utterance, part, 0.0)
            place = lax.broadcasted_iota(jnp.int32, (COLS, row_count), 0)
            stats = jnp.where(place == COLS - 3, peak_ref[...], picked)
            stats = jnp.where(place == COLS - 2, total_ref[...], stats)
            for copy in range(copies):
                stats_ref[copy] = stats

    shapes = (
        jax.ShapeDtypeStruct((blocks * BLOCK_ROWS, row_count), jnp.float32),
        jax.ShapeDtypeStruct((copies, COLS, row_count), jnp.float32),
    )
    return call(
        kernel,
        shapes,
        2 * blocks * BLOCK_ROWS * row_count * width,
        14 << 20,
        grid=(blocks,),
        in_specs=[
            pl.BlockSpec((row_count, width), lambda i: (0, 0)),
            pl.BlockSpec((BLOCK_ROWS, width), lambda i: (i, 0)),
            pl.BlockSpec(label_weight.shape, lambda i: (0, 0)),
        ],
        out_specs=(
            pl.BlockSpec((BLOCK_ROWS, row_count), lambda i: (i, 0)),
            pl.BlockSpec((copies, COLS, row_count), lambda i: (0, 0, 0)),
        ),
        scratch_shapes=[
            pltpu.VMEM((1, row_count), jnp.float32),
            pltpu.VMEM((1, row_count), jnp.float32),
        ],
    )(rows, weight, label_weight)


def log_add(first, second):
    peak = jnp.maximum(first, second)
    return peak + jnp.log(jnp.exp(first - peak) + jnp.exp(second - peak))


def log_add3(first, second, third):
    peak = jnp.maximum(jnp.maximum(first, second), third)
    return peak + jnp.log(
        jnp.exp(first - peak) + jnp.exp(second - peak) + jnp.exp(third - peak)
    )


def ctc_pass(stats, labels, frame_counts, label_counts, frame_count, label_max):
    sources, _, row_count = stats.shape
    utterances = labels.shape[0]

    def kernel(
        stats_ref,
        labels_ref,
        frames_ref,
        counts_ref,
        out_ref,
        loss_ref,
        emission_ref,
        blank_fwd,
        label_fwd,
        blank_bwd,
        label_bwd,
        occupancy_ref,
    ):
        joined = stats_ref[0]
        peak = stats_ref[0, COLS - 3 : COLS - 2]
        for source in range(1, sources):
            joined = joined + stats_ref[source]
            peak = jnp.maximum(peak, stats_ref[source, COLS - 3 : COLS - 2])
        total = jnp.zeros((1, row_count), jnp.float32)
        for source in range(sources):
            total = total + stats_ref[source, COLS - 2 : COLS - 1] * jnp.exp(
                stats_ref[source, COLS - 3 : COLS - 2] - peak
            )
        log_total = peak + jnp.log(total)
        emission = joined - log_total
        wide = jnp.concatenate(
            [emission, jnp.zeros((128 - COLS, row_count), jnp.float32)], axis=0
        )
        emission_ref[...] = jnp.transpose(wide, (1, 0))

        lane = lax.broadcasted_iota(jnp.int32, (utterances, 128), 1)
        is_label = lane < label_max
        is_blank = lane <= label_max
        names = labels_ref[...]
        earlier = pltpu.roll(names, 1, 1)
        skip = is_label & (lane >= 1) & (names != 0) & (names != earlier)
        later = pltpu.roll(names, 127, 1)
        skip_next = (lane < label_max - 1) & (later != 0) & (later != names)
        frames = frames_ref[...]
        counts = counts_ref[...]
        lowest = jnp.full((utterances, 128), LOG_ZERO, jnp.float32)
        ends_blank = jnp.where(lane == counts, 0.0, LOG_ZERO)
        ends_label = jnp.where(lane == counts - 1, 0.0, LOG_ZERO)

        def emitted(step):
            row = emission_ref[pl.ds(step, utterances, stride=frame_count), :]
            blank = jnp.sum(jnp.where(lane == label_max, row, 0.0), axis=1, keepdims=True)
            return (
                jnp.where(is_blank, blank, LOG_ZERO),
                jnp.where(is_label, row, LOG_ZERO),
            )

        def advance(step, carry):
            fwd_blank, fwd_label, bwd_blank, bwd_label = carry
            emit_blank, emit_label = emitted(step)
            moved = jnp.where(lane == 0, LOG_ZERO, pltpu.roll(fwd_label, 1, 1))
            new_blank = log_add(fwd_blank, moved) + emit_blank
            new_label = (
                log_add3(fwd_label, fwd_blank, jnp.where(skip, moved, LOG_ZERO)) + emit_label
            )
            start_blank = jnp.where(lane == 0, emit_blank, LOG_ZERO)
            start_label = jnp.where(lane == 0, emit_label, LOG_ZERO)
            first = step == 0
            new_blank = jnp.where(first, start_blank, new_blank)
            new_label = jnp.where(first, start_label, new_label)
            alive = step < frames
            fwd_blank = jnp.where(alive, jnp.where(is_blank, new_blank, LOG_ZERO), fwd_blank)
            fwd_label = jnp.where(alive, jnp.where(is_label, new_label, LOG_ZERO), fwd_label)
            blank_fwd[step] = fwd_blank
            label_fwd[step] = fwd_label

            back = frame_count - 1 - step
            emit_blank, emit_label = emitted(jnp.minimum(back + 1, frame_count - 1))
            out_blank = bwd_blank + emit_blank
            out_label = bwd_label + emit_label
            next_blank = pltpu.roll(out_blank, 127, 1)
            next_label = jnp.where(skip_next, pltpu.roll(out_label, 127, 1), LOG_ZERO)
            new_blank = log_add(out_blank, out_label)
            new_label = log_add3(out_label, next_blank, next_label)
            last = back == frames - 1
            inside = back < frames - 1
            bwd_blank = jnp.where(last, ends_blank, jnp.where(inside, new_blank, LOG_ZERO))
            bwd_label = jnp.where(last, ends_label, jnp.where(inside, new_label, LOG_ZERO))
            bwd_blank = jnp.where(is_blank, bwd_blank, LOG_ZERO)
            bwd_label = jnp.where(is_label, bwd_label, LOG_ZERO)
            blank_bwd[back] = bwd_blank
            label_bwd[back] = bwd_label
            return (fwd_blank, fwd_label, bwd_blank, bwd_label)

        fwd_blank, fwd_label, _, _ = lax.fori_loop(
            0, frame_count, advance, (lowest, lowest, lowest, lowest)
        )
        end_state = jnp.sum(jnp.where(lane == counts, fwd_blank, 0.0), axis=1, keepdims=True)
        near_state = jnp.sum(jnp.where(lane == counts - 1, fwd_label, 0.0), axis=1, keepdims=True)
        log_like = log_add(end_state, near_state)
        loss_ref[...] = jnp.broadcast_to(-log_like, (utterances, 128))

        def occupy(step, carry):
            alive = step < frames
            blank = jnp.exp(blank_fwd[step] + blank_bwd[step] - log_like)
            label = jnp.exp(label_fwd[step] + label_bwd[step] - log_like)
            blank = jnp.sum(jnp.where(is_blank, blank, 0.0), axis=1, keepdims=True)
            label = jnp.where(is_label, label, 0.0)
            whole = blank + jnp.sum(label, axis=1, keepdims=True)
            filled = jnp.where(lane == label_max, blank, label)
            filled = jnp.where(lane == COLS - 3, whole, filled)
            occupancy_ref[pl.ds(step, utterances, stride=frame_count), :] = jnp.where(
                alive, -filled, 0.0
            )
            return carry

        lax.fori_loop(0, frame_count, occupy, 0, unroll=8)
        turned = jnp.transpose(occupancy_ref[...], (1, 0))[:COLS]
        place = lax.broadcasted_iota(jnp.int32, (COLS, row_count), 0)
        out_ref[...] = jnp.where(place == COLS - 2, log_total, turned)

    held = pltpu.VMEM((frame_count, utterances, 128), jnp.float32)
    return call(
        kernel,
        (
            jax.ShapeDtypeStruct((COLS, row_count), jnp.float32),
            jax.ShapeDtypeStruct((utterances, 128), jnp.float32),
        ),
        1 << 26,
        1 << 20,
        in_specs=[vmem_spec()] * 4,
        out_specs=(vmem_spec(), vmem_spec()),
        scratch_shapes=[
            pltpu.VMEM((row_count, 128), jnp.float32),
            held,
            held,
            held,
            held,
            pltpu.VMEM((row_count, 128), jnp.float32),
        ],
    )(stats, labels, frame_counts, label_counts)


def head_gradient(logits, rows, occupancy, places, shard, frame_count, first_block, blocks):
    row_count, width = rows.shape
    entries = places.shape[1]

    def kernel(
        first_ref, logits_ref, rows_ref, occupancy_ref, places_ref, out_ref, high_ref, low_ref
    ):
        step = pl.program_id(0)

        @pl.when(step == 0)
        def _():
            lane_owner = lax.broadcasted_iota(jnp.int32, (COLS, row_count), 1) // frame_count
            place = lax.broadcasted_iota(jnp.int32, (COLS, row_count), 0)
            source = jnp.where(place < COLS - 3, occupancy_ref[...], 0.0)
            for utterance in range(entries // COLS):
                part = jnp.where(lane_owner == utterance, source, 0.0)
                high = part.astype(jnp.bfloat16)
                low = (part - high.astype(jnp.float32)).astype(jnp.bfloat16)
                high_ref[utterance * COLS : (utterance + 1) * COLS] = high
                low_ref[utterance * COLS : (utterance + 1) * COLS] = low

        entry = (first_ref[0] + step) * BLOCK_ROWS + lax.broadcasted_iota(
            jnp.int32, (BLOCK_ROWS, entries), 0
        )
        select = (entry == places_ref[...]).astype(jnp.float32).astype(jnp.bfloat16)
        scattered = lax.dot_general(
            select, high_ref[...], NN, preferred_element_type=jnp.float32
        ) + lax.dot_general(select, low_ref[...], NN, preferred_element_type=jnp.float32)
        whole = occupancy_ref[COLS - 3 : COLS - 2]
        log_total = occupancy_ref[COLS - 2 : COLS - 1]
        grad = scattered - jnp.exp(logits_ref[...] - log_total) * whole
        out_ref[...] = lax.dot_general(
            grad.astype(jnp.bfloat16), rows_ref[...], NN, preferred_element_type=jnp.float32
        ).astype(jnp.bfloat16)

    return call(
        kernel,
        jax.ShapeDtypeStruct((blocks * BLOCK_ROWS, width), jnp.bfloat16),
        2 * blocks * BLOCK_ROWS * row_count * (width + 2 * entries),
        10 << 20,
        grid_spec=pltpu.PrefetchScalarGridSpec(
            num_scalar_prefetch=1,
            grid=(blocks,),
            in_specs=[
                pl.BlockSpec((BLOCK_ROWS, row_count), lambda i, first: (first[0] + i, 0)),
                pl.BlockSpec((row_count, width), lambda i, first: (0, 0)),
                pl.BlockSpec((COLS, row_count), lambda i, first: (0, 0)),
                pl.BlockSpec((1, entries), lambda i, first: (0, 0)),
            ],
            out_specs=pl.BlockSpec((BLOCK_ROWS, width), lambda i, first: (i, 0)),
            scratch_shapes=[
                pltpu.VMEM((entries, row_count), jnp.bfloat16),
                pltpu.VMEM((entries, row_count), jnp.bfloat16),
            ],
        ),
    )(first_block, logits, rows, occupancy, places)


def swap(value, axis):
    return lax.ppermute(value, axis, [(0, 1), (1, 0)])


def per_device(
    frames,
    norm_gain,
    router,
    w_in,
    w_out,
    routing,
    head_gain,
    head_weight,
    frame_lengths,
    labels,
    label_lengths,
):
    sections = lax.axis_size("section")
    section_id = lax.axis_index("section")
    group_size = lax.axis_size("expert")
    member = lax.axis_index("expert")
    outer_size = lax.axis_size("dpo")
    inner_size = lax.axis_size("dpi")
    micro, utt_dev, frame_count, width = frames.shape
    label_max = labels.shape[2]
    tokens = utt_dev * frame_count
    experts = w_in.shape[1] * group_size
    pair_count = micro * utt_dev
    per_section = pair_count // sections
    row_count = per_section * frame_count
    first_pair = section_id * per_section
    share = (tokens * 9 + 8 * experts - 1) // (8 * experts)
    capacity = round_up(share * -(-row_count // tokens), 8)
    paired = sections == 2

    own_routes = routing.reshape(1, micro * tokens)
    own_table = jnp.concatenate(
        [norm_gain, jnp.transpose(router[0]).astype(jnp.float32)], axis=0
    )
    if paired:
        other_routes = swap(own_routes, "section")
        other_table = swap(own_table, "section")
        other_in = swap(w_in[0, 0], "section")
        other_out = swap(w_out[0, 0], "section")

    def of_layer(layer):
        if paired:
            mine = section_id == layer
            routes = jnp.where(mine, own_routes, other_routes)
            table = jnp.where(mine, own_table, other_table)
            weights = (w_in[0, 0], w_out[0, 0], other_in, other_out)
            return routes, table, weights, mine.astype(jnp.int32).reshape(1)
        routes = lax.all_gather(own_routes, "section")[layer]
        table = lax.all_gather(own_table, "section")[layer]
        weight_in = lax.all_gather(w_in[0, 0], "section")[layer]
        weight_out = lax.all_gather(w_out[0, 0], "section")[layer]
        weights = (weight_in, weight_out, weight_in, weight_out)
        return routes, table, weights, jnp.ones((1,), jnp.int32)

    layers = []
    for layer in range(sections):
        routes, table, weights, pick_own = of_layer(layer)
        ids = lax.dynamic_slice(routes, (0, section_id * row_count), (1, row_count))
        layers.append(
            (
                ids,
                ids.reshape(row_count, 1),
                table[:1],
                jnp.pad(table[1:], ((0, 128 - experts), (0, 0))).astype(jnp.bfloat16),
                weights,
                pick_own,
            )
        )

    def exchange(buffer):
        count = buffer.shape[0] // group_size
        split = buffer.reshape(group_size, count, width)
        moved = lax.all_to_all(split, "expert", split_axis=0, concat_axis=0, tiled=True)
        return moved.reshape(buffer.shape)

    current = lax.dynamic_slice_in_dim(
        frames.reshape(pair_count * frame_count, width), section_id * row_count, row_count, 0
    )
    outgoing = dispatch(current, layers[0][0], experts, capacity)

    notes = jnp.concatenate(
        [
            lax.dynamic_slice_in_dim(
                labels.reshape(pair_count, label_max), first_pair, per_section, 0
            ),
            lax.dynamic_slice_in_dim(
                jnp.stack(
                    [frame_lengths.reshape(pair_count), label_lengths.reshape(pair_count)], axis=1
                ),
                first_pair,
                per_section,
                0,
            ),
        ],
        axis=1,
    )
    notes = notes.reshape(1, -1)
    notes_all = lax.all_to_all(
        jnp.broadcast_to(notes, (group_size, notes.shape[1])),
        "expert",
        split_axis=0,
        concat_axis=0,
        tiled=True,
    ).reshape(group_size * per_section, label_max + 2)
    labels_all = notes_all[:, :label_max]
    frames_all = notes_all[:, label_max : label_max + 1]
    counts_all = notes_all[:, label_max + 1 :]
    utterances = group_size * per_section
    shard = head_weight.shape[1]
    weight_rows = jnp.transpose(head_weight)
    named = jnp.concatenate(
        [
            labels_all,
            jnp.zeros((utterances, 1), jnp.int32),
            jnp.full((utterances, COLS - label_max - 1), -1, jnp.int32),
        ],
        axis=1,
    ).reshape(utterances * COLS)
    local = named - member * shard
    held = (named >= 0) & (local >= 0) & (local < shard)
    places = jnp.where(held, local, -1)
    label_weight = jnp.where(
        held[:, None], weight_rows[jnp.clip(local, 0, shard - 1)], jnp.zeros((), jnp.bfloat16)
    )

    for layer in range(sections):
        ids_row, ids_column, gain, router_rows, weights, pick_own = layers[layer]
        received = exchange(outgoing)
        returned = exchange(run_expert(received, gain, *weights, pick_own))
        if layer < sections - 1:
            current, outgoing = combine_and_dispatch(
                current,
                returned,
                ids_column,
                gain,
                router_rows,
                layers[layer + 1][0],
                experts,
                capacity,
            )
        else:
            spread = combine_and_norm(
                current,
                returned,
                ids_column,
                gain,
                router_rows,
                head_gain.reshape(1, width),
                experts,
                capacity,
                group_size,
            )
    rows = lax.all_to_all(spread, "expert", split_axis=0, concat_axis=0, tiled=True).reshape(
        group_size * row_count, width
    )
    logits, stats = head_logits(rows, weight_rows, label_weight, frame_count, group_size)
    stats = lax.all_to_all(stats, "expert", split_axis=0, concat_axis=0, tiled=True)
    occupancy, losses = ctc_pass(
        stats,
        jnp.pad(labels_all, ((0, 0), (0, 128 - label_max))),
        frames_all,
        counts_all,
        frame_count,
        label_max,
    )
    my_losses = lax.dynamic_slice(losses, (member * per_section, 0), (per_section, 1))
    blocks = logits.shape[0] // BLOCK_ROWS
    gradient = functools.partial(
        head_gradient,
        logits,
        rows,
        occupancy,
        places.reshape(1, -1),
        shard,
        frame_count,
    )
    chips = sections * outer_size
    if inner_size == 2 and chips == 4 and blocks % 8 == 0:
        core = lax.axis_index("dpi")
        half = blocks // 2
        sent = gradient(((1 - core) * half).reshape(1), half)
        kept = gradient((core * half).reshape(1), half)
        arrived = swap(sent, "dpi")
        summed = (kept.astype(jnp.float32) + arrived.astype(jnp.float32)).astype(jnp.bfloat16)
        half_rows = half * BLOCK_ROWS
        quarters = lax.all_to_all(
            summed.reshape(chips, half_rows // chips, width),
            ("section", "dpo"),
            split_axis=0,
            concat_axis=0,
            tiled=True,
        )
        total = jnp.sum(quarters.astype(jnp.float32), axis=0).astype(jnp.bfloat16)
        mine = lax.all_to_all(
            jnp.broadcast_to(total, quarters.shape),
            ("section", "dpo"),
            split_axis=0,
            concat_axis=0,
            tiled=True,
        ).reshape(half_rows, width)
        theirs = swap(mine, "dpi")
        lower = jnp.where(core == 0, mine, theirs)
        upper = jnp.where(core == 0, theirs, mine)
        whole = jnp.concatenate([lower, upper], axis=0)[:shard]
    else:
        partial = gradient(jnp.zeros((1,), jnp.int32), blocks)[:shard]
        whole = lax.psum(partial.astype(jnp.float32), ("section", "dpo", "dpi")).astype(
            jnp.bfloat16
        )
    return (my_losses, jnp.transpose(whole))


def solution(mesh):
    sections, group_size, spread = (mesh.shape[name] for name in ("section", "expert", "dp"))
    inner = 2 if spread % 2 == 0 else 1
    split = Mesh(
        mesh.devices.reshape(sections, group_size, spread // inner, inner),
        ("section", "expert", "dpo", "dpi"),
    )
    block = ("expert", "dpo", "dpi")
    placed = (
        P(None, block, None, None),
        P("section", None),
        P("section", None, None),
        P("section", "expert", None, None),
        P("section", "expert", None, None),
        P("section", None, block, None, None),
        P(),
        P(None, "expert"),
        P(None, block),
        P(None, block, None),
        P(None, block),
    )
    return jax.shard_map(
        per_device,
        mesh=split,
        in_specs=placed,
        out_specs=(P("section", block), P(None, "expert")),
        check_vma=False,
    )
```

```python
import jax
import jax.numpy as jnp
import numpy as np
from jax import lax
from jax.experimental import pallas as pl
from jax.experimental.pallas import tpu as pltpu
from jax.sharding import Mesh, PartitionSpec as P

EPSILON = 1e-06
LOG_ZERO = -1e30
VMEM_LIMIT = 24 * 1024 * 1024
LANES = 128
COLS = 16
PEAK, TOTAL, WHOLE = COLS - 3, COLS - 2, COLS - 3
BLOCK_ROWS = 256
NT = (((1,), (1,)), ((), ()))
NN = (((1,), (0,)), ((), ()))


def round_up(value, unit):
    return -(-value // unit) * unit


def vmem_spec():
    return pl.BlockSpec(memory_space=pltpu.VMEM)


def smem_spec():
    return pl.BlockSpec(memory_space=pltpu.SMEM)


def call(kernel, out_shape, flops=0, moved=0, **options):
    return pl.pallas_call(
        kernel,
        out_shape=out_shape,
        compiler_params=pltpu.CompilerParams(vmem_limit_bytes=VMEM_LIMIT),
        cost_estimate=pl.CostEstimate(flops=flops, bytes_accessed=moved, transcendentals=0),
        **options,
    )


def bf16_rows(count, width):
    return jax.ShapeDtypeStruct((count, width), jnp.bfloat16)


def as_mask(values):
    return values.astype(jnp.float32).astype(jnp.bfloat16)


def rms_scale(values, gain):
    values = values.astype(jnp.float32)
    scale = lax.rsqrt(jnp.mean(values * values, axis=-1, keepdims=True) + EPSILON)
    return (values * scale * gain).astype(jnp.bfloat16)


def expert_column(ids, frame_count):
    pairs = ids.shape[0]
    square = jnp.concatenate(
        [ids.astype(jnp.float32), jnp.full((LANES - pairs, LANES), -1.0, jnp.float32)], axis=0
    )
    turned = jnp.transpose(square, (1, 0)).astype(jnp.int32)
    return jnp.concatenate([turned[:frame_count, p : p + 1] for p in range(pairs)], axis=0)


def placement(column, member, experts, capacity):
    count = column.shape[0]
    shifted = column - member
    relative = jnp.where(shifted < 0, shifted + experts, shifted)
    lane = lax.broadcasted_iota(jnp.int32, (count, LANES), 1)
    one_hot = (lane == relative).astype(jnp.float32)
    before = lax.broadcasted_iota(jnp.int32, (count, count), 1) <= lax.broadcasted_iota(
        jnp.int32, (count, count), 0
    )
    rank = lax.dot_general(
        as_mask(before), one_hot.astype(jnp.bfloat16), NN, preferred_element_type=jnp.float32
    )
    start = (lane * capacity - 1).astype(jnp.float32)
    slots = jnp.sum(one_hot * (rank + start), axis=1, keepdims=True).astype(jnp.int32)
    places = lax.broadcasted_iota(jnp.int32, (count, experts * capacity), 1)
    return (places == slots).astype(jnp.float32)


def scatter_rows(rows, ids, member, experts, capacity, frame_count, out_refs):
    count = rows.shape[0]
    chosen = placement(expert_column(ids, frame_count), member, experts, capacity)
    tall = round_up(count, LANES)
    if tall > count:
        chosen = jnp.concatenate(
            [chosen, jnp.zeros((tall - count, chosen.shape[1]), jnp.float32)], axis=0
        )
    pick = jnp.transpose(chosen, (1, 0))[:, :count].astype(jnp.bfloat16)
    placed = lax.dot_general(pick, rows, NN, preferred_element_type=jnp.float32).astype(
        jnp.bfloat16
    )
    for turn, out_ref in enumerate(out_refs):
        out_ref[...] = placed[turn * capacity : (turn + 1) * capacity]


def combine_rows(rows, returned, ids, table, member, experts, capacity, frame_count):
    column = expert_column(ids, frame_count)
    pick = placement(column, member, experts, capacity).astype(jnp.bfloat16)
    normed = rms_scale(rows, table[:1])
    router = jnp.concatenate(
        [table[8:], jnp.zeros((LANES + 8 - table.shape[0], rows.shape[1]), jnp.float32)], axis=0
    ).astype(jnp.bfloat16)
    logits = lax.dot_general(normed, router, NT, preferred_element_type=jnp.float32)
    lane = lax.broadcasted_iota(jnp.int32, logits.shape, 1)
    gate = jax.nn.sigmoid(jnp.sum(jnp.where(lane == column, logits, 0.0), axis=1, keepdims=True))
    stacked = jnp.concatenate(returned, axis=0)
    mixed = lax.dot_general(pick, stacked, NN, preferred_element_type=jnp.float32)
    return (rows.astype(jnp.float32) + gate * mixed).astype(jnp.bfloat16)


def dispatch(rows, ids, member, experts, capacity, frame_count):
    width = rows.shape[1]

    def kernel(member_ref, rows_ref, ids_ref, *out_refs):
        scatter_rows(
            rows_ref[...], ids_ref[...], member_ref[0], experts, capacity, frame_count, out_refs
        )

    return call(
        kernel,
        tuple(bf16_rows(capacity, width) for _ in range(experts)),
        1 << 27,
        1 << 20,
        in_specs=[smem_spec()] + [vmem_spec()] * 2,
        out_specs=tuple(vmem_spec() for _ in range(experts)),
    )(member, rows, ids)


def run_expert(received, table, own, other, pick_own):
    count = len(received)
    capacity, width = received[0].shape
    others = len(other)

    def kernel(pick_ref, table_ref, in_ref, out_weight_ref, *refs):
        other_refs, received_refs, out_refs = (
            refs[: 2 * others],
            refs[2 * others : 2 * others + count],
            refs[2 * others + count :],
        )

        def work(pieces):
            stacked = jnp.concatenate([ref[...] for ref in received_refs], axis=0)
            normed = rms_scale(stacked, table_ref[:1])
            total = None
            for weight_in, weight_out in pieces:
                hidden = lax.dot_general(
                    normed, weight_in[...], NN, preferred_element_type=jnp.float32
                )
                active = (hidden / (1.0 + jnp.exp(-hidden))).astype(jnp.bfloat16)
                part = lax.dot_general(
                    active, weight_out[...], NN, preferred_element_type=jnp.float32
                )
                total = part if total is None else total + part
            total = total.astype(jnp.bfloat16)
            for turn, out_ref in enumerate(out_refs):
                out_ref[...] = total[turn * capacity : (turn + 1) * capacity]

        if others == 0:
            work([(in_ref, out_weight_ref)])
            return

        @pl.when(pick_ref[0] == 1)
        def _():
            work([(in_ref, out_weight_ref)])

        @pl.when(pick_ref[0] != 1)
        def _():
            work([(other_refs[2 * i], other_refs[2 * i + 1]) for i in range(others)])

    flat = [weight for pair in other for weight in pair]
    return call(
        kernel,
        tuple(bf16_rows(capacity, width) for _ in range(count)),
        4 * count * capacity * width * own[0].shape[1],
        4 << 20,
        in_specs=[smem_spec()] + [vmem_spec()] * (3 + 2 * others + count),
        out_specs=tuple(vmem_spec() for _ in range(count)),
    )(pick_own, table, *own, *flat, *received)


def combine_and_dispatch(
    rows, returned, ids, table, next_ids, member, experts, capacity, frame_count
):
    width = rows.shape[1]

    def kernel(member_ref, rows_ref, ids_ref, table_ref, next_ref, *refs):
        returned_refs, x_ref, out_refs = refs[:experts], refs[experts], refs[experts + 1 :]
        mixed = combine_rows(
            rows_ref[...],
            [ref[...] for ref in returned_refs],
            ids_ref[...],
            table_ref[...],
            member_ref[0],
            experts,
            capacity,
            frame_count,
        )
        x_ref[...] = mixed
        scatter_rows(
            mixed, next_ref[...], member_ref[0], experts, capacity, frame_count, out_refs
        )

    shapes = (bf16_rows(*rows.shape),) + tuple(
        bf16_rows(capacity, width) for _ in range(experts)
    )
    result = call(
        kernel,
        shapes,
        1 << 28,
        2 << 20,
        in_specs=[smem_spec()] + [vmem_spec()] * (4 + experts),
        out_specs=tuple(vmem_spec() for _ in shapes),
    )(member, rows, ids, table, next_ids, *returned)
    return result[0], result[1:]


def combine_and_norm(
    rows, returned, ids, table, head_gain, member, experts, capacity, frame_count
):
    def kernel(member_ref, rows_ref, ids_ref, table_ref, head_ref, *refs):
        final = combine_rows(
            rows_ref[...],
            [ref[...] for ref in refs[:experts]],
            ids_ref[...],
            table_ref[...],
            member_ref[0],
            experts,
            capacity,
            frame_count,
        )
        refs[experts][...] = rms_scale(final, head_ref[...])

    return call(
        kernel,
        bf16_rows(*rows.shape),
        1 << 28,
        2 << 20,
        in_specs=[smem_spec()] + [vmem_spec()] * (4 + experts),
        out_specs=vmem_spec(),
    )(member, rows, ids, table, head_gain, *returned)


def label_rows(weight, places):
    shard, width = weight.shape
    entries = places.shape[0]
    blocks = -(-shard // BLOCK_ROWS)

    def kernel(places_ref, weight_ref, out_ref, total_ref):
        step = pl.program_id(0)
        inside = (
            step * BLOCK_ROWS + lax.broadcasted_iota(jnp.int32, (BLOCK_ROWS, 1), 0) < shard
        )
        entry = step * BLOCK_ROWS + lax.broadcasted_iota(jnp.int32, (entries, BLOCK_ROWS), 1)
        values = jnp.where(inside, weight_ref[...].astype(jnp.float32), 0.0).astype(jnp.bfloat16)
        part = lax.dot_general(
            as_mask(entry == places_ref[...]), values, NN, preferred_element_type=jnp.float32
        )

        @pl.when(step == 0)
        def _():
            total_ref[...] = part

        @pl.when(step > 0)
        def _():
            total_ref[...] += part

        @pl.when(step == blocks - 1)
        def _():
            out_ref[...] = total_ref[...].astype(jnp.bfloat16)

    return call(
        kernel,
        bf16_rows(entries, width),
        2 * blocks * BLOCK_ROWS * entries * width,
        6 << 20,
        grid=(blocks,),
        in_specs=[
            pl.BlockSpec((entries, 1), lambda i: (0, 0)),
            pl.BlockSpec((BLOCK_ROWS, width), lambda i: (i, 0)),
        ],
        out_specs=pl.BlockSpec((entries, width), lambda i: (0, 0)),
        scratch_shapes=[pltpu.VMEM((entries, width), jnp.float32)],
    )(places, weight)


def head_logits(pieces, weight, label_weight, frame_count):
    count = len(pieces)
    span, width = pieces[0].shape
    row_count = count * span
    shard = weight.shape[0]
    blocks = -(-shard // BLOCK_ROWS)
    used = shard - (blocks - 1) * BLOCK_ROWS
    entries = label_weight.shape[0]

    def kernel(weight_ref, label_ref, *refs):
        piece_refs = refs[:count]
        logits_ref, rows_ref, stats_ref, peak_ref, total_ref = refs[count:]
        step = pl.program_id(0)

        @pl.when(step == 0)
        def _():
            for slot in range(count):
                rows_ref[slot * span : (slot + 1) * span] = piece_refs[slot][...]
            peak_ref[...] = jnp.full(peak_ref.shape, LOG_ZERO, jnp.float32)
            total_ref[...] = jnp.zeros(total_ref.shape, jnp.float32)

        logits_ref[...] = lax.dot_general(
            weight_ref[...], rows_ref[...], NT, preferred_element_type=jnp.float32
        )
        if used < BLOCK_ROWS:

            @pl.when(step == blocks - 1)
            def _():
                logits_ref[used:] = jnp.full((BLOCK_ROWS - used, row_count), LOG_ZERO, jnp.float32)

        logits = logits_ref[...]
        before = peak_ref[...]
        peak = jnp.maximum(before, jnp.max(logits, axis=0, keepdims=True))
        total_ref[...] = total_ref[...] * jnp.exp(before - peak) + jnp.sum(
            jnp.exp(logits - peak), axis=0, keepdims=True
        )
        peak_ref[...] = peak

        @pl.when(step == blocks - 1)
        def _():
            crossed = lax.dot_general(
                label_ref[...], rows_ref[...], NT, preferred_element_type=jnp.float32
            )
            owner = lax.broadcasted_iota(jnp.int32, (COLS, row_count), 1) // frame_count
            picked = jnp.zeros((COLS, row_count), jnp.float32)
            for utterance in range(entries // COLS):
                part = crossed[utterance * COLS : (utterance + 1) * COLS]
                picked = picked + jnp.where(owner == utterance, part, 0.0)
            place = lax.broadcasted_iota(jnp.int32, (COLS, row_count), 0)
            stats = jnp.where(place == PEAK, peak_ref[...], picked)
            stats = jnp.where(place == TOTAL, total_ref[...], stats)
            for slot in range(count):
                stats_ref[slot] = stats[:, slot * span : (slot + 1) * span]

    return call(
        kernel,
        (
            jax.ShapeDtypeStruct((blocks * BLOCK_ROWS, row_count), jnp.float32),
            bf16_rows(row_count, width),
            jax.ShapeDtypeStruct((count, COLS, span), jnp.float32),
        ),
        2 * blocks * BLOCK_ROWS * row_count * width,
        9 << 20,
        grid=(blocks,),
        in_specs=[
            pl.BlockSpec((BLOCK_ROWS, width), lambda i: (i, 0)),
            pl.BlockSpec((entries, width), lambda i: (0, 0)),
        ]
        + [pl.BlockSpec((span, width), lambda i: (0, 0))] * count,
        out_specs=(
            pl.BlockSpec((BLOCK_ROWS, row_count), lambda i: (i, 0)),
            pl.BlockSpec((row_count, width), lambda i: (0, 0)),
            pl.BlockSpec((count, COLS, span), lambda i: (0, 0, 0)),
        ),
        scratch_shapes=[
            pltpu.VMEM((1, row_count), jnp.float32),
            pltpu.VMEM((1, row_count), jnp.float32),
        ],
    )(weight, label_weight, *pieces)


def log_add(first, second):
    peak = jnp.maximum(first, second)
    return peak + jnp.log(jnp.exp(first - peak) + jnp.exp(second - peak))


def log_add3(first, second, third):
    peak = jnp.maximum(jnp.maximum(first, second), third)
    return peak + jnp.log(
        jnp.exp(first - peak) + jnp.exp(second - peak) + jnp.exp(third - peak)
    )


def ctc_pass(stats, slots, labels, frame_counts, label_counts, frame_count, label_max):
    sources = len(stats)
    count, _, span = stats[0].shape
    row_count = count * span
    utterances = labels.shape[0]
    entries = utterances * COLS

    def kernel(slots_ref, labels_ref, frames_ref, counts_ref, *refs):
        stats_refs = refs[:sources]
        (
            out_ref,
            high_ref,
            low_ref,
            loss_ref,
            turn_ref,
            emission_ref,
            blank_fwd,
            label_fwd,
            blank_bwd,
            label_bwd,
            occupancy_ref,
        ) = refs[sources:]
        place = lax.broadcasted_iota(jnp.int32, (COLS, span), 0)
        turn_ref[...] = jnp.zeros(turn_ref.shape, jnp.float32)
        for slot in range(count):
            found = [stats_refs[k][slots_ref[k * count + slot]] for k in range(sources)]
            joined = found[0]
            peak = found[0][PEAK : PEAK + 1]
            for part in found[1:]:
                joined = joined + part
                peak = jnp.maximum(peak, part[PEAK : PEAK + 1])
            total = jnp.zeros((1, span), jnp.float32)
            for part in found:
                total = total + part[TOTAL : TOTAL + 1] * jnp.exp(part[PEAK : PEAK + 1] - peak)
            log_total = peak + jnp.log(total)
            turn_ref[:COLS, :span] = jnp.where(place == TOTAL, log_total, joined - log_total)
            emission_ref[slot * span : (slot + 1) * span] = jnp.transpose(turn_ref[...], (1, 0))[
                :span
            ]

        lane = lax.broadcasted_iota(jnp.int32, (utterances, 128), 1)
        is_label = lane < label_max
        is_blank = lane <= label_max
        names = labels_ref[...]
        earlier = pltpu.roll(names, 1, 1)
        skip = is_label & (lane >= 1) & (names != 0) & (names != earlier)
        later = pltpu.roll(names, 127, 1)
        skip_next = (lane < label_max - 1) & (later != 0) & (later != names)
        frames = frames_ref[...]
        counts = counts_ref[...]
        lowest = jnp.full((utterances, 128), LOG_ZERO, jnp.float32)
        ends_blank = jnp.where(lane == counts, 0.0, LOG_ZERO)
        ends_label = jnp.where(lane == counts - 1, 0.0, LOG_ZERO)

        def emitted(step):
            row = emission_ref[pl.ds(step, utterances, stride=frame_count), :]
            blank = jnp.sum(jnp.where(lane == label_max, row, 0.0), axis=1, keepdims=True)
            return (
                jnp.where(is_blank, blank, LOG_ZERO),
                jnp.where(is_label, row, LOG_ZERO),
            )

        def advance(step, carry):
            fwd_blank, fwd_label, bwd_blank, bwd_label = carry
            emit_blank, emit_label = emitted(step)
            moved = jnp.where(lane == 0, LOG_ZERO, pltpu.roll(fwd_label, 1, 1))
            new_blank = log_add(fwd_blank, moved) + emit_blank
            new_label = (
                log_add3(fwd_label, fwd_blank, jnp.where(skip, moved, LOG_ZERO)) + emit_label
            )
            start_blank = jnp.where(lane == 0, emit_blank, LOG_ZERO)
            start_label = jnp.where(lane == 0, emit_label, LOG_ZERO)
            first = step == 0
            new_blank = jnp.where(first, start_blank, new_blank)
            new_label = jnp.where(first, start_label, new_label)
            alive = step < frames
            fwd_blank = jnp.where(alive, jnp.where(is_blank, new_blank, LOG_ZERO), fwd_blank)
            fwd_label = jnp.where(alive, jnp.where(is_label, new_label, LOG_ZERO), fwd_label)
            blank_fwd[step] = fwd_blank
            label_fwd[step] = fwd_label

            back = frame_count - 1 - step
            emit_blank, emit_label = emitted(jnp.minimum(back + 1, frame_count - 1))
            out_blank = bwd_blank + emit_blank
            out_label = bwd_label + emit_label
            next_blank = pltpu.roll(out_blank, 127, 1)
            next_label = jnp.where(skip_next, pltpu.roll(out_label, 127, 1), LOG_ZERO)
            new_blank = log_add(out_blank, out_label)
            new_label = log_add3(out_label, next_blank, next_label)
            last = back == frames - 1
            inside = back < frames - 1
            bwd_blank = jnp.where(last, ends_blank, jnp.where(inside, new_blank, LOG_ZERO))
            bwd_label = jnp.where(last, ends_label, jnp.where(inside, new_label, LOG_ZERO))
            bwd_blank = jnp.where(is_blank, bwd_blank, LOG_ZERO)
            bwd_label = jnp.where(is_label, bwd_label, LOG_ZERO)
            blank_bwd[back] = bwd_blank
            label_bwd[back] = bwd_label
            return (fwd_blank, fwd_label, bwd_blank, bwd_label)

        fwd_blank, fwd_label, _, _ = lax.fori_loop(
            0, frame_count, advance, (lowest, lowest, lowest, lowest)
        )
        end_state = jnp.sum(jnp.where(lane == counts, fwd_blank, 0.0), axis=1, keepdims=True)
        near_state = jnp.sum(jnp.where(lane == counts - 1, fwd_label, 0.0), axis=1, keepdims=True)
        log_like = log_add(end_state, near_state)
        loss_ref[...] = jnp.broadcast_to(-log_like, (utterances, 128))

        def occupy(step, carry):
            alive = step < frames
            blank = jnp.exp(blank_fwd[step] + blank_bwd[step] - log_like)
            label = jnp.exp(label_fwd[step] + label_bwd[step] - log_like)
            blank = jnp.sum(jnp.where(is_blank, blank, 0.0), axis=1, keepdims=True)
            label = jnp.where(is_label, label, 0.0)
            whole = blank + jnp.sum(label, axis=1, keepdims=True)
            filled = jnp.where(lane == label_max, blank, label)
            filled = jnp.where(lane == WHOLE, whole, filled)
            filled = jnp.where(alive, -filled, 0.0)
            row = emission_ref[pl.ds(step, utterances, stride=frame_count), :]
            occupancy_ref[pl.ds(step, utterances, stride=frame_count), :] = jnp.where(
                lane == TOTAL, row, filled
            )
            return carry

        lax.fori_loop(0, frame_count, occupy, 0, unroll=8)
        turned = jnp.transpose(occupancy_ref[...], (1, 0))[:COLS]
        out_ref[...] = turned
        row_place = lax.broadcasted_iota(jnp.int32, (COLS, row_count), 0)
        owner = lax.broadcasted_iota(jnp.int32, (COLS, row_count), 1) // frame_count
        source = jnp.where(row_place < WHOLE, turned, 0.0)
        for utterance in range(utterances):
            part = jnp.where(owner == utterance, source, 0.0)
            high = part.astype(jnp.bfloat16)
            high_ref[utterance * COLS : (utterance + 1) * COLS] = high
            low_ref[utterance * COLS : (utterance + 1) * COLS] = (
                part - high.astype(jnp.float32)
            ).astype(jnp.bfloat16)

    held = pltpu.VMEM((frame_count, utterances, 128), jnp.float32)
    return call(
        kernel,
        (
            jax.ShapeDtypeStruct((COLS, row_count), jnp.float32),
            bf16_rows(entries, row_count),
            bf16_rows(entries, row_count),
            jax.ShapeDtypeStruct((utterances, 128), jnp.float32),
        ),
        1 << 26,
        1 << 20,
        in_specs=[smem_spec()] + [vmem_spec()] * (3 + sources),
        out_specs=tuple(vmem_spec() for _ in range(4)),
        scratch_shapes=[
            pltpu.VMEM((128, 128), jnp.float32),
            pltpu.VMEM((row_count, 128), jnp.float32),
            held,
            held,
            held,
            held,
            pltpu.VMEM((row_count, 128), jnp.float32),
        ],
    )(slots, labels, frame_counts, label_counts, *stats)


def head_gradient(groups, order, blocks):
    count = len(groups)
    row_count, width = groups[0]["rows"].shape
    entries = groups[0]["places"].shape[1]
    names = ("logits", "rows", "out", "high", "low", "places")

    def kernel(order_ref, *refs):
        out_ref, rows_ref = refs[count * len(names) :]
        sets = [
            dict(zip(names, refs[g * len(names) : (g + 1) * len(names)])) for g in range(count)
        ]
        step = pl.program_id(0)

        @pl.when(step == 0)
        def _():
            for g, held in enumerate(sets):
                rows_ref[g * row_count : (g + 1) * row_count] = held["rows"][...]

        entry = order_ref[step] * BLOCK_ROWS + lax.broadcasted_iota(
            jnp.int32, (BLOCK_ROWS, entries), 0
        )
        grads = []
        for held in sets:
            select = as_mask(entry == held["places"][...])
            scattered = lax.dot_general(
                select, held["high"][...], NN, preferred_element_type=jnp.float32
            ) + lax.dot_general(select, held["low"][...], NN, preferred_element_type=jnp.float32)
            whole = held["out"][WHOLE : WHOLE + 1]
            log_total = held["out"][TOTAL : TOTAL + 1]
            grad = scattered - jnp.exp(held["logits"][...] - log_total) * whole
            grads.append(grad.astype(jnp.bfloat16))
        out_ref[...] = lax.dot_general(
            jnp.concatenate(grads, axis=1),
            rows_ref[...],
            NN,
            preferred_element_type=jnp.float32,
        ).astype(jnp.bfloat16)

    specs = [
        pl.BlockSpec((BLOCK_ROWS, row_count), lambda i, order: (order[i], 0)),
        pl.BlockSpec((row_count, width), lambda i, order: (0, 0)),
        pl.BlockSpec((COLS, row_count), lambda i, order: (0, 0)),
        pl.BlockSpec((entries, row_count), lambda i, order: (0, 0)),
        pl.BlockSpec((entries, row_count), lambda i, order: (0, 0)),
        pl.BlockSpec((1, entries), lambda i, order: (0, 0)),
    ]
    return call(
        kernel,
        bf16_rows(blocks * BLOCK_ROWS, width),
        2 * blocks * BLOCK_ROWS * row_count * count * (width + 2 * entries),
        10 << 20,
        grid_spec=pltpu.PrefetchScalarGridSpec(
            num_scalar_prefetch=1,
            grid=(blocks,),
            in_specs=specs * count,
            out_specs=pl.BlockSpec((BLOCK_ROWS, width), lambda i, order: (i, 0)),
            scratch_shapes=[pltpu.VMEM((count * row_count, width), jnp.bfloat16)],
        ),
    )(order, *[group[name] for group in groups for name in names])


def assemble(pieces, offsets, height):
    count = len(pieces)
    part, width = pieces[0].shape
    short = height % part

    def kernel(offsets_ref, *refs):
        out_ref, sems = refs[count], refs[count + 1]

        def each(act):
            for index in range(count):
                offset = pl.multiple_of(offsets_ref[index], part)

                @pl.when(offset + part <= height)
                def _():
                    act(
                        pltpu.make_async_copy(
                            refs[index], out_ref.at[pl.ds(offset, part)], sems.at[index]
                        )
                    )

                if short:

                    @pl.when(offset + part > height)
                    def _():
                        act(
                            pltpu.make_async_copy(
                                refs[index].at[pl.ds(0, short)],
                                out_ref.at[pl.ds(height - short, short)],
                                sems.at[index],
                            )
                        )

        each(lambda copy: copy.start())
        each(lambda copy: copy.wait())

    return call(
        kernel,
        bf16_rows(height, width),
        0,
        2 * height * width * 2,
        in_specs=[smem_spec()] + [pl.BlockSpec(memory_space=pl.ANY)] * count,
        out_specs=pl.BlockSpec(memory_space=pl.ANY),
        scratch_shapes=[pltpu.SemaphoreType.DMA((count,))],
    )(offsets, *pieces)


def swap(value, axis):
    return lax.ppermute(value, axis, [(0, 1), (1, 0)])


def rotate(value, axis, by):
    count = lax.axis_size(axis)
    return lax.ppermute(value, axis, [(i, (i + by) % count) for i in range(count)])


def spread_rows(value, member):
    left = lax.ppermute(value, "expert", [(1, 0), (2, 1), (3, 2)])
    right = lax.ppermute(value, "expert", [(0, 1), (1, 2), (2, 3)])
    left_far = lax.ppermute(left, "expert", [(1, 0), (2, 1)])
    right_far = lax.ppermute(right, "expert", [(1, 2), (2, 3)])
    low = member < 2
    near = jnp.where(low, left, right)
    far = jnp.where(low, left_far, right_far)
    end = lax.ppermute(far, "expert", [(1, 0), (2, 3)])
    passed = jnp.where(low, right, left)
    last = jnp.where((member == 0) | (member == 3), end, passed)
    return [value, near, far, last]


LINE_ORDER = np.array([[0, 1, 2, 3], [1, 2, 3, 0], [2, 1, 0, 3], [3, 2, 1, 0]])


def slot_orders(count):
    return LINE_ORDER if count == 4 else np.tile(np.arange(count), (count, 1))


def slot_tables(count):
    orders = slot_orders(count)
    tables = np.zeros((count, count, count), np.int32)
    for member in range(count):
        for k in range(count):
            source = (member + k) % count
            for slot in range(count):
                tables[member, k, slot] = list(orders[source]).index(orders[member][slot])
    return tables.reshape(count, count * count)


def add(first, second):
    return (first.astype(jnp.float32) + second.astype(jnp.float32)).astype(jnp.bfloat16)


def per_device(
    frames,
    norm_gain,
    router,
    w_in,
    w_out,
    routing,
    head_gain,
    head_weight,
    frame_lengths,
    labels,
    label_lengths,
):
    sections = lax.axis_size("section")
    section_id = lax.axis_index("section")
    group_size = lax.axis_size("expert")
    member = lax.axis_index("expert")
    outer_size = lax.axis_size("dpo")
    inner_size = lax.axis_size("dpi")
    core = lax.axis_index("dpi")
    micro, utt_dev, frame_count, width = frames.shape
    label_max = labels.shape[2]
    experts = w_in.shape[1] * group_size
    hidden = w_in.shape[3]
    pair_count = micro * utt_dev
    per_section = pair_count // sections
    first_pair = section_id * per_section
    group_count = 2 if per_section % (2 * utt_dev) == 0 else 1
    group_pairs = per_section // group_count
    share = (utt_dev * frame_count * 9 + 8 * experts - 1) // (8 * experts)
    capacity = round_up(share * -(-group_pairs // utt_dev), 16)
    span = group_pairs * frame_count
    member_ref = member.astype(jnp.int32).reshape(1)

    def mine_of(value):
        return lax.dynamic_slice_in_dim(value, first_pair, per_section, 0)

    own_ids = routing.reshape(pair_count, frame_count)
    own_table = jnp.concatenate(
        [
            norm_gain,
            jnp.zeros((7, width), jnp.float32),
            jnp.transpose(router[0]).astype(jnp.float32),
            jnp.zeros((round_up(experts, 8) - experts, width), jnp.float32),
        ],
        axis=0,
    )
    own = (w_in[0, 0], w_out[0, 0])
    paired = sections == 2 and inner_size == 2
    if paired:
        other_ids = swap(own_ids, "section")
        other_table = swap(own_table, "section")
        half = hidden // 2
        sent_in = lax.dynamic_slice(own[0], (0, core * half), (width, half))
        sent_out = lax.dynamic_slice(own[1], (core * half, 0), (half, width))
        sent_in, sent_out, other_ids, other_table = lax.optimization_barrier(
            (sent_in, sent_out, other_ids, other_table)
        )
        came_in = swap(sent_in, "section")
        came_out = swap(sent_out, "section")
        other = [(came_in, came_out), (swap(came_in, "dpi"), swap(came_out, "dpi"))]
    else:
        all_ids = lax.all_gather(own_ids, "section")
        all_tables = lax.all_gather(own_table, "section")
        all_in = lax.all_gather(own[0], "section")
        all_out = lax.all_gather(own[1], "section")

    def of_layer(layer):
        if not paired:
            chosen = (all_in[layer], all_out[layer])
            return all_ids[layer], all_tables[layer], chosen, [], jnp.ones((1,), jnp.int32)
        mine = section_id == layer
        return (
            jnp.where(mine, own_ids, other_ids),
            jnp.where(mine, own_table, other_table),
            own,
            other,
            mine.astype(jnp.int32).reshape(1),
        )

    layers = []
    for layer in range(sections):
        ids, table, weights, others, pick_own = of_layer(layer)
        ids = jnp.pad(mine_of(ids), ((0, 0), (0, LANES - frame_count)), constant_values=-1)
        parts = [ids[g * group_pairs : (g + 1) * group_pairs] for g in range(group_count)]
        layers.append((parts, table, weights, others, pick_own))

    rows = lax.dynamic_slice_in_dim(
        frames.reshape(pair_count * frame_count, width),
        first_pair * frame_count,
        per_section * frame_count,
        0,
    )
    current = [rows[g * span : (g + 1) * span] for g in range(group_count)]

    def exchange(blocks, sign):
        return [blocks[0]] + [
            rotate(blocks[k], "expert", sign * k) for k in range(1, group_size)
        ]

    outgoing = [
        dispatch(current[g], layers[0][0][g], member_ref, experts, capacity, frame_count)
        for g in range(group_count)
    ]
    received = [exchange(blocks, 1) for blocks in outgoing]

    notes = jnp.concatenate(
        [
            mine_of(labels.reshape(pair_count, label_max)),
            mine_of(frame_lengths.reshape(pair_count, 1)),
            mine_of(label_lengths.reshape(pair_count, 1)),
        ],
        axis=1,
    )
    if group_size == 4:
        found = [notes] + [rotate(notes, "expert", -k) for k in range(1, group_size)]
        low = member < 2
        notes_all = jnp.stack(
            [
                found[0],
                jnp.where(low, found[1], found[3]),
                found[2],
                jnp.where(low, found[3], found[1]),
            ]
        )
    else:
        notes_all = lax.all_gather(notes, "expert")
    shard = head_weight.shape[1]
    weight_rows = jnp.transpose(head_weight)
    known, all_places = [], []
    for g in range(group_count):
        part = notes_all[:, g * group_pairs : (g + 1) * group_pairs].reshape(
            group_size * group_pairs, label_max + 2
        )
        utterances = part.shape[0]
        names = part[:, :label_max]
        named = jnp.concatenate(
            [
                names,
                jnp.zeros((utterances, 1), jnp.int32),
                jnp.full((utterances, COLS - label_max - 1), -1, jnp.int32),
            ],
            axis=1,
        ).reshape(utterances * COLS)
        local = named - member * shard
        places = jnp.where((named >= 0) & (local >= 0) & (local < shard), local, -1)
        all_places.append(places)
        known.append(
            (
                jnp.pad(names, ((0, 0), (0, LANES - label_max))),
                part[:, label_max : label_max + 1],
                part[:, label_max + 1 :],
                places.reshape(1, -1),
            )
        )
    label_weight = label_rows(weight_rows, jnp.concatenate(all_places).reshape(-1, 1))
    entries = all_places[0].shape[0]
    received, label_weight = lax.optimization_barrier((received, label_weight))

    spread = []
    for layer in range(sections):
        ids, table, weights, others, pick_own = layers[layer]
        for g in range(group_count):
            done = run_expert(received[g], table, weights, others, pick_own)
            returned = exchange(done, -1)
            if layer < sections - 1:
                current[g], blocks = combine_and_dispatch(
                    current[g],
                    returned,
                    ids[g],
                    table,
                    layers[layer + 1][0][g],
                    member_ref,
                    experts,
                    capacity,
                    frame_count,
                )
                received[g] = exchange(blocks, 1)
            else:
                normed = combine_and_norm(
                    current[g],
                    returned,
                    ids[g],
                    table,
                    head_gain.reshape(1, width),
                    member_ref,
                    experts,
                    capacity,
                    frame_count,
                )
                if group_size == 4:
                    spread.append(spread_rows(normed, member))
                else:
                    gathered = lax.all_gather(normed, "expert")
                    spread.append([gathered[k] for k in range(group_size)])

    tables = jnp.asarray(slot_tables(group_size))
    slots = lax.dynamic_index_in_dim(tables, member, 0, keepdims=False)
    groups, my_losses = [], []
    for g in range(group_count):
        logits, rows_all, stats = head_logits(
            spread[g], weight_rows, label_weight[g * entries : (g + 1) * entries], frame_count
        )
        if group_size == 4:
            found = [stats] + [rotate(stats, "expert", -k) for k in range(1, group_size)]
        else:
            gathered = lax.all_gather(stats, "expert")
            found = [
                lax.dynamic_index_in_dim(gathered, (member + k) % group_size, 0, keepdims=False)
                for k in range(group_size)
            ]
        names, frames_all, counts_all, places = known[g]
        out, high, low, losses = ctc_pass(
            found, slots, names, frames_all, counts_all, frame_count, label_max
        )
        own_slot = 0 if group_size == 4 else member
        my_losses.append(
            lax.dynamic_slice(losses, (own_slot * group_pairs, 0), (group_pairs, 1))
        )
        groups.append(
            dict(logits=logits, rows=rows_all, out=out, high=high, low=low, places=places)
        )
    my_losses = jnp.concatenate(my_losses, axis=0)
    blocks = groups[0]["logits"].shape[0] // BLOCK_ROWS
    if paired and outer_size == 2 and blocks == 8:
        outer = lax.axis_index("dpo")

        def pair_of(side, first, second):
            return jnp.stack([side * 4 + first, side * 4 + 2 + second]).astype(jnp.int32)

        sibling_sent = head_gradient(groups, pair_of(1 - core, 1 - section_id, 1 - outer), 2)
        sibling_kept = head_gradient(groups, pair_of(1 - core, section_id, outer), 2)
        came_sent = swap(sibling_sent, "dpi")
        came_kept = swap(sibling_kept, "dpi")
        sent = add(head_gradient(groups, pair_of(core, 1 - section_id, 1 - outer), 2), came_sent)
        first_in = swap(sent[:BLOCK_ROWS], "section")
        second_in = swap(sent[BLOCK_ROWS:], "dpo")
        kept = add(head_gradient(groups, pair_of(core, section_id, outer), 2), came_kept)
        first = add(kept[:BLOCK_ROWS], first_in)
        second = add(kept[BLOCK_ROWS:], second_in)
        part = BLOCK_ROWS // 2

        def piece(value, index):
            return lax.dynamic_slice_in_dim(value, index * part, part, 0)

        first_far = swap(piece(first, 1 - outer), "dpo")
        second_far = swap(piece(second, 1 - section_id), "section")
        final = jnp.concatenate(
            [add(piece(first, outer), first_far), add(piece(second, section_id), second_far)],
            axis=0,
        )
        across = swap(final, "section")
        beside = swap(final, "dpo")
        first_diagonal = swap(beside[:part], "section")
        second_diagonal = swap(across[part:], "dpo")
        mine = [final, across, beside, first_diagonal, second_diagonal]
        theirs = [swap(value, "dpi") for value in mine]
        pieces, offsets = [], []
        for side, held in ((core, mine), (1 - core, theirs)):
            where = (
                (section_id, outer),
                (1 - section_id, outer),
                (section_id, 1 - outer),
            )
            for value, (s, y) in zip(held[:3], where):
                pieces += [value[:part], value[part:]]
                offsets += [
                    side * 1024 + s * 256 + y * 128,
                    side * 1024 + 512 + y * 256 + s * 128,
                ]
            pieces += held[3:]
            s, y = 1 - section_id, 1 - outer
            offsets += [
                side * 1024 + s * 256 + y * 128,
                side * 1024 + 512 + y * 256 + s * 128,
            ]
        whole = assemble(pieces, jnp.stack(offsets).astype(jnp.int32), shard)
    else:
        partial = head_gradient(groups, jnp.arange(blocks, dtype=jnp.int32), blocks)[:shard]
        whole = lax.psum(partial.astype(jnp.float32), ("section", "dpo", "dpi")).astype(
            jnp.bfloat16
        )
    return (my_losses, jnp.transpose(whole))


def solution(mesh):
    sections, group_size, spread = (mesh.shape[name] for name in ("section", "expert", "dp"))
    inner = 2 if spread % 2 == 0 else 1
    split = Mesh(
        mesh.devices.reshape(sections, group_size, spread // inner, inner),
        ("section", "expert", "dpo", "dpi"),
    )
    block = ("expert", "dpo", "dpi")
    placed = (
        P(None, block, None, None),
        P("section", None),
        P("section", None, None),
        P("section", "expert", None, None),
        P("section", "expert", None, None),
        P("section", None, block, None, None),
        P(),
        P(None, "expert"),
        P(None, block),
        P(None, block, None),
        P(None, block),
    )
    return jax.shard_map(
        per_device,
        mesh=split,
        in_specs=placed,
        out_specs=(P("section", block), P(None, "expert")),
        check_vma=False,
    )
```

```python
import jax
import jax.numpy as jnp
import numpy as np
from jax import lax
from jax.experimental import pallas as pl
from jax.experimental.pallas import tpu as pltpu
from jax.sharding import Mesh, PartitionSpec as P

EPSILON = 1e-06
LOG_ZERO = -1e30
VMEM_LIMIT = 24 * 1024 * 1024
STREAM_LIMIT = 58 * 1024 * 1024
LANES = 128
COLS = 16
PEAK, TOTAL, WHOLE = COLS - 3, COLS - 2, COLS - 3
BLOCK_ROWS = 256
NT = (((1,), (1,)), ((), ()))
NN = (((1,), (0,)), ((), ()))


def round_up(value, unit):
    return -(-value // unit) * unit


def vmem_spec():
    return pl.BlockSpec(memory_space=pltpu.VMEM)


def smem_spec():
    return pl.BlockSpec(memory_space=pltpu.SMEM)


def call(kernel, out_shape, flops=0, moved=0, limit=VMEM_LIMIT, **options):
    return pl.pallas_call(
        kernel,
        out_shape=out_shape,
        compiler_params=pltpu.CompilerParams(vmem_limit_bytes=limit),
        cost_estimate=pl.CostEstimate(flops=flops, bytes_accessed=moved, transcendentals=0),
        **options,
    )


def bf16_rows(count, width):
    return jax.ShapeDtypeStruct((count, width), jnp.bfloat16)


def as_mask(values):
    return values.astype(jnp.float32).astype(jnp.bfloat16)


def rms_scale(values, gain):
    values = values.astype(jnp.float32)
    scale = lax.rsqrt(jnp.mean(values * values, axis=-1, keepdims=True) + EPSILON)
    return (values * scale * gain).astype(jnp.bfloat16)


def expert_column(ids, frame_count):
    pairs = ids.shape[0]
    square = jnp.concatenate(
        [ids.astype(jnp.float32), jnp.full((LANES - pairs, LANES), -1.0, jnp.float32)], axis=0
    )
    turned = jnp.transpose(square, (1, 0)).astype(jnp.int32)
    return jnp.concatenate([turned[:frame_count, p : p + 1] for p in range(pairs)], axis=0)


def placement(column, member, experts, capacity):
    count = column.shape[0]
    shifted = column - member
    relative = jnp.where(shifted < 0, shifted + experts, shifted)
    lane = lax.broadcasted_iota(jnp.int32, (count, LANES), 1)
    one_hot = (lane == relative).astype(jnp.float32)
    before = lax.broadcasted_iota(jnp.int32, (count, count), 1) <= lax.broadcasted_iota(
        jnp.int32, (count, count), 0
    )
    rank = lax.dot_general(
        as_mask(before), one_hot.astype(jnp.bfloat16), NN, preferred_element_type=jnp.float32
    )
    start = (lane * capacity - 1).astype(jnp.float32)
    slots = jnp.sum(one_hot * (rank + start), axis=1, keepdims=True).astype(jnp.int32)
    places = lax.broadcasted_iota(jnp.int32, (count, experts * capacity), 1)
    return (places == slots).astype(jnp.float32)


def scatter_rows(rows, ids, member, experts, capacity, frame_count, out_refs):
    count = rows.shape[0]
    chosen = placement(expert_column(ids, frame_count), member, experts, capacity)
    tall = round_up(count, LANES)
    if tall > count:
        chosen = jnp.concatenate(
            [chosen, jnp.zeros((tall - count, chosen.shape[1]), jnp.float32)], axis=0
        )
    pick = jnp.transpose(chosen, (1, 0))[:, :count].astype(jnp.bfloat16)
    placed = lax.dot_general(pick, rows, NN, preferred_element_type=jnp.float32).astype(
        jnp.bfloat16
    )
    for turn, out_ref in enumerate(out_refs):
        out_ref[...] = placed[turn * capacity : (turn + 1) * capacity]


def combine_rows(rows, returned, ids, table, member, experts, capacity, frame_count):
    column = expert_column(ids, frame_count)
    pick = placement(column, member, experts, capacity).astype(jnp.bfloat16)
    normed = rms_scale(rows, table[:1])
    router = jnp.concatenate(
        [table[8:], jnp.zeros((LANES + 8 - table.shape[0], rows.shape[1]), jnp.float32)], axis=0
    ).astype(jnp.bfloat16)
    logits = lax.dot_general(normed, router, NT, preferred_element_type=jnp.float32)
    lane = lax.broadcasted_iota(jnp.int32, logits.shape, 1)
    gate = jax.nn.sigmoid(jnp.sum(jnp.where(lane == column, logits, 0.0), axis=1, keepdims=True))
    stacked = jnp.concatenate(returned, axis=0)
    mixed = lax.dot_general(pick, stacked, NN, preferred_element_type=jnp.float32)
    return (rows.astype(jnp.float32) + gate * mixed).astype(jnp.bfloat16)


def dispatch(rows, ids, member, experts, capacity, frame_count):
    width = rows.shape[1]

    def kernel(member_ref, rows_ref, ids_ref, *out_refs):
        scatter_rows(
            rows_ref[...], ids_ref[...], member_ref[0], experts, capacity, frame_count, out_refs
        )

    return call(
        kernel,
        tuple(bf16_rows(capacity, width) for _ in range(experts)),
        1 << 27,
        1 << 20,
        in_specs=[smem_spec()] + [vmem_spec()] * 2,
        out_specs=tuple(vmem_spec() for _ in range(experts)),
    )(member, rows, ids)


def run_expert(received, table, own, other, pick_own):
    count = len(received)
    capacity, width = received[0].shape
    others = len(other)

    def kernel(pick_ref, table_ref, in_ref, out_weight_ref, *refs):
        other_refs, received_refs, out_refs = (
            refs[: 2 * others],
            refs[2 * others : 2 * others + count],
            refs[2 * others + count :],
        )

        def work(pieces):
            stacked = jnp.concatenate([ref[...] for ref in received_refs], axis=0)
            normed = rms_scale(stacked, table_ref[:1])
            total = None
            for weight_in, weight_out in pieces:
                hidden = lax.dot_general(
                    normed, weight_in[...], NN, preferred_element_type=jnp.float32
                )
                active = (hidden / (1.0 + jnp.exp(-hidden))).astype(jnp.bfloat16)
                part = lax.dot_general(
                    active, weight_out[...], NN, preferred_element_type=jnp.float32
                )
                total = part if total is None else total + part
            total = total.astype(jnp.bfloat16)
            for turn, out_ref in enumerate(out_refs):
                out_ref[...] = total[turn * capacity : (turn + 1) * capacity]

        if others == 0:
            work([(in_ref, out_weight_ref)])
            return

        @pl.when(pick_ref[0] == 1)
        def _():
            work([(in_ref, out_weight_ref)])

        @pl.when(pick_ref[0] != 1)
        def _():
            work([(other_refs[2 * i], other_refs[2 * i + 1]) for i in range(others)])

    flat = [weight for pair in other for weight in pair]
    return call(
        kernel,
        tuple(bf16_rows(capacity, width) for _ in range(count)),
        4 * count * capacity * width * own[0].shape[1],
        4 << 20,
        in_specs=[smem_spec()] + [vmem_spec()] * (3 + 2 * others + count),
        out_specs=tuple(vmem_spec() for _ in range(count)),
    )(pick_own, table, *own, *flat, *received)


def combine_and_dispatch(
    rows, returned, ids, table, next_ids, member, experts, capacity, frame_count
):
    width = rows.shape[1]

    def kernel(member_ref, rows_ref, ids_ref, table_ref, next_ref, *refs):
        returned_refs, x_ref, out_refs = refs[:experts], refs[experts], refs[experts + 1 :]
        mixed = combine_rows(
            rows_ref[...],
            [ref[...] for ref in returned_refs],
            ids_ref[...],
            table_ref[...],
            member_ref[0],
            experts,
            capacity,
            frame_count,
        )
        x_ref[...] = mixed
        scatter_rows(
            mixed, next_ref[...], member_ref[0], experts, capacity, frame_count, out_refs
        )

    shapes = (bf16_rows(*rows.shape),) + tuple(
        bf16_rows(capacity, width) for _ in range(experts)
    )
    result = call(
        kernel,
        shapes,
        1 << 28,
        2 << 20,
        in_specs=[smem_spec()] + [vmem_spec()] * (4 + experts),
        out_specs=tuple(vmem_spec() for _ in shapes),
    )(member, rows, ids, table, next_ids, *returned)
    return result[0], result[1:]


def combine_and_norm(
    rows, returned, ids, table, head_gain, member, experts, capacity, frame_count
):
    def kernel(member_ref, rows_ref, ids_ref, table_ref, head_ref, *refs):
        final = combine_rows(
            rows_ref[...],
            [ref[...] for ref in refs[:experts]],
            ids_ref[...],
            table_ref[...],
            member_ref[0],
            experts,
            capacity,
            frame_count,
        )
        refs[experts][...] = rms_scale(final, head_ref[...])

    return call(
        kernel,
        bf16_rows(*rows.shape),
        1 << 28,
        2 << 20,
        in_specs=[smem_spec()] + [vmem_spec()] * (4 + experts),
        out_specs=vmem_spec(),
    )(member, rows, ids, table, head_gain, *returned)


def label_rows(weight, places):
    shard, width = weight.shape
    entries = places.shape[0]
    blocks = -(-shard // BLOCK_ROWS)

    def kernel(places_ref, weight_ref, out_ref, total_ref):
        step = pl.program_id(0)
        inside = (
            step * BLOCK_ROWS + lax.broadcasted_iota(jnp.int32, (BLOCK_ROWS, 1), 0) < shard
        )
        entry = step * BLOCK_ROWS + lax.broadcasted_iota(jnp.int32, (entries, BLOCK_ROWS), 1)
        values = jnp.where(inside, weight_ref[...].astype(jnp.float32), 0.0).astype(jnp.bfloat16)
        part = lax.dot_general(
            as_mask(entry == places_ref[...]), values, NN, preferred_element_type=jnp.float32
        )

        @pl.when(step == 0)
        def _():
            total_ref[...] = part

        @pl.when(step > 0)
        def _():
            total_ref[...] += part

        @pl.when(step == blocks - 1)
        def _():
            out_ref[...] = total_ref[...].astype(jnp.bfloat16)

    return call(
        kernel,
        bf16_rows(entries, width),
        2 * blocks * BLOCK_ROWS * entries * width,
        6 << 20,
        STREAM_LIMIT,
        grid=(blocks,),
        in_specs=[
            pl.BlockSpec((entries, 1), lambda i: (0, 0)),
            pl.BlockSpec((BLOCK_ROWS, width), lambda i: (i, 0)),
        ],
        out_specs=pl.BlockSpec((entries, width), lambda i: (0, 0)),
        scratch_shapes=[pltpu.VMEM((entries, width), jnp.float32)],
    )(places, weight)


def head_logits(pieces, member, weight, label_weight, frame_count):
    given = len(pieces)
    line = given == 5
    count = 4 if line else given
    span, width = pieces[0].shape
    row_count = count * span
    shard = weight.shape[0]
    blocks = -(-shard // BLOCK_ROWS)
    used = shard - (blocks - 1) * BLOCK_ROWS
    entries = label_weight.shape[0]

    def kernel(member_ref, weight_ref, label_ref, *refs):
        piece_refs = refs[:given]
        logits_ref, rows_ref, stats_ref, peak_ref, total_ref = refs[given:]
        step = pl.program_id(0)

        @pl.when(step == 0)
        def _():
            def put(slot, piece_ref):
                rows_ref[slot * span : (slot + 1) * span] = piece_ref[...]

            def put_if(condition, slot, piece_ref):
                @pl.when(condition)
                def _():
                    put(slot, piece_ref)

            if line:
                value_ref, left_ref, right_ref, far_ref, end_ref = piece_refs
                place = member_ref[0]
                put(0, value_ref)
                put_if(place < 2, 1, left_ref)
                put_if(place >= 2, 1, right_ref)
                put(2, far_ref)
                put_if((place == 0) | (place == 3), 3, end_ref)
                put_if(place == 1, 3, right_ref)
                put_if(place == 2, 3, left_ref)
            else:
                for slot in range(count):
                    put(slot, piece_refs[slot])
            peak_ref[...] = jnp.full(peak_ref.shape, LOG_ZERO, jnp.float32)
            total_ref[...] = jnp.zeros(total_ref.shape, jnp.float32)

        logits_ref[...] = lax.dot_general(
            weight_ref[...], rows_ref[...], NT, preferred_element_type=jnp.float32
        )
        if used < BLOCK_ROWS:

            @pl.when(step == blocks - 1)
            def _():
                logits_ref[used:] = jnp.full((BLOCK_ROWS - used, row_count), LOG_ZERO, jnp.float32)

        logits = logits_ref[...]
        before = peak_ref[...]
        peak = jnp.maximum(before, jnp.max(logits, axis=0, keepdims=True))
        total_ref[...] = total_ref[...] * jnp.exp(before - peak) + jnp.sum(
            jnp.exp(logits - peak), axis=0, keepdims=True
        )
        peak_ref[...] = peak

        @pl.when(step == blocks - 1)
        def _():
            crossed = lax.dot_general(
                label_ref[...], rows_ref[...], NT, preferred_element_type=jnp.float32
            )
            owner = lax.broadcasted_iota(jnp.int32, (COLS, row_count), 1) // frame_count
            picked = jnp.zeros((COLS, row_count), jnp.float32)
            for utterance in range(entries // COLS):
                part = crossed[utterance * COLS : (utterance + 1) * COLS]
                picked = picked + jnp.where(owner == utterance, part, 0.0)
            place = lax.broadcasted_iota(jnp.int32, (COLS, row_count), 0)
            stats = jnp.where(place == PEAK, peak_ref[...], picked)
            stats = jnp.where(place == TOTAL, total_ref[...], stats)
            for slot in range(count):
                stats_ref[slot] = stats[:, slot * span : (slot + 1) * span]

    return call(
        kernel,
        (
            jax.ShapeDtypeStruct((blocks * BLOCK_ROWS, row_count), jnp.float32),
            bf16_rows(row_count, width),
            jax.ShapeDtypeStruct((count, COLS, span), jnp.float32),
        ),
        2 * blocks * BLOCK_ROWS * row_count * width,
        9 << 20,
        STREAM_LIMIT,
        grid=(blocks,),
        in_specs=[
            smem_spec(),
            pl.BlockSpec((BLOCK_ROWS, width), lambda i: (i, 0)),
            pl.BlockSpec((entries, width), lambda i: (0, 0)),
        ]
        + [pl.BlockSpec((span, width), lambda i: (0, 0))] * given,
        out_specs=(
            pl.BlockSpec((BLOCK_ROWS, row_count), lambda i: (i, 0)),
            pl.BlockSpec((row_count, width), lambda i: (0, 0)),
            pl.BlockSpec((count, COLS, span), lambda i: (0, 0, 0)),
        ),
        scratch_shapes=[
            pltpu.VMEM((1, row_count), jnp.float32),
            pltpu.VMEM((1, row_count), jnp.float32),
        ],
    )(member, weight, label_weight, *pieces)


def log_add(first, second):
    peak = jnp.maximum(first, second)
    return peak + jnp.log(jnp.exp(first - peak) + jnp.exp(second - peak))


def log_add3(first, second, third):
    peak = jnp.maximum(jnp.maximum(first, second), third)
    return peak + jnp.log(
        jnp.exp(first - peak) + jnp.exp(second - peak) + jnp.exp(third - peak)
    )


def ctc_pass(stats, slots, labels, frame_counts, label_counts, frame_count, label_max):
    group_count, sources = len(stats), len(stats[0])
    count, _, span = stats[0][0].shape
    row_count = group_count * count * span
    utterances = labels.shape[0]
    entries = utterances * COLS
    given = group_count * sources

    def kernel(slots_ref, labels_ref, frames_ref, counts_ref, *refs):
        (
            out_ref,
            high_ref,
            low_ref,
            loss_ref,
            turn_ref,
            emission_ref,
            emit_blank,
            emit_label,
            blank_fwd,
            label_fwd,
            blank_bwd,
            label_bwd,
            occupancy_ref,
        ) = refs[given:]
        place = lax.broadcasted_iota(jnp.int32, (COLS, span), 0)
        turn_ref[...] = jnp.zeros(turn_ref.shape, jnp.float32)
        for part in range(group_count * count):
            group, slot = part // count, part % count
            found = [
                refs[group * sources + k][slots_ref[k * count + slot]] for k in range(sources)
            ]
            joined = found[0]
            peak = found[0][PEAK : PEAK + 1]
            for other in found[1:]:
                joined = joined + other
                peak = jnp.maximum(peak, other[PEAK : PEAK + 1])
            total = jnp.zeros((1, span), jnp.float32)
            for other in found:
                total = total + other[TOTAL : TOTAL + 1] * jnp.exp(other[PEAK : PEAK + 1] - peak)
            log_total = peak + jnp.log(total)
            turn_ref[:COLS, :span] = jnp.where(place == TOTAL, log_total, joined - log_total)
            emission_ref[part * span : (part + 1) * span] = jnp.transpose(turn_ref[...], (1, 0))[
                :span
            ]

        lane = lax.broadcasted_iota(jnp.int32, (utterances, LANES), 1)
        is_label = lane < label_max
        is_blank = lane <= label_max
        names = labels_ref[...]
        earlier = pltpu.roll(names, 1, 1)
        skip = is_label & (lane >= 1) & (names != 0) & (names != earlier)
        later = pltpu.roll(names, LANES - 1, 1)
        skip_next = (lane < label_max - 1) & (later != 0) & (later != names)
        frames = frames_ref[...]
        counts = counts_ref[...]
        ends_blank = jnp.where(lane == counts, 0.0, LOG_ZERO)
        ends_label = jnp.where(lane == counts - 1, 0.0, LOG_ZERO)

        def spread(step, carry):
            row = emission_ref[pl.ds(step, utterances, stride=frame_count), :]
            blank = jnp.sum(jnp.where(lane == label_max, row, 0.0), axis=1, keepdims=True)
            emit_blank[step] = jnp.where(is_blank, blank, LOG_ZERO)
            emit_label[step] = jnp.where(is_label, row, LOG_ZERO)
            return carry

        lax.fori_loop(0, frame_count, spread, 0, unroll=16)

        def advance(step, carry):
            fwd_blank, fwd_label, bwd_blank, bwd_label = carry
            moved = jnp.where(lane == 0, LOG_ZERO, pltpu.roll(fwd_label, 1, 1))
            new_blank = log_add(fwd_blank, moved) + emit_blank[step]
            new_label = (
                log_add3(fwd_label, fwd_blank, jnp.where(skip, moved, LOG_ZERO))
                + emit_label[step]
            )
            alive = step < frames
            fwd_blank = jnp.where(alive, new_blank, fwd_blank)
            fwd_label = jnp.where(alive, new_label, fwd_label)
            blank_fwd[step] = fwd_blank
            label_fwd[step] = fwd_label

            back = frame_count - 1 - step
            out_blank = bwd_blank + emit_blank[back + 1]
            out_label = bwd_label + emit_label[back + 1]
            next_blank = pltpu.roll(out_blank, LANES - 1, 1)
            next_label = jnp.where(skip_next, pltpu.roll(out_label, LANES - 1, 1), LOG_ZERO)
            ended = back >= frames - 1
            bwd_blank = jnp.where(ended, ends_blank, log_add(out_blank, out_label))
            bwd_label = jnp.where(
                ended, ends_label, log_add3(out_label, next_blank, next_label)
            )
            blank_bwd[back] = bwd_blank
            label_bwd[back] = bwd_label
            return (fwd_blank, fwd_label, bwd_blank, bwd_label)

        first_blank = jnp.where(lane == 0, emit_blank[0], LOG_ZERO)
        first_label = jnp.where(lane == 0, emit_label[0], LOG_ZERO)
        blank_fwd[0] = first_blank
        label_fwd[0] = first_label
        blank_bwd[frame_count - 1] = ends_blank
        label_bwd[frame_count - 1] = ends_label
        fwd_blank, fwd_label, _, _ = lax.fori_loop(
            1, frame_count, advance, (first_blank, first_label, ends_blank, ends_label), unroll=4
        )
        end_state = jnp.sum(jnp.where(lane == counts, fwd_blank, 0.0), axis=1, keepdims=True)
        near_state = jnp.sum(jnp.where(lane == counts - 1, fwd_label, 0.0), axis=1, keepdims=True)
        log_like = log_add(end_state, near_state)
        loss_ref[...] = jnp.broadcast_to(-log_like, (utterances, LANES))

        def occupy(step, carry):
            blank = jnp.exp(blank_fwd[step] + blank_bwd[step] - log_like)
            label = jnp.exp(label_fwd[step] + label_bwd[step] - log_like)
            blank = jnp.sum(jnp.where(is_blank, blank, 0.0), axis=1, keepdims=True)
            label = jnp.where(is_label, label, 0.0)
            whole = blank + jnp.sum(label, axis=1, keepdims=True)
            filled = jnp.where(lane == label_max, blank, label)
            filled = jnp.where(lane == WHOLE, whole, filled)
            filled = jnp.where(step < frames, -filled, 0.0)
            row = emission_ref[pl.ds(step, utterances, stride=frame_count), :]
            occupancy_ref[pl.ds(step, utterances, stride=frame_count), :] = jnp.where(
                lane == TOTAL, row, filled
            )
            return carry

        lax.fori_loop(0, frame_count, occupy, 0, unroll=16)
        turned = jnp.transpose(occupancy_ref[...], (1, 0))[:COLS]
        out_ref[...] = turned
        row_place = lax.broadcasted_iota(jnp.int32, (COLS, row_count), 0)
        owner = lax.broadcasted_iota(jnp.int32, (COLS, row_count), 1) // frame_count
        source = jnp.where(row_place < WHOLE, turned, 0.0)
        for utterance in range(utterances):
            part = jnp.where(owner == utterance, source, 0.0)
            high = part.astype(jnp.bfloat16)
            high_ref[utterance * COLS : (utterance + 1) * COLS] = high
            low_ref[utterance * COLS : (utterance + 1) * COLS] = (
                part - high.astype(jnp.float32)
            ).astype(jnp.bfloat16)

    held = pltpu.VMEM((frame_count, utterances, LANES), jnp.float32)
    table = pltpu.VMEM((row_count, LANES), jnp.float32)
    flat = [value for group in stats for value in group]
    return call(
        kernel,
        (
            jax.ShapeDtypeStruct((COLS, row_count), jnp.float32),
            bf16_rows(entries, row_count),
            bf16_rows(entries, row_count),
            jax.ShapeDtypeStruct((utterances, LANES), jnp.float32),
        ),
        1 << 26,
        1 << 20,
        in_specs=[smem_spec()] + [vmem_spec()] * (3 + given),
        out_specs=tuple(vmem_spec() for _ in range(4)),
        scratch_shapes=[pltpu.VMEM((LANES, LANES), jnp.float32), table]
        + [held] * 6
        + [table],
    )(slots, labels, frame_counts, label_counts, *flat)


def head_gradient(logits, rows, occupancy, high, low, places, order, blocks):
    count = len(logits)
    row_count, width = rows[0].shape
    whole_count = count * row_count
    entries = places.shape[1]

    def kernel(order_ref, *refs):
        logits_refs, rows_refs = refs[:count], refs[count : 2 * count]
        occupancy_ref, high_ref, low_ref, places_ref, out_ref, joined_ref = refs[2 * count :]
        step = pl.program_id(0)

        @pl.when(step == 0)
        def _():
            for g in range(count):
                joined_ref[g * row_count : (g + 1) * row_count] = rows_refs[g][...]

        entry = order_ref[step] * BLOCK_ROWS + lax.broadcasted_iota(
            jnp.int32, (BLOCK_ROWS, entries), 0
        )
        select = as_mask(entry == places_ref[...])
        scattered = lax.dot_general(
            select, high_ref[...], NN, preferred_element_type=jnp.float32
        ) + lax.dot_general(select, low_ref[...], NN, preferred_element_type=jnp.float32)
        values = jnp.concatenate([ref[...] for ref in logits_refs], axis=1)
        whole = occupancy_ref[WHOLE : WHOLE + 1]
        log_total = occupancy_ref[TOTAL : TOTAL + 1]
        grad = (scattered - jnp.exp(values - log_total) * whole).astype(jnp.bfloat16)
        out_ref[...] = lax.dot_general(
            grad, joined_ref[...], NN, preferred_element_type=jnp.float32
        ).astype(jnp.bfloat16)

    def fixed(*shape):
        return pl.BlockSpec(shape, lambda i, order: (0, 0))

    return call(
        kernel,
        bf16_rows(blocks * BLOCK_ROWS, width),
        2 * blocks * BLOCK_ROWS * whole_count * (width + 2 * entries),
        10 << 20,
        STREAM_LIMIT,
        grid_spec=pltpu.PrefetchScalarGridSpec(
            num_scalar_prefetch=1,
            grid=(blocks,),
            in_specs=[pl.BlockSpec((BLOCK_ROWS, row_count), lambda i, order: (order[i], 0))] * count
            + [fixed(row_count, width)] * count
            + [
                fixed(COLS, whole_count),
                fixed(entries, whole_count),
                fixed(entries, whole_count),
                fixed(1, entries),
            ],
            out_specs=pl.BlockSpec((BLOCK_ROWS, width), lambda i, order: (i, 0)),
            scratch_shapes=[pltpu.VMEM((whole_count, width), jnp.bfloat16)],
        ),
    )(order, *logits, *rows, occupancy, high, low, places)


def assemble(pieces, offsets, height):
    count = len(pieces)
    part, width = pieces[0].shape
    short = height % part

    def kernel(offsets_ref, *refs):
        out_ref, sems = refs[count], refs[count + 1]

        def each(act):
            for index in range(count):
                offset = pl.multiple_of(offsets_ref[index], part)

                @pl.when(offset + part <= height)
                def _():
                    act(
                        pltpu.make_async_copy(
                            refs[index], out_ref.at[pl.ds(offset, part)], sems.at[index]
                        )
                    )

                if short:

                    @pl.when(offset + part > height)
                    def _():
                        act(
                            pltpu.make_async_copy(
                                refs[index].at[pl.ds(0, short)],
                                out_ref.at[pl.ds(height - short, short)],
                                sems.at[index],
                            )
                        )

        each(lambda copy: copy.start())
        each(lambda copy: copy.wait())

    return call(
        kernel,
        bf16_rows(height, width),
        0,
        2 * height * width * 2,
        in_specs=[smem_spec()] + [pl.BlockSpec(memory_space=pl.ANY)] * count,
        out_specs=pl.BlockSpec(memory_space=pl.ANY),
        scratch_shapes=[pltpu.SemaphoreType.DMA((count,))],
    )(offsets, *pieces)


def swap(value, axis):
    return lax.ppermute(value, axis, [(0, 1), (1, 0)])


def rotate(value, axis, by):
    count = lax.axis_size(axis)
    return lax.ppermute(value, axis, [(i, (i + by) % count) for i in range(count)])


def after(value, *others):
    return lax.optimization_barrier((value,) + others)[0]


def line_near(value):
    left = lax.ppermute(value, "expert", [(1, 0), (2, 1), (3, 2)])
    right = lax.ppermute(value, "expert", [(0, 1), (1, 2), (2, 3)])
    return left, right


def line_far(near, member):
    left = lax.ppermute(near[0], "expert", [(1, 0), (2, 1)])
    right = lax.ppermute(near[1], "expert", [(1, 2), (2, 3)])
    return jnp.where(member < 2, left, right)


def line_end(far):
    return lax.ppermute(far, "expert", [(1, 0), (2, 3)])


LINE_ORDER = np.array([[0, 1, 2, 3], [1, 2, 3, 0], [2, 1, 0, 3], [3, 2, 1, 0]])


def slot_orders(count):
    return LINE_ORDER if count == 4 else np.tile(np.arange(count), (count, 1))


def slot_tables(count):
    orders = slot_orders(count)
    tables = np.zeros((count, count, count), np.int32)
    for member in range(count):
        for k in range(count):
            source = (member + k) % count
            for slot in range(count):
                tables[member, k, slot] = list(orders[source]).index(orders[member][slot])
    return tables.reshape(count, count * count)


def add(first, second):
    return (first.astype(jnp.float32) + second.astype(jnp.float32)).astype(jnp.bfloat16)


def per_device(
    frames,
    norm_gain,
    router,
    w_in,
    w_out,
    routing,
    head_gain,
    head_weight,
    frame_lengths,
    labels,
    label_lengths,
):
    sections = lax.axis_size("section")
    section_id = lax.axis_index("section")
    group_size = lax.axis_size("expert")
    member = lax.axis_index("expert")
    outer_size = lax.axis_size("dpo")
    inner_size = lax.axis_size("dpi")
    core = lax.axis_index("dpi")
    micro, utt_dev, frame_count, width = frames.shape
    label_max = labels.shape[2]
    experts = w_in.shape[1] * group_size
    hidden = w_in.shape[3]
    pair_count = micro * utt_dev
    per_section = pair_count // sections
    first_pair = section_id * per_section
    group_count = 2 if per_section % (2 * utt_dev) == 0 else 1
    group_pairs = per_section // group_count
    share = (utt_dev * frame_count * 9 + 8 * experts - 1) // (8 * experts)
    capacity = round_up(share * -(-group_pairs // utt_dev), 16)
    span = group_pairs * frame_count
    member_ref = member.astype(jnp.int32).reshape(1)

    def mine_of(value):
        return lax.dynamic_slice_in_dim(value, first_pair, per_section, 0)

    def exchange(blocks, sign):
        return [blocks[0]] + [
            rotate(blocks[k], "expert", sign * k) for k in range(1, group_size)
        ]

    def lanes_of(ids):
        ids = jnp.pad(mine_of(ids), ((0, 0), (0, LANES - frame_count)), constant_values=-1)
        return [ids[g * group_pairs : (g + 1) * group_pairs] for g in range(group_count)]

    rows = lax.dynamic_slice_in_dim(
        frames.reshape(pair_count * frame_count, width),
        first_pair * frame_count,
        per_section * frame_count,
        0,
    )
    current = [rows[g * span : (g + 1) * span] for g in range(group_count)]
    own_ids = routing.reshape(pair_count, frame_count)
    paired = sections == 2 and inner_size == 2
    if paired:
        other_ids = swap(own_ids, "section")
        all_ids = [
            jnp.where(section_id == layer, own_ids, other_ids) for layer in range(sections)
        ]
    else:
        all_ids = lax.all_gather(own_ids, "section")
    layer_ids = [lanes_of(all_ids[layer]) for layer in range(sections)]
    outgoing = [
        dispatch(current[g], layer_ids[0][g], member_ref, experts, capacity, frame_count)
        for g in range(group_count)
    ]
    received = [exchange(blocks, 1) for blocks in outgoing]

    held_gain, held_router, held_in, held_out = lax.optimization_barrier(
        (norm_gain, router, w_in, w_out, outgoing[0][0])
    )[:4]
    own_table = jnp.concatenate(
        [
            held_gain,
            jnp.zeros((7, width), jnp.float32),
            jnp.transpose(held_router[0]).astype(jnp.float32),
            jnp.zeros((round_up(experts, 8) - experts, width), jnp.float32),
        ],
        axis=0,
    )
    own = (held_in[0, 0], held_out[0, 0])
    if paired:
        other_table = swap(own_table, "section")
        half = hidden // 2
        sent_in = lax.dynamic_slice(own[0], (0, core * half), (width, half))
        sent_out = lax.dynamic_slice(own[1], (core * half, 0), (half, width))
        sent_in, sent_out, other_table = lax.optimization_barrier((sent_in, sent_out, other_table))
        came_in = swap(sent_in, "section")
        came_out = swap(sent_out, "section")
        other = [(came_in, came_out), (swap(came_in, "dpi"), swap(came_out, "dpi"))]
    else:
        all_tables = lax.all_gather(own_table, "section")
        all_in = lax.all_gather(own[0], "section")
        all_out = lax.all_gather(own[1], "section")

    layers = []
    for layer in range(sections):
        if paired:
            mine = section_id == layer
            table = jnp.where(mine, own_table, other_table)
            layers.append((table, own, other, mine.astype(jnp.int32).reshape(1)))
        else:
            chosen = (all_in[layer], all_out[layer])
            layers.append((all_tables[layer], chosen, [], jnp.ones((1,), jnp.int32)))

    labels, frame_lengths, label_lengths = lax.optimization_barrier(
        (labels, frame_lengths, label_lengths, outgoing[-1][0])
    )[:3]
    notes = jnp.concatenate(
        [
            mine_of(labels.reshape(pair_count, label_max)),
            mine_of(frame_lengths.reshape(pair_count, 1)),
            mine_of(label_lengths.reshape(pair_count, 1)),
        ],
        axis=1,
    )
    if group_size == 4:
        found = [notes] + [rotate(notes, "expert", -k) for k in range(1, group_size)]
        low = member < 2
        notes_all = jnp.stack(
            [
                found[0],
                jnp.where(low, found[1], found[3]),
                found[2],
                jnp.where(low, found[3], found[1]),
            ]
        )
    else:
        notes_all = lax.all_gather(notes, "expert")
    shard = head_weight.shape[1]
    weight_rows = jnp.transpose(head_weight)
    split = notes_all.reshape(group_size, group_count, group_pairs, label_max + 2)
    notes_all = jnp.transpose(split, (1, 0, 2, 3)).reshape(-1, label_max + 2)
    utterances = notes_all.shape[0]
    names = notes_all[:, :label_max]
    named = jnp.concatenate(
        [
            names,
            jnp.zeros((utterances, 1), jnp.int32),
            jnp.full((utterances, COLS - label_max - 1), -1, jnp.int32),
        ],
        axis=1,
    ).reshape(utterances * COLS)
    local = named - member * shard
    places = jnp.where((named >= 0) & (local >= 0) & (local < shard), local, -1)
    label_weight = label_rows(weight_rows, places.reshape(-1, 1))
    entries = utterances * COLS // group_count

    normed = []
    for layer in range(sections):
        table, weights, others, pick_own = layers[layer]
        ids = layer_ids[layer]
        for g in range(group_count):
            done = run_expert(received[g], table, weights, others, pick_own)
            returned = exchange(done, -1)
            if layer == 0 and g == 0:
                returned, label_weight = lax.optimization_barrier((returned, label_weight))
            if layer < sections - 1:
                current[g], blocks = combine_and_dispatch(
                    current[g],
                    returned,
                    ids[g],
                    table,
                    layer_ids[layer + 1][g],
                    member_ref,
                    experts,
                    capacity,
                    frame_count,
                )
                received[g] = exchange(blocks, 1)
            else:
                normed.append(
                    combine_and_norm(
                        current[g],
                        returned,
                        ids[g],
                        table,
                        head_gain.reshape(1, width),
                        member_ref,
                        experts,
                        capacity,
                        frame_count,
                    )
                )

    def logits_of(g, pieces):
        return head_logits(
            pieces,
            member_ref,
            weight_rows,
            label_weight[g * entries : (g + 1) * entries],
            frame_count,
        )

    def stats_of(stats):
        if group_size == 4:
            return [stats] + [rotate(stats, "expert", -k) for k in range(1, group_size)]
        gathered = lax.all_gather(stats, "expert")
        return [
            lax.dynamic_index_in_dim(gathered, (member + k) % group_size, 0, keepdims=False)
            for k in range(group_size)
        ]

    heads, found = [], []
    previous = None
    for g in range(group_count):
        value = normed[g]
        if group_size == 4:
            if previous is not None:
                value = after(value, *previous[0])
            near = line_near(value)
            if previous is not None:
                near = lax.optimization_barrier((near, previous[1]))[0]
            far = line_far(near, member)
            if previous is not None:
                far = after(far, previous[2])
            pieces = [value, *near, far, line_end(far)]
        else:
            gathered = lax.all_gather(value, "expert")
            near, far = None, None
            pieces = [gathered[k] for k in range(group_size)]
        logits, rows_all, stats = logits_of(g, pieces)
        previous = (near, far, stats)
        heads.append((logits, rows_all))
        found.append(stats_of(stats))
    tables = jnp.asarray(slot_tables(group_size))
    slots = lax.dynamic_index_in_dim(tables, member, 0, keepdims=False)
    occupancy, high, low, losses = ctc_pass(
        found,
        slots,
        jnp.pad(names, ((0, 0), (0, LANES - label_max))),
        notes_all[:, label_max : label_max + 1],
        notes_all[:, label_max + 1 :],
        frame_count,
        label_max,
    )
    own_slot = 0 if group_size == 4 else member
    held_utterances = group_size * group_pairs
    my_losses = jnp.concatenate(
        [
            lax.dynamic_slice(
                losses, (g * held_utterances + own_slot * group_pairs, 0), (group_pairs, 1)
            )
            for g in range(group_count)
        ],
        axis=0,
    )

    def gradient(order, count):
        return head_gradient(
            [head[0] for head in heads],
            [head[1] for head in heads],
            occupancy,
            high,
            low,
            places.reshape(1, -1),
            order,
            count,
        )

    blocks = heads[0][0].shape[0] // BLOCK_ROWS
    if paired and outer_size == 2 and blocks == 8:
        outer = lax.axis_index("dpo")

        def pair_of(side, first, second):
            return jnp.stack([side * 4 + first, side * 4 + 2 + second]).astype(jnp.int32)

        sibling_sent = gradient(pair_of(1 - core, 1 - section_id, 1 - outer), 2)
        came_sent = swap(sibling_sent, "dpi")
        own_order = after(pair_of(core, 1 - section_id, 1 - outer), sibling_sent)
        sent = add(gradient(own_order, 2), came_sent)
        first_in = swap(sent[:BLOCK_ROWS], "section")
        second_in = swap(sent[BLOCK_ROWS:], "dpo")
        kept_order = after(pair_of(1 - core, section_id, outer), sent)
        came_kept = swap(gradient(kept_order, 2), "dpi")
        kept = add(gradient(after(pair_of(core, section_id, outer), sent), 2), came_kept)
        first = add(kept[:BLOCK_ROWS], first_in)
        second = add(kept[BLOCK_ROWS:], second_in)
        part = BLOCK_ROWS // 2

        def piece(value, index):
            return lax.dynamic_slice_in_dim(value, index * part, part, 0)

        first_far = swap(piece(first, 1 - outer), "dpo")
        second_far = swap(piece(second, 1 - section_id), "section")
        final = jnp.concatenate(
            [add(piece(first, outer), first_far), add(piece(second, section_id), second_far)],
            axis=0,
        )
        across = swap(final, "section")
        beside = swap(final, "dpo")
        first_diagonal = swap(beside[:part], "section")
        second_diagonal = swap(across[part:], "dpo")
        mine = [final, across, beside, first_diagonal, second_diagonal]
        theirs = [swap(value, "dpi") for value in mine]
        pieces, offsets = [], []
        for side, held in ((core, mine), (1 - core, theirs)):
            where = (
                (section_id, outer),
                (1 - section_id, outer),
                (section_id, 1 - outer),
            )
            for value, (s, y) in zip(held[:3], where):
                pieces += [value[:part], value[part:]]
                offsets += [
                    side * 1024 + s * 256 + y * 128,
                    side * 1024 + 512 + y * 256 + s * 128,
                ]
            pieces += held[3:]
            s, y = 1 - section_id, 1 - outer
            offsets += [
                side * 1024 + s * 256 + y * 128,
                side * 1024 + 512 + y * 256 + s * 128,
            ]
        whole = assemble(pieces, jnp.stack(offsets).astype(jnp.int32), shard)
    else:
        partial = gradient(jnp.arange(blocks, dtype=jnp.int32), blocks)[:shard]
        whole = lax.psum(partial.astype(jnp.float32), ("section", "dpo", "dpi")).astype(
            jnp.bfloat16
        )
    return (my_losses, jnp.transpose(whole))


def solution(mesh):
    sections, group_size, spread = (mesh.shape[name] for name in ("section", "expert", "dp"))
    inner = 2 if spread % 2 == 0 else 1
    split = Mesh(
        mesh.devices.reshape(sections, group_size, spread // inner, inner),
        ("section", "expert", "dpo", "dpi"),
    )
    block = ("expert", "dpo", "dpi")
    placed = (
        P(None, block, None, None),
        P("section", None),
        P("section", None, None),
        P("section", "expert", None, None),
        P("section", "expert", None, None),
        P("section", None, block, None, None),
        P(),
        P(None, "expert"),
        P(None, block),
        P(None, block, None),
        P(None, block),
    )
    return jax.shard_map(
        per_device,
        mesh=split,
        in_specs=placed,
        out_specs=(P("section", block), P(None, "expert")),
        check_vma=False,
    )
```

```python
import jax
import jax.numpy as jnp
import numpy as np
from jax import lax
from jax.experimental import pallas as pl
from jax.experimental.pallas import tpu as pltpu
from jax.sharding import Mesh, PartitionSpec as P

EPSILON = 1e-06
LOG_ZERO = -1e30
VMEM_LIMIT = 16 * 1024 * 1024
LANES = 128
COLS = 16
PEAK, TOTAL, WHOLE = COLS - 3, COLS - 2, COLS - 3
BLOCK_ROWS = 256
NT = (((1,), (1,)), ((), ()))
NN = (((1,), (0,)), ((), ()))


def round_up(value, unit):
    return -(-value // unit) * unit


def vmem_spec():
    return pl.BlockSpec(memory_space=pltpu.VMEM)


def smem_spec():
    return pl.BlockSpec(memory_space=pltpu.SMEM)


def call(kernel, out_shape, flops=0, moved=0, **options):
    return pl.pallas_call(
        kernel,
        out_shape=out_shape,
        compiler_params=pltpu.CompilerParams(vmem_limit_bytes=VMEM_LIMIT),
        cost_estimate=pl.CostEstimate(flops=flops, bytes_accessed=moved, transcendentals=0),
        **options,
    )


def bf16_rows(count, width):
    return jax.ShapeDtypeStruct((count, width), jnp.bfloat16)


def as_mask(values):
    return values.astype(jnp.float32).astype(jnp.bfloat16)


def rms_scale(values, gain):
    values = values.astype(jnp.float32)
    scale = lax.rsqrt(jnp.mean(values * values, axis=-1, keepdims=True) + EPSILON)
    return (values * scale * gain).astype(jnp.bfloat16)


def expert_column(ids, frame_count):
    pairs = ids.shape[0]
    square = jnp.concatenate(
        [ids.astype(jnp.float32), jnp.full((LANES - pairs, LANES), -1.0, jnp.float32)], axis=0
    )
    turned = jnp.transpose(square, (1, 0)).astype(jnp.int32)
    return jnp.concatenate([turned[:frame_count, p : p + 1] for p in range(pairs)], axis=0)


def placement(column, member, experts, capacity):
    count = column.shape[0]
    shifted = column - member
    relative = jnp.where(shifted < 0, shifted + experts, shifted)
    lane = lax.broadcasted_iota(jnp.int32, (count, LANES), 1)
    one_hot = (lane == relative).astype(jnp.float32)
    before = lax.broadcasted_iota(jnp.int32, (count, count), 1) <= lax.broadcasted_iota(
        jnp.int32, (count, count), 0
    )
    rank = lax.dot_general(
        as_mask(before), one_hot.astype(jnp.bfloat16), NN, preferred_element_type=jnp.float32
    )
    start = (lane * capacity - 1).astype(jnp.float32)
    slots = jnp.sum(one_hot * (rank + start), axis=1, keepdims=True).astype(jnp.int32)
    places = lax.broadcasted_iota(jnp.int32, (count, experts * capacity), 1)
    return (places == slots).astype(jnp.float32)


def scatter_rows(rows, ids, member, experts, capacity, frame_count, out_refs):
    count = rows.shape[0]
    chosen = placement(expert_column(ids, frame_count), member, experts, capacity)
    tall = round_up(count, LANES)
    if tall > count:
        chosen = jnp.concatenate(
            [chosen, jnp.zeros((tall - count, chosen.shape[1]), jnp.float32)], axis=0
        )
    pick = jnp.transpose(chosen, (1, 0))[:, :count].astype(jnp.bfloat16)
    placed = lax.dot_general(pick, rows, NN, preferred_element_type=jnp.float32).astype(
        jnp.bfloat16
    )
    for turn, out_ref in enumerate(out_refs):
        out_ref[...] = placed[turn * capacity : (turn + 1) * capacity]


def combine_rows(rows, returned, ids, table, member, experts, capacity, frame_count):
    column = expert_column(ids, frame_count)
    pick = placement(column, member, experts, capacity).astype(jnp.bfloat16)
    normed = rms_scale(rows, table[:1])
    router = jnp.concatenate(
        [table[8:], jnp.zeros((LANES + 8 - table.shape[0], rows.shape[1]), jnp.float32)], axis=0
    ).astype(jnp.bfloat16)
    logits = lax.dot_general(normed, router, NT, preferred_element_type=jnp.float32)
    lane = lax.broadcasted_iota(jnp.int32, logits.shape, 1)
    gate = jax.nn.sigmoid(jnp.sum(jnp.where(lane == column, logits, 0.0), axis=1, keepdims=True))
    stacked = jnp.concatenate(returned, axis=0)
    mixed = lax.dot_general(pick, stacked, NN, preferred_element_type=jnp.float32)
    return (rows.astype(jnp.float32) + gate * mixed).astype(jnp.bfloat16)


def dispatch(rows, ids, member, experts, capacity, frame_count):
    width = rows.shape[1]

    def kernel(member_ref, rows_ref, ids_ref, *out_refs):
        scatter_rows(
            rows_ref[...], ids_ref[...], member_ref[0], experts, capacity, frame_count, out_refs
        )

    return call(
        kernel,
        tuple(bf16_rows(capacity, width) for _ in range(experts)),
        1 << 27,
        1 << 20,
        in_specs=[smem_spec()] + [vmem_spec()] * 2,
        out_specs=tuple(vmem_spec() for _ in range(experts)),
    )(member, rows, ids)


def run_expert(received, table, own, other, pick_own):
    count = len(received)
    capacity, width = received[0].shape
    others = len(other)

    def kernel(pick_ref, table_ref, in_ref, out_weight_ref, *refs):
        other_refs, received_refs, out_refs = (
            refs[: 2 * others],
            refs[2 * others : 2 * others + count],
            refs[2 * others + count :],
        )

        def work(pieces):
            stacked = jnp.concatenate([ref[...] for ref in received_refs], axis=0)
            normed = rms_scale(stacked, table_ref[:1])
            total = None
            for weight_in, weight_out in pieces:
                hidden = lax.dot_general(
                    normed, weight_in[...], NN, preferred_element_type=jnp.float32
                )
                active = (hidden / (1.0 + jnp.exp(-hidden))).astype(jnp.bfloat16)
                part = lax.dot_general(
                    active, weight_out[...], NN, preferred_element_type=jnp.float32
                )
                total = part if total is None else total + part
            total = total.astype(jnp.bfloat16)
            for turn, out_ref in enumerate(out_refs):
                out_ref[...] = total[turn * capacity : (turn + 1) * capacity]

        if others == 0:
            work([(in_ref, out_weight_ref)])
            return

        @pl.when(pick_ref[0] == 1)
        def _():
            work([(in_ref, out_weight_ref)])

        @pl.when(pick_ref[0] != 1)
        def _():
            work([(other_refs[2 * i], other_refs[2 * i + 1]) for i in range(others)])

    flat = [weight for pair in other for weight in pair]
    return call(
        kernel,
        tuple(bf16_rows(capacity, width) for _ in range(count)),
        4 * count * capacity * width * own[0].shape[1],
        4 << 20,
        in_specs=[smem_spec()] + [vmem_spec()] * (3 + 2 * others + count),
        out_specs=tuple(vmem_spec() for _ in range(count)),
    )(pick_own, table, *own, *flat, *received)


def combine_and_dispatch(
    rows, returned, ids, table, next_ids, member, experts, capacity, frame_count
):
    width = rows.shape[1]

    def kernel(member_ref, rows_ref, ids_ref, table_ref, next_ref, *refs):
        returned_refs, x_ref, out_refs = refs[:experts], refs[experts], refs[experts + 1 :]
        mixed = combine_rows(
            rows_ref[...],
            [ref[...] for ref in returned_refs],
            ids_ref[...],
            table_ref[...],
            member_ref[0],
            experts,
            capacity,
            frame_count,
        )
        x_ref[...] = mixed
        scatter_rows(
            mixed, next_ref[...], member_ref[0], experts, capacity, frame_count, out_refs
        )

    shapes = (bf16_rows(*rows.shape),) + tuple(
        bf16_rows(capacity, width) for _ in range(experts)
    )
    result = call(
        kernel,
        shapes,
        1 << 28,
        2 << 20,
        in_specs=[smem_spec()] + [vmem_spec()] * (4 + experts),
        out_specs=tuple(vmem_spec() for _ in shapes),
    )(member, rows, ids, table, next_ids, *returned)
    return result[0], result[1:]


def combine_and_norm(
    rows, returned, ids, table, head_gain, member, experts, capacity, frame_count
):
    def kernel(member_ref, rows_ref, ids_ref, table_ref, head_ref, *refs):
        final = combine_rows(
            rows_ref[...],
            [ref[...] for ref in refs[:experts]],
            ids_ref[...],
            table_ref[...],
            member_ref[0],
            experts,
            capacity,
            frame_count,
        )
        refs[experts][...] = rms_scale(final, head_ref[...])

    return call(
        kernel,
        bf16_rows(*rows.shape),
        1 << 28,
        2 << 20,
        in_specs=[smem_spec()] + [vmem_spec()] * (4 + experts),
        out_specs=vmem_spec(),
    )(member, rows, ids, table, head_gain, *returned)


def block_list(shard):
    return [(i, min(BLOCK_ROWS, shard - i)) for i in range(0, shard, BLOCK_ROWS)]


def label_rows(weight, places):
    shard, width = weight.shape
    entries = places.shape[0]

    def kernel(places_ref, weight_ref, out_ref):
        total = jnp.zeros((entries, width), jnp.float32)
        for first, size in block_list(shard):
            entry = first + lax.broadcasted_iota(jnp.int32, (entries, size), 1)
            total = total + lax.dot_general(
                as_mask(entry == places_ref[...]),
                weight_ref[first : first + size],
                NN,
                preferred_element_type=jnp.float32,
            )
        out_ref[...] = total.astype(jnp.bfloat16)

    return call(
        kernel,
        bf16_rows(entries, width),
        2 * shard * entries * width,
        6 << 20,
        in_specs=[vmem_spec()] * 2,
        out_specs=vmem_spec(),
    )(places, weight)


def head_logits(pieces, member, weight, label_weight, frame_count):
    given = len(pieces)
    line = given == 5
    count = 4 if line else given
    span, width = pieces[0].shape
    row_count = count * span
    shard = weight.shape[0]
    height = round_up(shard, BLOCK_ROWS)
    entries = label_weight.shape[0]

    def kernel(member_ref, weight_ref, label_ref, *refs):
        piece_refs = refs[:given]
        logits_ref, rows_ref, stats_ref = refs[given:]

        def put(slot, piece_ref):
            rows_ref[slot * span : (slot + 1) * span] = piece_ref[...]

        def put_if(condition, slot, piece_ref):
            @pl.when(condition)
            def _():
                put(slot, piece_ref)

        if line:
            value_ref, left_ref, right_ref, far_ref, end_ref = piece_refs
            place = member_ref[0]
            put(0, value_ref)
            put_if(place < 2, 1, left_ref)
            put_if(place >= 2, 1, right_ref)
            put(2, far_ref)
            put_if((place == 0) | (place == 3), 3, end_ref)
            put_if(place == 1, 3, right_ref)
            put_if(place == 2, 3, left_ref)
        else:
            for slot in range(count):
                put(slot, piece_refs[slot])

        peak = jnp.full((1, row_count), LOG_ZERO, jnp.float32)
        total = jnp.zeros((1, row_count), jnp.float32)
        for first, size in block_list(shard):
            logits = lax.dot_general(
                weight_ref[first : first + size],
                rows_ref[...],
                NT,
                preferred_element_type=jnp.float32,
            )
            logits_ref[first : first + size] = logits
            before = peak
            peak = jnp.maximum(before, jnp.max(logits, axis=0, keepdims=True))
            total = total * jnp.exp(before - peak) + jnp.sum(
                jnp.exp(logits - peak), axis=0, keepdims=True
            )
        if height > shard:
            logits_ref[shard:] = jnp.full((height - shard, row_count), LOG_ZERO, jnp.float32)
        crossed = lax.dot_general(
            label_ref[...], rows_ref[...], NT, preferred_element_type=jnp.float32
        )
        owner = lax.broadcasted_iota(jnp.int32, (COLS, row_count), 1) // frame_count
        picked = jnp.zeros((COLS, row_count), jnp.float32)
        for utterance in range(entries // COLS):
            part = crossed[utterance * COLS : (utterance + 1) * COLS]
            picked = picked + jnp.where(owner == utterance, part, 0.0)
        place = lax.broadcasted_iota(jnp.int32, (COLS, row_count), 0)
        stats = jnp.where(place == PEAK, peak, picked)
        stats = jnp.where(place == TOTAL, total, stats)
        for slot in range(count):
            stats_ref[slot] = stats[:, slot * span : (slot + 1) * span]

    return call(
        kernel,
        (
            jax.ShapeDtypeStruct((height, row_count), jnp.float32),
            bf16_rows(row_count, width),
            jax.ShapeDtypeStruct((count, COLS, span), jnp.float32),
        ),
        2 * height * row_count * width,
        9 << 20,
        in_specs=[smem_spec()] + [vmem_spec()] * (2 + given),
        out_specs=tuple(vmem_spec() for _ in range(3)),
    )(member, weight, label_weight, *pieces)


def log_add(first, second):
    peak = jnp.maximum(first, second)
    return peak + jnp.log(jnp.exp(first - peak) + jnp.exp(second - peak))


def log_add3(first, second, third):
    peak = jnp.maximum(jnp.maximum(first, second), third)
    return peak + jnp.log(
        jnp.exp(first - peak) + jnp.exp(second - peak) + jnp.exp(third - peak)
    )


def ctc_pass(stats, slots, labels, frame_counts, label_counts, frame_count, label_max):
    group_count, sources = len(stats), len(stats[0])
    count, _, span = stats[0][0].shape
    row_count = group_count * count * span
    utterances = labels.shape[0]
    entries = utterances * COLS
    given = group_count * sources

    def kernel(slots_ref, labels_ref, frames_ref, counts_ref, *refs):
        (
            out_ref,
            high_ref,
            low_ref,
            loss_ref,
            turn_ref,
            emission_ref,
            emit_blank,
            emit_label,
            blank_fwd,
            label_fwd,
            blank_bwd,
            label_bwd,
            occupancy_ref,
        ) = refs[given:]
        place = lax.broadcasted_iota(jnp.int32, (COLS, span), 0)
        turn_ref[...] = jnp.zeros(turn_ref.shape, jnp.float32)
        for part in range(group_count * count):
            group, slot = part // count, part % count
            found = [
                refs[group * sources + k][slots_ref[k * count + slot]] for k in range(sources)
            ]
            joined = found[0]
            peak = found[0][PEAK : PEAK + 1]
            for other in found[1:]:
                joined = joined + other
                peak = jnp.maximum(peak, other[PEAK : PEAK + 1])
            total = jnp.zeros((1, span), jnp.float32)
            for other in found:
                total = total + other[TOTAL : TOTAL + 1] * jnp.exp(other[PEAK : PEAK + 1] - peak)
            log_total = peak + jnp.log(total)
            turn_ref[:COLS, :span] = jnp.where(place == TOTAL, log_total, joined - log_total)
            emission_ref[part * span : (part + 1) * span] = jnp.transpose(turn_ref[...], (1, 0))[
                :span
            ]

        lane = lax.broadcasted_iota(jnp.int32, (utterances, LANES), 1)
        is_label = lane < label_max
        is_blank = lane <= label_max
        names = labels_ref[...]
        earlier = pltpu.roll(names, 1, 1)
        skip = is_label & (lane >= 1) & (names != 0) & (names != earlier)
        later = pltpu.roll(names, LANES - 1, 1)
        skip_next = (lane < label_max - 1) & (later != 0) & (later != names)
        frames = frames_ref[...]
        counts = counts_ref[...]
        ends_blank = jnp.where(lane == counts, 0.0, LOG_ZERO)
        ends_label = jnp.where(lane == counts - 1, 0.0, LOG_ZERO)

        def spread(step, carry):
            row = emission_ref[pl.ds(step, utterances, stride=frame_count), :]
            blank = jnp.sum(jnp.where(lane == label_max, row, 0.0), axis=1, keepdims=True)
            emit_blank[step] = jnp.where(is_blank, blank, LOG_ZERO)
            emit_label[step] = jnp.where(is_label, row, LOG_ZERO)
            return carry

        lax.fori_loop(0, frame_count, spread, 0, unroll=16)

        def advance(step, carry):
            fwd_blank, fwd_label, bwd_blank, bwd_label = carry
            moved = jnp.where(lane == 0, LOG_ZERO, pltpu.roll(fwd_label, 1, 1))
            new_blank = log_add(fwd_blank, moved) + emit_blank[step]
            new_label = (
                log_add3(fwd_label, fwd_blank, jnp.where(skip, moved, LOG_ZERO))
                + emit_label[step]
            )
            alive = step < frames
            fwd_blank = jnp.where(alive, new_blank, fwd_blank)
            fwd_label = jnp.where(alive, new_label, fwd_label)
            blank_fwd[step] = fwd_blank
            label_fwd[step] = fwd_label

            back = frame_count - 1 - step
            out_blank = bwd_blank + emit_blank[back + 1]
            out_label = bwd_label + emit_label[back + 1]
            next_blank = pltpu.roll(out_blank, LANES - 1, 1)
            next_label = jnp.where(skip_next, pltpu.roll(out_label, LANES - 1, 1), LOG_ZERO)
            ended = back >= frames - 1
            bwd_blank = jnp.where(ended, ends_blank, log_add(out_blank, out_label))
            bwd_label = jnp.where(
                ended, ends_label, log_add3(out_label, next_blank, next_label)
            )
            blank_bwd[back] = bwd_blank
            label_bwd[back] = bwd_label
            return (fwd_blank, fwd_label, bwd_blank, bwd_label)

        first_blank = jnp.where(lane == 0, emit_blank[0], LOG_ZERO)
        first_label = jnp.where(lane == 0, emit_label[0], LOG_ZERO)
        blank_fwd[0] = first_blank
        label_fwd[0] = first_label
        blank_bwd[frame_count - 1] = ends_blank
        label_bwd[frame_count - 1] = ends_label
        fwd_blank, fwd_label, _, _ = lax.fori_loop(
            1, frame_count, advance, (first_blank, first_label, ends_blank, ends_label), unroll=4
        )
        end_state = jnp.sum(jnp.where(lane == counts, fwd_blank, 0.0), axis=1, keepdims=True)
        near_state = jnp.sum(jnp.where(lane == counts - 1, fwd_label, 0.0), axis=1, keepdims=True)
        log_like = log_add(end_state, near_state)
        loss_ref[...] = jnp.broadcast_to(-log_like, (utterances, LANES))

        def occupy(step, carry):
            blank = jnp.exp(blank_fwd[step] + blank_bwd[step] - log_like)
            label = jnp.exp(label_fwd[step] + label_bwd[step] - log_like)
            blank = jnp.sum(jnp.where(is_blank, blank, 0.0), axis=1, keepdims=True)
            label = jnp.where(is_label, label, 0.0)
            whole = blank + jnp.sum(label, axis=1, keepdims=True)
            filled = jnp.where(lane == label_max, blank, label)
            filled = jnp.where(lane == WHOLE, whole, filled)
            filled = jnp.where(step < frames, -filled, 0.0)
            row = emission_ref[pl.ds(step, utterances, stride=frame_count), :]
            occupancy_ref[pl.ds(step, utterances, stride=frame_count), :] = jnp.where(
                lane == TOTAL, row, filled
            )
            return carry

        lax.fori_loop(0, frame_count, occupy, 0, unroll=16)
        turned = jnp.transpose(occupancy_ref[...], (1, 0))[:COLS]
        out_ref[...] = turned
        row_place = lax.broadcasted_iota(jnp.int32, (COLS, row_count), 0)
        owner = lax.broadcasted_iota(jnp.int32, (COLS, row_count), 1) // frame_count
        source = jnp.where(row_place < WHOLE, turned, 0.0)
        for utterance in range(utterances):
            part = jnp.where(owner == utterance, source, 0.0)
            high = part.astype(jnp.bfloat16)
            high_ref[utterance * COLS : (utterance + 1) * COLS] = high
            low_ref[utterance * COLS : (utterance + 1) * COLS] = (
                part - high.astype(jnp.float32)
            ).astype(jnp.bfloat16)

    held = pltpu.VMEM((frame_count, utterances, LANES), jnp.float32)
    table = pltpu.VMEM((row_count, LANES), jnp.float32)
    flat = [value for group in stats for value in group]
    return call(
        kernel,
        (
            jax.ShapeDtypeStruct((COLS, row_count), jnp.float32),
            bf16_rows(entries, row_count),
            bf16_rows(entries, row_count),
            jax.ShapeDtypeStruct((utterances, LANES), jnp.float32),
        ),
        1 << 26,
        1 << 20,
        in_specs=[smem_spec()] + [vmem_spec()] * (3 + given),
        out_specs=tuple(vmem_spec() for _ in range(4)),
        scratch_shapes=[pltpu.VMEM((LANES, LANES), jnp.float32), table]
        + [held] * 6
        + [table],
    )(slots, labels, frame_counts, label_counts, *flat)


def head_gradient(logits, rows, occupancy, high, low, places, order, blocks):
    count = len(logits)
    row_count, width = rows[0].shape
    entries = places.shape[1]

    def kernel(order_ref, *refs):
        logits_refs, rows_refs = refs[:count], refs[count : 2 * count]
        occupancy_ref, high_ref, low_ref, places_ref, out_ref = refs[2 * count :]
        for block in range(blocks):
            start = pl.multiple_of(order_ref[block] * BLOCK_ROWS, BLOCK_ROWS)
            entry = start + lax.broadcasted_iota(jnp.int32, (BLOCK_ROWS, entries), 0)
            select = as_mask(entry == places_ref[...])
            total = None
            for g in range(count):
                lanes = slice(g * row_count, (g + 1) * row_count)
                scattered = lax.dot_general(
                    select, high_ref[:, lanes], NN, preferred_element_type=jnp.float32
                ) + lax.dot_general(
                    select, low_ref[:, lanes], NN, preferred_element_type=jnp.float32
                )
                whole = occupancy_ref[WHOLE : WHOLE + 1, lanes]
                log_total = occupancy_ref[TOTAL : TOTAL + 1, lanes]
                values = logits_refs[g][pl.ds(start, BLOCK_ROWS), :]
                grad = (scattered - jnp.exp(values - log_total) * whole).astype(jnp.bfloat16)
                part = lax.dot_general(
                    grad, rows_refs[g][...], NN, preferred_element_type=jnp.float32
                )
                total = part if total is None else total + part
            out_ref[block * BLOCK_ROWS : (block + 1) * BLOCK_ROWS] = total.astype(jnp.bfloat16)

    return call(
        kernel,
        bf16_rows(blocks * BLOCK_ROWS, width),
        2 * blocks * BLOCK_ROWS * count * row_count * (width + 2 * entries),
        10 << 20,
        in_specs=[smem_spec()] + [vmem_spec()] * (2 * count + 4),
        out_specs=vmem_spec(),
    )(order, *logits, *rows, occupancy, high, low, places)


def assemble(pieces, offsets, height):
    count = len(pieces)
    part, width = pieces[0].shape
    short = height % part

    def kernel(offsets_ref, *refs):
        out_ref, sems = refs[count], refs[count + 1]

        def each(act):
            for index in range(count):
                offset = pl.multiple_of(offsets_ref[index], part)

                @pl.when(offset + part <= height)
                def _():
                    act(
                        pltpu.make_async_copy(
                            refs[index], out_ref.at[pl.ds(offset, part)], sems.at[index]
                        )
                    )

                if short:

                    @pl.when(offset + part > height)
                    def _():
                        act(
                            pltpu.make_async_copy(
                                refs[index].at[pl.ds(0, short)],
                                out_ref.at[pl.ds(height - short, short)],
                                sems.at[index],
                            )
                        )

        each(lambda copy: copy.start())
        each(lambda copy: copy.wait())

    return call(
        kernel,
        bf16_rows(height, width),
        0,
        2 * height * width * 2,
        in_specs=[smem_spec()] + [pl.BlockSpec(memory_space=pl.ANY)] * count,
        out_specs=pl.BlockSpec(memory_space=pl.ANY),
        scratch_shapes=[pltpu.SemaphoreType.DMA((count,))],
    )(offsets, *pieces)


def swap(value, axis):
    return lax.ppermute(value, axis, [(0, 1), (1, 0)])


def rotate(value, axis, by):
    count = lax.axis_size(axis)
    return lax.ppermute(value, axis, [(i, (i + by) % count) for i in range(count)])


def after(value, *others):
    return lax.optimization_barrier((value,) + others)[0]


def line_near(value):
    left = lax.ppermute(value, "expert", [(1, 0), (2, 1), (3, 2)])
    right = lax.ppermute(value, "expert", [(0, 1), (1, 2), (2, 3)])
    return left, right


def line_far(near, member):
    left = lax.ppermute(near[0], "expert", [(1, 0), (2, 1)])
    right = lax.ppermute(near[1], "expert", [(1, 2), (2, 3)])
    return jnp.where(member < 2, left, right)


def line_end(far):
    return lax.ppermute(far, "expert", [(1, 0), (2, 3)])


LINE_ORDER = np.array([[0, 1, 2, 3], [1, 2, 3, 0], [2, 1, 0, 3], [3, 2, 1, 0]])


def slot_orders(count):
    return LINE_ORDER if count == 4 else np.tile(np.arange(count), (count, 1))


def slot_tables(count):
    orders = slot_orders(count)
    tables = np.zeros((count, count, count), np.int32)
    for member in range(count):
        for k in range(count):
            source = (member + k) % count
            for slot in range(count):
                tables[member, k, slot] = list(orders[source]).index(orders[member][slot])
    return tables.reshape(count, count * count)


def add(first, second):
    return (first.astype(jnp.float32) + second.astype(jnp.float32)).astype(jnp.bfloat16)


def per_device(
    frames,
    norm_gain,
    router,
    w_in,
    w_out,
    routing,
    head_gain,
    head_weight,
    frame_lengths,
    labels,
    label_lengths,
):
    sections = lax.axis_size("section")
    section_id = lax.axis_index("section")
    group_size = lax.axis_size("expert")
    member = lax.axis_index("expert")
    outer_size = lax.axis_size("dpo")
    inner_size = lax.axis_size("dpi")
    core = lax.axis_index("dpi")
    micro, utt_dev, frame_count, width = frames.shape
    label_max = labels.shape[2]
    experts = w_in.shape[1] * group_size
    hidden = w_in.shape[3]
    pair_count = micro * utt_dev
    per_section = pair_count // sections
    first_pair = section_id * per_section
    group_count = 2 if per_section % (2 * utt_dev) == 0 else 1
    group_pairs = per_section // group_count
    share = (utt_dev * frame_count * 9 + 8 * experts - 1) // (8 * experts)
    capacity = round_up(share * -(-group_pairs // utt_dev), 16)
    span = group_pairs * frame_count
    member_ref = member.astype(jnp.int32).reshape(1)

    def mine_of(value):
        return lax.dynamic_slice_in_dim(value, first_pair, per_section, 0)

    def exchange(blocks, sign):
        return [blocks[0]] + [
            rotate(blocks[k], "expert", sign * k) for k in range(1, group_size)
        ]

    def lanes_of(ids):
        ids = jnp.pad(mine_of(ids), ((0, 0), (0, LANES - frame_count)), constant_values=-1)
        return [ids[g * group_pairs : (g + 1) * group_pairs] for g in range(group_count)]

    rows = lax.dynamic_slice_in_dim(
        frames.reshape(pair_count * frame_count, width),
        first_pair * frame_count,
        per_section * frame_count,
        0,
    )
    current = [rows[g * span : (g + 1) * span] for g in range(group_count)]
    own_ids = routing.reshape(pair_count, frame_count)
    paired = sections == 2 and inner_size == 2
    if paired:
        other_ids = swap(own_ids, "section")
        all_ids = [
            jnp.where(section_id == layer, own_ids, other_ids) for layer in range(sections)
        ]
    else:
        all_ids = lax.all_gather(own_ids, "section")
    layer_ids = [lanes_of(all_ids[layer]) for layer in range(sections)]
    last = [None]

    def tied(value):
        return value if last[0] is None else after(value, last[0])

    def then(*results):
        last[0] = results[0]

    outgoing = []
    for g in range(group_count):
        outgoing.append(
            dispatch(
                current[g], layer_ids[0][g], tied(member_ref), experts, capacity, frame_count
            )
        )
        then(*outgoing[g])
    received = [exchange(blocks, 1) for blocks in outgoing]

    own_table = jnp.concatenate(
        [
            norm_gain,
            jnp.zeros((7, width), jnp.float32),
            jnp.transpose(router[0]).astype(jnp.float32),
            jnp.zeros((round_up(experts, 8) - experts, width), jnp.float32),
        ],
        axis=0,
    )
    own = (w_in[0, 0], w_out[0, 0])
    if paired:
        other_table = swap(own_table, "section")
        half = hidden // 2
        sent_in = lax.dynamic_slice(own[0], (0, core * half), (width, half))
        sent_out = lax.dynamic_slice(own[1], (core * half, 0), (half, width))
        sent_in, sent_out = lax.optimization_barrier((sent_in, sent_out, other_ids))[:2]
        came_in = swap(sent_in, "section")
        came_out = swap(sent_out, "section")
        other = [(came_in, came_out), (swap(came_in, "dpi"), swap(came_out, "dpi"))]
    else:
        all_tables = lax.all_gather(own_table, "section")
        all_in = lax.all_gather(own[0], "section")
        all_out = lax.all_gather(own[1], "section")

    layers = []
    for layer in range(sections):
        if paired:
            mine = section_id == layer
            table = jnp.where(mine, own_table, other_table)
            layers.append((table, own, other, mine.astype(jnp.int32).reshape(1)))
        else:
            chosen = (all_in[layer], all_out[layer])
            layers.append((all_tables[layer], chosen, [], jnp.ones((1,), jnp.int32)))

    labels, frame_lengths, label_lengths = lax.optimization_barrier(
        (labels, frame_lengths, label_lengths, outgoing[-1][0])
    )[:3]
    notes = jnp.concatenate(
        [
            mine_of(labels.reshape(pair_count, label_max)),
            mine_of(frame_lengths.reshape(pair_count, 1)),
            mine_of(label_lengths.reshape(pair_count, 1)),
        ],
        axis=1,
    )
    if group_size == 4:
        found = [notes] + [rotate(notes, "expert", -k) for k in range(1, group_size)]
        low = member < 2
        notes_all = jnp.stack(
            [
                found[0],
                jnp.where(low, found[1], found[3]),
                found[2],
                jnp.where(low, found[3], found[1]),
            ]
        )
    else:
        notes_all = lax.all_gather(notes, "expert")
    shard = head_weight.shape[1]
    weight_rows = jnp.transpose(head_weight)
    split = notes_all.reshape(group_size, group_count, group_pairs, label_max + 2)
    notes_all = jnp.transpose(split, (1, 0, 2, 3)).reshape(-1, label_max + 2)
    utterances = notes_all.shape[0]
    names = notes_all[:, :label_max]
    named = jnp.concatenate(
        [
            names,
            jnp.zeros((utterances, 1), jnp.int32),
            jnp.full((utterances, COLS - label_max - 1), -1, jnp.int32),
        ],
        axis=1,
    ).reshape(utterances * COLS)
    local = named - member * shard
    places = jnp.where((named >= 0) & (local >= 0) & (local < shard), local, -1)
    label_weight = label_rows(weight_rows, tied(places.reshape(-1, 1)))
    then(label_weight)
    entries = utterances * COLS // group_count

    normed = []
    for layer in range(sections):
        table, weights, others, pick_own = layers[layer]
        ids = layer_ids[layer]
        arrived = []
        for g in range(group_count):
            done = run_expert(received[g], table, weights, others, tied(pick_own))
            then(*done)
            arrived.append(exchange(done, -1))
        for g in range(group_count):
            returned = arrived[g]
            if layer < sections - 1:
                current[g], blocks = combine_and_dispatch(
                    current[g],
                    returned,
                    ids[g],
                    table,
                    layer_ids[layer + 1][g],
                    tied(member_ref),
                    experts,
                    capacity,
                    frame_count,
                )
                then(*blocks)
                received[g] = exchange(blocks, 1)
            else:
                normed.append(
                    combine_and_norm(
                        current[g],
                        returned,
                        ids[g],
                        table,
                        head_gain.reshape(1, width),
                        tied(member_ref),
                        experts,
                        capacity,
                        frame_count,
                    )
                )
                then(normed[g])

    def logits_of(g, pieces):
        return head_logits(
            pieces,
            member_ref,
            weight_rows,
            label_weight[g * entries : (g + 1) * entries],
            frame_count,
        )

    def stats_of(stats):
        if group_size == 4:
            return [stats] + [rotate(stats, "expert", -k) for k in range(1, group_size)]
        gathered = lax.all_gather(stats, "expert")
        return [
            lax.dynamic_index_in_dim(gathered, (member + k) % group_size, 0, keepdims=False)
            for k in range(group_size)
        ]

    heads, found = [], []
    for g in range(group_count):
        value = normed[g]
        if group_size == 4:
            near = line_near(value)
            far = line_far(near, member)
            pieces = [value, *near, far, line_end(far)]
        else:
            gathered = lax.all_gather(value, "expert")
            pieces = [gathered[k] for k in range(group_size)]
        logits, rows_all, stats = logits_of(g, pieces)
        heads.append((logits, rows_all))
        found.append(stats_of(stats))
    tables = jnp.asarray(slot_tables(group_size))
    slots = lax.dynamic_index_in_dim(tables, member, 0, keepdims=False)
    occupancy, high, low, losses = ctc_pass(
        found,
        slots,
        jnp.pad(names, ((0, 0), (0, LANES - label_max))),
        notes_all[:, label_max : label_max + 1],
        notes_all[:, label_max + 1 :],
        frame_count,
        label_max,
    )
    own_slot = 0 if group_size == 4 else member
    held_utterances = group_size * group_pairs
    my_losses = jnp.concatenate(
        [
            lax.dynamic_slice(
                losses, (g * held_utterances + own_slot * group_pairs, 0), (group_pairs, 1)
            )
            for g in range(group_count)
        ],
        axis=0,
    )

    def gradient(order, count):
        return head_gradient(
            [head[0] for head in heads],
            [head[1] for head in heads],
            occupancy,
            high,
            low,
            places.reshape(1, -1),
            order,
            count,
        )

    blocks = heads[0][0].shape[0] // BLOCK_ROWS
    if paired and outer_size == 2 and blocks == 8:
        outer = lax.axis_index("dpo")

        def pair_of(side, first, second):
            return jnp.stack([side * 4 + first, side * 4 + 2 + second]).astype(jnp.int32)

        sibling_sent = gradient(pair_of(1 - core, 1 - section_id, 1 - outer), 2)
        came_sent = swap(sibling_sent, "dpi")
        own_order = after(pair_of(core, 1 - section_id, 1 - outer), sibling_sent)
        sent = add(gradient(own_order, 2), came_sent)
        first_in = swap(sent[:BLOCK_ROWS], "section")
        second_in = swap(sent[BLOCK_ROWS:], "dpo")
        kept_order = after(pair_of(1 - core, section_id, outer), sent)
        came_kept = swap(gradient(kept_order, 2), "dpi")
        kept = add(gradient(after(pair_of(core, section_id, outer), sent), 2), came_kept)
        first = add(kept[:BLOCK_ROWS], first_in)
        second = add(kept[BLOCK_ROWS:], second_in)
        part = BLOCK_ROWS // 2

        def piece(value, index):
            return lax.dynamic_slice_in_dim(value, index * part, part, 0)

        first_far = swap(piece(first, 1 - outer), "dpo")
        second_far = swap(piece(second, 1 - section_id), "section")
        final = jnp.concatenate(
            [add(piece(first, outer), first_far), add(piece(second, section_id), second_far)],
            axis=0,
        )
        across = swap(final, "section")
        beside = swap(final, "dpo")
        first_diagonal = swap(beside[:part], "section")
        second_diagonal = swap(across[part:], "dpo")
        mine = [final, across, beside, first_diagonal, second_diagonal]
        theirs = [swap(value, "dpi") for value in mine]
        pieces, offsets = [], []
        for side, held in ((core, mine), (1 - core, theirs)):
            where = (
                (section_id, outer),
                (1 - section_id, outer),
                (section_id, 1 - outer),
            )
            for value, (s, y) in zip(held[:3], where):
                pieces += [value[:part], value[part:]]
                offsets += [
                    side * 1024 + s * 256 + y * 128,
                    side * 1024 + 512 + y * 256 + s * 128,
                ]
            pieces += held[3:]
            s, y = 1 - section_id, 1 - outer
            offsets += [
                side * 1024 + s * 256 + y * 128,
                side * 1024 + 512 + y * 256 + s * 128,
            ]
        whole = assemble(pieces, jnp.stack(offsets).astype(jnp.int32), shard)
    else:
        partial = gradient(jnp.arange(blocks, dtype=jnp.int32), blocks)[:shard]
        whole = lax.psum(partial.astype(jnp.float32), ("section", "dpo", "dpi")).astype(
            jnp.bfloat16
        )
    return (my_losses, jnp.transpose(whole))


def solution(mesh):
    sections, group_size, spread = (mesh.shape[name] for name in ("section", "expert", "dp"))
    inner = 2 if spread % 2 == 0 else 1
    split = Mesh(
        mesh.devices.reshape(sections, group_size, spread // inner, inner),
        ("section", "expert", "dpo", "dpi"),
    )
    block = ("expert", "dpo", "dpi")
    placed = (
        P(None, block, None, None),
        P("section", None),
        P("section", None, None),
        P("section", "expert", None, None),
        P("section", "expert", None, None),
        P("section", None, block, None, None),
        P(),
        P(None, "expert"),
        P(None, block),
        P(None, block, None),
        P(None, block),
    )
    return jax.shard_map(
        per_device,
        mesh=split,
        in_specs=placed,
        out_specs=(P("section", block), P(None, "expert")),
        check_vma=False,
    )
```

```python
import jax
import jax.numpy as jnp
import numpy as np
from jax import lax
from jax.experimental import pallas as pl
from jax.experimental.pallas import tpu as pltpu
from jax.sharding import Mesh, PartitionSpec as P

EPSILON = 1e-06
LOG_ZERO = -1e30
VMEM_LIMIT = 24 * 1024 * 1024
LANES = 128
COLS = 16
PEAK, TOTAL, WHOLE = COLS - 3, COLS - 2, COLS - 3
BLOCK_ROWS = 256
NT = (((1,), (1,)), ((), ()))
NN = (((1,), (0,)), ((), ()))


def round_up(value, unit):
    return -(-value // unit) * unit


def vmem_spec():
    return pl.BlockSpec(memory_space=pltpu.VMEM)


def hbm_spec():
    return pl.BlockSpec(memory_space=pltpu.HBM)


def smem_spec():
    return pl.BlockSpec(memory_space=pltpu.SMEM)


def call(kernel, out_shape, flops=0, moved=0, **options):
    return pl.pallas_call(
        kernel,
        out_shape=out_shape,
        compiler_params=pltpu.CompilerParams(vmem_limit_bytes=VMEM_LIMIT),
        cost_estimate=pl.CostEstimate(flops=flops, bytes_accessed=moved, transcendentals=0),
        **options,
    )


def bf16_rows(count, width):
    return jax.ShapeDtypeStruct((count, width), jnp.bfloat16)


def as_mask(values):
    return values.astype(jnp.float32).astype(jnp.bfloat16)


def split_rows(values, out_refs):
    size = out_refs[0].shape[0]
    for turn, out_ref in enumerate(out_refs):
        out_ref[...] = values[turn * size : (turn + 1) * size].astype(jnp.bfloat16)


def join_rows(refs):
    return jnp.concatenate([ref[...].astype(jnp.float32) for ref in refs], axis=0)


def rms_scale(values, gain):
    values = values.astype(jnp.float32)
    scale = lax.rsqrt(jnp.mean(values * values, axis=-1, keepdims=True) + EPSILON)
    return (values * scale * gain).astype(jnp.bfloat16)


def expert_column(ids, frame_count):
    pairs = ids.shape[0]
    square = jnp.concatenate(
        [ids.astype(jnp.float32), jnp.full((LANES - pairs, LANES), -1.0, jnp.float32)], axis=0
    )
    turned = jnp.transpose(square, (1, 0)).astype(jnp.int32)
    return jnp.concatenate([turned[:frame_count, p : p + 1] for p in range(pairs)], axis=0)


def placement(column, member, experts, capacity):
    count = column.shape[0]
    shifted = column - member
    relative = jnp.where(shifted < 0, shifted + experts, shifted)
    lane = lax.broadcasted_iota(jnp.int32, (count, LANES), 1)
    one_hot = (lane == relative).astype(jnp.float32)
    before = lax.broadcasted_iota(jnp.int32, (count, count), 1) <= lax.broadcasted_iota(
        jnp.int32, (count, count), 0
    )
    rank = lax.dot_general(
        as_mask(before), one_hot.astype(jnp.bfloat16), NN, preferred_element_type=jnp.float32
    )
    start = (lane * capacity - 1).astype(jnp.float32)
    slots = jnp.sum(one_hot * (rank + start), axis=1, keepdims=True).astype(jnp.int32)
    places = lax.broadcasted_iota(jnp.int32, (count, experts * capacity), 1)
    return (places == slots).astype(jnp.float32)


def scatter_rows(rows, ids, member, experts, capacity, frame_count, out_refs):
    count = rows.shape[0]
    chosen = placement(expert_column(ids, frame_count), member, experts, capacity)
    tall = round_up(count, LANES)
    if tall > count:
        chosen = jnp.concatenate(
            [chosen, jnp.zeros((tall - count, chosen.shape[1]), jnp.float32)], axis=0
        )
    pick = jnp.transpose(chosen, (1, 0))[:, :count].astype(jnp.bfloat16)
    placed = lax.dot_general(pick, rows, NN, preferred_element_type=jnp.float32)
    split_rows(placed, out_refs)


def combine_rows(rows, returned, ids, table, member, experts, capacity, frame_count):
    column = expert_column(ids, frame_count)
    pick = placement(column, member, experts, capacity).astype(jnp.bfloat16)
    normed = rms_scale(rows, table[:1])
    router = jnp.concatenate(
        [table[8:], jnp.zeros((LANES + 8 - table.shape[0], rows.shape[1]), jnp.float32)], axis=0
    ).astype(jnp.bfloat16)
    logits = lax.dot_general(normed, router, NT, preferred_element_type=jnp.float32)
    lane = lax.broadcasted_iota(jnp.int32, logits.shape, 1)
    gate = jax.nn.sigmoid(jnp.sum(jnp.where(lane == column, logits, 0.0), axis=1, keepdims=True))
    stacked = join_rows(returned).astype(jnp.bfloat16)
    mixed = lax.dot_general(pick, stacked, NN, preferred_element_type=jnp.float32)
    return (rows.astype(jnp.float32) + gate * mixed).astype(jnp.bfloat16)


def dispatch(rows, ids, member, experts, capacity, frame_count):
    width = rows.shape[1]

    def kernel(member_ref, rows_ref, ids_ref, *out_refs):
        scatter_rows(
            rows_ref[...], ids_ref[...], member_ref[0], experts, capacity, frame_count, out_refs
        )

    return call(
        kernel,
        tuple(bf16_rows(capacity, width) for _ in range(experts)),
        1 << 27,
        1 << 20,
        in_specs=[smem_spec()] + [vmem_spec()] * 2,
        out_specs=tuple(vmem_spec() for _ in range(experts)),
    )(member, rows, ids)


def run_expert(received, table, own, other, pick_own):
    count = len(received)
    capacity, width = received[0].shape
    others = len(other)

    def kernel(pick_ref, table_ref, in_ref, out_weight_ref, *refs):
        other_refs, received_refs, out_refs = (
            refs[: 2 * others],
            refs[2 * others : 2 * others + count],
            refs[2 * others + count :],
        )

        def work(pieces):
            normed = rms_scale(join_rows(received_refs), table_ref[:1])
            total = None
            for weight_in, weight_out in pieces:
                hidden = lax.dot_general(
                    normed, weight_in[...], NN, preferred_element_type=jnp.float32
                )
                active = (hidden / (1.0 + jnp.exp(-hidden))).astype(jnp.bfloat16)
                part = lax.dot_general(
                    active, weight_out[...], NN, preferred_element_type=jnp.float32
                )
                total = part if total is None else total + part
            split_rows(total, out_refs)

        if others == 0:
            work([(in_ref, out_weight_ref)])
            return

        @pl.when(pick_ref[0] == 1)
        def _():
            work([(in_ref, out_weight_ref)])

        @pl.when(pick_ref[0] != 1)
        def _():
            work([(other_refs[2 * i], other_refs[2 * i + 1]) for i in range(others)])

    flat = [weight for pair in other for weight in pair]
    return call(
        kernel,
        tuple(bf16_rows(capacity, width) for _ in range(count)),
        4 * count * capacity * width * own[0].shape[1],
        4 << 20,
        in_specs=[smem_spec()] + [vmem_spec()] * (3 + 2 * others + count),
        out_specs=tuple(vmem_spec() for _ in range(count)),
    )(pick_own, table, *own, *flat, *received)


def combine_and_dispatch(
    rows, returned, ids, table, next_ids, member, experts, capacity, frame_count
):
    width = rows.shape[1]

    def kernel(member_ref, rows_ref, ids_ref, table_ref, next_ref, *refs):
        returned_refs, x_ref, out_refs = refs[:experts], refs[experts], refs[experts + 1 :]
        mixed = combine_rows(
            rows_ref[...],
            returned_refs,
            ids_ref[...],
            table_ref[...],
            member_ref[0],
            experts,
            capacity,
            frame_count,
        )
        x_ref[...] = mixed
        scatter_rows(
            mixed, next_ref[...], member_ref[0], experts, capacity, frame_count, out_refs
        )

    shapes = (bf16_rows(*rows.shape),) + tuple(
        bf16_rows(capacity, width) for _ in range(experts)
    )
    result = call(
        kernel,
        shapes,
        1 << 28,
        2 << 20,
        in_specs=[smem_spec()] + [vmem_spec()] * (4 + experts),
        out_specs=tuple(vmem_spec() for _ in shapes),
    )(member, rows, ids, table, next_ids, *returned)
    return result[0], result[1:]


def combine_and_norm(
    rows, returned, ids, table, head_gain, member, experts, capacity, frame_count
):
    def kernel(member_ref, rows_ref, ids_ref, table_ref, head_ref, *refs):
        final = combine_rows(
            rows_ref[...],
            refs[:experts],
            ids_ref[...],
            table_ref[...],
            member_ref[0],
            experts,
            capacity,
            frame_count,
        )
        refs[experts][...] = rms_scale(final, head_ref[...])

    return call(
        kernel,
        bf16_rows(*rows.shape),
        1 << 28,
        2 << 20,
        in_specs=[smem_spec()] + [vmem_spec()] * (4 + experts),
        out_specs=vmem_spec(),
    )(member, rows, ids, table, head_gain, *returned)


def block_list(shard):
    return [(i, min(BLOCK_ROWS, shard - i)) for i in range(0, shard, BLOCK_ROWS)]


def weight_copies(weight_ref, held_ref, sems, shard):
    return [
        pltpu.make_async_copy(
            weight_ref.at[pl.ds(first, size)], held_ref.at[pl.ds(first, size)], sems.at[index]
        )
        for index, (first, size) in enumerate(block_list(shard))
    ]


def label_rows(weight, places):
    shard, width = weight.shape
    entries = places.shape[0]

    def kernel(places_ref, weight_ref, out_ref, held_ref, sems):
        copies = weight_copies(weight_ref, held_ref, sems, shard)
        for copy in copies:
            copy.start()
        total = jnp.zeros((entries, width), jnp.float32)
        for copy, (first, size) in zip(copies, block_list(shard)):
            entry = first + lax.broadcasted_iota(jnp.int32, (entries, size), 1)
            chosen = as_mask(entry == places_ref[...])
            copy.wait()
            total = total + lax.dot_general(
                chosen, held_ref[first : first + size], NN, preferred_element_type=jnp.float32
            )
        out_ref[...] = total.astype(jnp.bfloat16)

    return call(
        kernel,
        bf16_rows(entries, width),
        2 * shard * entries * width,
        6 << 20,
        in_specs=[vmem_spec(), hbm_spec()],
        out_specs=vmem_spec(),
        scratch_shapes=[
            pltpu.VMEM((shard, width), jnp.bfloat16),
            pltpu.SemaphoreType.DMA((len(block_list(shard)),)),
        ],
    )(places, weight)


def head_logits(fill, count, pieces, member, weight, label_weight, frame_count, earlier):
    given = len(pieces)
    ahead = 0 if earlier is None else earlier.shape[0]
    span, width = pieces[0].shape
    row_count = count * span
    shard = weight.shape[0]
    height = round_up(shard, BLOCK_ROWS)
    entries = label_weight.shape[0]
    others = [] if earlier is None else [earlier]

    def kernel(member_ref, weight_ref, label_ref, *refs):
        piece_refs = refs[:given]
        logits_ref, rows_ref, stats_ref, held_ref, sems = refs[given + len(others) :]
        copies = weight_copies(weight_ref, held_ref, sems, shard)
        for copy in copies:
            copy.start()

        def put(slot, piece_ref):
            rows_ref[slot * span : (slot + 1) * span] = piece_ref[...]

        def put_if(condition, slot, piece_ref):
            @pl.when(condition)
            def _():
                put(slot, piece_ref)

        fill(member_ref[0], piece_refs, put, put_if)
        peak = jnp.full((1, row_count), LOG_ZERO, jnp.float32)
        total = jnp.zeros((1, row_count), jnp.float32)
        for copy, (first, size) in zip(copies, block_list(shard)):
            copy.wait()
            logits = lax.dot_general(
                held_ref[first : first + size],
                rows_ref[...],
                NT,
                preferred_element_type=jnp.float32,
            )
            logits_ref[first : first + size] = logits
            before = peak
            peak = jnp.maximum(before, jnp.max(logits, axis=0, keepdims=True))
            total = total * jnp.exp(before - peak) + jnp.sum(
                jnp.exp(logits - peak), axis=0, keepdims=True
            )
        if height > shard:
            logits_ref[shard:] = jnp.full((height - shard, row_count), LOG_ZERO, jnp.float32)
        crossed = lax.dot_general(
            label_ref[...], rows_ref[...], NT, preferred_element_type=jnp.float32
        )
        owner = lax.broadcasted_iota(jnp.int32, (COLS, row_count), 1) // frame_count
        picked = jnp.zeros((COLS, row_count), jnp.float32)
        for utterance in range(entries // COLS):
            part = crossed[utterance * COLS : (utterance + 1) * COLS]
            picked = picked + jnp.where(owner == utterance, part, 0.0)
        place = lax.broadcasted_iota(jnp.int32, (COLS, row_count), 0)
        stats = jnp.where(place == PEAK, peak, picked)
        stats = jnp.where(place == TOTAL, total, stats)
        for slot in range(ahead):
            stats_ref[slot] = refs[given][slot]
        for slot in range(count):
            stats_ref[ahead + slot] = stats[:, slot * span : (slot + 1) * span]

    return call(
        kernel,
        (
            jax.ShapeDtypeStruct((height, row_count), jnp.float32),
            bf16_rows(row_count, width),
            jax.ShapeDtypeStruct((ahead + count, COLS, span), jnp.float32),
        ),
        2 * height * row_count * width,
        9 << 20,
        in_specs=[smem_spec(), hbm_spec()] + [vmem_spec()] * (1 + given + len(others)),
        out_specs=tuple(vmem_spec() for _ in range(3)),
        scratch_shapes=[
            pltpu.VMEM((shard, width), jnp.bfloat16),
            pltpu.SemaphoreType.DMA((len(block_list(shard)),)),
        ],
    )(member, weight, label_weight, *pieces, *others)


def fill_near(place, piece_refs, put, put_if):
    value_ref, left_ref, right_ref = piece_refs
    put(0, value_ref)
    put_if(place < 2, 1, left_ref)
    put_if(place >= 2, 1, right_ref)


def fill_far(place, piece_refs, put, put_if):
    far_ref, end_ref, left_ref, right_ref = piece_refs
    put(0, far_ref)
    put_if((place == 0) | (place == 3), 1, end_ref)
    put_if(place == 1, 1, right_ref)
    put_if(place == 2, 1, left_ref)


def fill_all(place, piece_refs, put, put_if):
    for slot, piece_ref in enumerate(piece_refs):
        put(slot, piece_ref)


def log_add(first, second):
    peak = jnp.maximum(first, second)
    return peak + jnp.log(jnp.exp(first - peak) + jnp.exp(second - peak))


def log_add3(first, second, third):
    peak = jnp.maximum(jnp.maximum(first, second), third)
    return peak + jnp.log(
        jnp.exp(first - peak) + jnp.exp(second - peak) + jnp.exp(third - peak)
    )


def ctc_pass(stats, slots, labels, frame_counts, label_counts, frame_count, label_max):
    sources = len(stats)
    count, _, span = stats[0].shape
    row_count = count * span
    utterances = labels.shape[0]
    entries = utterances * COLS
    tall = round_up(span, LANES)

    def kernel(slots_ref, labels_ref, frames_ref, counts_ref, *refs):
        (
            out_ref,
            high_ref,
            low_ref,
            loss_ref,
            turn_ref,
            emission_ref,
            emit_blank,
            emit_label,
            blank_fwd,
            label_fwd,
            blank_bwd,
            label_bwd,
            occupancy_ref,
        ) = refs[sources:]
        place = lax.broadcasted_iota(jnp.int32, (COLS, span), 0)
        turn_ref[...] = jnp.zeros(turn_ref.shape, jnp.float32)
        for slot in range(count):
            found = [refs[k][slots_ref[k * count + slot]] for k in range(sources)]
            joined = found[0]
            peak = found[0][PEAK : PEAK + 1]
            for other in found[1:]:
                joined = joined + other
                peak = jnp.maximum(peak, other[PEAK : PEAK + 1])
            total = jnp.zeros((1, span), jnp.float32)
            for other in found:
                total = total + other[TOTAL : TOTAL + 1] * jnp.exp(other[PEAK : PEAK + 1] - peak)
            log_total = peak + jnp.log(total)
            turn_ref[:COLS, :span] = jnp.where(place == TOTAL, log_total, joined - log_total)
            emission_ref[slot * span : (slot + 1) * span] = jnp.transpose(turn_ref[...], (1, 0))[
                :span
            ]

        lane = lax.broadcasted_iota(jnp.int32, (utterances, LANES), 1)
        is_label = lane < label_max
        is_blank = lane <= label_max
        names = labels_ref[...]
        earlier = pltpu.roll(names, 1, 1)
        skip = is_label & (lane >= 1) & (names != 0) & (names != earlier)
        later = pltpu.roll(names, LANES - 1, 1)
        skip_next = (lane < label_max - 1) & (later != 0) & (later != names)
        frames = frames_ref[...]
        counts = counts_ref[...]
        ends_blank = jnp.where(lane == counts, 0.0, LOG_ZERO)
        ends_label = jnp.where(lane == counts - 1, 0.0, LOG_ZERO)

        def spread(step, carry):
            row = emission_ref[pl.ds(step, utterances, stride=frame_count), :]
            blank = jnp.sum(jnp.where(lane == label_max, row, 0.0), axis=1, keepdims=True)
            emit_blank[step] = jnp.where(is_blank, blank, LOG_ZERO)
            emit_label[step] = jnp.where(is_label, row, LOG_ZERO)
            return carry

        lax.fori_loop(0, frame_count, spread, 0, unroll=16)

        def advance(step, carry):
            fwd_blank, fwd_label, bwd_blank, bwd_label = carry
            moved = jnp.where(lane == 0, LOG_ZERO, pltpu.roll(fwd_label, 1, 1))
            new_blank = log_add(fwd_blank, moved) + emit_blank[step]
            new_label = (
                log_add3(fwd_label, fwd_blank, jnp.where(skip, moved, LOG_ZERO))
                + emit_label[step]
            )
            alive = step < frames
            fwd_blank = jnp.where(alive, new_blank, fwd_blank)
            fwd_label = jnp.where(alive, new_label, fwd_label)
            blank_fwd[step] = fwd_blank
            label_fwd[step] = fwd_label

            back = frame_count - 1 - step
            out_blank = bwd_blank + emit_blank[back + 1]
            out_label = bwd_label + emit_label[back + 1]
            next_blank = pltpu.roll(out_blank, LANES - 1, 1)
            next_label = jnp.where(skip_next, pltpu.roll(out_label, LANES - 1, 1), LOG_ZERO)
            ended = back >= frames - 1
            bwd_blank = jnp.where(ended, ends_blank, log_add(out_blank, out_label))
            bwd_label = jnp.where(
                ended, ends_label, log_add3(out_label, next_blank, next_label)
            )
            blank_bwd[back] = bwd_blank
            label_bwd[back] = bwd_label
            return (fwd_blank, fwd_label, bwd_blank, bwd_label)

        first_blank = jnp.where(lane == 0, emit_blank[0], LOG_ZERO)
        first_label = jnp.where(lane == 0, emit_label[0], LOG_ZERO)
        blank_fwd[0] = first_blank
        label_fwd[0] = first_label
        blank_bwd[frame_count - 1] = ends_blank
        label_bwd[frame_count - 1] = ends_label
        fwd_blank, fwd_label, _, _ = lax.fori_loop(
            1, frame_count, advance, (first_blank, first_label, ends_blank, ends_label), unroll=4
        )
        end_state = jnp.sum(jnp.where(lane == counts, fwd_blank, 0.0), axis=1, keepdims=True)
        near_state = jnp.sum(jnp.where(lane == counts - 1, fwd_label, 0.0), axis=1, keepdims=True)
        log_like = log_add(end_state, near_state)
        loss_ref[...] = jnp.broadcast_to(-log_like, (utterances, LANES))

        def occupy(step, carry):
            blank = jnp.exp(blank_fwd[step] + blank_bwd[step] - log_like)
            label = jnp.exp(label_fwd[step] + label_bwd[step] - log_like)
            blank = jnp.sum(jnp.where(is_blank, blank, 0.0), axis=1, keepdims=True)
            label = jnp.where(is_label, label, 0.0)
            whole = blank + jnp.sum(label, axis=1, keepdims=True)
            filled = jnp.where(lane == label_max, blank, label)
            filled = jnp.where(lane == WHOLE, whole, filled)
            filled = jnp.where(step < frames, -filled, 0.0)
            row = emission_ref[pl.ds(step, utterances, stride=frame_count), :]
            occupancy_ref[pl.ds(step, utterances, stride=frame_count), :] = jnp.where(
                lane == TOTAL, row, filled
            )
            return carry

        lax.fori_loop(0, frame_count, occupy, 0, unroll=16)
        turned = jnp.transpose(occupancy_ref[...], (1, 0))[:COLS]
        out_ref[...] = turned
        row_place = lax.broadcasted_iota(jnp.int32, (COLS, row_count), 0)
        owner = lax.broadcasted_iota(jnp.int32, (COLS, row_count), 1) // frame_count
        source = jnp.where(row_place < WHOLE, turned, 0.0)
        for utterance in range(utterances):
            part = jnp.where(owner == utterance, source, 0.0)
            high = part.astype(jnp.bfloat16)
            high_ref[utterance * COLS : (utterance + 1) * COLS] = high
            low_ref[utterance * COLS : (utterance + 1) * COLS] = (
                part - high.astype(jnp.float32)
            ).astype(jnp.bfloat16)

    held = pltpu.VMEM((frame_count, utterances, LANES), jnp.float32)
    table = pltpu.VMEM((row_count, LANES), jnp.float32)
    return call(
        kernel,
        (
            jax.ShapeDtypeStruct((COLS, row_count), jnp.float32),
            bf16_rows(entries, row_count),
            bf16_rows(entries, row_count),
            jax.ShapeDtypeStruct((utterances, LANES), jnp.float32),
        ),
        1 << 26,
        1 << 20,
        in_specs=[smem_spec()] + [vmem_spec()] * (3 + sources),
        out_specs=tuple(vmem_spec() for _ in range(4)),
        scratch_shapes=[pltpu.VMEM((LANES, tall), jnp.float32), table]
        + [held] * 6
        + [table],
    )(slots, labels, frame_counts, label_counts, *stats)


def head_gradient(logits, rows, occupancy, high, low, places, order, outputs, each):
    count = len(logits)
    row_count, width = rows[0].shape
    entries = places.shape[1]
    blocks = outputs * each

    def kernel(order_ref, *refs):
        logits_refs, rows_refs = refs[:count], refs[count : 2 * count]
        occupancy_ref, high_ref, low_ref, places_ref = refs[2 * count : 2 * count + 4]
        out_refs = refs[2 * count + 4 :]
        for block in range(blocks):
            start = pl.multiple_of(order_ref[block] * BLOCK_ROWS, BLOCK_ROWS)
            entry = start + lax.broadcasted_iota(jnp.int32, (BLOCK_ROWS, entries), 0)
            select = as_mask(entry == places_ref[...])
            total = None
            for g in range(count):
                lanes = slice(g * row_count, (g + 1) * row_count)
                scattered = lax.dot_general(
                    select, high_ref[:, lanes], NN, preferred_element_type=jnp.float32
                ) + lax.dot_general(
                    select, low_ref[:, lanes], NN, preferred_element_type=jnp.float32
                )
                whole = occupancy_ref[WHOLE : WHOLE + 1, lanes]
                log_total = occupancy_ref[TOTAL : TOTAL + 1, lanes]
                values = logits_refs[g][pl.ds(start, BLOCK_ROWS), :]
                grad = (scattered - jnp.exp(values - log_total) * whole).astype(jnp.bfloat16)
                part = lax.dot_general(
                    grad, rows_refs[g][...], NN, preferred_element_type=jnp.float32
                )
                total = part if total is None else total + part
            out_refs[block // each][
                block % each * BLOCK_ROWS : (block % each + 1) * BLOCK_ROWS
            ] = total.astype(jnp.bfloat16)

    return call(
        kernel,
        tuple(bf16_rows(each * BLOCK_ROWS, width) for _ in range(outputs)),
        2 * blocks * BLOCK_ROWS * count * row_count * (width + 2 * entries),
        10 << 20,
        in_specs=[smem_spec()] + [vmem_spec()] * (2 * count + 4),
        out_specs=tuple(vmem_spec() for _ in range(outputs)),
    )(order, *logits, *rows, occupancy, high, low, places)


def assemble(pieces, offsets, height):
    count = len(pieces)
    part, width = pieces[0].shape
    short = height % part

    def kernel(offsets_ref, *refs):
        out_ref, sems = refs[count], refs[count + 1]

        def each(act):
            for index in range(count):
                offset = pl.multiple_of(offsets_ref[index], part)

                @pl.when(offset + part <= height)
                def _():
                    act(
                        pltpu.make_async_copy(
                            refs[index], out_ref.at[pl.ds(offset, part)], sems.at[index]
                        )
                    )

                if short:

                    @pl.when(offset + part > height)
                    def _():
                        act(
                            pltpu.make_async_copy(
                                refs[index].at[pl.ds(0, short)],
                                out_ref.at[pl.ds(height - short, short)],
                                sems.at[index],
                            )
                        )

        each(lambda copy: copy.start())
        each(lambda copy: copy.wait())

    return call(
        kernel,
        bf16_rows(height, width),
        0,
        2 * height * width * 2,
        in_specs=[smem_spec()] + [pl.BlockSpec(memory_space=pl.ANY)] * count,
        out_specs=pl.BlockSpec(memory_space=pl.ANY),
        scratch_shapes=[pltpu.SemaphoreType.DMA((count,))],
    )(offsets, *pieces)


def swap(value, axis):
    return lax.ppermute(value, axis, [(0, 1), (1, 0)])


def rotate(value, axis, by):
    count = lax.axis_size(axis)
    return lax.ppermute(value, axis, [(i, (i + by) % count) for i in range(count)])


def after(value, *others):
    return lax.optimization_barrier((value,) + others)[0]


def line_near(value):
    left = lax.ppermute(value, "expert", [(1, 0), (2, 1), (3, 2)])
    right = lax.ppermute(value, "expert", [(0, 1), (1, 2), (2, 3)])
    return left, right


def line_far(near, member):
    left = lax.ppermute(near[0], "expert", [(1, 0), (2, 1)])
    right = lax.ppermute(near[1], "expert", [(1, 2), (2, 3)])
    return jnp.where(member < 2, left, right)


def line_end(far):
    return lax.ppermute(far, "expert", [(1, 0), (2, 3)])


LINE_ORDER = np.array([[0, 1, 2, 3], [1, 2, 3, 0], [2, 1, 0, 3], [3, 2, 1, 0]])


def slot_orders(count):
    return LINE_ORDER if count == 4 else np.tile(np.arange(count), (count, 1))


def slot_tables(count):
    orders = slot_orders(count)
    tables = np.zeros((count, count, count), np.int32)
    for member in range(count):
        for k in range(count):
            source = (member + k) % count
            for slot in range(count):
                tables[member, k, slot] = list(orders[source]).index(orders[member][slot])
    return tables.reshape(count, count * count)


def add(first, second):
    return (first.astype(jnp.float32) + second.astype(jnp.float32)).astype(jnp.bfloat16)


def per_device(
    frames,
    norm_gain,
    router,
    w_in,
    w_out,
    routing,
    head_gain,
    head_weight,
    frame_lengths,
    labels,
    label_lengths,
):
    sections = lax.axis_size("section")
    section_id = lax.axis_index("section")
    group_size = lax.axis_size("expert")
    member = lax.axis_index("expert")
    outer_size = lax.axis_size("dpo")
    inner_size = lax.axis_size("dpi")
    core = lax.axis_index("dpi")
    micro, utt_dev, frame_count, width = frames.shape
    label_max = labels.shape[2]
    experts = w_in.shape[1] * group_size
    hidden = w_in.shape[3]
    pair_count = micro * utt_dev
    per_section = pair_count // sections
    first_pair = section_id * per_section
    share = (utt_dev * frame_count * 9 + 8 * experts - 1) // (8 * experts)
    capacity = round_up(share * -(-per_section // utt_dev), 8)
    span = per_section * frame_count
    member_ref = member.astype(jnp.int32).reshape(1)

    def mine_of(value):
        return lax.dynamic_slice_in_dim(value, first_pair, per_section, 0)

    def exchange(blocks, sign):
        return [blocks[0]] + [
            rotate(blocks[k], "expert", sign * k) for k in range(1, group_size)
        ]

    def lanes_of(ids):
        return jnp.pad(mine_of(ids), ((0, 0), (0, LANES - frame_count)), constant_values=-1)

    current = lax.dynamic_slice_in_dim(
        frames.reshape(pair_count * frame_count, width), first_pair * frame_count, span, 0
    )
    own_ids = routing.reshape(pair_count, frame_count)
    paired = sections == 2 and inner_size == 2
    if paired:
        other_ids = swap(own_ids, "section")
        all_ids = [
            jnp.where(section_id == layer, own_ids, other_ids) for layer in range(sections)
        ]
    else:
        all_ids = lax.all_gather(own_ids, "section")
    layer_ids = [lanes_of(all_ids[layer]) for layer in range(sections)]
    outgoing = dispatch(current, layer_ids[0], member_ref, experts, capacity, frame_count)
    received = exchange(outgoing, 1)

    own_table = jnp.concatenate(
        [
            norm_gain,
            jnp.zeros((7, width), jnp.float32),
            jnp.transpose(router[0]).astype(jnp.float32),
            jnp.zeros((round_up(experts, 8) - experts, width), jnp.float32),
        ],
        axis=0,
    )
    own = (w_in[0, 0], w_out[0, 0])
    if paired:
        other_table = swap(own_table, "section")
        half = hidden // 2
        sent_in = lax.dynamic_slice(own[0], (0, core * half), (width, half))
        sent_out = lax.dynamic_slice(own[1], (core * half, 0), (half, width))
        sent_in, sent_out = lax.optimization_barrier((sent_in, sent_out, own_table))[:2]
        came_in = swap(sent_in, "section")
        came_out = swap(sent_out, "section")
        other = [(came_in, came_out), (swap(came_in, "dpi"), swap(came_out, "dpi"))]
    else:
        all_tables = lax.all_gather(own_table, "section")
        all_in = lax.all_gather(own[0], "section")
        all_out = lax.all_gather(own[1], "section")

    layers = []
    for layer in range(sections):
        if paired:
            mine = section_id == layer
            table = jnp.where(mine, own_table, other_table)
            layers.append((table, own, other, mine.astype(jnp.int32).reshape(1)))
        else:
            chosen = (all_in[layer], all_out[layer])
            layers.append((all_tables[layer], chosen, [], jnp.ones((1,), jnp.int32)))

    labels, frame_lengths, label_lengths = lax.optimization_barrier(
        (labels, frame_lengths, label_lengths, outgoing[0])
    )[:3]
    notes = jnp.concatenate(
        [
            mine_of(labels.reshape(pair_count, label_max)),
            mine_of(frame_lengths.reshape(pair_count, 1)),
            mine_of(label_lengths.reshape(pair_count, 1)),
        ],
        axis=1,
    )
    if group_size == 4:
        found = [notes] + [rotate(notes, "expert", -k) for k in range(1, group_size)]
        low = member < 2
        notes_all = jnp.stack(
            [
                found[0],
                jnp.where(low, found[1], found[3]),
                found[2],
                jnp.where(low, found[3], found[1]),
            ]
        )
    else:
        notes_all = lax.all_gather(notes, "expert")
    shard = head_weight.shape[1]
    weight_rows = jnp.transpose(head_weight)
    notes_all = notes_all.reshape(-1, label_max + 2)
    utterances = notes_all.shape[0]
    names = notes_all[:, :label_max]
    named = jnp.concatenate(
        [
            names,
            jnp.zeros((utterances, 1), jnp.int32),
            jnp.full((utterances, COLS - label_max - 1), -1, jnp.int32),
        ],
        axis=1,
    ).reshape(utterances * COLS)
    local = named - member * shard
    places = jnp.where((named >= 0) & (local >= 0) & (local < shard), local, -1)
    label_weight = label_rows(weight_rows, places.reshape(-1, 1))
    received, label_weight = lax.optimization_barrier((received, label_weight))
    slot_entries = per_section * COLS

    for layer in range(sections):
        table, weights, others, pick_own = layers[layer]
        done = run_expert(received, table, weights, others, pick_own)
        returned = exchange(done, -1)
        if layer < sections - 1:
            current, outgoing = combine_and_dispatch(
                current,
                returned,
                layer_ids[layer],
                table,
                layer_ids[layer + 1],
                member_ref,
                experts,
                capacity,
                frame_count,
            )
            received = exchange(outgoing, 1)
        else:
            normed = combine_and_norm(
                current,
                returned,
                layer_ids[layer],
                table,
                head_gain.reshape(1, width),
                member_ref,
                experts,
                capacity,
                frame_count,
            )

    def logits_of(fill, first, count, pieces, earlier):
        chosen = label_weight[first * slot_entries : (first + count) * slot_entries]
        return head_logits(
            fill, count, pieces, member_ref, weight_rows, chosen, frame_count, earlier
        )

    if group_size == 4:
        left, right = line_near(normed)
        far = line_far((left, right), member)
        end = line_end(far)
        heads = [logits_of(fill_near, 0, 2, [normed, left, right], None)]
        heads.append(logits_of(fill_far, 2, 2, [far, end, left, right], heads[0][2]))
        stats = heads[1][2]
        found = [stats] + [rotate(stats, "expert", -k) for k in range(1, group_size)]
    else:
        gathered = lax.all_gather(normed, "expert")
        pieces = [gathered[k] for k in range(group_size)]
        heads = [logits_of(fill_all, 0, group_size, pieces, None)]
        gathered = lax.all_gather(heads[0][2], "expert")
        found = [
            lax.dynamic_index_in_dim(gathered, (member + k) % group_size, 0, keepdims=False)
            for k in range(group_size)
        ]
    tables = jnp.asarray(slot_tables(group_size))
    slots = lax.dynamic_index_in_dim(tables, member, 0, keepdims=False)
    occupancy, high, low, losses = ctc_pass(
        found,
        slots,
        jnp.pad(names, ((0, 0), (0, LANES - label_max))),
        notes_all[:, label_max : label_max + 1],
        notes_all[:, label_max + 1 :],
        frame_count,
        label_max,
    )
    own_slot = 0 if group_size == 4 else member
    my_losses = lax.dynamic_slice(losses, (own_slot * per_section, 0), (per_section, 1))

    def gradient(order, outputs, each):
        return head_gradient(
            [head[0] for head in heads],
            [head[1] for head in heads],
            occupancy,
            high,
            low,
            places.reshape(1, -1),
            order,
            outputs,
            each,
        )

    blocks = heads[0][0].shape[0] // BLOCK_ROWS
    if paired and outer_size == 2 and blocks == 8:
        outer = lax.axis_index("dpo")

        def pair_of(side, first, second):
            return jnp.stack([side * 4 + first, side * 4 + 2 + second]).astype(jnp.int32)

        came_sent = swap(
            gradient(pair_of(1 - core, 1 - section_id, 1 - outer), 1, 2)[0], "dpi"
        )
        sent = add(gradient(pair_of(core, 1 - section_id, 1 - outer), 1, 2)[0], came_sent)
        first_in = swap(sent[:BLOCK_ROWS], "section")
        second_in = swap(sent[BLOCK_ROWS:], "dpo")
        order = jnp.concatenate(
            [pair_of(1 - core, section_id, outer), pair_of(core, section_id, outer)]
        )
        sibling_kept, own_kept = gradient(after(order, sent), 2, 2)
        kept = add(own_kept, swap(sibling_kept, "dpi"))
        first = add(kept[:BLOCK_ROWS], first_in)
        second = add(kept[BLOCK_ROWS:], second_in)
        part = BLOCK_ROWS // 2

        def piece(value, index):
            return lax.dynamic_slice_in_dim(value, index * part, part, 0)

        first_far = swap(piece(first, 1 - outer), "dpo")
        second_far = swap(piece(second, 1 - section_id), "section")
        final = jnp.concatenate(
            [add(piece(first, outer), first_far), add(piece(second, section_id), second_far)],
            axis=0,
        )
        across = swap(final, "section")
        beside = swap(final, "dpo")
        first_diagonal = swap(beside[:part], "section")
        second_diagonal = swap(across[part:], "dpo")
        mine = [final, across, beside, first_diagonal, second_diagonal]
        theirs = [swap(value, "dpi") for value in mine]
        pieces, offsets = [], []
        for side, held in ((core, mine), (1 - core, theirs)):
            where = (
                (section_id, outer),
                (1 - section_id, outer),
                (section_id, 1 - outer),
            )
            for value, (s, y) in zip(held[:3], where):
                pieces += [value[:part], value[part:]]
                offsets += [
                    side * 1024 + s * 256 + y * 128,
                    side * 1024 + 512 + y * 256 + s * 128,
                ]
            pieces += held[3:]
            s, y = 1 - section_id, 1 - outer
            offsets += [
                side * 1024 + s * 256 + y * 128,
                side * 1024 + 512 + y * 256 + s * 128,
            ]
        whole = assemble(pieces, jnp.stack(offsets).astype(jnp.int32), shard)
    else:
        partial = gradient(jnp.arange(blocks, dtype=jnp.int32), 1, blocks)[0][:shard]
        whole = lax.psum(partial.astype(jnp.float32), ("section", "dpo", "dpi")).astype(
            jnp.bfloat16
        )
    return (my_losses, jnp.transpose(whole))


def solution(mesh):
    sections, group_size, spread = (mesh.shape[name] for name in ("section", "expert", "dp"))
    inner = 2 if spread % 2 == 0 else 1
    split = Mesh(
        mesh.devices.reshape(sections, group_size, spread // inner, inner),
        ("section", "expert", "dpo", "dpi"),
    )
    block = ("expert", "dpo", "dpi")
    placed = (
        P(None, block, None, None),
        P("section", None),
        P("section", None, None),
        P("section", "expert", None, None),
        P("section", "expert", None, None),
        P("section", None, block, None, None),
        P(),
        P(None, "expert"),
        P(None, block),
        P(None, block, None),
        P(None, block),
    )
    return jax.shard_map(
        per_device,
        mesh=split,
        in_specs=placed,
        out_specs=(P("section", block), P(None, "expert")),
        check_vma=False,
    )
```

```python
import jax
import jax.numpy as jnp
import numpy as np
from jax import lax
from jax.experimental import pallas as pl
from jax.experimental.pallas import tpu as pltpu
from jax.sharding import Mesh, PartitionSpec as P

EPSILON = 1e-06
LOG_ZERO = -1e30
VMEM_LIMIT = 24 * 1024 * 1024
LANES = 128
COLS = 16
PEAK, TOTAL, WHOLE = COLS - 3, COLS - 2, COLS - 3
BLOCK_ROWS = 256
NT = (((1,), (1,)), ((), ()))
NN = (((1,), (0,)), ((), ()))


def round_up(value, unit):
    return -(-value // unit) * unit


def vmem_spec():
    return pl.BlockSpec(memory_space=pltpu.VMEM)


def smem_spec():
    return pl.BlockSpec(memory_space=pltpu.SMEM)


def call(kernel, out_shape, flops=0, **options):
    return pl.pallas_call(
        kernel,
        out_shape=out_shape,
        compiler_params=pltpu.CompilerParams(vmem_limit_bytes=VMEM_LIMIT),
        cost_estimate=pl.CostEstimate(flops=flops, bytes_accessed=0, transcendentals=0),
        **options,
    )


def bf16_rows(count, width):
    return jax.ShapeDtypeStruct((count, width), jnp.bfloat16)


def as_mask(values):
    return values.astype(jnp.float32).astype(jnp.bfloat16)


def split_rows(values, out_refs):
    size = out_refs[0].shape[0]
    for turn, out_ref in enumerate(out_refs):
        out_ref[...] = values[turn * size : (turn + 1) * size].astype(jnp.bfloat16)


def join_rows(refs):
    return jnp.concatenate([ref[...].astype(jnp.float32) for ref in refs], axis=0)


def rms_scale(values, gain):
    values = values.astype(jnp.float32)
    scale = lax.rsqrt(jnp.mean(values * values, axis=-1, keepdims=True) + EPSILON)
    return (values * scale * gain).astype(jnp.bfloat16)


def expert_column(ids, frame_count):
    pairs = ids.shape[0]
    square = jnp.concatenate(
        [ids.astype(jnp.float32), jnp.full((LANES - pairs, LANES), -1.0, jnp.float32)], axis=0
    )
    turned = jnp.transpose(square, (1, 0)).astype(jnp.int32)
    return jnp.concatenate([turned[:frame_count, p : p + 1] for p in range(pairs)], axis=0)


def placement(column, member, experts, capacity):
    count = column.shape[0]
    shifted = column - member
    relative = jnp.where(shifted < 0, shifted + experts, shifted)
    lane = lax.broadcasted_iota(jnp.int32, (count, LANES), 1)
    one_hot = (lane == relative).astype(jnp.float32)
    before = lax.broadcasted_iota(jnp.int32, (count, count), 1) <= lax.broadcasted_iota(
        jnp.int32, (count, count), 0
    )
    rank = lax.dot_general(
        as_mask(before), one_hot.astype(jnp.bfloat16), NN, preferred_element_type=jnp.float32
    )
    start = (lane * capacity - 1).astype(jnp.float32)
    slots = jnp.sum(one_hot * (rank + start), axis=1, keepdims=True).astype(jnp.int32)
    places = lax.broadcasted_iota(jnp.int32, (count, experts * capacity), 1)
    return (places == slots).astype(jnp.float32)


def scatter_rows(rows, ids, member, experts, capacity, frame_count, out_refs):
    count = rows.shape[0]
    chosen = placement(expert_column(ids, frame_count), member, experts, capacity)
    tall = round_up(count, LANES)
    if tall > count:
        chosen = jnp.concatenate(
            [chosen, jnp.zeros((tall - count, chosen.shape[1]), jnp.float32)], axis=0
        )
    pick = jnp.transpose(chosen, (1, 0))[:, :count].astype(jnp.bfloat16)
    placed = lax.dot_general(pick, rows, NN, preferred_element_type=jnp.float32)
    split_rows(placed, out_refs)


def combine_rows(rows, returned, ids, table, member, experts, capacity, frame_count):
    column = expert_column(ids, frame_count)
    pick = placement(column, member, experts, capacity).astype(jnp.bfloat16)
    normed = rms_scale(rows, table[:1])
    router = jnp.concatenate(
        [table[8:], jnp.zeros((LANES + 8 - table.shape[0], rows.shape[1]), jnp.float32)], axis=0
    ).astype(jnp.bfloat16)
    logits = lax.dot_general(normed, router, NT, preferred_element_type=jnp.float32)
    lane = lax.broadcasted_iota(jnp.int32, logits.shape, 1)
    gate = jax.nn.sigmoid(jnp.sum(jnp.where(lane == column, logits, 0.0), axis=1, keepdims=True))
    stacked = join_rows(returned).astype(jnp.bfloat16)
    mixed = lax.dot_general(pick, stacked, NN, preferred_element_type=jnp.float32)
    return (rows.astype(jnp.float32) + gate * mixed).astype(jnp.bfloat16)


def dispatch(rows, ids, member, experts, capacity, frame_count):
    width = rows.shape[1]

    def kernel(member_ref, rows_ref, ids_ref, *out_refs):
        scatter_rows(
            rows_ref[...], ids_ref[...], member_ref[0], experts, capacity, frame_count, out_refs
        )

    return call(
        kernel,
        tuple(bf16_rows(capacity, width) for _ in range(experts)),
        1 << 27,
        in_specs=[smem_spec()] + [vmem_spec()] * 2,
        out_specs=tuple(vmem_spec() for _ in range(experts)),
    )(member, rows, ids)


def run_expert(received, table, own, other, pick_own):
    count = len(received)
    capacity, width = received[0].shape
    others = len(other)

    def kernel(pick_ref, table_ref, in_ref, out_weight_ref, *refs):
        other_refs, received_refs, out_refs = (
            refs[: 2 * others],
            refs[2 * others : 2 * others + count],
            refs[2 * others + count :],
        )

        def work(pieces):
            normed = rms_scale(join_rows(received_refs), table_ref[:1])
            total = None
            for weight_in, weight_out in pieces:
                hidden = lax.dot_general(
                    normed, weight_in[...], NN, preferred_element_type=jnp.float32
                )
                active = (hidden / (1.0 + jnp.exp(-hidden))).astype(jnp.bfloat16)
                part = lax.dot_general(
                    active, weight_out[...], NN, preferred_element_type=jnp.float32
                )
                total = part if total is None else total + part
            split_rows(total, out_refs)

        if others == 0:
            work([(in_ref, out_weight_ref)])
            return

        @pl.when(pick_ref[0] == 1)
        def _():
            work([(in_ref, out_weight_ref)])

        @pl.when(pick_ref[0] != 1)
        def _():
            work([(other_refs[2 * i], other_refs[2 * i + 1]) for i in range(others)])

    flat = [weight for pair in other for weight in pair]
    return call(
        kernel,
        tuple(bf16_rows(capacity, width) for _ in range(count)),
        4 * count * capacity * width * own[0].shape[1],
        in_specs=[smem_spec()] + [vmem_spec()] * (3 + 2 * others + count),
        out_specs=tuple(vmem_spec() for _ in range(count)),
    )(pick_own, table, *own, *flat, *received)


def combine_and_dispatch(
    rows, returned, ids, table, next_ids, member, experts, capacity, frame_count
):
    width = rows.shape[1]

    def kernel(member_ref, rows_ref, ids_ref, table_ref, next_ref, *refs):
        returned_refs, x_ref, out_refs = refs[:experts], refs[experts], refs[experts + 1 :]
        mixed = combine_rows(
            rows_ref[...],
            returned_refs,
            ids_ref[...],
            table_ref[...],
            member_ref[0],
            experts,
            capacity,
            frame_count,
        )
        x_ref[...] = mixed
        scatter_rows(
            mixed, next_ref[...], member_ref[0], experts, capacity, frame_count, out_refs
        )

    shapes = (bf16_rows(*rows.shape),) + tuple(
        bf16_rows(capacity, width) for _ in range(experts)
    )
    result = call(
        kernel,
        shapes,
        1 << 28,
        in_specs=[smem_spec()] + [vmem_spec()] * (4 + experts),
        out_specs=tuple(vmem_spec() for _ in shapes),
    )(member, rows, ids, table, next_ids, *returned)
    return result[0], result[1:]


def combine_and_norm(
    rows, returned, ids, table, head_gain, member, experts, capacity, frame_count
):
    def kernel(member_ref, rows_ref, ids_ref, table_ref, head_ref, *refs):
        final = combine_rows(
            rows_ref[...],
            refs[:experts],
            ids_ref[...],
            table_ref[...],
            member_ref[0],
            experts,
            capacity,
            frame_count,
        )
        refs[experts][...] = rms_scale(final, head_ref[...])

    return call(
        kernel,
        bf16_rows(*rows.shape),
        1 << 28,
        in_specs=[smem_spec()] + [vmem_spec()] * (4 + experts),
        out_specs=vmem_spec(),
    )(member, rows, ids, table, head_gain, *returned)


def block_list(shard):
    return [(i, min(BLOCK_ROWS, shard - i)) for i in range(0, shard, BLOCK_ROWS)]


def label_rows(weight, places):
    shard, width = weight.shape
    entries = places.shape[0]

    def kernel(places_ref, weight_ref, out_ref):
        total = jnp.zeros((entries, width), jnp.float32)
        for first, size in block_list(shard):
            entry = first + lax.broadcasted_iota(jnp.int32, (entries, size), 1)
            chosen = as_mask(entry == places_ref[...])
            total = total + lax.dot_general(
                chosen, weight_ref[first : first + size], NN, preferred_element_type=jnp.float32
            )
        out_ref[...] = total.astype(jnp.bfloat16)

    return call(
        kernel,
        bf16_rows(entries, width),
        2 * shard * entries * width,
        in_specs=[vmem_spec()] * 2,
        out_specs=vmem_spec(),
    )(places, weight)


def head_logits(fill, count, pieces, member, weight, label_weight, frame_count, earlier):
    given = len(pieces)
    ahead = 0 if earlier is None else earlier.shape[0]
    span, width = pieces[0].shape
    row_count = count * span
    shard = weight.shape[0]
    height = round_up(shard, BLOCK_ROWS)
    entries = label_weight.shape[0]
    others = [] if earlier is None else [earlier]

    def kernel(member_ref, weight_ref, label_ref, *refs):
        piece_refs = refs[:given]
        logits_ref, rows_ref, stats_ref = refs[given + len(others) :]

        def put(slot, piece_ref):
            rows_ref[slot * span : (slot + 1) * span] = piece_ref[...]

        def put_if(condition, slot, piece_ref):
            @pl.when(condition)
            def _():
                put(slot, piece_ref)

        fill(member_ref[0], piece_refs, put, put_if)
        peak = jnp.full((1, row_count), LOG_ZERO, jnp.float32)
        total = jnp.zeros((1, row_count), jnp.float32)
        for first, size in block_list(shard):
            logits = lax.dot_general(
                weight_ref[first : first + size],
                rows_ref[...],
                NT,
                preferred_element_type=jnp.float32,
            )
            logits_ref[first : first + size] = logits
            before = peak
            peak = jnp.maximum(before, jnp.max(logits, axis=0, keepdims=True))
            total = total * jnp.exp(before - peak) + jnp.sum(
                jnp.exp(logits - peak), axis=0, keepdims=True
            )
        if height > shard:
            logits_ref[shard:] = jnp.full((height - shard, row_count), LOG_ZERO, jnp.float32)
        crossed = lax.dot_general(
            label_ref[...], rows_ref[...], NT, preferred_element_type=jnp.float32
        )
        owner = lax.broadcasted_iota(jnp.int32, (COLS, row_count), 1) // frame_count
        picked = jnp.zeros((COLS, row_count), jnp.float32)
        for utterance in range(entries // COLS):
            part = crossed[utterance * COLS : (utterance + 1) * COLS]
            picked = picked + jnp.where(owner == utterance, part, 0.0)
        place = lax.broadcasted_iota(jnp.int32, (COLS, row_count), 0)
        stats = jnp.where(place == PEAK, peak, picked)
        stats = jnp.where(place == TOTAL, total, stats)
        for slot in range(ahead):
            stats_ref[slot] = refs[given][slot]
        for slot in range(count):
            stats_ref[ahead + slot] = stats[:, slot * span : (slot + 1) * span]

    return call(
        kernel,
        (
            jax.ShapeDtypeStruct((height, row_count), jnp.float32),
            bf16_rows(row_count, width),
            jax.ShapeDtypeStruct((ahead + count, COLS, span), jnp.float32),
        ),
        2 * height * row_count * width,
        in_specs=[smem_spec()] + [vmem_spec()] * (2 + given + len(others)),
        out_specs=tuple(vmem_spec() for _ in range(3)),
    )(member, weight, label_weight, *pieces, *others)


def fill_near(place, piece_refs, put, put_if):
    value_ref, left_ref, right_ref = piece_refs
    put(0, value_ref)
    put_if(place < 2, 1, left_ref)
    put_if(place >= 2, 1, right_ref)


def fill_far(place, piece_refs, put, put_if):
    far_ref, end_ref, left_ref, right_ref = piece_refs
    put(0, far_ref)
    put_if((place == 0) | (place == 3), 1, end_ref)
    put_if(place == 1, 1, right_ref)
    put_if(place == 2, 1, left_ref)


def fill_all(place, piece_refs, put, put_if):
    for slot, piece_ref in enumerate(piece_refs):
        put(slot, piece_ref)


def log_add(first, second):
    peak = jnp.maximum(first, second)
    return peak + jnp.log(jnp.exp(first - peak) + jnp.exp(second - peak))


def log_add3(first, second, third):
    peak = jnp.maximum(jnp.maximum(first, second), third)
    return peak + jnp.log(
        jnp.exp(first - peak) + jnp.exp(second - peak) + jnp.exp(third - peak)
    )


def ctc_pass(stats, slots, labels, frame_counts, label_counts, frame_count, label_max):
    sources = len(stats)
    count, _, span = stats[0].shape
    row_count = count * span
    utterances = labels.shape[0]
    entries = utterances * COLS
    tall = round_up(span, LANES)

    def kernel(slots_ref, labels_ref, frames_ref, counts_ref, *refs):
        (
            out_ref,
            high_ref,
            low_ref,
            loss_ref,
            turn_ref,
            emission_ref,
            emit_blank,
            emit_label,
            blank_fwd,
            label_fwd,
            blank_bwd,
            label_bwd,
            occupancy_ref,
        ) = refs[sources:]
        place = lax.broadcasted_iota(jnp.int32, (COLS, span), 0)
        turn_ref[...] = jnp.zeros(turn_ref.shape, jnp.float32)
        for slot in range(count):
            found = [refs[k][slots_ref[k * count + slot]] for k in range(sources)]
            joined = found[0]
            peak = found[0][PEAK : PEAK + 1]
            for other in found[1:]:
                joined = joined + other
                peak = jnp.maximum(peak, other[PEAK : PEAK + 1])
            total = jnp.zeros((1, span), jnp.float32)
            for other in found:
                total = total + other[TOTAL : TOTAL + 1] * jnp.exp(other[PEAK : PEAK + 1] - peak)
            log_total = peak + jnp.log(total)
            turn_ref[:COLS, :span] = jnp.where(place == TOTAL, log_total, joined - log_total)
            emission_ref[slot * span : (slot + 1) * span] = jnp.transpose(turn_ref[...], (1, 0))[
                :span
            ]

        lane = lax.broadcasted_iota(jnp.int32, (utterances, LANES), 1)
        is_label = lane < label_max
        is_blank = lane <= label_max
        names = labels_ref[...]
        earlier = pltpu.roll(names, 1, 1)
        skip = is_label & (lane >= 1) & (names != 0) & (names != earlier)
        later = pltpu.roll(names, LANES - 1, 1)
        skip_next = (lane < label_max - 1) & (later != 0) & (later != names)
        frames = frames_ref[...]
        counts = counts_ref[...]
        ends_blank = jnp.where(lane == counts, 0.0, LOG_ZERO)
        ends_label = jnp.where(lane == counts - 1, 0.0, LOG_ZERO)

        def spread(step, carry):
            row = emission_ref[pl.ds(step, utterances, stride=frame_count), :]
            blank = jnp.sum(jnp.where(lane == label_max, row, 0.0), axis=1, keepdims=True)
            emit_blank[step] = jnp.where(is_blank, blank, LOG_ZERO)
            emit_label[step] = jnp.where(is_label, row, LOG_ZERO)
            return carry

        lax.fori_loop(0, frame_count, spread, 0, unroll=16)

        def advance(step, carry):
            fwd_blank, fwd_label, bwd_blank, bwd_label = carry
            moved = jnp.where(lane == 0, LOG_ZERO, pltpu.roll(fwd_label, 1, 1))
            new_blank = log_add(fwd_blank, moved) + emit_blank[step]
            new_label = (
                log_add3(fwd_label, fwd_blank, jnp.where(skip, moved, LOG_ZERO))
                + emit_label[step]
            )
            alive = step < frames
            fwd_blank = jnp.where(alive, new_blank, fwd_blank)
            fwd_label = jnp.where(alive, new_label, fwd_label)
            blank_fwd[step] = fwd_blank
            label_fwd[step] = fwd_label

            back = frame_count - 1 - step
            out_blank = bwd_blank + emit_blank[back + 1]
            out_label = bwd_label + emit_label[back + 1]
            next_blank = pltpu.roll(out_blank, LANES - 1, 1)
            next_label = jnp.where(skip_next, pltpu.roll(out_label, LANES - 1, 1), LOG_ZERO)
            ended = back >= frames - 1
            bwd_blank = jnp.where(ended, ends_blank, log_add(out_blank, out_label))
            bwd_label = jnp.where(
                ended, ends_label, log_add3(out_label, next_blank, next_label)
            )
            blank_bwd[back] = bwd_blank
            label_bwd[back] = bwd_label
            return (fwd_blank, fwd_label, bwd_blank, bwd_label)

        first_blank = jnp.where(lane == 0, emit_blank[0], LOG_ZERO)
        first_label = jnp.where(lane == 0, emit_label[0], LOG_ZERO)
        blank_fwd[0] = first_blank
        label_fwd[0] = first_label
        blank_bwd[frame_count - 1] = ends_blank
        label_bwd[frame_count - 1] = ends_label
        fwd_blank, fwd_label, _, _ = lax.fori_loop(
            1, frame_count, advance, (first_blank, first_label, ends_blank, ends_label), unroll=4
        )
        end_state = jnp.sum(jnp.where(lane == counts, fwd_blank, 0.0), axis=1, keepdims=True)
        near_state = jnp.sum(jnp.where(lane == counts - 1, fwd_label, 0.0), axis=1, keepdims=True)
        log_like = log_add(end_state, near_state)
        loss_ref[...] = jnp.broadcast_to(-log_like, (utterances, LANES))

        def occupy(step, carry):
            blank = jnp.exp(blank_fwd[step] + blank_bwd[step] - log_like)
            label = jnp.exp(label_fwd[step] + label_bwd[step] - log_like)
            blank = jnp.sum(jnp.where(is_blank, blank, 0.0), axis=1, keepdims=True)
            label = jnp.where(is_label, label, 0.0)
            whole = blank + jnp.sum(label, axis=1, keepdims=True)
            filled = jnp.where(lane == label_max, blank, label)
            filled = jnp.where(lane == WHOLE, whole, filled)
            filled = jnp.where(step < frames, -filled, 0.0)
            row = emission_ref[pl.ds(step, utterances, stride=frame_count), :]
            occupancy_ref[pl.ds(step, utterances, stride=frame_count), :] = jnp.where(
                lane == TOTAL, row, filled
            )
            return carry

        lax.fori_loop(0, frame_count, occupy, 0, unroll=16)
        turned = jnp.transpose(occupancy_ref[...], (1, 0))[:COLS]
        out_ref[...] = turned
        row_place = lax.broadcasted_iota(jnp.int32, (COLS, row_count), 0)
        owner = lax.broadcasted_iota(jnp.int32, (COLS, row_count), 1) // frame_count
        source = jnp.where(row_place < WHOLE, turned, 0.0)
        for utterance in range(utterances):
            part = jnp.where(owner == utterance, source, 0.0)
            high = part.astype(jnp.bfloat16)
            high_ref[utterance * COLS : (utterance + 1) * COLS] = high
            low_ref[utterance * COLS : (utterance + 1) * COLS] = (
                part - high.astype(jnp.float32)
            ).astype(jnp.bfloat16)

    held = pltpu.VMEM((frame_count, utterances, LANES), jnp.float32)
    table = pltpu.VMEM((row_count, LANES), jnp.float32)
    return call(
        kernel,
        (
            jax.ShapeDtypeStruct((COLS, row_count), jnp.float32),
            bf16_rows(entries, row_count),
            bf16_rows(entries, row_count),
            jax.ShapeDtypeStruct((utterances, LANES), jnp.float32),
        ),
        1 << 26,
        in_specs=[smem_spec()] + [vmem_spec()] * (3 + sources),
        out_specs=tuple(vmem_spec() for _ in range(4)),
        scratch_shapes=[pltpu.VMEM((LANES, tall), jnp.float32), table]
        + [held] * 6
        + [table],
    )(slots, labels, frame_counts, label_counts, *stats)


def head_gradient(logits, rows, occupancy, high, low, places, order, outputs, each):
    count = len(logits)
    row_count, width = rows[0].shape
    entries = places.shape[1]
    blocks = outputs * each

    def kernel(order_ref, *refs):
        logits_refs, rows_refs = refs[:count], refs[count : 2 * count]
        occupancy_ref, high_ref, low_ref, places_ref = refs[2 * count : 2 * count + 4]
        out_refs = refs[2 * count + 4 :]
        for block in range(blocks):
            start = pl.multiple_of(order_ref[block] * BLOCK_ROWS, BLOCK_ROWS)
            entry = start + lax.broadcasted_iota(jnp.int32, (BLOCK_ROWS, entries), 0)
            select = as_mask(entry == places_ref[...])
            total = None
            for g in range(count):
                lanes = slice(g * row_count, (g + 1) * row_count)
                scattered = lax.dot_general(
                    select, high_ref[:, lanes], NN, preferred_element_type=jnp.float32
                ) + lax.dot_general(
                    select, low_ref[:, lanes], NN, preferred_element_type=jnp.float32
                )
                whole = occupancy_ref[WHOLE : WHOLE + 1, lanes]
                log_total = occupancy_ref[TOTAL : TOTAL + 1, lanes]
                values = logits_refs[g][pl.ds(start, BLOCK_ROWS), :]
                grad = (scattered - jnp.exp(values - log_total) * whole).astype(jnp.bfloat16)
                part = lax.dot_general(
                    grad, rows_refs[g][...], NN, preferred_element_type=jnp.float32
                )
                total = part if total is None else total + part
            out_refs[block // each][
                block % each * BLOCK_ROWS : (block % each + 1) * BLOCK_ROWS
            ] = total.astype(jnp.bfloat16)

    return call(
        kernel,
        tuple(bf16_rows(each * BLOCK_ROWS, width) for _ in range(outputs)),
        2 * blocks * BLOCK_ROWS * count * row_count * (width + 2 * entries),
        in_specs=[smem_spec()] + [vmem_spec()] * (2 * count + 4),
        out_specs=tuple(vmem_spec() for _ in range(outputs)),
    )(order, *logits, *rows, occupancy, high, low, places)


def assemble(pieces, offsets, height):
    count = len(pieces)
    part, width = pieces[0].shape
    short = height % part

    def kernel(offsets_ref, *refs):
        out_ref, sems = refs[count], refs[count + 1]

        def each(act):
            for index in range(count):
                offset = pl.multiple_of(offsets_ref[index], part)

                @pl.when(offset + part <= height)
                def _():
                    act(
                        pltpu.make_async_copy(
                            refs[index], out_ref.at[pl.ds(offset, part)], sems.at[index]
                        )
                    )

                if short:

                    @pl.when(offset + part > height)
                    def _():
                        act(
                            pltpu.make_async_copy(
                                refs[index].at[pl.ds(0, short)],
                                out_ref.at[pl.ds(height - short, short)],
                                sems.at[index],
                            )
                        )

        each(lambda copy: copy.start())
        each(lambda copy: copy.wait())

    return call(
        kernel,
        bf16_rows(height, width),
        0,
        in_specs=[smem_spec()] + [pl.BlockSpec(memory_space=pl.ANY)] * count,
        out_specs=pl.BlockSpec(memory_space=pl.ANY),
        scratch_shapes=[pltpu.SemaphoreType.DMA((count,))],
    )(offsets, *pieces)


def swap(value, axis):
    return lax.ppermute(value, axis, [(0, 1), (1, 0)])


def rotate(value, axis, by):
    count = lax.axis_size(axis)
    return lax.ppermute(value, axis, [(i, (i + by) % count) for i in range(count)])


def after(value, *others):
    return lax.optimization_barrier((value,) + others)[0]


def line_near(value):
    left = lax.ppermute(value, "expert", [(1, 0), (2, 1), (3, 2)])
    right = lax.ppermute(value, "expert", [(0, 1), (1, 2), (2, 3)])
    return left, right


def line_far(near, member):
    left = lax.ppermute(near[0], "expert", [(1, 0), (2, 1)])
    right = lax.ppermute(near[1], "expert", [(1, 2), (2, 3)])
    return jnp.where(member < 2, left, right)


def line_end(far):
    return lax.ppermute(far, "expert", [(1, 0), (2, 3)])


LINE_ORDER = np.array([[0, 1, 2, 3], [1, 2, 3, 0], [2, 1, 0, 3], [3, 2, 1, 0]])


def slot_orders(count):
    return LINE_ORDER if count == 4 else np.tile(np.arange(count), (count, 1))


def slot_tables(count):
    orders = slot_orders(count)
    tables = np.zeros((count, count, count), np.int32)
    for member in range(count):
        for k in range(count):
            source = (member + k) % count
            for slot in range(count):
                tables[member, k, slot] = list(orders[source]).index(orders[member][slot])
    return tables.reshape(count, count * count)


def add(first, second):
    return (first.astype(jnp.float32) + second.astype(jnp.float32)).astype(jnp.bfloat16)


def per_device(
    frames,
    norm_gain,
    router,
    w_in,
    w_out,
    routing,
    head_gain,
    head_weight,
    frame_lengths,
    labels,
    label_lengths,
):
    sections = lax.axis_size("section")
    section_id = lax.axis_index("section")
    group_size = lax.axis_size("expert")
    member = lax.axis_index("expert")
    outer_size = lax.axis_size("dpo")
    inner_size = lax.axis_size("dpi")
    core = lax.axis_index("dpi")
    micro, utt_dev, frame_count, width = frames.shape
    label_max = labels.shape[2]
    experts = w_in.shape[1] * group_size
    hidden = w_in.shape[3]
    pair_count = micro * utt_dev
    per_section = pair_count // sections
    first_pair = section_id * per_section
    share = (utt_dev * frame_count * 9 + 8 * experts - 1) // (8 * experts)
    capacity = round_up(share * -(-per_section // utt_dev), 8)
    span = per_section * frame_count
    member_ref = member.astype(jnp.int32).reshape(1)

    def mine_of(value):
        return lax.dynamic_slice_in_dim(value, first_pair, per_section, 0)

    def exchange(blocks, sign):
        return [blocks[0]] + [
            rotate(blocks[k], "expert", sign * k) for k in range(1, group_size)
        ]

    def lanes_of(ids):
        return jnp.pad(mine_of(ids), ((0, 0), (0, LANES - frame_count)), constant_values=-1)

    current = lax.dynamic_slice_in_dim(
        frames.reshape(pair_count * frame_count, width), first_pair * frame_count, span, 0
    )
    own_ids = routing.reshape(pair_count, frame_count)
    paired = sections == 2 and inner_size == 2
    if paired:
        other_ids = swap(own_ids, "section")
        all_ids = [
            jnp.where(section_id == layer, own_ids, other_ids) for layer in range(sections)
        ]
    else:
        all_ids = lax.all_gather(own_ids, "section")
    layer_ids = [lanes_of(all_ids[layer]) for layer in range(sections)]
    outgoing = dispatch(current, layer_ids[0], member_ref, experts, capacity, frame_count)
    received = exchange(outgoing, 1)

    own_table = jnp.concatenate(
        [
            norm_gain,
            jnp.zeros((7, width), jnp.float32),
            jnp.transpose(router[0]).astype(jnp.float32),
            jnp.zeros((round_up(experts, 8) - experts, width), jnp.float32),
        ],
        axis=0,
    )
    own = (w_in[0, 0], w_out[0, 0])
    if paired:
        other_table = swap(own_table, "section")
        half = hidden // 2
        sent_in = lax.dynamic_slice(own[0], (0, core * half), (width, half))
        sent_out = lax.dynamic_slice(own[1], (core * half, 0), (half, width))
        sent_in, sent_out = lax.optimization_barrier((sent_in, sent_out, own_table))[:2]
        came_in = swap(sent_in, "section")
        came_out = swap(sent_out, "section")
        other = [(came_in, came_out), (swap(came_in, "dpi"), swap(came_out, "dpi"))]
    else:
        all_tables = lax.all_gather(own_table, "section")
        all_in = lax.all_gather(own[0], "section")
        all_out = lax.all_gather(own[1], "section")

    layers = []
    for layer in range(sections):
        if paired:
            mine = section_id == layer
            table = jnp.where(mine, own_table, other_table)
            layers.append((table, own, other, mine.astype(jnp.int32).reshape(1)))
        else:
            chosen = (all_in[layer], all_out[layer])
            layers.append((all_tables[layer], chosen, [], jnp.ones((1,), jnp.int32)))

    labels, frame_lengths, label_lengths = lax.optimization_barrier(
        (labels, frame_lengths, label_lengths, received[1])
    )[:3]
    notes = jnp.concatenate(
        [
            mine_of(labels.reshape(pair_count, label_max)),
            mine_of(frame_lengths.reshape(pair_count, 1)),
            mine_of(label_lengths.reshape(pair_count, 1)),
        ],
        axis=1,
    )
    if group_size == 4:
        found = [notes] + [rotate(notes, "expert", -k) for k in range(1, group_size)]
        low = member < 2
        notes_all = jnp.stack(
            [
                found[0],
                jnp.where(low, found[1], found[3]),
                found[2],
                jnp.where(low, found[3], found[1]),
            ]
        )
    else:
        notes_all = lax.all_gather(notes, "expert")
    shard = head_weight.shape[1]
    weight_rows = jnp.transpose(head_weight)
    notes_all = notes_all.reshape(-1, label_max + 2)
    utterances = notes_all.shape[0]
    names = notes_all[:, :label_max]
    named = jnp.concatenate(
        [
            names,
            jnp.zeros((utterances, 1), jnp.int32),
            jnp.full((utterances, COLS - label_max - 1), -1, jnp.int32),
        ],
        axis=1,
    ).reshape(utterances * COLS)
    local = named - member * shard
    places = jnp.where((named >= 0) & (local >= 0) & (local < shard), local, -1)
    slot_entries = per_section * COLS

    for layer in range(sections):
        table, weights, others, pick_own = layers[layer]
        done = run_expert(received, table, weights, others, pick_own)
        returned = exchange(done, -1)
        if layer == 0:
            label_weight = label_rows(weight_rows, after(places.reshape(-1, 1), done[0]))
            returned, label_weight = lax.optimization_barrier((returned, label_weight))
        if layer < sections - 1:
            current, outgoing = combine_and_dispatch(
                current,
                returned,
                layer_ids[layer],
                table,
                layer_ids[layer + 1],
                member_ref,
                experts,
                capacity,
                frame_count,
            )
            received = exchange(outgoing, 1)
        else:
            normed = combine_and_norm(
                current,
                returned,
                layer_ids[layer],
                table,
                head_gain.reshape(1, width),
                member_ref,
                experts,
                capacity,
                frame_count,
            )

    def logits_of(fill, first, count, pieces, earlier):
        chosen = label_weight[first * slot_entries : (first + count) * slot_entries]
        return head_logits(
            fill, count, pieces, member_ref, weight_rows, chosen, frame_count, earlier
        )

    if group_size == 4:
        left, right = line_near(normed)
        far = line_far((left, right), member)
        heads = [logits_of(fill_near, 0, 2, [normed, left, right], None)]
        far, heads[0] = lax.optimization_barrier((far, heads[0]))
        end = line_end(far)
        heads.append(logits_of(fill_far, 2, 2, [far, end, left, right], heads[0][2]))
        stats = heads[1][2]
        found = [stats] + [rotate(stats, "expert", -k) for k in range(1, group_size)]
    else:
        gathered = lax.all_gather(normed, "expert")
        pieces = [gathered[k] for k in range(group_size)]
        heads = [logits_of(fill_all, 0, group_size, pieces, None)]
        gathered = lax.all_gather(heads[0][2], "expert")
        found = [
            lax.dynamic_index_in_dim(gathered, (member + k) % group_size, 0, keepdims=False)
            for k in range(group_size)
        ]
    tables = jnp.asarray(slot_tables(group_size))
    slots = lax.dynamic_index_in_dim(tables, member, 0, keepdims=False)
    occupancy, high, low, losses = ctc_pass(
        found,
        slots,
        jnp.pad(names, ((0, 0), (0, LANES - label_max))),
        notes_all[:, label_max : label_max + 1],
        notes_all[:, label_max + 1 :],
        frame_count,
        label_max,
    )
    own_slot = 0 if group_size == 4 else member
    my_losses = lax.dynamic_slice(losses, (own_slot * per_section, 0), (per_section, 1))

    def gradient(order, outputs, each):
        return head_gradient(
            [head[0] for head in heads],
            [head[1] for head in heads],
            occupancy,
            high,
            low,
            places.reshape(1, -1),
            order,
            outputs,
            each,
        )

    blocks = heads[0][0].shape[0] // BLOCK_ROWS
    if paired and outer_size == 2 and blocks == 8:
        outer = lax.axis_index("dpo")

        def pair_of(side, first, second):
            return jnp.stack([side * 4 + first, side * 4 + 2 + second]).astype(jnp.int32)

        came_sent = swap(
            gradient(pair_of(1 - core, 1 - section_id, 1 - outer), 1, 2)[0], "dpi"
        )
        sent = add(gradient(pair_of(core, 1 - section_id, 1 - outer), 1, 2)[0], came_sent)
        first_in = swap(sent[:BLOCK_ROWS], "section")
        second_in = swap(sent[BLOCK_ROWS:], "dpo")
        order = jnp.concatenate(
            [pair_of(1 - core, section_id, outer), pair_of(core, section_id, outer)]
        )
        sibling_kept, own_kept = gradient(after(order, sent), 2, 2)
        kept = add(own_kept, swap(sibling_kept, "dpi"))
        first = add(kept[:BLOCK_ROWS], first_in)
        second = add(kept[BLOCK_ROWS:], second_in)
        part = BLOCK_ROWS // 2

        def piece(value, index):
            return lax.dynamic_slice_in_dim(value, index * part, part, 0)

        first_far = swap(piece(first, 1 - outer), "dpo")
        second_far = swap(piece(second, 1 - section_id), "section")
        final = jnp.concatenate(
            [add(piece(first, outer), first_far), add(piece(second, section_id), second_far)],
            axis=0,
        )
        across = swap(final, "section")
        beside = swap(final, "dpo")
        first_diagonal = swap(beside[:part], "section")
        second_diagonal = swap(across[part:], "dpo")
        mine = [final, across, beside, first_diagonal, second_diagonal]
        theirs = [swap(value, "dpi") for value in mine]
        pieces, offsets = [], []
        for side, held in ((core, mine), (1 - core, theirs)):
            where = (
                (section_id, outer),
                (1 - section_id, outer),
                (section_id, 1 - outer),
            )
            for value, (s, y) in zip(held[:3], where):
                pieces += [value[:part], value[part:]]
                offsets += [
                    side * 1024 + s * 256 + y * 128,
                    side * 1024 + 512 + y * 256 + s * 128,
                ]
            pieces += held[3:]
            s, y = 1 - section_id, 1 - outer
            offsets += [
                side * 1024 + s * 256 + y * 128,
                side * 1024 + 512 + y * 256 + s * 128,
            ]
        whole = assemble(pieces, jnp.stack(offsets).astype(jnp.int32), shard)
    else:
        partial = gradient(jnp.arange(blocks, dtype=jnp.int32), 1, blocks)[0][:shard]
        whole = lax.psum(partial.astype(jnp.float32), ("section", "dpo", "dpi")).astype(
            jnp.bfloat16
        )
    return (my_losses, jnp.transpose(whole))


def solution(mesh):
    sections, group_size, spread = (mesh.shape[name] for name in ("section", "expert", "dp"))
    inner = 2 if spread % 2 == 0 else 1
    split = Mesh(
        mesh.devices.reshape(sections, group_size, spread // inner, inner),
        ("section", "expert", "dpo", "dpi"),
    )
    block = ("expert", "dpo", "dpi")
    placed = (
        P(None, block, None, None),
        P("section", None),
        P("section", None, None),
        P("section", "expert", None, None),
        P("section", "expert", None, None),
        P("section", None, block, None, None),
        P(),
        P(None, "expert"),
        P(None, block),
        P(None, block, None),
        P(None, block),
    )
    return jax.shard_map(
        per_device,
        mesh=split,
        in_specs=placed,
        out_specs=(P("section", block), P(None, "expert")),
        check_vma=False,
    )
```

```python
import jax
import jax.numpy as jnp
import numpy as np
from jax import lax
from jax.experimental import pallas as pl
from jax.experimental.pallas import tpu as pltpu
from jax.sharding import Mesh, PartitionSpec as P

EPSILON = 1e-06
LOG_ZERO = -1e30
VMEM_LIMIT = 24 * 1024 * 1024
LANES = 128
COLS = 16
PEAK, TOTAL, WHOLE = COLS - 3, COLS - 2, COLS - 3
BLOCK_ROWS = 256
NT = (((1,), (1,)), ((), ()))
NN = (((1,), (0,)), ((), ()))


def round_up(value, unit):
    return -(-value // unit) * unit


def vmem_spec():
    return pl.BlockSpec(memory_space=pltpu.VMEM)


def smem_spec():
    return pl.BlockSpec(memory_space=pltpu.SMEM)


def call(kernel, out_shape, flops=0, **options):
    return pl.pallas_call(
        kernel,
        out_shape=out_shape,
        compiler_params=pltpu.CompilerParams(vmem_limit_bytes=VMEM_LIMIT),
        cost_estimate=pl.CostEstimate(flops=flops, bytes_accessed=0, transcendentals=0),
        **options,
    )


def bf16_rows(count, width):
    return jax.ShapeDtypeStruct((count, width), jnp.bfloat16)


def as_mask(values):
    return values.astype(jnp.float32).astype(jnp.bfloat16)


def split_rows(values, out_refs):
    size = out_refs[0].shape[0]
    for turn, out_ref in enumerate(out_refs):
        out_ref[...] = values[turn * size : (turn + 1) * size].astype(jnp.bfloat16)


def join_rows(refs):
    return jnp.concatenate([ref[...].astype(jnp.float32) for ref in refs], axis=0)


def rms_scale(values, gain):
    values = values.astype(jnp.float32)
    scale = lax.rsqrt(jnp.mean(values * values, axis=-1, keepdims=True) + EPSILON)
    return (values * scale * gain).astype(jnp.bfloat16)


def expert_column(ids, frame_count):
    pairs = ids.shape[0]
    square = jnp.concatenate(
        [ids.astype(jnp.float32), jnp.full((LANES - pairs, LANES), -1.0, jnp.float32)], axis=0
    )
    turned = jnp.transpose(square, (1, 0)).astype(jnp.int32)
    return jnp.concatenate([turned[:frame_count, p : p + 1] for p in range(pairs)], axis=0)


def placement(column, member, experts, capacity):
    count = column.shape[0]
    shifted = column - member
    relative = jnp.where(shifted < 0, shifted + experts, shifted)
    lane = lax.broadcasted_iota(jnp.int32, (count, LANES), 1)
    one_hot = (lane == relative).astype(jnp.float32)
    before = lax.broadcasted_iota(jnp.int32, (count, count), 1) <= lax.broadcasted_iota(
        jnp.int32, (count, count), 0
    )
    rank = lax.dot_general(
        as_mask(before), one_hot.astype(jnp.bfloat16), NN, preferred_element_type=jnp.float32
    )
    start = (lane * capacity - 1).astype(jnp.float32)
    slots = jnp.sum(one_hot * (rank + start), axis=1, keepdims=True).astype(jnp.int32)
    places = lax.broadcasted_iota(jnp.int32, (count, experts * capacity), 1)
    return (places == slots).astype(jnp.float32)


def scatter_rows(rows, ids, member, experts, capacity, frame_count, out_refs):
    count = rows.shape[0]
    chosen = placement(expert_column(ids, frame_count), member, experts, capacity)
    tall = round_up(count, LANES)
    if tall > count:
        chosen = jnp.concatenate(
            [chosen, jnp.zeros((tall - count, chosen.shape[1]), jnp.float32)], axis=0
        )
    pick = jnp.transpose(chosen, (1, 0))[:, :count].astype(jnp.bfloat16)
    placed = lax.dot_general(pick, rows, NN, preferred_element_type=jnp.float32)
    split_rows(placed, out_refs)


def combine_rows(rows, returned, ids, table, member, experts, capacity, frame_count):
    column = expert_column(ids, frame_count)
    pick = placement(column, member, experts, capacity).astype(jnp.bfloat16)
    normed = rms_scale(rows, table[:1])
    router = jnp.concatenate(
        [table[8:], jnp.zeros((LANES + 8 - table.shape[0], rows.shape[1]), jnp.float32)], axis=0
    ).astype(jnp.bfloat16)
    logits = lax.dot_general(normed, router, NT, preferred_element_type=jnp.float32)
    lane = lax.broadcasted_iota(jnp.int32, logits.shape, 1)
    gate = jax.nn.sigmoid(jnp.sum(jnp.where(lane == column, logits, 0.0), axis=1, keepdims=True))
    stacked = join_rows(returned).astype(jnp.bfloat16)
    mixed = lax.dot_general(pick, stacked, NN, preferred_element_type=jnp.float32)
    return (rows.astype(jnp.float32) + gate * mixed).astype(jnp.bfloat16)


def dispatch(rows, ids, member, experts, capacity, frame_count):
    width = rows.shape[1]

    def kernel(member_ref, rows_ref, ids_ref, *out_refs):
        scatter_rows(
            rows_ref[...], ids_ref[...], member_ref[0], experts, capacity, frame_count, out_refs
        )

    return call(
        kernel,
        tuple(bf16_rows(capacity, width) for _ in range(experts)),
        1 << 27,
        in_specs=[smem_spec()] + [vmem_spec()] * 2,
        out_specs=tuple(vmem_spec() for _ in range(experts)),
    )(member, rows, ids)


def pick_table(pick_ref, tables):
    if len(tables) == 1:
        return tables[0][...]
    return jnp.where(pick_ref[0] == 1, tables[0][...], tables[1][...])


def run_expert(received, tables, own, other, pick_own):
    count = len(received)
    capacity, width = received[0].shape
    others, choices = len(other), len(tables)

    def kernel(pick_ref, in_ref, out_weight_ref, *refs):
        table_refs, refs = refs[:choices], refs[choices:]
        other_refs, refs = refs[: 2 * others], refs[2 * others :]
        received_refs, out_refs = refs[:count], refs[count:]

        def work(pieces):
            gain = pick_table(pick_ref, table_refs)[:1]
            normed = rms_scale(join_rows(received_refs), gain)
            total = None
            for weight_in, weight_out in pieces:
                hidden = lax.dot_general(
                    normed, weight_in[...], NN, preferred_element_type=jnp.float32
                )
                active = (hidden / (1.0 + jnp.exp(-hidden))).astype(jnp.bfloat16)
                part = lax.dot_general(
                    active, weight_out[...], NN, preferred_element_type=jnp.float32
                )
                total = part if total is None else total + part
            split_rows(total, out_refs)

        if others == 0:
            work([(in_ref, out_weight_ref)])
            return

        @pl.when(pick_ref[0] == 1)
        def _():
            work([(in_ref, out_weight_ref)])

        @pl.when(pick_ref[0] != 1)
        def _():
            work([(other_refs[2 * i], other_refs[2 * i + 1]) for i in range(others)])

    flat = [weight for pair in other for weight in pair]
    return call(
        kernel,
        tuple(bf16_rows(capacity, width) for _ in range(count)),
        4 * count * capacity * width * own[0].shape[1],
        in_specs=[smem_spec()] + [vmem_spec()] * (2 + choices + 2 * others + count),
        out_specs=tuple(vmem_spec() for _ in range(count)),
    )(pick_own, *own, *tables, *flat, *received)


def combine_and_dispatch(
    rows, returned, ids, tables, pick_own, next_ids, member, experts, capacity, frame_count
):
    width = rows.shape[1]
    choices = len(tables)

    def kernel(member_ref, pick_ref, rows_ref, ids_ref, next_ref, *refs):
        table_refs, refs = refs[:choices], refs[choices:]
        returned_refs, x_ref, out_refs = refs[:experts], refs[experts], refs[experts + 1 :]
        mixed = combine_rows(
            rows_ref[...],
            returned_refs,
            ids_ref[...],
            pick_table(pick_ref, table_refs),
            member_ref[0],
            experts,
            capacity,
            frame_count,
        )
        x_ref[...] = mixed
        scatter_rows(
            mixed, next_ref[...], member_ref[0], experts, capacity, frame_count, out_refs
        )

    shapes = (bf16_rows(*rows.shape),) + tuple(
        bf16_rows(capacity, width) for _ in range(experts)
    )
    result = call(
        kernel,
        shapes,
        1 << 28,
        in_specs=[smem_spec()] * 2 + [vmem_spec()] * (3 + choices + experts),
        out_specs=tuple(vmem_spec() for _ in shapes),
    )(member, pick_own, rows, ids, next_ids, *tables, *returned)
    return result[0], result[1:]


def combine_and_norm(
    rows, returned, ids, tables, pick_own, head_gain, member, experts, capacity, frame_count
):
    choices = len(tables)

    def kernel(member_ref, pick_ref, rows_ref, ids_ref, head_ref, *refs):
        table_refs, refs = refs[:choices], refs[choices:]
        final = combine_rows(
            rows_ref[...],
            refs[:experts],
            ids_ref[...],
            pick_table(pick_ref, table_refs),
            member_ref[0],
            experts,
            capacity,
            frame_count,
        )
        refs[experts][...] = rms_scale(final, head_ref[...])

    return call(
        kernel,
        bf16_rows(*rows.shape),
        1 << 28,
        in_specs=[smem_spec()] * 2 + [vmem_spec()] * (3 + choices + experts),
        out_specs=vmem_spec(),
    )(member, pick_own, rows, ids, head_gain, *tables, *returned)


def block_list(shard):
    return [(i, min(BLOCK_ROWS, shard - i)) for i in range(0, shard, BLOCK_ROWS)]


def label_rows(weight, notes, member, label_max, line):
    shard, width = weight.shape
    sources = len(notes)
    pairs, columns = notes[0].shape
    utterances = sources * pairs
    entries = utterances * COLS

    def kernel(member_ref, weight_ref, *refs):
        note_refs = refs[:sources]
        out_ref, places_ref, names_ref, turned_ref = refs[sources:]
        place = member_ref[0]
        found = [ref[...] for ref in note_refs]
        if line:
            low = place < 2
            found = [
                found[0],
                jnp.where(low, found[1], found[3]),
                found[2],
                jnp.where(low, found[3], found[1]),
            ]
        names_ref[...] = jnp.zeros(names_ref.shape, jnp.int32)
        for slot in range(sources):
            names_ref[slot * pairs : (slot + 1) * pairs, :columns] = found[slot]
        lane = lax.broadcasted_iota(jnp.int32, (utterances, LANES), 1)
        named = jnp.where(lane < label_max, names_ref[...], jnp.where(lane == label_max, 0, -1))
        local = named - place * shard
        local = jnp.where((named >= 0) & (local >= 0) & (local < shard), local, -1)
        square = jnp.concatenate(
            [
                local.astype(jnp.float32),
                jnp.full((LANES - utterances, LANES), -1.0, jnp.float32),
            ],
            axis=0,
        )
        turned = jnp.transpose(square, (1, 0))
        for utterance in range(utterances):
            turned_ref[utterance * COLS : (utterance + 1) * COLS] = jnp.broadcast_to(
                turned[:COLS, utterance : utterance + 1], (COLS, LANES)
            )
        places = turned_ref[:, :1].astype(jnp.int32)
        places_ref[...] = jnp.transpose(turned_ref[...], (1, 0))[:1].astype(jnp.int32)
        total = jnp.zeros((entries, width), jnp.float32)
        for first, size in block_list(shard):
            entry = first + lax.broadcasted_iota(jnp.int32, (entries, size), 1)
            total = total + lax.dot_general(
                as_mask(entry == places),
                weight_ref[first : first + size],
                NN,
                preferred_element_type=jnp.float32,
            )
        out_ref[...] = total.astype(jnp.bfloat16)

    return call(
        kernel,
        (
            bf16_rows(entries, width),
            jax.ShapeDtypeStruct((1, entries), jnp.int32),
            jax.ShapeDtypeStruct((utterances, LANES), jnp.int32),
        ),
        2 * shard * entries * width,
        in_specs=[smem_spec()] + [vmem_spec()] * (1 + sources),
        out_specs=tuple(vmem_spec() for _ in range(3)),
        scratch_shapes=[pltpu.VMEM((entries, LANES), jnp.float32)],
    )(member, weight, *notes)


def head_logits(
    fill, first_slot, count, pieces, member, weight, label_weight, frame_count, earlier
):
    given = len(pieces)
    ahead = 0 if earlier is None else earlier.shape[0]
    span, width = pieces[0].shape
    row_count = count * span
    shard = weight.shape[0]
    height = round_up(shard, BLOCK_ROWS)
    entries = row_count // frame_count * COLS
    first_entry = first_slot * entries // count
    others = [] if earlier is None else [earlier]

    def kernel(member_ref, weight_ref, label_ref, *refs):
        piece_refs = refs[:given]
        logits_ref, rows_ref, stats_ref = refs[given + len(others) :]

        def put(slot, piece_ref):
            rows_ref[slot * span : (slot + 1) * span] = piece_ref[...]

        def put_if(condition, slot, piece_ref):
            @pl.when(condition)
            def _():
                put(slot, piece_ref)

        fill(member_ref[0], piece_refs, put, put_if)
        peak = jnp.full((1, row_count), LOG_ZERO, jnp.float32)
        total = jnp.zeros((1, row_count), jnp.float32)
        for first, size in block_list(shard):
            logits = lax.dot_general(
                weight_ref[first : first + size],
                rows_ref[...],
                NT,
                preferred_element_type=jnp.float32,
            )
            logits_ref[first : first + size] = logits
            before = peak
            peak = jnp.maximum(before, jnp.max(logits, axis=0, keepdims=True))
            total = total * jnp.exp(before - peak) + jnp.sum(
                jnp.exp(logits - peak), axis=0, keepdims=True
            )
        if height > shard:
            logits_ref[shard:] = jnp.full((height - shard, row_count), LOG_ZERO, jnp.float32)
        crossed = lax.dot_general(
            label_ref[first_entry : first_entry + entries],
            rows_ref[...],
            NT,
            preferred_element_type=jnp.float32,
        )
        owner = lax.broadcasted_iota(jnp.int32, (COLS, row_count), 1) // frame_count
        picked = jnp.zeros((COLS, row_count), jnp.float32)
        for utterance in range(entries // COLS):
            part = crossed[utterance * COLS : (utterance + 1) * COLS]
            picked = picked + jnp.where(owner == utterance, part, 0.0)
        place = lax.broadcasted_iota(jnp.int32, (COLS, row_count), 0)
        stats = jnp.where(place == PEAK, peak, picked)
        stats = jnp.where(place == TOTAL, total, stats)
        for slot in range(ahead):
            stats_ref[slot] = refs[given][slot]
        for slot in range(count):
            stats_ref[ahead + slot] = stats[:, slot * span : (slot + 1) * span]

    return call(
        kernel,
        (
            jax.ShapeDtypeStruct((height, row_count), jnp.float32),
            bf16_rows(row_count, width),
            jax.ShapeDtypeStruct((ahead + count, COLS, span), jnp.float32),
        ),
        2 * height * row_count * width,
        in_specs=[smem_spec()] + [vmem_spec()] * (2 + given + len(others)),
        out_specs=tuple(vmem_spec() for _ in range(3)),
    )(member, weight, label_weight, *pieces, *others)


def fill_near(place, piece_refs, put, put_if):
    value_ref, left_ref, right_ref = piece_refs
    put(0, value_ref)
    put_if(place < 2, 1, left_ref)
    put_if(place >= 2, 1, right_ref)


def fill_far(place, piece_refs, put, put_if):
    left_far, right_far, left_end, right_end, left_ref, right_ref = piece_refs
    put_if(place < 2, 0, left_far)
    put_if(place >= 2, 0, right_far)
    put_if(place == 0, 1, left_end)
    put_if(place == 3, 1, right_end)
    put_if(place == 1, 1, right_ref)
    put_if(place == 2, 1, left_ref)


def fill_all(place, piece_refs, put, put_if):
    for slot, piece_ref in enumerate(piece_refs):
        put(slot, piece_ref)


def log_add(first, second):
    peak = jnp.maximum(first, second)
    return peak + jnp.log(jnp.exp(first - peak) + jnp.exp(second - peak))


def log_add3(first, second, third):
    peak = jnp.maximum(jnp.maximum(first, second), third)
    return peak + jnp.log(
        jnp.exp(first - peak) + jnp.exp(second - peak) + jnp.exp(third - peak)
    )


def ctc_pass(stats, slots, notes, frame_count, label_max, kept):
    sources = len(stats)
    count, _, span = stats[0].shape
    row_count = count * span
    utterances = notes.shape[0]
    entries = utterances * COLS
    tall = round_up(span, LANES)

    def kernel(slots_ref, notes_ref, *refs):
        (
            out_ref,
            high_ref,
            low_ref,
            loss_ref,
            turn_ref,
            emission_ref,
            emit_blank,
            emit_label,
            blank_fwd,
            label_fwd,
            blank_bwd,
            label_bwd,
            occupancy_ref,
        ) = refs[sources:]
        place = lax.broadcasted_iota(jnp.int32, (COLS, span), 0)
        turn_ref[...] = jnp.zeros(turn_ref.shape, jnp.float32)
        for slot in range(count):
            found = [refs[k][slots_ref[k * count + slot]] for k in range(sources)]
            joined = found[0]
            peak = found[0][PEAK : PEAK + 1]
            for other in found[1:]:
                joined = joined + other
                peak = jnp.maximum(peak, other[PEAK : PEAK + 1])
            total = jnp.zeros((1, span), jnp.float32)
            for other in found:
                total = total + other[TOTAL : TOTAL + 1] * jnp.exp(other[PEAK : PEAK + 1] - peak)
            log_total = peak + jnp.log(total)
            turn_ref[:COLS, :span] = jnp.where(place == TOTAL, log_total, joined - log_total)
            emission_ref[slot * span : (slot + 1) * span] = jnp.transpose(turn_ref[...], (1, 0))[
                :span
            ]

        lane = lax.broadcasted_iota(jnp.int32, (utterances, LANES), 1)
        is_label = lane < label_max
        is_blank = lane <= label_max
        names = jnp.where(is_label, notes_ref[...], 0)
        earlier = pltpu.roll(names, 1, 1)
        skip = is_label & (lane >= 1) & (names != 0) & (names != earlier)
        later = pltpu.roll(names, LANES - 1, 1)
        skip_next = (lane < label_max - 1) & (later != 0) & (later != names)
        frames = notes_ref[:, label_max : label_max + 1]
        counts = notes_ref[:, label_max + 1 : label_max + 2]
        ends_blank = jnp.where(lane == counts, 0.0, LOG_ZERO)
        ends_label = jnp.where(lane == counts - 1, 0.0, LOG_ZERO)

        def spread(step, carry):
            row = emission_ref[pl.ds(step, utterances, stride=frame_count), :]
            blank = jnp.sum(jnp.where(lane == label_max, row, 0.0), axis=1, keepdims=True)
            emit_blank[step] = jnp.where(is_blank, blank, LOG_ZERO)
            emit_label[step] = jnp.where(is_label, row, LOG_ZERO)
            return carry

        lax.fori_loop(0, frame_count, spread, 0, unroll=16)

        def advance(step, carry):
            fwd_blank, fwd_label, bwd_blank, bwd_label = carry
            moved = jnp.where(lane == 0, LOG_ZERO, pltpu.roll(fwd_label, 1, 1))
            new_blank = log_add(fwd_blank, moved) + emit_blank[step]
            new_label = (
                log_add3(fwd_label, fwd_blank, jnp.where(skip, moved, LOG_ZERO))
                + emit_label[step]
            )
            alive = step < frames
            fwd_blank = jnp.where(alive, new_blank, fwd_blank)
            fwd_label = jnp.where(alive, new_label, fwd_label)
            blank_fwd[step] = fwd_blank
            label_fwd[step] = fwd_label

            back = frame_count - 1 - step
            out_blank = bwd_blank + emit_blank[back + 1]
            out_label = bwd_label + emit_label[back + 1]
            next_blank = pltpu.roll(out_blank, LANES - 1, 1)
            next_label = jnp.where(skip_next, pltpu.roll(out_label, LANES - 1, 1), LOG_ZERO)
            ended = back >= frames - 1
            bwd_blank = jnp.where(ended, ends_blank, log_add(out_blank, out_label))
            bwd_label = jnp.where(
                ended, ends_label, log_add3(out_label, next_blank, next_label)
            )
            blank_bwd[back] = bwd_blank
            label_bwd[back] = bwd_label
            return (fwd_blank, fwd_label, bwd_blank, bwd_label)

        first_blank = jnp.where(lane == 0, emit_blank[0], LOG_ZERO)
        first_label = jnp.where(lane == 0, emit_label[0], LOG_ZERO)
        blank_fwd[0] = first_blank
        label_fwd[0] = first_label
        blank_bwd[frame_count - 1] = ends_blank
        label_bwd[frame_count - 1] = ends_label
        fwd_blank, fwd_label, _, _ = lax.fori_loop(
            1, frame_count, advance, (first_blank, first_label, ends_blank, ends_label), unroll=4
        )
        end_state = jnp.sum(jnp.where(lane == counts, fwd_blank, 0.0), axis=1, keepdims=True)
        near_state = jnp.sum(jnp.where(lane == counts - 1, fwd_label, 0.0), axis=1, keepdims=True)
        log_like = log_add(end_state, near_state)
        loss_ref[...] = -log_like[:kept]

        def occupy(step, carry):
            blank = jnp.exp(blank_fwd[step] + blank_bwd[step] - log_like)
            label = jnp.exp(label_fwd[step] + label_bwd[step] - log_like)
            blank = jnp.sum(jnp.where(is_blank, blank, 0.0), axis=1, keepdims=True)
            label = jnp.where(is_label, label, 0.0)
            whole = blank + jnp.sum(label, axis=1, keepdims=True)
            filled = jnp.where(lane == label_max, blank, label)
            filled = jnp.where(lane == WHOLE, whole, filled)
            filled = jnp.where(step < frames, -filled, 0.0)
            row = emission_ref[pl.ds(step, utterances, stride=frame_count), :]
            occupancy_ref[pl.ds(step, utterances, stride=frame_count), :] = jnp.where(
                lane == TOTAL, row, filled
            )
            return carry

        lax.fori_loop(0, frame_count, occupy, 0, unroll=16)
        turned = jnp.transpose(occupancy_ref[...], (1, 0))[:COLS]
        out_ref[...] = turned
        row_place = lax.broadcasted_iota(jnp.int32, (COLS, row_count), 0)
        owner = lax.broadcasted_iota(jnp.int32, (COLS, row_count), 1) // frame_count
        source = jnp.where(row_place < WHOLE, turned, 0.0)
        for utterance in range(utterances):
            part = jnp.where(owner == utterance, source, 0.0)
            high = part.astype(jnp.bfloat16)
            high_ref[utterance * COLS : (utterance + 1) * COLS] = high
            low_ref[utterance * COLS : (utterance + 1) * COLS] = (
                part - high.astype(jnp.float32)
            ).astype(jnp.bfloat16)

    held = pltpu.VMEM((frame_count, utterances, LANES), jnp.float32)
    table = pltpu.VMEM((row_count, LANES), jnp.float32)
    return call(
        kernel,
        (
            jax.ShapeDtypeStruct((COLS, row_count), jnp.float32),
            bf16_rows(entries, row_count),
            bf16_rows(entries, row_count),
            jax.ShapeDtypeStruct((kept, 1), jnp.float32),
        ),
        1 << 26,
        in_specs=[smem_spec()] + [vmem_spec()] * (1 + sources),
        out_specs=tuple(vmem_spec() for _ in range(4)),
        scratch_shapes=[pltpu.VMEM((LANES, tall), jnp.float32), table]
        + [held] * 6
        + [table],
    )(slots, notes, *stats)


def head_gradient(logits, rows, occupancy, high, low, places, order, outputs, each):
    count = len(logits)
    row_count, width = rows[0].shape
    entries = places.shape[1]
    blocks = outputs * each

    def kernel(order_ref, *refs):
        logits_refs, rows_refs = refs[:count], refs[count : 2 * count]
        occupancy_ref, high_ref, low_ref, places_ref = refs[2 * count : 2 * count + 4]
        out_refs = refs[2 * count + 4 :]
        for block in range(blocks):
            start = pl.multiple_of(order_ref[block] * BLOCK_ROWS, BLOCK_ROWS)
            entry = start + lax.broadcasted_iota(jnp.int32, (BLOCK_ROWS, entries), 0)
            select = as_mask(entry == places_ref[...])
            total = None
            for g in range(count):
                lanes = slice(g * row_count, (g + 1) * row_count)
                scattered = lax.dot_general(
                    select, high_ref[:, lanes], NN, preferred_element_type=jnp.float32
                ) + lax.dot_general(
                    select, low_ref[:, lanes], NN, preferred_element_type=jnp.float32
                )
                whole = occupancy_ref[WHOLE : WHOLE + 1, lanes]
                log_total = occupancy_ref[TOTAL : TOTAL + 1, lanes]
                values = logits_refs[g][pl.ds(start, BLOCK_ROWS), :]
                grad = (scattered - jnp.exp(values - log_total) * whole).astype(jnp.bfloat16)
                part = lax.dot_general(
                    grad, rows_refs[g][...], NN, preferred_element_type=jnp.float32
                )
                total = part if total is None else total + part
            out_refs[block // each][
                block % each * BLOCK_ROWS : (block % each + 1) * BLOCK_ROWS
            ] = total.astype(jnp.bfloat16)

    return call(
        kernel,
        tuple(bf16_rows(each * BLOCK_ROWS, width) for _ in range(outputs)),
        2 * blocks * BLOCK_ROWS * count * row_count * (width + 2 * entries),
        in_specs=[smem_spec()] + [vmem_spec()] * (2 * count + 4),
        out_specs=tuple(vmem_spec() for _ in range(outputs)),
    )(order, *logits, *rows, occupancy, high, low, places)


def assemble(pieces, offsets, height):
    count = len(pieces)
    part, width = pieces[0].shape
    short = height % part

    def kernel(offsets_ref, *refs):
        out_ref, sems = refs[count], refs[count + 1]

        def each(act):
            for index in range(count):
                offset = pl.multiple_of(offsets_ref[index], part)

                @pl.when(offset + part <= height)
                def _():
                    act(
                        pltpu.make_async_copy(
                            refs[index], out_ref.at[pl.ds(offset, part)], sems.at[index]
                        )
                    )

                if short:

                    @pl.when(offset + part > height)
                    def _():
                        act(
                            pltpu.make_async_copy(
                                refs[index].at[pl.ds(0, short)],
                                out_ref.at[pl.ds(height - short, short)],
                                sems.at[index],
                            )
                        )

        each(lambda copy: copy.start())
        each(lambda copy: copy.wait())

    return call(
        kernel,
        bf16_rows(height, width),
        0,
        in_specs=[smem_spec()] + [pl.BlockSpec(memory_space=pl.ANY)] * count,
        out_specs=pl.BlockSpec(memory_space=pl.ANY),
        scratch_shapes=[pltpu.SemaphoreType.DMA((count,))],
    )(offsets, *pieces)


def swap(value, axis):
    return lax.ppermute(value, axis, [(0, 1), (1, 0)])


def rotate(value, axis, by):
    count = lax.axis_size(axis)
    return lax.ppermute(value, axis, [(i, (i + by) % count) for i in range(count)])


def after(value, *others):
    return lax.optimization_barrier((value,) + others)[0]


def line_near(value):
    left = lax.ppermute(value, "expert", [(1, 0), (2, 1), (3, 2)])
    right = lax.ppermute(value, "expert", [(0, 1), (1, 2), (2, 3)])
    return left, right


def line_far(left, right):
    return (
        lax.ppermute(left, "expert", [(1, 0), (2, 1)]),
        lax.ppermute(right, "expert", [(1, 2), (2, 3)]),
    )


def line_end(left_far, right_far):
    return (
        lax.ppermute(left_far, "expert", [(1, 0)]),
        lax.ppermute(right_far, "expert", [(2, 3)]),
    )


LINE_ORDER = np.array([[0, 1, 2, 3], [1, 2, 3, 0], [2, 1, 0, 3], [3, 2, 1, 0]])


def slot_orders(count):
    return LINE_ORDER if count == 4 else np.tile(np.arange(count), (count, 1))


def slot_tables(count):
    orders = slot_orders(count)
    tables = np.zeros((count, count, count), np.int32)
    for member in range(count):
        for k in range(count):
            source = (member + k) % count
            for slot in range(count):
                tables[member, k, slot] = list(orders[source]).index(orders[member][slot])
    return tables.reshape(count, count * count)


def wide(ref, start, size):
    return ref[pl.ds(start, size), :].astype(jnp.float32)


def sum_sent(own, came, places):
    height, width = own.shape
    part = height // 4

    def kernel(places_ref, own_ref, came_ref, *out_refs):
        section, outer = places_ref[0], places_ref[1]
        starts = (
            (1 - outer) * part,
            outer * part,
            (2 + 1 - section) * part,
            (2 + section) * part,
        )
        for start, out_ref in zip(starts, out_refs):
            start = pl.multiple_of(start, part)
            out_ref[...] = (wide(own_ref, start, part) + wide(came_ref, start, part)).astype(
                jnp.bfloat16
            )

    return call(
        kernel,
        tuple(bf16_rows(part, width) for _ in range(4)),
        1 << 20,
        in_specs=[smem_spec()] + [vmem_spec()] * 2,
        out_specs=tuple(vmem_spec() for _ in range(4)),
    )(places, own, came)


def sum_kept(own, came, arrived, places, keep):
    height, width = own.shape
    part = height // 4
    count = len(arrived) // 2

    def kernel(places_ref, own_ref, came_ref, *refs):
        section, outer = places_ref[0], places_ref[1]
        if not keep:
            section, outer = 1 - section, 1 - outer
        for side, start in enumerate((outer * part, (2 + section) * part)):
            start = pl.multiple_of(start, part)
            total = wide(own_ref, start, part) + wide(came_ref, start, part)
            for ref in refs[side * count : (side + 1) * count]:
                total = total + ref[...].astype(jnp.float32)
            refs[2 * count + side][...] = total.astype(jnp.bfloat16)

    return call(
        kernel,
        (bf16_rows(part, width), bf16_rows(part, width)),
        1 << 20,
        in_specs=[smem_spec()] + [vmem_spec()] * (2 + 2 * count),
        out_specs=(vmem_spec(), vmem_spec()),
    )(places, own, came, *arrived)


def per_device(
    frames,
    norm_gain,
    router,
    w_in,
    w_out,
    routing,
    head_gain,
    head_weight,
    frame_lengths,
    labels,
    label_lengths,
):
    sections = lax.axis_size("section")
    section_id = lax.axis_index("section")
    group_size = lax.axis_size("expert")
    member = lax.axis_index("expert")
    outer_size = lax.axis_size("dpo")
    inner_size = lax.axis_size("dpi")
    core = lax.axis_index("dpi")
    micro, utt_dev, frame_count, width = frames.shape
    label_max = labels.shape[2]
    experts = w_in.shape[1] * group_size
    hidden = w_in.shape[3]
    pair_count = micro * utt_dev
    per_section = pair_count // sections
    first_pair = section_id * per_section
    share = (utt_dev * frame_count * 9 + 8 * experts - 1) // (8 * experts)
    capacity = round_up(share * -(-per_section // utt_dev), 8)
    span = per_section * frame_count
    member_ref = member.astype(jnp.int32).reshape(1)

    def mine_of(value):
        return lax.dynamic_slice_in_dim(value, first_pair, per_section, 0)

    def exchange(blocks, sign):
        return [blocks[0]] + [
            rotate(blocks[k], "expert", sign * k) for k in range(1, group_size)
        ]

    def lanes_of(ids):
        return jnp.pad(mine_of(ids), ((0, 0), (0, LANES - frame_count)), constant_values=-1)

    current = lax.dynamic_slice_in_dim(
        frames.reshape(pair_count * frame_count, width), first_pair * frame_count, span, 0
    )
    own_ids = routing.reshape(pair_count, frame_count)
    paired = sections == 2 and inner_size == 2
    if paired:
        other_ids = swap(own_ids, "section")
        all_ids = [
            jnp.where(section_id == layer, own_ids, other_ids) for layer in range(sections)
        ]
    else:
        all_ids = lax.all_gather(own_ids, "section")
    layer_ids = [lanes_of(all_ids[layer]) for layer in range(sections)]
    own_table = jnp.concatenate(
        [
            norm_gain,
            jnp.zeros((7, width), jnp.float32),
            jnp.transpose(router[0]).astype(jnp.float32),
            jnp.zeros((round_up(experts, 8) - experts, width), jnp.float32),
        ],
        axis=0,
    )
    own = (w_in[0, 0], w_out[0, 0])
    layers = []
    if paired:
        other_table = swap(own_table, "section")
        half = hidden // 2
        sent_in = lax.dynamic_slice(own[0], (0, core * half), (width, half))
        sent_out = lax.dynamic_slice(own[1], (core * half, 0), (half, width))
        sent_in, sent_out = lax.optimization_barrier((sent_in, sent_out, own_table))[:2]
        came_in = swap(sent_in, "section")
        came_out = swap(sent_out, "section")
        other = [(came_in, came_out), (swap(came_in, "dpi"), swap(came_out, "dpi"))]
        for layer in range(sections):
            mine = (section_id == layer).astype(jnp.int32).reshape(1)
            layers.append(((own_table, other_table), own, other, mine))
    else:
        all_tables = lax.all_gather(own_table, "section")
        all_in = lax.all_gather(own[0], "section")
        all_out = lax.all_gather(own[1], "section")
        for layer in range(sections):
            chosen = (all_in[layer], all_out[layer])
            layers.append(((all_tables[layer],), chosen, [], jnp.ones((1,), jnp.int32)))

    outgoing = dispatch(current, layer_ids[0], member_ref, experts, capacity, frame_count)
    received = exchange(outgoing, 1)

    labels, frame_lengths, label_lengths = lax.optimization_barrier(
        (labels, frame_lengths, label_lengths, outgoing[0])
    )[:3]
    notes = jnp.concatenate(
        [
            mine_of(labels.reshape(pair_count, label_max)),
            mine_of(frame_lengths.reshape(pair_count, 1)),
            mine_of(label_lengths.reshape(pair_count, 1)),
        ],
        axis=1,
    )
    shard = head_weight.shape[1]
    weight_rows = jnp.transpose(head_weight)
    line = group_size == 4
    tables = jnp.asarray(slot_tables(group_size))
    slots = lax.dynamic_index_in_dim(tables, member, 0, keepdims=False)
    outer = lax.axis_index("dpo")
    blocks = -(-shard // BLOCK_ROWS)
    tree = paired and outer_size == 2 and blocks == 8

    def pair_of(side, first, second):
        return [side * 4 + first, side * 4 + 2 + second]

    def offset_of(side, s, y):
        base = side * 4 * BLOCK_ROWS
        part = BLOCK_ROWS // 2
        return [
            base + s * BLOCK_ROWS + y * part,
            base + 2 * BLOCK_ROWS + y * BLOCK_ROWS + s * part,
        ]

    def whole_numbers(values):
        return jnp.stack([jnp.asarray(value, jnp.int32) for value in values])

    here, there = (section_id, outer), (1 - section_id, 1 - outer)
    sibling_sent_order = whole_numbers(pair_of(1 - core, *there))
    own_sent_order = whole_numbers(pair_of(core, *there))
    kept_order = whole_numbers(pair_of(1 - core, *here) + pair_of(core, *here))
    chip_place = whole_numbers(here)
    offsets = []
    for side in (core, 1 - core):
        for s in (section_id, 1 - section_id):
            for y in (outer, 1 - outer):
                offsets += offset_of(side, s, y)
    offsets = whole_numbers(offsets)
    early = (
        notes,
        slots,
        head_gain.reshape(1, width),
        layer_ids[1:],
        sibling_sent_order,
        own_sent_order,
        kept_order,
        chip_place,
        offsets,
    )
    early, received = lax.optimization_barrier((early, received))
    notes, slots, head_row, later_ids, sibling_sent_order, own_sent_order = early[:6]
    kept_order, chip_place, offsets = early[6:]
    layer_ids = [layer_ids[0]] + list(later_ids)

    for layer in range(sections):
        choices, weights, others, pick_own = layers[layer]
        done = run_expert(received, choices, weights, others, pick_own)
        returned = exchange(done, -1)
        if layer == 0:
            notes = after(notes, done[0])
            if line:
                found = [notes] + [rotate(notes, "expert", -k) for k in range(1, group_size)]
            else:
                gathered = lax.all_gather(notes, "expert")
                found = [gathered[k] for k in range(group_size)]
        if layer < sections - 1:
            current, outgoing = combine_and_dispatch(
                current,
                returned,
                layer_ids[layer],
                choices,
                pick_own,
                layer_ids[layer + 1],
                member_ref,
                experts,
                capacity,
                frame_count,
            )
            received = exchange(outgoing, 1)
            if layer == 0:
                found[0] = after(found[0], current)
                label_weight, places, names = label_rows(
                    weight_rows, found, member_ref, label_max, line
                )
                received, label_weight = lax.optimization_barrier((received, label_weight))
        else:
            normed = combine_and_norm(
                current,
                returned,
                layer_ids[layer],
                choices,
                pick_own,
                head_row,
                member_ref,
                experts,
                capacity,
                frame_count,
            )

    def logits_of(fill, first, count, pieces, earlier):
        return head_logits(
            fill, first, count, pieces, member_ref, weight_rows, label_weight, frame_count, earlier
        )

    if line:
        left, right = line_near(normed)
        far = line_far(left, right)
        heads = [logits_of(fill_near, 0, 2, [normed, left, right], None)]
        far, heads[0] = lax.optimization_barrier((far, heads[0]))
        end = line_end(*far)
        heads.append(logits_of(fill_far, 2, 2, [*far, *end, left, right], heads[0][2]))
        stats = heads[1][2]
        found = [stats] + [rotate(stats, "expert", -k) for k in range(1, group_size)]
    else:
        gathered = lax.all_gather(normed, "expert")
        pieces = [gathered[k] for k in range(group_size)]
        heads = [logits_of(fill_all, 0, group_size, pieces, None)]
        gathered = lax.all_gather(heads[0][2], "expert")
        found = [
            lax.dynamic_index_in_dim(gathered, (member + k) % group_size, 0, keepdims=False)
            for k in range(group_size)
        ]
    kept_losses = per_section if line else group_size * per_section
    occupancy, high, low, losses = ctc_pass(
        found, slots, names, frame_count, label_max, kept_losses
    )
    if not line:
        losses = lax.dynamic_slice(losses, (member * per_section, 0), (per_section, 1))

    def gradient(order, outputs, each):
        return head_gradient(
            [head[0] for head in heads],
            [head[1] for head in heads],
            occupancy,
            high,
            low,
            places,
            order,
            outputs,
            each,
        )

    if tree:
        came_sent = swap(gradient(sibling_sent_order, 1, 2)[0], "dpi")
        own_sent = gradient(own_sent_order, 1, 2)[0]
        a_far, a_near, b_far, b_near = sum_sent(own_sent, came_sent, chip_place)
        a_far, b_far = swap(a_far, "section"), swap(b_far, "dpo")
        a_near, b_near = swap(a_near, "section"), swap(b_near, "dpo")
        sibling_kept, own_kept = gradient(after(kept_order, own_sent), 2, 2)
        came_kept = swap(sibling_kept, "dpi")
        a_on, b_on = sum_kept(own_kept, came_kept, [a_far, b_far], chip_place, False)
        a_in, b_in = swap(a_on, "dpo"), swap(b_on, "section")
        a, b = sum_kept(own_kept, came_kept, [a_near, a_in, b_near, b_in], chip_place, True)
        a_y, b_x = swap(a, "dpo"), swap(b, "section")
        b_y, a_x = swap(b, "dpo"), swap(a, "section")
        a_xy, b_xy = swap(a_y, "section"), swap(b_x, "dpo")
        mine = [a, b, a_y, b_y, a_x, b_x, a_xy, b_xy]
        whole = assemble(mine + [swap(value, "dpi") for value in mine], offsets, shard)
    else:
        partial = gradient(jnp.arange(blocks, dtype=jnp.int32), 1, blocks)[0][:shard]
        whole = lax.psum(partial.astype(jnp.float32), ("section", "dpo", "dpi")).astype(
            jnp.bfloat16
        )
    return (losses, jnp.transpose(whole))


def solution(mesh):
    sections, group_size, spread = (mesh.shape[name] for name in ("section", "expert", "dp"))
    inner = 2 if spread % 2 == 0 else 1
    split = Mesh(
        mesh.devices.reshape(sections, group_size, spread // inner, inner),
        ("section", "expert", "dpo", "dpi"),
    )
    block = ("expert", "dpo", "dpi")
    placed = (
        P(None, block, None, None),
        P("section", None),
        P("section", None, None),
        P("section", "expert", None, None),
        P("section", "expert", None, None),
        P("section", None, block, None, None),
        P(),
        P(None, "expert"),
        P(None, block),
        P(None, block, None),
        P(None, block),
    )
    return jax.shard_map(
        per_device,
        mesh=split,
        in_specs=placed,
        out_specs=(P("section", block), P(None, "expert")),
        check_vma=False,
    )
```

```python
import jax
import jax.numpy as jnp
import numpy as np
from jax import lax
from jax.experimental import pallas as pl
from jax.experimental.pallas import tpu as pltpu
from jax.sharding import Mesh, PartitionSpec as P

EPSILON = 1e-06
LOG_ZERO = -1e30
VMEM_LIMIT = 24 * 1024 * 1024
LANES = 128
COLS = 16
PEAK, TOTAL, WHOLE = COLS - 3, COLS - 2, COLS - 3
BLOCK_ROWS = 256
NT = (((1,), (1,)), ((), ()))
NN = (((1,), (0,)), ((), ()))


def round_up(value, unit):
    return -(-value // unit) * unit


def vmem_spec():
    return pl.BlockSpec(memory_space=pltpu.VMEM)


def smem_spec():
    return pl.BlockSpec(memory_space=pltpu.SMEM)


def call(kernel, out_shape, flops=0, **options):
    return pl.pallas_call(
        kernel,
        out_shape=out_shape,
        compiler_params=pltpu.CompilerParams(vmem_limit_bytes=VMEM_LIMIT),
        cost_estimate=pl.CostEstimate(flops=flops, bytes_accessed=0, transcendentals=0),
        **options,
    )


def bf16_rows(count, width):
    return jax.ShapeDtypeStruct((count, width), jnp.bfloat16)


def as_mask(values):
    return values.astype(jnp.float32).astype(jnp.bfloat16)


def split_rows(values, out_refs, spare=None, note=None):
    size, width = out_refs[0].shape
    for turn, out_ref in enumerate(out_refs):
        part = values[turn * size : (turn + 1) * size]
        if note is not None:
            row = lax.broadcasted_iota(jnp.int32, (size, width), 0)
            part = jnp.where(row == spare, note, part)
        out_ref[...] = part.astype(jnp.bfloat16)


def join_rows(refs):
    return jnp.concatenate([ref[...].astype(jnp.float32) for ref in refs], axis=0)


def rms_scale(values, gain):
    values = values.astype(jnp.float32)
    scale = lax.rsqrt(jnp.mean(values * values, axis=-1, keepdims=True) + EPSILON)
    return (values * scale * gain).astype(jnp.bfloat16)


def expert_column(ids, frame_count):
    pairs = ids.shape[0]
    square = jnp.concatenate(
        [ids.astype(jnp.float32), jnp.full((LANES - pairs, LANES), -1.0, jnp.float32)], axis=0
    )
    turned = jnp.transpose(square, (1, 0)).astype(jnp.int32)
    return jnp.concatenate([turned[:frame_count, p : p + 1] for p in range(pairs)], axis=0)


def placement(column, member, experts, capacity):
    count = column.shape[0]
    shifted = column - member
    relative = jnp.where(shifted < 0, shifted + experts, shifted)
    lane = lax.broadcasted_iota(jnp.int32, (count, LANES), 1)
    one_hot = (lane == relative).astype(jnp.float32)
    before = lax.broadcasted_iota(jnp.int32, (count, count), 1) <= lax.broadcasted_iota(
        jnp.int32, (count, count), 0
    )
    rank = lax.dot_general(
        as_mask(before), one_hot.astype(jnp.bfloat16), NN, preferred_element_type=jnp.float32
    )
    start = (lane * capacity - 1).astype(jnp.float32)
    slots = jnp.sum(one_hot * (rank + start), axis=1, keepdims=True).astype(jnp.int32)
    places = lax.broadcasted_iota(jnp.int32, (count, experts * capacity), 1)
    return (places == slots).astype(jnp.float32)


def scatter_rows(rows, ids, member, experts, capacity, frame_count, out_refs):
    count = rows.shape[0]
    chosen = placement(expert_column(ids, frame_count), member, experts, capacity)
    tall = round_up(count, LANES)
    if tall > count:
        chosen = jnp.concatenate(
            [chosen, jnp.zeros((tall - count, chosen.shape[1]), jnp.float32)], axis=0
        )
    pick = jnp.transpose(chosen, (1, 0))[:, :count].astype(jnp.bfloat16)
    placed = lax.dot_general(pick, rows, NN, preferred_element_type=jnp.float32)
    split_rows(placed, out_refs)


def combine_rows(rows, returned, ids, table, member, experts, capacity, frame_count):
    column = expert_column(ids, frame_count)
    pick = placement(column, member, experts, capacity).astype(jnp.bfloat16)
    normed = rms_scale(rows, table[:1])
    router = jnp.concatenate(
        [table[8:], jnp.zeros((LANES + 8 - table.shape[0], rows.shape[1]), jnp.float32)], axis=0
    ).astype(jnp.bfloat16)
    logits = lax.dot_general(normed, router, NT, preferred_element_type=jnp.float32)
    lane = lax.broadcasted_iota(jnp.int32, logits.shape, 1)
    gate = jax.nn.sigmoid(jnp.sum(jnp.where(lane == column, logits, 0.0), axis=1, keepdims=True))
    stacked = join_rows(returned).astype(jnp.bfloat16)
    mixed = lax.dot_general(pick, stacked, NN, preferred_element_type=jnp.float32)
    return (rows.astype(jnp.float32) + gate * mixed).astype(jnp.bfloat16)


def dispatch(rows, ids, member, experts, capacity, frame_count):
    width = rows.shape[1]

    def kernel(member_ref, rows_ref, ids_ref, *out_refs):
        scatter_rows(
            rows_ref[...], ids_ref[...], member_ref[0], experts, capacity, frame_count, out_refs
        )

    return call(
        kernel,
        tuple(bf16_rows(capacity, width) for _ in range(experts)),
        1 << 27,
        in_specs=[smem_spec()] + [vmem_spec()] * 2,
        out_specs=tuple(vmem_spec() for _ in range(experts)),
    )(member, rows, ids)


def pick_table(pick_ref, tables):
    if len(tables) == 1:
        return tables[0][...]
    return jnp.where(pick_ref[0] == 1, tables[0][...], tables[1][...])


def run_expert(received, tables, own, other, pick_own, spare, note):
    count = len(received)
    capacity, width = received[0].shape
    others, choices = len(other), len(tables)
    noted = [] if note is None else [note]

    def kernel(pick_ref, in_ref, out_weight_ref, *refs):
        table_refs, refs = refs[:choices], refs[choices:]
        other_refs, refs = refs[: 2 * others], refs[2 * others :]
        received_refs, refs = refs[:count], refs[count:]
        out_refs = refs[len(noted) :]

        def work(pieces):
            gain = pick_table(pick_ref, table_refs)[:1]
            normed = rms_scale(join_rows(received_refs), gain)
            total = None
            for weight_in, weight_out in pieces:
                hidden = lax.dot_general(
                    normed, weight_in[...], NN, preferred_element_type=jnp.float32
                )
                active = (hidden / (1.0 + jnp.exp(-hidden))).astype(jnp.bfloat16)
                part = lax.dot_general(
                    active, weight_out[...], NN, preferred_element_type=jnp.float32
                )
                total = part if total is None else total + part
            split_rows(total, out_refs, spare, refs[0][...] if noted else None)

        if others == 0:
            work([(in_ref, out_weight_ref)])
            return

        @pl.when(pick_ref[0] == 1)
        def _():
            work([(in_ref, out_weight_ref)])

        @pl.when(pick_ref[0] != 1)
        def _():
            work([(other_refs[2 * i], other_refs[2 * i + 1]) for i in range(others)])

    flat = [weight for pair in other for weight in pair]
    return call(
        kernel,
        tuple(bf16_rows(capacity, width) for _ in range(count)),
        4 * count * capacity * width * own[0].shape[1],
        in_specs=[smem_spec()] + [vmem_spec()] * (2 + choices + 2 * others + count + len(noted)),
        out_specs=tuple(vmem_spec() for _ in range(count)),
    )(pick_own, *own, *tables, *flat, *received, *noted)


def combine_and_dispatch(
    rows, returned, ids, tables, pick_own, next_ids, member, experts, capacity, frame_count
):
    width = rows.shape[1]
    choices = len(tables)

    def kernel(member_ref, pick_ref, rows_ref, ids_ref, next_ref, *refs):
        table_refs, refs = refs[:choices], refs[choices:]
        returned_refs, x_ref, out_refs = refs[:experts], refs[experts], refs[experts + 1 :]
        mixed = combine_rows(
            rows_ref[...],
            returned_refs,
            ids_ref[...],
            pick_table(pick_ref, table_refs),
            member_ref[0],
            experts,
            capacity,
            frame_count,
        )
        x_ref[...] = mixed
        scatter_rows(
            mixed, next_ref[...], member_ref[0], experts, capacity, frame_count, out_refs
        )

    shapes = (bf16_rows(*rows.shape),) + tuple(
        bf16_rows(capacity, width) for _ in range(experts)
    )
    result = call(
        kernel,
        shapes,
        1 << 28,
        in_specs=[smem_spec()] * 2 + [vmem_spec()] * (3 + choices + experts),
        out_specs=tuple(vmem_spec() for _ in shapes),
    )(member, pick_own, rows, ids, next_ids, *tables, *returned)
    return result[0], result[1:]


def combine_and_norm(
    rows, returned, ids, tables, pick_own, head_gain, member, experts, capacity, frame_count
):
    choices = len(tables)

    def kernel(member_ref, pick_ref, rows_ref, ids_ref, head_ref, *refs):
        table_refs, refs = refs[:choices], refs[choices:]
        final = combine_rows(
            rows_ref[...],
            refs[:experts],
            ids_ref[...],
            pick_table(pick_ref, table_refs),
            member_ref[0],
            experts,
            capacity,
            frame_count,
        )
        refs[experts][...] = rms_scale(final, head_ref[...])

    return call(
        kernel,
        bf16_rows(*rows.shape),
        1 << 28,
        in_specs=[smem_spec()] * 2 + [vmem_spec()] * (3 + choices + experts),
        out_specs=vmem_spec(),
    )(member, pick_own, rows, ids, head_gain, *tables, *returned)


def half_weights(core, weight_in, weight_out):
    width, hidden = weight_in.shape
    half = hidden // 2

    def kernel(core_ref, in_ref, out_ref, half_in, half_out, sems):
        start = pl.multiple_of(core_ref[0] * half, half)
        copies = (
            pltpu.make_async_copy(in_ref.at[:, pl.ds(start, half)], half_in, sems.at[0]),
            pltpu.make_async_copy(out_ref.at[pl.ds(start, half)], half_out, sems.at[1]),
        )
        for copy in copies:
            copy.start()
        for copy in copies:
            copy.wait()

    return call(
        kernel,
        (bf16_rows(width, half), bf16_rows(half, width)),
        1 << 20,
        in_specs=[smem_spec()] + [pl.BlockSpec(memory_space=pl.ANY)] * 2,
        out_specs=(vmem_spec(), vmem_spec()),
        scratch_shapes=[pltpu.SemaphoreType.DMA((2,))],
    )(core, weight_in, weight_out)


def block_list(shard):
    return [(i, min(BLOCK_ROWS, shard - i)) for i in range(0, shard, BLOCK_ROWS)]


def label_rows(weight, notes, member, pairs, spare, label_max, line):
    shard, width = weight.shape
    sources = len(notes)
    utterances = sources * pairs
    entries = utterances * COLS

    def kernel(member_ref, weight_ref, *refs):
        note_refs = refs[:sources]
        out_ref, places_ref, names_ref, turned_ref = refs[sources:]
        place = member_ref[0]
        found = []
        for ref in note_refs:
            row = ref[...].astype(jnp.float32)[spare : spare + 1]
            found.append((row[:, :LANES] * LANES + row[:, LANES : 2 * LANES]).astype(jnp.int32))
        if line:
            low = place < 2
            found = [
                found[0],
                jnp.where(low, found[1], found[3]),
                found[2],
                jnp.where(low, found[3], found[1]),
            ]
        names_ref[...] = jnp.zeros(names_ref.shape, jnp.int32)
        for slot in range(sources):
            for pair in range(pairs):
                row = slot * pairs + pair
                names_ref[row : row + 1, :COLS] = found[slot][:, pair * COLS : (pair + 1) * COLS]
        lane = lax.broadcasted_iota(jnp.int32, (utterances, LANES), 1)
        named = jnp.where(lane < label_max, names_ref[...], jnp.where(lane == label_max, 0, -1))
        local = named - place * shard
        local = jnp.where((named >= 0) & (local >= 0) & (local < shard), local, -1)
        square = jnp.concatenate(
            [
                local.astype(jnp.float32),
                jnp.full((LANES - utterances, LANES), -1.0, jnp.float32),
            ],
            axis=0,
        )
        turned = jnp.transpose(square, (1, 0))
        for utterance in range(utterances):
            turned_ref[utterance * COLS : (utterance + 1) * COLS] = jnp.broadcast_to(
                turned[:COLS, utterance : utterance + 1], (COLS, LANES)
            )
        places = turned_ref[:, :1].astype(jnp.int32)
        places_ref[...] = jnp.transpose(turned_ref[...], (1, 0))[:1].astype(jnp.int32)
        total = jnp.zeros((entries, width), jnp.float32)
        for first, size in block_list(shard):
            entry = first + lax.broadcasted_iota(jnp.int32, (entries, size), 1)
            total = total + lax.dot_general(
                as_mask(entry == places),
                weight_ref[first : first + size],
                NN,
                preferred_element_type=jnp.float32,
            )
        out_ref[...] = total.astype(jnp.bfloat16)

    return call(
        kernel,
        (
            bf16_rows(entries, width),
            jax.ShapeDtypeStruct((1, entries), jnp.int32),
            jax.ShapeDtypeStruct((utterances, LANES), jnp.int32),
        ),
        2 * shard * entries * width,
        in_specs=[smem_spec()] + [vmem_spec()] * (1 + sources),
        out_specs=tuple(vmem_spec() for _ in range(3)),
        scratch_shapes=[pltpu.VMEM((entries, LANES), jnp.float32)],
    )(member, weight, *notes)


def head_logits(
    fill, first_slot, count, pieces, member, weight, label_weight, frame_count, earlier
):
    given = len(pieces)
    ahead = 0 if earlier is None else earlier.shape[0]
    span, width = pieces[0].shape
    row_count = count * span
    shard = weight.shape[0]
    height = round_up(shard, BLOCK_ROWS)
    entries = row_count // frame_count * COLS
    first_entry = first_slot * entries // count
    others = [] if earlier is None else [earlier]

    def kernel(member_ref, weight_ref, label_ref, *refs):
        piece_refs = refs[:given]
        logits_ref, rows_ref, stats_ref = refs[given + len(others) :]

        def put(slot, piece_ref):
            rows_ref[slot * span : (slot + 1) * span] = piece_ref[...]

        def put_if(condition, slot, piece_ref):
            @pl.when(condition)
            def _():
                put(slot, piece_ref)

        fill(member_ref[0], piece_refs, put, put_if)
        peak = jnp.full((1, row_count), LOG_ZERO, jnp.float32)
        total = jnp.zeros((1, row_count), jnp.float32)
        for first, size in block_list(shard):
            logits = lax.dot_general(
                weight_ref[first : first + size],
                rows_ref[...],
                NT,
                preferred_element_type=jnp.float32,
            )
            logits_ref[first : first + size] = logits
            before = peak
            peak = jnp.maximum(before, jnp.max(logits, axis=0, keepdims=True))
            total = total * jnp.exp(before - peak) + jnp.sum(
                jnp.exp(logits - peak), axis=0, keepdims=True
            )
        if height > shard:
            logits_ref[shard:] = jnp.full((height - shard, row_count), LOG_ZERO, jnp.float32)
        crossed = lax.dot_general(
            label_ref[first_entry : first_entry + entries],
            rows_ref[...],
            NT,
            preferred_element_type=jnp.float32,
        )
        owner = lax.broadcasted_iota(jnp.int32, (COLS, row_count), 1) // frame_count
        picked = jnp.zeros((COLS, row_count), jnp.float32)
        for utterance in range(entries // COLS):
            part = crossed[utterance * COLS : (utterance + 1) * COLS]
            picked = picked + jnp.where(owner == utterance, part, 0.0)
        place = lax.broadcasted_iota(jnp.int32, (COLS, row_count), 0)
        stats = jnp.where(place == PEAK, peak, picked)
        stats = jnp.where(place == TOTAL, total, stats)
        for slot in range(ahead):
            stats_ref[slot] = refs[given][slot]
        for slot in range(count):
            stats_ref[ahead + slot] = stats[:, slot * span : (slot + 1) * span]

    return call(
        kernel,
        (
            jax.ShapeDtypeStruct((height, row_count), jnp.float32),
            bf16_rows(row_count, width),
            jax.ShapeDtypeStruct((ahead + count, COLS, span), jnp.float32),
        ),
        2 * height * row_count * width,
        in_specs=[smem_spec()] + [vmem_spec()] * (2 + given + len(others)),
        out_specs=tuple(vmem_spec() for _ in range(3)),
    )(member, weight, label_weight, *pieces, *others)


def fill_near(place, piece_refs, put, put_if):
    value_ref, left_ref, right_ref = piece_refs
    put(0, value_ref)
    put_if(place < 2, 1, left_ref)
    put_if(place >= 2, 1, right_ref)


def fill_far(place, piece_refs, put, put_if):
    left_far, right_far, left_end, right_end, left_ref, right_ref = piece_refs
    put_if(place < 2, 0, left_far)
    put_if(place >= 2, 0, right_far)
    put_if(place == 0, 1, left_end)
    put_if(place == 3, 1, right_end)
    put_if(place == 1, 1, right_ref)
    put_if(place == 2, 1, left_ref)


def fill_all(place, piece_refs, put, put_if):
    for slot, piece_ref in enumerate(piece_refs):
        put(slot, piece_ref)


def log_add(first, second):
    peak = jnp.maximum(first, second)
    return peak + jnp.log(jnp.exp(first - peak) + jnp.exp(second - peak))


def log_add3(first, second, third):
    peak = jnp.maximum(jnp.maximum(first, second), third)
    return peak + jnp.log(
        jnp.exp(first - peak) + jnp.exp(second - peak) + jnp.exp(third - peak)
    )


def ctc_pass(stats, slots, notes, frame_count, label_max, kept):
    sources = len(stats)
    count, _, span = stats[0].shape
    row_count = count * span
    utterances = notes.shape[0]
    entries = utterances * COLS
    tall = round_up(span, LANES)

    def kernel(slots_ref, notes_ref, *refs):
        (
            out_ref,
            high_ref,
            low_ref,
            loss_ref,
            turn_ref,
            emission_ref,
            emit_blank,
            emit_label,
            blank_fwd,
            label_fwd,
            blank_bwd,
            label_bwd,
            occupancy_ref,
        ) = refs[sources:]
        place = lax.broadcasted_iota(jnp.int32, (COLS, span), 0)
        turn_ref[...] = jnp.zeros(turn_ref.shape, jnp.float32)
        for slot in range(count):
            found = [refs[k][slots_ref[k * count + slot]] for k in range(sources)]
            joined = found[0]
            peak = found[0][PEAK : PEAK + 1]
            for other in found[1:]:
                joined = joined + other
                peak = jnp.maximum(peak, other[PEAK : PEAK + 1])
            total = jnp.zeros((1, span), jnp.float32)
            for other in found:
                total = total + other[TOTAL : TOTAL + 1] * jnp.exp(other[PEAK : PEAK + 1] - peak)
            log_total = peak + jnp.log(total)
            turn_ref[:COLS, :span] = jnp.where(place == TOTAL, log_total, joined - log_total)
            emission_ref[slot * span : (slot + 1) * span] = jnp.transpose(turn_ref[...], (1, 0))[
                :span
            ]

        lane = lax.broadcasted_iota(jnp.int32, (utterances, LANES), 1)
        is_label = lane < label_max
        is_blank = lane <= label_max
        names = jnp.where(is_label, notes_ref[...], 0)
        earlier = pltpu.roll(names, 1, 1)
        skip = is_label & (lane >= 1) & (names != 0) & (names != earlier)
        later = pltpu.roll(names, LANES - 1, 1)
        skip_next = (lane < label_max - 1) & (later != 0) & (later != names)
        frames = notes_ref[:, label_max : label_max + 1]
        counts = notes_ref[:, label_max + 1 : label_max + 2]
        ends_blank = jnp.where(lane == counts, 0.0, LOG_ZERO)
        ends_label = jnp.where(lane == counts - 1, 0.0, LOG_ZERO)

        def spread(step, carry):
            row = emission_ref[pl.ds(step, utterances, stride=frame_count), :]
            blank = jnp.sum(jnp.where(lane == label_max, row, 0.0), axis=1, keepdims=True)
            emit_blank[step] = jnp.where(is_blank, blank, LOG_ZERO)
            emit_label[step] = jnp.where(is_label, row, LOG_ZERO)
            return carry

        lax.fori_loop(0, frame_count, spread, 0, unroll=16)

        def advance(step, carry):
            fwd_blank, fwd_label, bwd_blank, bwd_label = carry
            moved = jnp.where(lane == 0, LOG_ZERO, pltpu.roll(fwd_label, 1, 1))
            new_blank = log_add(fwd_blank, moved) + emit_blank[step]
            new_label = (
                log_add3(fwd_label, fwd_blank, jnp.where(skip, moved, LOG_ZERO))
                + emit_label[step]
            )
            alive = step < frames
            fwd_blank = jnp.where(alive, new_blank, fwd_blank)
            fwd_label = jnp.where(alive, new_label, fwd_label)
            blank_fwd[step] = fwd_blank
            label_fwd[step] = fwd_label

            back = frame_count - 1 - step
            out_blank = bwd_blank + emit_blank[back + 1]
            out_label = bwd_label + emit_label[back + 1]
            next_blank = pltpu.roll(out_blank, LANES - 1, 1)
            next_label = jnp.where(skip_next, pltpu.roll(out_label, LANES - 1, 1), LOG_ZERO)
            ended = back >= frames - 1
            bwd_blank = jnp.where(ended, ends_blank, log_add(out_blank, out_label))
            bwd_label = jnp.where(
                ended, ends_label, log_add3(out_label, next_blank, next_label)
            )
            blank_bwd[back] = bwd_blank
            label_bwd[back] = bwd_label
            return (fwd_blank, fwd_label, bwd_blank, bwd_label)

        first_blank = jnp.where(lane == 0, emit_blank[0], LOG_ZERO)
        first_label = jnp.where(lane == 0, emit_label[0], LOG_ZERO)
        blank_fwd[0] = first_blank
        label_fwd[0] = first_label
        blank_bwd[frame_count - 1] = ends_blank
        label_bwd[frame_count - 1] = ends_label
        fwd_blank, fwd_label, _, _ = lax.fori_loop(
            1, frame_count, advance, (first_blank, first_label, ends_blank, ends_label), unroll=4
        )
        end_state = jnp.sum(jnp.where(lane == counts, fwd_blank, 0.0), axis=1, keepdims=True)
        near_state = jnp.sum(jnp.where(lane == counts - 1, fwd_label, 0.0), axis=1, keepdims=True)
        log_like = log_add(end_state, near_state)
        loss_ref[...] = -log_like[:kept]

        def occupy(step, carry):
            blank = jnp.exp(blank_fwd[step] + blank_bwd[step] - log_like)
            label = jnp.exp(label_fwd[step] + label_bwd[step] - log_like)
            blank = jnp.sum(jnp.where(is_blank, blank, 0.0), axis=1, keepdims=True)
            label = jnp.where(is_label, label, 0.0)
            whole = blank + jnp.sum(label, axis=1, keepdims=True)
            filled = jnp.where(lane == label_max, blank, label)
            filled = jnp.where(lane == WHOLE, whole, filled)
            filled = jnp.where(step < frames, -filled, 0.0)
            row = emission_ref[pl.ds(step, utterances, stride=frame_count), :]
            occupancy_ref[pl.ds(step, utterances, stride=frame_count), :] = jnp.where(
                lane == TOTAL, row, filled
            )
            return carry

        lax.fori_loop(0, frame_count, occupy, 0, unroll=16)
        turned = jnp.transpose(occupancy_ref[...], (1, 0))[:COLS]
        out_ref[...] = turned
        row_place = lax.broadcasted_iota(jnp.int32, (COLS, row_count), 0)
        owner = lax.broadcasted_iota(jnp.int32, (COLS, row_count), 1) // frame_count
        source = jnp.where(row_place < WHOLE, turned, 0.0)
        for utterance in range(utterances):
            part = jnp.where(owner == utterance, source, 0.0)
            high = part.astype(jnp.bfloat16)
            high_ref[utterance * COLS : (utterance + 1) * COLS] = high
            low_ref[utterance * COLS : (utterance + 1) * COLS] = (
                part - high.astype(jnp.float32)
            ).astype(jnp.bfloat16)

    held = pltpu.VMEM((frame_count, utterances, LANES), jnp.float32)
    table = pltpu.VMEM((row_count, LANES), jnp.float32)
    return call(
        kernel,
        (
            jax.ShapeDtypeStruct((COLS, row_count), jnp.float32),
            bf16_rows(entries, row_count),
            bf16_rows(entries, row_count),
            jax.ShapeDtypeStruct((kept, 1), jnp.float32),
        ),
        1 << 26,
        in_specs=[smem_spec()] + [vmem_spec()] * (1 + sources),
        out_specs=tuple(vmem_spec() for _ in range(4)),
        scratch_shapes=[pltpu.VMEM((LANES, tall), jnp.float32), table]
        + [held] * 6
        + [table],
    )(slots, notes, *stats)


def head_gradient(logits, rows, occupancy, high, low, places, order, outputs, each):
    count = len(logits)
    row_count, width = rows[0].shape
    entries = places.shape[1]
    blocks = outputs * each

    def kernel(order_ref, *refs):
        logits_refs, rows_refs = refs[:count], refs[count : 2 * count]
        occupancy_ref, high_ref, low_ref, places_ref = refs[2 * count : 2 * count + 4]
        out_refs = refs[2 * count + 4 :]
        for block in range(blocks):
            start = pl.multiple_of(order_ref[block] * BLOCK_ROWS, BLOCK_ROWS)
            entry = start + lax.broadcasted_iota(jnp.int32, (BLOCK_ROWS, entries), 0)
            select = as_mask(entry == places_ref[...])
            total = None
            for g in range(count):
                lanes = slice(g * row_count, (g + 1) * row_count)
                scattered = lax.dot_general(
                    select, high_ref[:, lanes], NN, preferred_element_type=jnp.float32
                ) + lax.dot_general(
                    select, low_ref[:, lanes], NN, preferred_element_type=jnp.float32
                )
                whole = occupancy_ref[WHOLE : WHOLE + 1, lanes]
                log_total = occupancy_ref[TOTAL : TOTAL + 1, lanes]
                values = logits_refs[g][pl.ds(start, BLOCK_ROWS), :]
                grad = (scattered - jnp.exp(values - log_total) * whole).astype(jnp.bfloat16)
                part = lax.dot_general(
                    grad, rows_refs[g][...], NN, preferred_element_type=jnp.float32
                )
                total = part if total is None else total + part
            out_refs[block // each][
                block % each * BLOCK_ROWS : (block % each + 1) * BLOCK_ROWS
            ] = total.astype(jnp.bfloat16)

    return call(
        kernel,
        tuple(bf16_rows(each * BLOCK_ROWS, width) for _ in range(outputs)),
        2 * blocks * BLOCK_ROWS * count * row_count * (width + 2 * entries),
        in_specs=[smem_spec()] + [vmem_spec()] * (2 * count + 4),
        out_specs=tuple(vmem_spec() for _ in range(outputs)),
    )(order, *logits, *rows, occupancy, high, low, places)


def assemble(pieces, offsets, height):
    count = len(pieces)
    part, width = pieces[0].shape
    short = height % part

    def kernel(offsets_ref, *refs):
        out_ref, sems = refs[count], refs[count + 1]

        def each(act):
            for index in range(count):
                offset = pl.multiple_of(offsets_ref[index], part)

                @pl.when(offset + part <= height)
                def _():
                    act(
                        pltpu.make_async_copy(
                            refs[index], out_ref.at[pl.ds(offset, part)], sems.at[index]
                        )
                    )

                if short:

                    @pl.when(offset + part > height)
                    def _():
                        act(
                            pltpu.make_async_copy(
                                refs[index].at[pl.ds(0, short)],
                                out_ref.at[pl.ds(height - short, short)],
                                sems.at[index],
                            )
                        )

        each(lambda copy: copy.start())
        each(lambda copy: copy.wait())

    return call(
        kernel,
        bf16_rows(height, width),
        0,
        in_specs=[smem_spec()] + [vmem_spec()] * count,
        out_specs=pl.BlockSpec(memory_space=pl.ANY),
        scratch_shapes=[pltpu.SemaphoreType.DMA((count,))],
    )(offsets, *pieces)


def swap(value, axis):
    return lax.ppermute(value, axis, [(0, 1), (1, 0)])


def rotate(value, axis, by):
    count = lax.axis_size(axis)
    return lax.ppermute(value, axis, [(i, (i + by) % count) for i in range(count)])


def after(value, *others):
    return lax.optimization_barrier((value,) + others)[0]


def line_near(value):
    left = lax.ppermute(value, "expert", [(1, 0), (2, 1), (3, 2)])
    right = lax.ppermute(value, "expert", [(0, 1), (1, 2), (2, 3)])
    return left, right


def line_far(left, right):
    return (
        lax.ppermute(left, "expert", [(1, 0), (2, 1)]),
        lax.ppermute(right, "expert", [(1, 2), (2, 3)]),
    )


def line_end(left_far, right_far):
    return (
        lax.ppermute(left_far, "expert", [(1, 0)]),
        lax.ppermute(right_far, "expert", [(2, 3)]),
    )


LINE_ORDER = np.array([[0, 1, 2, 3], [1, 2, 3, 0], [2, 1, 0, 3], [3, 2, 1, 0]])


def slot_orders(count):
    return LINE_ORDER if count == 4 else np.tile(np.arange(count), (count, 1))


def slot_tables(count):
    orders = slot_orders(count)
    tables = np.zeros((count, count, count), np.int32)
    for member in range(count):
        for k in range(count):
            source = (member + k) % count
            for slot in range(count):
                tables[member, k, slot] = list(orders[source]).index(orders[member][slot])
    return tables.reshape(count, count * count)


def wide(ref, start, size):
    return ref[pl.ds(start, size), :].astype(jnp.float32)


def sum_sent(own, came, places):
    height, width = own.shape
    part = height // 4

    def kernel(places_ref, own_ref, came_ref, *out_refs):
        section, outer = places_ref[0], places_ref[1]
        starts = (
            (1 - outer) * part,
            outer * part,
            (2 + 1 - section) * part,
            (2 + section) * part,
        )
        for start, out_ref in zip(starts, out_refs):
            start = pl.multiple_of(start, part)
            out_ref[...] = (wide(own_ref, start, part) + wide(came_ref, start, part)).astype(
                jnp.bfloat16
            )

    return call(
        kernel,
        tuple(bf16_rows(part, width) for _ in range(4)),
        1 << 20,
        in_specs=[smem_spec()] + [vmem_spec()] * 2,
        out_specs=tuple(vmem_spec() for _ in range(4)),
    )(places, own, came)


def sum_kept(own, came, arrived, places, keep):
    height, width = own.shape
    part = height // 4
    count = len(arrived) // 2

    def kernel(places_ref, own_ref, came_ref, *refs):
        section, outer = places_ref[0], places_ref[1]
        if not keep:
            section, outer = 1 - section, 1 - outer
        for side, start in enumerate((outer * part, (2 + section) * part)):
            start = pl.multiple_of(start, part)
            total = wide(own_ref, start, part) + wide(came_ref, start, part)
            for ref in refs[side * count : (side + 1) * count]:
                total = total + ref[...].astype(jnp.float32)
            refs[2 * count + side][...] = total.astype(jnp.bfloat16)

    return call(
        kernel,
        (bf16_rows(part, width), bf16_rows(part, width)),
        1 << 20,
        in_specs=[smem_spec()] + [vmem_spec()] * (2 + 2 * count),
        out_specs=(vmem_spec(), vmem_spec()),
    )(places, own, came, *arrived)


def per_device(
    frames,
    norm_gain,
    router,
    w_in,
    w_out,
    routing,
    head_gain,
    head_weight,
    frame_lengths,
    labels,
    label_lengths,
):
    sections = lax.axis_size("section")
    section_id = lax.axis_index("section")
    group_size = lax.axis_size("expert")
    member = lax.axis_index("expert")
    outer_size = lax.axis_size("dpo")
    inner_size = lax.axis_size("dpi")
    core = lax.axis_index("dpi")
    micro, utt_dev, frame_count, width = frames.shape
    label_max = labels.shape[2]
    experts = w_in.shape[1] * group_size
    pair_count = micro * utt_dev
    per_section = pair_count // sections
    first_pair = section_id * per_section
    share = (utt_dev * frame_count * 9 + 8 * experts - 1) // (8 * experts)
    filled = share * -(-per_section // utt_dev)
    capacity = round_up(filled + 1, 8)
    span = per_section * frame_count
    member_ref = member.astype(jnp.int32).reshape(1)

    def mine_of(value):
        return lax.dynamic_slice_in_dim(value, first_pair, per_section, 0)

    def exchange(blocks, sign):
        return [blocks[0]] + [
            rotate(blocks[k], "expert", sign * k) for k in range(1, group_size)
        ]

    def lanes_of(ids):
        return jnp.pad(mine_of(ids), ((0, 0), (0, LANES - frame_count)), constant_values=-1)

    current = lax.dynamic_slice_in_dim(
        frames.reshape(pair_count * frame_count, width), first_pair * frame_count, span, 0
    )
    own_ids = routing.reshape(pair_count, frame_count)
    paired = sections == 2 and inner_size == 2
    if paired:
        other_ids = swap(own_ids, "section")
        all_ids = [
            jnp.where(section_id == layer, own_ids, other_ids) for layer in range(sections)
        ]
    else:
        all_ids = lax.all_gather(own_ids, "section")
    layer_ids = [lanes_of(all_ids[layer]) for layer in range(sections)]
    own_table = jnp.concatenate(
        [
            norm_gain,
            jnp.zeros((7, width), jnp.float32),
            jnp.transpose(router[0]).astype(jnp.float32),
            jnp.zeros((round_up(experts, 8) - experts, width), jnp.float32),
        ],
        axis=0,
    )
    own = (w_in[0, 0], w_out[0, 0])
    layers = []
    if paired:
        other_table = swap(own_table, "section")
        sent_in, sent_out = half_weights(
            after(core.astype(jnp.int32).reshape(1), own_table), *own
        )
        came_in = swap(sent_in, "section")
        came_out = swap(sent_out, "section")
    else:
        all_tables = lax.all_gather(own_table, "section")
        all_in = lax.all_gather(own[0], "section")
        all_out = lax.all_gather(own[1], "section")
        for layer in range(sections):
            chosen = (all_in[layer], all_out[layer])
            layers.append(((all_tables[layer],), chosen, [], jnp.ones((1,), jnp.int32)))

    outgoing = dispatch(current, layer_ids[0], member_ref, experts, capacity, frame_count)
    received = exchange(outgoing, 1)
    if paired:
        (came_in, came_out), received = lax.optimization_barrier(((came_in, came_out), received))
        other = [(came_in, came_out), (swap(came_in, "dpi"), swap(came_out, "dpi"))]
        for layer in range(sections):
            mine = (section_id == layer).astype(jnp.int32).reshape(1)
            layers.append(((own_table, other_table), own, other, mine))

    labels, frame_lengths, label_lengths = lax.optimization_barrier(
        (labels, frame_lengths, label_lengths, outgoing[0])
    )[:3]
    notes = jnp.concatenate(
        [
            mine_of(labels.reshape(pair_count, label_max)),
            mine_of(frame_lengths.reshape(pair_count, 1)),
            mine_of(label_lengths.reshape(pair_count, 1)),
        ],
        axis=1,
    )
    notes = jnp.pad(notes, ((0, 0), (0, COLS - label_max - 2))).reshape(1, per_section * COLS)
    notes = jnp.pad(notes, ((0, 0), (0, LANES - per_section * COLS)))
    notes = jnp.concatenate([notes // LANES, notes % LANES], axis=1).astype(jnp.float32)
    notes = jnp.pad(notes, ((0, 0), (0, width - 2 * LANES)))
    shard = head_weight.shape[1]
    weight_rows = jnp.transpose(head_weight)
    line = group_size == 4
    tables = jnp.asarray(slot_tables(group_size))
    slots = lax.dynamic_index_in_dim(tables, member, 0, keepdims=False)
    outer = lax.axis_index("dpo")
    blocks = -(-shard // BLOCK_ROWS)
    tree = paired and outer_size == 2 and blocks == 8

    def pair_of(side, first, second):
        return [side * 4 + first, side * 4 + 2 + second]

    def offset_of(side, s, y):
        base = side * 4 * BLOCK_ROWS
        part = BLOCK_ROWS // 2
        return [
            base + s * BLOCK_ROWS + y * part,
            base + 2 * BLOCK_ROWS + y * BLOCK_ROWS + s * part,
        ]

    def whole_numbers(values):
        return jnp.stack([jnp.asarray(value, jnp.int32) for value in values])

    here, there = (section_id, outer), (1 - section_id, 1 - outer)
    sibling_sent_order = whole_numbers(pair_of(1 - core, *there))
    own_sent_order = whole_numbers(pair_of(core, *there))
    kept_order = whole_numbers(pair_of(1 - core, *here) + pair_of(core, *here))
    chip_place = whole_numbers(here)
    offsets = []
    for side in (core, 1 - core):
        for s in (section_id, 1 - section_id):
            for y in (outer, 1 - outer):
                offsets += offset_of(side, s, y)
    offsets = whole_numbers(offsets)
    early = (
        notes,
        slots,
        head_gain.reshape(1, width),
        layer_ids[1:],
        sibling_sent_order,
        own_sent_order,
        kept_order,
        chip_place,
        offsets,
    )
    early, received = lax.optimization_barrier((early, received))
    notes, slots, head_row, later_ids, sibling_sent_order, own_sent_order = early[:6]
    kept_order, chip_place, offsets = early[6:]
    layer_ids = [layer_ids[0]] + list(later_ids)

    for layer in range(sections):
        choices, weights, others, pick_own = layers[layer]
        note = notes if layer == 0 else None
        done = run_expert(received, choices, weights, others, pick_own, filled, note)
        returned = exchange(done, -1)
        if layer == 0:
            found = returned
            if not line:
                stacked = jnp.stack(returned)
                found = [
                    lax.dynamic_index_in_dim(stacked, (k - member) % group_size, 0, keepdims=False)
                    for k in range(group_size)
                ]
        if layer < sections - 1:
            current, outgoing = combine_and_dispatch(
                current,
                returned,
                layer_ids[layer],
                choices,
                pick_own,
                layer_ids[layer + 1],
                member_ref,
                experts,
                capacity,
                frame_count,
            )
            received = exchange(outgoing, 1)
            if layer == 0:
                found = [after(found[0], current)] + list(found[1:])
                label_weight, places, names = label_rows(
                    weight_rows, found, member_ref, per_section, filled, label_max, line
                )
                received, label_weight = lax.optimization_barrier((received, label_weight))
        else:
            normed = combine_and_norm(
                current,
                returned,
                layer_ids[layer],
                choices,
                pick_own,
                head_row,
                member_ref,
                experts,
                capacity,
                frame_count,
            )

    def logits_of(fill, first, count, pieces, earlier):
        return head_logits(
            fill, first, count, pieces, member_ref, weight_rows, label_weight, frame_count, earlier
        )

    if line:
        left, right = line_near(normed)
        far = line_far(left, right)
        heads = [logits_of(fill_near, 0, 2, [normed, left, right], None)]
        far, heads[0] = lax.optimization_barrier((far, heads[0]))
        end = line_end(*far)
        heads.append(logits_of(fill_far, 2, 2, [*far, *end, left, right], heads[0][2]))
        stats = heads[1][2]
        found = [stats] + [rotate(stats, "expert", -k) for k in range(1, group_size)]
    else:
        gathered = lax.all_gather(normed, "expert")
        pieces = [gathered[k] for k in range(group_size)]
        heads = [logits_of(fill_all, 0, group_size, pieces, None)]
        gathered = lax.all_gather(heads[0][2], "expert")
        found = [
            lax.dynamic_index_in_dim(gathered, (member + k) % group_size, 0, keepdims=False)
            for k in range(group_size)
        ]
    kept_losses = per_section if line else group_size * per_section
    occupancy, high, low, losses = ctc_pass(
        found, slots, names, frame_count, label_max, kept_losses
    )
    if not line:
        losses = lax.dynamic_slice(losses, (member * per_section, 0), (per_section, 1))

    def gradient(order, outputs, each):
        return head_gradient(
            [head[0] for head in heads],
            [head[1] for head in heads],
            occupancy,
            high,
            low,
            places,
            order,
            outputs,
            each,
        )

    if tree:
        came_sent = swap(gradient(sibling_sent_order, 1, 2)[0], "dpi")
        own_sent = gradient(own_sent_order, 1, 2)[0]
        a_far, a_near, b_far, b_near = sum_sent(own_sent, came_sent, chip_place)
        kept_order = after(kept_order, a_far)
        a_far, b_far = swap(a_far, "section"), swap(b_far, "dpo")
        a_near, b_near = swap(a_near, "section"), swap(b_near, "dpo")
        sibling_kept, own_kept = gradient(kept_order, 2, 2)
        came_kept = swap(sibling_kept, "dpi")
        a_on, b_on = sum_kept(own_kept, came_kept, [a_far, b_far], chip_place, False)
        a_in, b_in = swap(a_on, "dpo"), swap(b_on, "section")
        a, b = sum_kept(own_kept, came_kept, [a_near, a_in, b_near, b_in], chip_place, True)
        a_y, b_x = swap(a, "dpo"), swap(b, "section")
        b_y, a_x = swap(b, "dpo"), swap(a, "section")
        a_xy, b_xy = swap(a_y, "section"), swap(b_x, "dpo")
        mine = [a, b, a_y, b_y, a_x, b_x, a_xy, b_xy]
        whole = assemble(mine + [swap(value, "dpi") for value in mine], offsets, shard)
    else:
        partial = gradient(jnp.arange(blocks, dtype=jnp.int32), 1, blocks)[0][:shard]
        whole = lax.psum(partial.astype(jnp.float32), ("section", "dpo", "dpi")).astype(
            jnp.bfloat16
        )
    return (losses, jnp.transpose(whole))


def solution(mesh):
    sections, group_size, spread = (mesh.shape[name] for name in ("section", "expert", "dp"))
    inner = 2 if spread % 2 == 0 else 1
    split = Mesh(
        mesh.devices.reshape(sections, group_size, spread // inner, inner),
        ("section", "expert", "dpo", "dpi"),
    )
    block = ("expert", "dpo", "dpi")
    placed = (
        P(None, block, None, None),
        P("section", None),
        P("section", None, None),
        P("section", "expert", None, None),
        P("section", "expert", None, None),
        P("section", None, block, None, None),
        P(),
        P(None, "expert"),
        P(None, block),
        P(None, block, None),
        P(None, block),
    )
    return jax.shard_map(
        per_device,
        mesh=split,
        in_specs=placed,
        out_specs=(P("section", block), P(None, "expert")),
        check_vma=False,
    )
```

```python
import jax
import jax.numpy as jnp
import numpy as np
from jax import lax
from jax.experimental import pallas as pl
from jax.experimental.pallas import tpu as pltpu
from jax.sharding import Mesh, PartitionSpec as P

EPSILON = 1e-06
LOG_ZERO = -1e30
VMEM_LIMIT = 12 * 1024 * 1024
LARGE_LIMIT = 24 * 1024 * 1024
LANES = 128
COLS = 16
PEAK, TOTAL, WHOLE = COLS - 3, COLS - 2, COLS - 3
BLOCK_ROWS = 256
NT = (((1,), (1,)), ((), ()))
NN = (((1,), (0,)), ((), ()))


def round_up(value, unit):
    return -(-value // unit) * unit


def vmem_spec():
    return pl.BlockSpec(memory_space=pltpu.VMEM)


def smem_spec():
    return pl.BlockSpec(memory_space=pltpu.SMEM)


def call(kernel, out_shape, flops=0, limit=VMEM_LIMIT, **options):
    return pl.pallas_call(
        kernel,
        out_shape=out_shape,
        compiler_params=pltpu.CompilerParams(vmem_limit_bytes=limit),
        cost_estimate=pl.CostEstimate(flops=flops, bytes_accessed=0, transcendentals=0),
        **options,
    )


def bf16_rows(count, width):
    return jax.ShapeDtypeStruct((count, width), jnp.bfloat16)


def as_mask(values):
    return values.astype(jnp.float32).astype(jnp.bfloat16)


def split_rows(values, out_refs, spare=None, note=None):
    size, width = out_refs[0].shape
    for turn, out_ref in enumerate(out_refs):
        part = values[turn * size : (turn + 1) * size]
        if note is not None:
            row = lax.broadcasted_iota(jnp.int32, (size, width), 0)
            part = jnp.where(row == spare, note, part)
        out_ref[...] = part.astype(jnp.bfloat16)


def join_rows(refs):
    return jnp.concatenate([ref[...].astype(jnp.float32) for ref in refs], axis=0)


def rms_scale(values, gain):
    values = values.astype(jnp.float32)
    scale = lax.rsqrt(jnp.mean(values * values, axis=-1, keepdims=True) + EPSILON)
    return (values * scale * gain).astype(jnp.bfloat16)


def expert_column(ids, frame_count):
    pairs = ids.shape[0]
    square = jnp.concatenate(
        [ids.astype(jnp.float32), jnp.full((LANES - pairs, LANES), -1.0, jnp.float32)], axis=0
    )
    turned = jnp.transpose(square, (1, 0)).astype(jnp.int32)
    return jnp.concatenate([turned[:frame_count, p : p + 1] for p in range(pairs)], axis=0)


def placement(column, member, experts, capacity):
    count = column.shape[0]
    shifted = column - member
    relative = jnp.where(shifted < 0, shifted + experts, shifted)
    lane = lax.broadcasted_iota(jnp.int32, (count, LANES), 1)
    one_hot = (lane == relative).astype(jnp.float32)
    before = lax.broadcasted_iota(jnp.int32, (count, count), 1) <= lax.broadcasted_iota(
        jnp.int32, (count, count), 0
    )
    rank = lax.dot_general(
        as_mask(before), one_hot.astype(jnp.bfloat16), NN, preferred_element_type=jnp.float32
    )
    start = (lane * capacity - 1).astype(jnp.float32)
    slots = jnp.sum(one_hot * (rank + start), axis=1, keepdims=True).astype(jnp.int32)
    places = lax.broadcasted_iota(jnp.int32, (count, experts * capacity), 1)
    return (places == slots).astype(jnp.float32)


def scatter_rows(rows, ids, member, experts, capacity, frame_count, out_refs):
    count = rows.shape[0]
    chosen = placement(expert_column(ids, frame_count), member, experts, capacity)
    tall = round_up(count, LANES)
    if tall > count:
        chosen = jnp.concatenate(
            [chosen, jnp.zeros((tall - count, chosen.shape[1]), jnp.float32)], axis=0
        )
    pick = jnp.transpose(chosen, (1, 0))[:, :count].astype(jnp.bfloat16)
    placed = lax.dot_general(pick, rows, NN, preferred_element_type=jnp.float32)
    split_rows(placed, out_refs)


def combine_rows(rows, returned, ids, table, member, experts, capacity, frame_count):
    column = expert_column(ids, frame_count)
    pick = placement(column, member, experts, capacity).astype(jnp.bfloat16)
    normed = rms_scale(rows, table[:1])
    router = jnp.concatenate(
        [table[8:], jnp.zeros((LANES + 8 - table.shape[0], rows.shape[1]), jnp.float32)], axis=0
    ).astype(jnp.bfloat16)
    logits = lax.dot_general(normed, router, NT, preferred_element_type=jnp.float32)
    lane = lax.broadcasted_iota(jnp.int32, logits.shape, 1)
    gate = jax.nn.sigmoid(jnp.sum(jnp.where(lane == column, logits, 0.0), axis=1, keepdims=True))
    stacked = join_rows(returned).astype(jnp.bfloat16)
    mixed = lax.dot_general(pick, stacked, NN, preferred_element_type=jnp.float32)
    return (rows.astype(jnp.float32) + gate * mixed).astype(jnp.bfloat16)


def dispatch(rows, ids, member, experts, capacity, frame_count):
    width = rows.shape[1]

    def kernel(member_ref, rows_ref, ids_ref, *out_refs):
        scatter_rows(
            rows_ref[...], ids_ref[...], member_ref[0], experts, capacity, frame_count, out_refs
        )

    return call(
        kernel,
        tuple(bf16_rows(capacity, width) for _ in range(experts)),
        1 << 27,
        in_specs=[smem_spec()] + [vmem_spec()] * 2,
        out_specs=tuple(vmem_spec() for _ in range(experts)),
    )(member, rows, ids)


def pick_table(pick_ref, tables):
    if len(tables) == 1:
        return tables[0][...]
    return jnp.where(pick_ref[0] == 1, tables[0][...], tables[1][...])


def run_expert(received, tables, own, other, pick_own, spare, note):
    count = len(received)
    capacity, width = received[0].shape
    others, choices = len(other), len(tables)
    noted = [] if note is None else [note]

    def kernel(pick_ref, in_ref, out_weight_ref, *refs):
        table_refs, refs = refs[:choices], refs[choices:]
        other_refs, refs = refs[: 2 * others], refs[2 * others :]
        received_refs, refs = refs[:count], refs[count:]
        out_refs = refs[len(noted) :]

        def work(pieces):
            gain = pick_table(pick_ref, table_refs)[:1]
            normed = rms_scale(join_rows(received_refs), gain)
            total = None
            for weight_in, weight_out in pieces:
                hidden = lax.dot_general(
                    normed, weight_in[...], NN, preferred_element_type=jnp.float32
                )
                active = (hidden / (1.0 + jnp.exp(-hidden))).astype(jnp.bfloat16)
                part = lax.dot_general(
                    active, weight_out[...], NN, preferred_element_type=jnp.float32
                )
                total = part if total is None else total + part
            split_rows(total, out_refs, spare, refs[0][...] if noted else None)

        if others == 0:
            work([(in_ref, out_weight_ref)])
            return

        @pl.when(pick_ref[0] == 1)
        def _():
            work([(in_ref, out_weight_ref)])

        @pl.when(pick_ref[0] != 1)
        def _():
            work([(other_refs[2 * i], other_refs[2 * i + 1]) for i in range(others)])

    flat = [weight for pair in other for weight in pair]
    return call(
        kernel,
        tuple(bf16_rows(capacity, width) for _ in range(count)),
        4 * count * capacity * width * own[0].shape[1],
        in_specs=[smem_spec()] + [vmem_spec()] * (2 + choices + 2 * others + count + len(noted)),
        out_specs=tuple(vmem_spec() for _ in range(count)),
    )(pick_own, *own, *tables, *flat, *received, *noted)


def combine_and_dispatch(
    rows, returned, ids, tables, pick_own, next_ids, member, experts, capacity, frame_count
):
    width = rows.shape[1]
    choices = len(tables)

    def kernel(member_ref, pick_ref, rows_ref, ids_ref, next_ref, *refs):
        table_refs, refs = refs[:choices], refs[choices:]
        returned_refs, x_ref, out_refs = refs[:experts], refs[experts], refs[experts + 1 :]
        mixed = combine_rows(
            rows_ref[...],
            returned_refs,
            ids_ref[...],
            pick_table(pick_ref, table_refs),
            member_ref[0],
            experts,
            capacity,
            frame_count,
        )
        x_ref[...] = mixed
        scatter_rows(
            mixed, next_ref[...], member_ref[0], experts, capacity, frame_count, out_refs
        )

    shapes = (bf16_rows(*rows.shape),) + tuple(
        bf16_rows(capacity, width) for _ in range(experts)
    )
    result = call(
        kernel,
        shapes,
        1 << 28,
        in_specs=[smem_spec()] * 2 + [vmem_spec()] * (3 + choices + experts),
        out_specs=tuple(vmem_spec() for _ in shapes),
    )(member, pick_own, rows, ids, next_ids, *tables, *returned)
    return result[0], result[1:]


def combine_and_norm(
    rows, returned, ids, tables, pick_own, head_gain, member, experts, capacity, frame_count
):
    choices = len(tables)

    def kernel(member_ref, pick_ref, rows_ref, ids_ref, head_ref, *refs):
        table_refs, refs = refs[:choices], refs[choices:]
        final = combine_rows(
            rows_ref[...],
            refs[:experts],
            ids_ref[...],
            pick_table(pick_ref, table_refs),
            member_ref[0],
            experts,
            capacity,
            frame_count,
        )
        refs[experts][...] = rms_scale(final, head_ref[...])

    return call(
        kernel,
        bf16_rows(*rows.shape),
        1 << 28,
        in_specs=[smem_spec()] * 2 + [vmem_spec()] * (3 + choices + experts),
        out_specs=vmem_spec(),
    )(member, pick_own, rows, ids, head_gain, *tables, *returned)


def half_weights(core, weight_in, weight_out):
    width, hidden = weight_in.shape
    half = hidden // 2

    def kernel(core_ref, in_ref, out_ref, half_in, half_out, sems):
        start = pl.multiple_of(core_ref[0] * half, half)
        copies = (
            pltpu.make_async_copy(in_ref.at[:, pl.ds(start, half)], half_in, sems.at[0]),
            pltpu.make_async_copy(out_ref.at[pl.ds(start, half)], half_out, sems.at[1]),
        )
        for copy in copies:
            copy.start()
        for copy in copies:
            copy.wait()

    return call(
        kernel,
        (bf16_rows(width, half), bf16_rows(half, width)),
        1 << 20,
        in_specs=[smem_spec()] + [pl.BlockSpec(memory_space=pl.ANY)] * 2,
        out_specs=(vmem_spec(), vmem_spec()),
        scratch_shapes=[pltpu.SemaphoreType.DMA((2,))],
    )(core, weight_in, weight_out)


def block_list(shard):
    return [(i, min(BLOCK_ROWS, shard - i)) for i in range(0, shard, BLOCK_ROWS)]


def label_rows(weight, notes, member, pairs, spare, label_max, line):
    shard, width = weight.shape
    sources = len(notes)
    utterances = sources * pairs
    entries = utterances * COLS

    def kernel(member_ref, weight_ref, *refs):
        note_refs = refs[:sources]
        out_ref, places_ref, names_ref, turned_ref = refs[sources:]
        place = member_ref[0]
        found = []
        for ref in note_refs:
            row = ref[...].astype(jnp.float32)[spare : spare + 1]
            found.append((row[:, :LANES] * LANES + row[:, LANES : 2 * LANES]).astype(jnp.int32))
        if line:
            low = place < 2
            found = [
                found[0],
                jnp.where(low, found[1], found[3]),
                found[2],
                jnp.where(low, found[3], found[1]),
            ]
        names_ref[...] = jnp.zeros(names_ref.shape, jnp.int32)
        for slot in range(sources):
            for pair in range(pairs):
                row = slot * pairs + pair
                names_ref[row : row + 1, :COLS] = found[slot][:, pair * COLS : (pair + 1) * COLS]
        lane = lax.broadcasted_iota(jnp.int32, (utterances, LANES), 1)
        named = jnp.where(lane < label_max, names_ref[...], jnp.where(lane == label_max, 0, -1))
        local = named - place * shard
        local = jnp.where((named >= 0) & (local >= 0) & (local < shard), local, -1)
        square = jnp.concatenate(
            [
                local.astype(jnp.float32),
                jnp.full((LANES - utterances, LANES), -1.0, jnp.float32),
            ],
            axis=0,
        )
        turned = jnp.transpose(square, (1, 0))
        for utterance in range(utterances):
            turned_ref[utterance * COLS : (utterance + 1) * COLS] = jnp.broadcast_to(
                turned[:COLS, utterance : utterance + 1], (COLS, LANES)
            )
        places = turned_ref[:, :1].astype(jnp.int32)
        places_ref[...] = jnp.transpose(turned_ref[...], (1, 0))[:1].astype(jnp.int32)
        total = jnp.zeros((entries, width), jnp.float32)
        for first, size in block_list(shard):
            entry = first + lax.broadcasted_iota(jnp.int32, (entries, size), 1)
            total = total + lax.dot_general(
                as_mask(entry == places),
                weight_ref[first : first + size],
                NN,
                preferred_element_type=jnp.float32,
            )
        out_ref[...] = total.astype(jnp.bfloat16)

    return call(
        kernel,
        (
            bf16_rows(entries, width),
            jax.ShapeDtypeStruct((1, entries), jnp.int32),
            jax.ShapeDtypeStruct((utterances, LANES), jnp.int32),
        ),
        2 * shard * entries * width,
        LARGE_LIMIT,
        in_specs=[smem_spec()] + [vmem_spec()] * (1 + sources),
        out_specs=tuple(vmem_spec() for _ in range(3)),
        scratch_shapes=[pltpu.VMEM((entries, LANES), jnp.float32)],
    )(member, weight, *notes)


def head_logits(
    fill, first_slot, count, pieces, member, weight, label_weight, frame_count, earlier
):
    given = len(pieces)
    ahead = 0 if earlier is None else earlier.shape[0]
    span, width = pieces[0].shape
    row_count = count * span
    shard = weight.shape[0]
    height = round_up(shard, BLOCK_ROWS)
    entries = row_count // frame_count * COLS
    first_entry = first_slot * entries // count
    others = [] if earlier is None else [earlier]

    def kernel(member_ref, weight_ref, label_ref, *refs):
        piece_refs = refs[:given]
        logits_ref, rows_ref, stats_ref = refs[given + len(others) :]

        def put(slot, piece_ref):
            rows_ref[slot * span : (slot + 1) * span] = piece_ref[...]

        def put_if(condition, slot, piece_ref):
            @pl.when(condition)
            def _():
                put(slot, piece_ref)

        fill(member_ref[0], piece_refs, put, put_if)
        peak = jnp.full((1, row_count), LOG_ZERO, jnp.float32)
        total = jnp.zeros((1, row_count), jnp.float32)
        for first, size in block_list(shard):
            logits = lax.dot_general(
                weight_ref[first : first + size],
                rows_ref[...],
                NT,
                preferred_element_type=jnp.float32,
            )
            logits_ref[first : first + size] = logits
            before = peak
            peak = jnp.maximum(before, jnp.max(logits, axis=0, keepdims=True))
            total = total * jnp.exp(before - peak) + jnp.sum(
                jnp.exp(logits - peak), axis=0, keepdims=True
            )
        if height > shard:
            logits_ref[shard:] = jnp.full((height - shard, row_count), LOG_ZERO, jnp.float32)
        crossed = lax.dot_general(
            label_ref[first_entry : first_entry + entries],
            rows_ref[...],
            NT,
            preferred_element_type=jnp.float32,
        )
        owner = lax.broadcasted_iota(jnp.int32, (COLS, row_count), 1) // frame_count
        picked = jnp.zeros((COLS, row_count), jnp.float32)
        for utterance in range(entries // COLS):
            part = crossed[utterance * COLS : (utterance + 1) * COLS]
            picked = picked + jnp.where(owner == utterance, part, 0.0)
        place = lax.broadcasted_iota(jnp.int32, (COLS, row_count), 0)
        stats = jnp.where(place == PEAK, peak, picked)
        stats = jnp.where(place == TOTAL, total, stats)
        for slot in range(ahead):
            stats_ref[slot] = refs[given][slot]
        for slot in range(count):
            stats_ref[ahead + slot] = stats[:, slot * span : (slot + 1) * span]

    return call(
        kernel,
        (
            jax.ShapeDtypeStruct((height, row_count), jnp.float32),
            bf16_rows(row_count, width),
            jax.ShapeDtypeStruct((ahead + count, COLS, span), jnp.float32),
        ),
        2 * height * row_count * width,
        LARGE_LIMIT,
        in_specs=[smem_spec()] + [vmem_spec()] * (2 + given + len(others)),
        out_specs=tuple(vmem_spec() for _ in range(3)),
    )(member, weight, label_weight, *pieces, *others)


def fill_near(place, piece_refs, put, put_if):
    value_ref, left_ref, right_ref = piece_refs
    put(0, value_ref)
    put_if(place < 2, 1, left_ref)
    put_if(place >= 2, 1, right_ref)


def fill_far(place, piece_refs, put, put_if):
    left_far, right_far, left_end, right_end, left_ref, right_ref = piece_refs
    put_if(place < 2, 0, left_far)
    put_if(place >= 2, 0, right_far)
    put_if(place == 0, 1, left_end)
    put_if(place == 3, 1, right_end)
    put_if(place == 1, 1, right_ref)
    put_if(place == 2, 1, left_ref)


def fill_all(place, piece_refs, put, put_if):
    for slot, piece_ref in enumerate(piece_refs):
        put(slot, piece_ref)


def log_add(first, second):
    peak = jnp.maximum(first, second)
    return peak + jnp.log(jnp.exp(first - peak) + jnp.exp(second - peak))


def log_add3(first, second, third):
    peak = jnp.maximum(jnp.maximum(first, second), third)
    return peak + jnp.log(
        jnp.exp(first - peak) + jnp.exp(second - peak) + jnp.exp(third - peak)
    )


def ctc_pass(stats, slots, notes, frame_count, label_max, kept):
    sources = len(stats)
    count, _, span = stats[0].shape
    row_count = count * span
    utterances = notes.shape[0]
    entries = utterances * COLS
    tall = round_up(span, LANES)

    def kernel(slots_ref, notes_ref, *refs):
        (
            out_ref,
            high_ref,
            low_ref,
            loss_ref,
            turn_ref,
            emission_ref,
            emit_blank,
            emit_label,
            blank_fwd,
            label_fwd,
            blank_bwd,
            label_bwd,
            occupancy_ref,
        ) = refs[sources:]
        place = lax.broadcasted_iota(jnp.int32, (COLS, span), 0)
        turn_ref[...] = jnp.zeros(turn_ref.shape, jnp.float32)
        for slot in range(count):
            found = [refs[k][slots_ref[k * count + slot]] for k in range(sources)]
            joined = found[0]
            peak = found[0][PEAK : PEAK + 1]
            for other in found[1:]:
                joined = joined + other
                peak = jnp.maximum(peak, other[PEAK : PEAK + 1])
            total = jnp.zeros((1, span), jnp.float32)
            for other in found:
                total = total + other[TOTAL : TOTAL + 1] * jnp.exp(other[PEAK : PEAK + 1] - peak)
            log_total = peak + jnp.log(total)
            turn_ref[:COLS, :span] = jnp.where(place == TOTAL, log_total, joined - log_total)
            emission_ref[slot * span : (slot + 1) * span] = jnp.transpose(turn_ref[...], (1, 0))[
                :span
            ]

        lane = lax.broadcasted_iota(jnp.int32, (utterances, LANES), 1)
        is_label = lane < label_max
        is_blank = lane <= label_max
        names = jnp.where(is_label, notes_ref[...], 0)
        earlier = pltpu.roll(names, 1, 1)
        skip = is_label & (lane >= 1) & (names != 0) & (names != earlier)
        later = pltpu.roll(names, LANES - 1, 1)
        skip_next = (lane < label_max - 1) & (later != 0) & (later != names)
        frames = notes_ref[:, label_max : label_max + 1]
        counts = notes_ref[:, label_max + 1 : label_max + 2]
        ends_blank = jnp.where(lane == counts, 0.0, LOG_ZERO)
        ends_label = jnp.where(lane == counts - 1, 0.0, LOG_ZERO)

        def spread(step, carry):
            row = emission_ref[pl.ds(step, utterances, stride=frame_count), :]
            blank = jnp.sum(jnp.where(lane == label_max, row, 0.0), axis=1, keepdims=True)
            emit_blank[step] = jnp.where(is_blank, blank, LOG_ZERO)
            emit_label[step] = jnp.where(is_label, row, LOG_ZERO)
            return carry

        lax.fori_loop(0, frame_count, spread, 0, unroll=16)

        def advance(step, carry):
            fwd_blank, fwd_label, bwd_blank, bwd_label = carry
            moved = jnp.where(lane == 0, LOG_ZERO, pltpu.roll(fwd_label, 1, 1))
            new_blank = log_add(fwd_blank, moved) + emit_blank[step]
            new_label = (
                log_add3(fwd_label, fwd_blank, jnp.where(skip, moved, LOG_ZERO))
                + emit_label[step]
            )
            alive = step < frames
            fwd_blank = jnp.where(alive, new_blank, fwd_blank)
            fwd_label = jnp.where(alive, new_label, fwd_label)
            blank_fwd[step] = fwd_blank
            label_fwd[step] = fwd_label

            back = frame_count - 1 - step
            out_blank = bwd_blank + emit_blank[back + 1]
            out_label = bwd_label + emit_label[back + 1]
            next_blank = pltpu.roll(out_blank, LANES - 1, 1)
            next_label = jnp.where(skip_next, pltpu.roll(out_label, LANES - 1, 1), LOG_ZERO)
            ended = back >= frames - 1
            bwd_blank = jnp.where(ended, ends_blank, log_add(out_blank, out_label))
            bwd_label = jnp.where(
                ended, ends_label, log_add3(out_label, next_blank, next_label)
            )
            blank_bwd[back] = bwd_blank
            label_bwd[back] = bwd_label
            return (fwd_blank, fwd_label, bwd_blank, bwd_label)

        first_blank = jnp.where(lane == 0, emit_blank[0], LOG_ZERO)
        first_label = jnp.where(lane == 0, emit_label[0], LOG_ZERO)
        blank_fwd[0] = first_blank
        label_fwd[0] = first_label
        blank_bwd[frame_count - 1] = ends_blank
        label_bwd[frame_count - 1] = ends_label
        fwd_blank, fwd_label, _, _ = lax.fori_loop(
            1, frame_count, advance, (first_blank, first_label, ends_blank, ends_label), unroll=4
        )
        end_state = jnp.sum(jnp.where(lane == counts, fwd_blank, 0.0), axis=1, keepdims=True)
        near_state = jnp.sum(jnp.where(lane == counts - 1, fwd_label, 0.0), axis=1, keepdims=True)
        log_like = log_add(end_state, near_state)
        loss_ref[...] = -log_like[:kept]

        def occupy(step, carry):
            blank = jnp.exp(blank_fwd[step] + blank_bwd[step] - log_like)
            label = jnp.exp(label_fwd[step] + label_bwd[step] - log_like)
            blank = jnp.sum(jnp.where(is_blank, blank, 0.0), axis=1, keepdims=True)
            label = jnp.where(is_label, label, 0.0)
            whole = blank + jnp.sum(label, axis=1, keepdims=True)
            filled = jnp.where(lane == label_max, blank, label)
            filled = jnp.where(lane == WHOLE, whole, filled)
            filled = jnp.where(step < frames, -filled, 0.0)
            row = emission_ref[pl.ds(step, utterances, stride=frame_count), :]
            occupancy_ref[pl.ds(step, utterances, stride=frame_count), :] = jnp.where(
                lane == TOTAL, row, filled
            )
            return carry

        lax.fori_loop(0, frame_count, occupy, 0, unroll=16)
        turned = jnp.transpose(occupancy_ref[...], (1, 0))[:COLS]
        out_ref[...] = turned
        row_place = lax.broadcasted_iota(jnp.int32, (COLS, row_count), 0)
        owner = lax.broadcasted_iota(jnp.int32, (COLS, row_count), 1) // frame_count
        source = jnp.where(row_place < WHOLE, turned, 0.0)
        for utterance in range(utterances):
            part = jnp.where(owner == utterance, source, 0.0)
            high = part.astype(jnp.bfloat16)
            high_ref[utterance * COLS : (utterance + 1) * COLS] = high
            low_ref[utterance * COLS : (utterance + 1) * COLS] = (
                part - high.astype(jnp.float32)
            ).astype(jnp.bfloat16)

    held = pltpu.VMEM((frame_count, utterances, LANES), jnp.float32)
    table = pltpu.VMEM((row_count, LANES), jnp.float32)
    return call(
        kernel,
        (
            jax.ShapeDtypeStruct((COLS, row_count), jnp.float32),
            bf16_rows(entries, row_count),
            bf16_rows(entries, row_count),
            jax.ShapeDtypeStruct((kept, 1), jnp.float32),
        ),
        1 << 26,
        in_specs=[smem_spec()] + [vmem_spec()] * (1 + sources),
        out_specs=tuple(vmem_spec() for _ in range(4)),
        scratch_shapes=[pltpu.VMEM((LANES, tall), jnp.float32), table]
        + [held] * 6
        + [table],
    )(slots, notes, *stats)


def head_gradient(logits, rows, occupancy, high, low, places, order, outputs, each):
    count = len(logits)
    row_count, width = rows[0].shape
    entries = places.shape[1]
    blocks = outputs * each

    def kernel(order_ref, *refs):
        logits_refs, rows_refs = refs[:count], refs[count : 2 * count]
        occupancy_ref, high_ref, low_ref, places_ref = refs[2 * count : 2 * count + 4]
        out_refs = refs[2 * count + 4 :]
        for block in range(blocks):
            start = pl.multiple_of(order_ref[block] * BLOCK_ROWS, BLOCK_ROWS)
            entry = start + lax.broadcasted_iota(jnp.int32, (BLOCK_ROWS, entries), 0)
            select = as_mask(entry == places_ref[...])
            total = None
            for g in range(count):
                lanes = slice(g * row_count, (g + 1) * row_count)
                scattered = lax.dot_general(
                    select, high_ref[:, lanes], NN, preferred_element_type=jnp.float32
                ) + lax.dot_general(
                    select, low_ref[:, lanes], NN, preferred_element_type=jnp.float32
                )
                whole = occupancy_ref[WHOLE : WHOLE + 1, lanes]
                log_total = occupancy_ref[TOTAL : TOTAL + 1, lanes]
                values = logits_refs[g][pl.ds(start, BLOCK_ROWS), :]
                grad = (scattered - jnp.exp(values - log_total) * whole).astype(jnp.bfloat16)
                part = lax.dot_general(
                    grad, rows_refs[g][...], NN, preferred_element_type=jnp.float32
                )
                total = part if total is None else total + part
            out_refs[block // each][
                block % each * BLOCK_ROWS : (block % each + 1) * BLOCK_ROWS
            ] = total.astype(jnp.bfloat16)

    return call(
        kernel,
        tuple(bf16_rows(each * BLOCK_ROWS, width) for _ in range(outputs)),
        2 * blocks * BLOCK_ROWS * count * row_count * (width + 2 * entries),
        LARGE_LIMIT,
        in_specs=[smem_spec()] + [vmem_spec()] * (2 * count + 4),
        out_specs=tuple(vmem_spec() for _ in range(outputs)),
    )(order, *logits, *rows, occupancy, high, low, places)


def assemble(pieces, offsets, height, whole=None):
    count = len(pieces)
    part, width = pieces[0].shape
    short = height % part
    started = [] if whole is None else [whole]

    def kernel(offsets_ref, *refs):
        out_ref, sems = refs[count + len(started) :]

        def each(act):
            for index in range(count):
                offset = pl.multiple_of(offsets_ref[index], part)

                @pl.when(offset + part <= height)
                def _():
                    act(
                        pltpu.make_async_copy(
                            refs[index], out_ref.at[pl.ds(offset, part)], sems.at[index]
                        )
                    )

                if short:

                    @pl.when(offset + part > height)
                    def _():
                        act(
                            pltpu.make_async_copy(
                                refs[index].at[pl.ds(0, short)],
                                out_ref.at[pl.ds(height - short, short)],
                                sems.at[index],
                            )
                        )

        each(lambda copy: copy.start())
        each(lambda copy: copy.wait())

    anywhere = pl.BlockSpec(memory_space=pl.ANY)
    return call(
        kernel,
        bf16_rows(height, width),
        in_specs=[smem_spec()] + [vmem_spec()] * count + [anywhere] * len(started),
        out_specs=anywhere,
        scratch_shapes=[pltpu.SemaphoreType.DMA((count,))],
        input_output_aliases={} if whole is None else {1 + count: 0},
    )(offsets, *pieces, *started)


def swap(value, axis):
    return lax.ppermute(value, axis, [(0, 1), (1, 0)])


def rotate(value, axis, by):
    count = lax.axis_size(axis)
    return lax.ppermute(value, axis, [(i, (i + by) % count) for i in range(count)])


def after(value, *others):
    return lax.optimization_barrier((value,) + others)[0]


def line_near(value):
    left = lax.ppermute(value, "expert", [(1, 0), (2, 1), (3, 2)])
    right = lax.ppermute(value, "expert", [(0, 1), (1, 2), (2, 3)])
    return left, right


def line_far(left, right):
    return (
        lax.ppermute(left, "expert", [(1, 0), (2, 1)]),
        lax.ppermute(right, "expert", [(1, 2), (2, 3)]),
    )


def line_end(left_far, right_far):
    return (
        lax.ppermute(left_far, "expert", [(1, 0)]),
        lax.ppermute(right_far, "expert", [(2, 3)]),
    )


LINE_ORDER = np.array([[0, 1, 2, 3], [1, 2, 3, 0], [2, 1, 0, 3], [3, 2, 1, 0]])


def slot_orders(count):
    return LINE_ORDER if count == 4 else np.tile(np.arange(count), (count, 1))


def slot_tables(count):
    orders = slot_orders(count)
    tables = np.zeros((count, count, count), np.int32)
    for member in range(count):
        for k in range(count):
            source = (member + k) % count
            for slot in range(count):
                tables[member, k, slot] = list(orders[source]).index(orders[member][slot])
    return tables.reshape(count, count * count)


def wide(ref, start, size):
    return ref[pl.ds(start, size), :].astype(jnp.float32)


def sum_sent(own, came, places):
    height, width = own.shape
    part = height // 4

    def kernel(places_ref, own_ref, came_ref, *out_refs):
        section, outer = places_ref[0], places_ref[1]
        starts = (
            (1 - outer) * part,
            outer * part,
            (2 + 1 - section) * part,
            (2 + section) * part,
        )
        for start, out_ref in zip(starts, out_refs):
            start = pl.multiple_of(start, part)
            out_ref[...] = (wide(own_ref, start, part) + wide(came_ref, start, part)).astype(
                jnp.bfloat16
            )

    return call(
        kernel,
        tuple(bf16_rows(part, width) for _ in range(4)),
        1 << 20,
        in_specs=[smem_spec()] + [vmem_spec()] * 2,
        out_specs=tuple(vmem_spec() for _ in range(4)),
    )(places, own, came)


def sum_kept(own, came, arrived, places, keep):
    height, width = own.shape
    part = height // 4
    count = len(arrived) // 2

    def kernel(places_ref, own_ref, came_ref, *refs):
        section, outer = places_ref[0], places_ref[1]
        if not keep:
            section, outer = 1 - section, 1 - outer
        for side, start in enumerate((outer * part, (2 + section) * part)):
            start = pl.multiple_of(start, part)
            total = wide(own_ref, start, part) + wide(came_ref, start, part)
            for ref in refs[side * count : (side + 1) * count]:
                total = total + ref[...].astype(jnp.float32)
            refs[2 * count + side][...] = total.astype(jnp.bfloat16)

    return call(
        kernel,
        (bf16_rows(part, width), bf16_rows(part, width)),
        1 << 20,
        in_specs=[smem_spec()] + [vmem_spec()] * (2 + 2 * count),
        out_specs=(vmem_spec(), vmem_spec()),
    )(places, own, came, *arrived)


def per_device(
    frames,
    norm_gain,
    router,
    w_in,
    w_out,
    routing,
    head_gain,
    head_weight,
    frame_lengths,
    labels,
    label_lengths,
):
    sections = lax.axis_size("section")
    section_id = lax.axis_index("section")
    group_size = lax.axis_size("expert")
    member = lax.axis_index("expert")
    outer_size = lax.axis_size("dpo")
    inner_size = lax.axis_size("dpi")
    core = lax.axis_index("dpi")
    micro, utt_dev, frame_count, width = frames.shape
    label_max = labels.shape[2]
    experts = w_in.shape[1] * group_size
    pair_count = micro * utt_dev
    per_section = pair_count // sections
    first_pair = section_id * per_section
    share = (utt_dev * frame_count * 9 + 8 * experts - 1) // (8 * experts)
    filled = share * -(-per_section // utt_dev)
    capacity = round_up(filled + 1, 8)
    span = per_section * frame_count
    member_ref = member.astype(jnp.int32).reshape(1)

    def mine_of(value):
        return lax.dynamic_slice_in_dim(value, first_pair, per_section, 0)

    def exchange(blocks, sign):
        return [blocks[0]] + [
            rotate(blocks[k], "expert", sign * k) for k in range(1, group_size)
        ]

    def lanes_of(ids):
        return jnp.pad(mine_of(ids), ((0, 0), (0, LANES - frame_count)), constant_values=-1)

    current = lax.dynamic_slice_in_dim(
        frames.reshape(pair_count * frame_count, width), first_pair * frame_count, span, 0
    )
    own_ids = routing.reshape(pair_count, frame_count)
    paired = sections == 2 and inner_size == 2
    if paired:
        other_ids = swap(own_ids, "section")
        all_ids = [
            jnp.where(section_id == layer, own_ids, other_ids) for layer in range(sections)
        ]
    else:
        all_ids = lax.all_gather(own_ids, "section")
    layer_ids = [lanes_of(all_ids[layer]) for layer in range(sections)]
    own_table = jnp.concatenate(
        [
            norm_gain,
            jnp.zeros((7, width), jnp.float32),
            jnp.transpose(router[0]).astype(jnp.float32),
            jnp.zeros((round_up(experts, 8) - experts, width), jnp.float32),
        ],
        axis=0,
    )
    own = (w_in[0, 0], w_out[0, 0])
    layers = []
    if paired:
        other_table = swap(own_table, "section")
        sent_in, sent_out = half_weights(core.astype(jnp.int32).reshape(1), *own)
        came_in = swap(sent_in, "section")
        came_out = swap(sent_out, "section")
    else:
        all_tables = lax.all_gather(own_table, "section")
        all_in = lax.all_gather(own[0], "section")
        all_out = lax.all_gather(own[1], "section")
        for layer in range(sections):
            chosen = (all_in[layer], all_out[layer])
            layers.append(((all_tables[layer],), chosen, [], jnp.ones((1,), jnp.int32)))

    outgoing = dispatch(current, layer_ids[0], member_ref, experts, capacity, frame_count)
    received = exchange(outgoing, 1)
    if paired:
        (came_in, came_out), received = lax.optimization_barrier(((came_in, came_out), received))
        other = [(came_in, came_out), (swap(came_in, "dpi"), swap(came_out, "dpi"))]
        for layer in range(sections):
            mine = (section_id == layer).astype(jnp.int32).reshape(1)
            layers.append(((own_table, other_table), own, other, mine))

    labels, frame_lengths, label_lengths = lax.optimization_barrier(
        (labels, frame_lengths, label_lengths, outgoing[0])
    )[:3]
    notes = jnp.concatenate(
        [
            mine_of(labels.reshape(pair_count, label_max)),
            mine_of(frame_lengths.reshape(pair_count, 1)),
            mine_of(label_lengths.reshape(pair_count, 1)),
        ],
        axis=1,
    )
    notes = jnp.pad(notes, ((0, 0), (0, COLS - label_max - 2))).reshape(1, per_section * COLS)
    notes = jnp.pad(notes, ((0, 0), (0, LANES - per_section * COLS)))
    notes = jnp.concatenate([notes // LANES, notes % LANES], axis=1).astype(jnp.float32)
    notes = jnp.pad(notes, ((0, 0), (0, width - 2 * LANES)))
    shard = head_weight.shape[1]
    weight_rows = jnp.transpose(head_weight)
    line = group_size == 4
    tables = jnp.asarray(slot_tables(group_size))
    slots = lax.dynamic_index_in_dim(tables, member, 0, keepdims=False)
    outer = lax.axis_index("dpo")
    blocks = -(-shard // BLOCK_ROWS)
    tree = paired and outer_size == 2 and blocks == 8

    def pair_of(side, first, second):
        return [side * 4 + first, side * 4 + 2 + second]

    def offset_of(side, s, y):
        base = side * 4 * BLOCK_ROWS
        part = BLOCK_ROWS // 2
        return [
            base + s * BLOCK_ROWS + y * part,
            base + 2 * BLOCK_ROWS + y * BLOCK_ROWS + s * part,
        ]

    def whole_numbers(values):
        return jnp.stack([jnp.asarray(value, jnp.int32) for value in values])

    here, there = (section_id, outer), (1 - section_id, 1 - outer)
    sibling_order = whole_numbers(pair_of(1 - core, *there) + pair_of(1 - core, *here))
    sent_order = whole_numbers(pair_of(core, *there))
    kept_order = whole_numbers(pair_of(core, *here))
    chip_place = whole_numbers(here)
    first_offsets, last_offsets = [], offset_of(core, *there) + offset_of(1 - core, *there)
    for side in (core, 1 - core):
        for s, y in (here, (section_id, 1 - outer), (1 - section_id, outer)):
            first_offsets += offset_of(side, s, y)
    first_offsets, last_offsets = whole_numbers(first_offsets), whole_numbers(last_offsets)
    early = (
        notes,
        slots,
        head_gain.reshape(1, width),
        layer_ids[1:],
        sibling_order,
        sent_order,
        kept_order,
        chip_place,
        first_offsets,
        last_offsets,
    )
    early, received = lax.optimization_barrier((early, received))
    notes, slots, head_row, later_ids, sibling_order, sent_order = early[:6]
    kept_order, chip_place, first_offsets, last_offsets = early[6:]
    layer_ids = [layer_ids[0]] + list(later_ids)

    for layer in range(sections):
        choices, weights, others, pick_own = layers[layer]
        note = notes if layer == 0 else None
        done = run_expert(received, choices, weights, others, pick_own, filled, note)
        returned = exchange(done, -1)
        if layer == 0:
            found = returned
            if not line:
                stacked = jnp.stack(returned)
                found = [
                    lax.dynamic_index_in_dim(stacked, (k - member) % group_size, 0, keepdims=False)
                    for k in range(group_size)
                ]
        if layer < sections - 1:
            current, outgoing = combine_and_dispatch(
                current,
                returned,
                layer_ids[layer],
                choices,
                pick_own,
                layer_ids[layer + 1],
                member_ref,
                experts,
                capacity,
                frame_count,
            )
            received = exchange(outgoing, 1)
            if layer == 0:
                found = [after(found[0], current)] + list(found[1:])
                label_weight, places, names = label_rows(
                    weight_rows, found, member_ref, per_section, filled, label_max, line
                )
                received, label_weight = lax.optimization_barrier((received, label_weight))
        else:
            normed = combine_and_norm(
                current,
                returned,
                layer_ids[layer],
                choices,
                pick_own,
                head_row,
                member_ref,
                experts,
                capacity,
                frame_count,
            )

    def logits_of(fill, first, count, pieces, earlier):
        return head_logits(
            fill, first, count, pieces, member_ref, weight_rows, label_weight, frame_count, earlier
        )

    if line:
        left, right = line_near(normed)
        far = line_far(left, right)
        heads = [logits_of(fill_near, 0, 2, [normed, left, right], None)]
        far, heads[0] = lax.optimization_barrier((far, heads[0]))
        end = line_end(*far)
        heads.append(logits_of(fill_far, 2, 2, [*far, *end, left, right], heads[0][2]))
        stats = heads[1][2]
        found = [stats] + [rotate(stats, "expert", -k) for k in range(1, group_size)]
    else:
        gathered = lax.all_gather(normed, "expert")
        pieces = [gathered[k] for k in range(group_size)]
        heads = [logits_of(fill_all, 0, group_size, pieces, None)]
        gathered = lax.all_gather(heads[0][2], "expert")
        found = [
            lax.dynamic_index_in_dim(gathered, (member + k) % group_size, 0, keepdims=False)
            for k in range(group_size)
        ]
    kept_losses = per_section if line else group_size * per_section
    occupancy, high, low, losses = ctc_pass(
        found, slots, names, frame_count, label_max, kept_losses
    )
    if not line:
        losses = lax.dynamic_slice(losses, (member * per_section, 0), (per_section, 1))

    def gradient(order, outputs, each):
        return head_gradient(
            [head[0] for head in heads],
            [head[1] for head in heads],
            occupancy,
            high,
            low,
            places,
            order,
            outputs,
            each,
        )

    if tree:
        sibling_sent, sibling_kept = gradient(sibling_order, 2, 2)
        came_sent, came_kept = swap(sibling_sent, "dpi"), swap(sibling_kept, "dpi")
        own_sent = gradient(after(sent_order, sibling_sent), 1, 2)[0]
        a_far, a_near, b_far, b_near = sum_sent(own_sent, came_sent, chip_place)
        kept_order = after(kept_order, a_far)
        a_far, b_far = swap(a_far, "section"), swap(b_far, "dpo")
        a_near, b_near = swap(a_near, "section"), swap(b_near, "dpo")
        own_kept = gradient(kept_order, 1, 2)[0]
        a_on, b_on = sum_kept(own_kept, came_kept, [a_far, b_far], chip_place, False)
        a_in, b_in = swap(a_on, "dpo"), swap(b_on, "section")
        a, b = sum_kept(own_kept, came_kept, [a_near, a_in, b_near, b_in], chip_place, True)
        a_y, b_x = swap(a, "dpo"), swap(b, "section")
        b_y, a_x = swap(b, "dpo"), swap(a, "section")
        a_xy, b_xy = swap(a_y, "section"), swap(b_x, "dpo")
        a_y, b_y, a_x, b_x = lax.optimization_barrier((a_y, b_y, a_x, b_x))
        mine = [a, b, a_y, b_y, a_x, b_x]
        theirs = [swap(value, "dpi") for value in mine]
        whole = assemble(mine + theirs, first_offsets, shard)
        last = [a_xy, b_xy, swap(a_xy, "dpi"), swap(b_xy, "dpi")]
        whole = assemble(last, last_offsets, shard, whole)
    else:
        partial = gradient(jnp.arange(blocks, dtype=jnp.int32), 1, blocks)[0][:shard]
        whole = lax.psum(partial.astype(jnp.float32), ("section", "dpo", "dpi")).astype(
            jnp.bfloat16
        )
    return (losses, jnp.transpose(whole))


def solution(mesh):
    sections, group_size, spread = (mesh.shape[name] for name in ("section", "expert", "dp"))
    inner = 2 if spread % 2 == 0 else 1
    split = Mesh(
        mesh.devices.reshape(sections, group_size, spread // inner, inner),
        ("section", "expert", "dpo", "dpi"),
    )
    block = ("expert", "dpo", "dpi")
    placed = (
        P(None, block, None, None),
        P("section", None),
        P("section", None, None),
        P("section", "expert", None, None),
        P("section", "expert", None, None),
        P("section", None, block, None, None),
        P(),
        P(None, "expert"),
        P(None, block),
        P(None, block, None),
        P(None, block),
    )
    return jax.shard_map(
        per_device,
        mesh=split,
        in_specs=placed,
        out_specs=(P("section", block), P(None, "expert")),
        check_vma=False,
    )
```

```python
import jax
import jax.numpy as jnp
import numpy as np
from jax import lax
from jax.experimental import pallas as pl
from jax.experimental.pallas import tpu as pltpu
from jax.sharding import Mesh, PartitionSpec as P

EPSILON = 1e-06
LOG_ZERO = -1e30
VMEM_LIMIT = 12 * 1024 * 1024
LARGE_LIMIT = 24 * 1024 * 1024
LANES = 128
COLS = 16
PEAK, TOTAL, WHOLE = COLS - 3, COLS - 2, COLS - 3
BLOCK_ROWS = 256
NT = (((1,), (1,)), ((), ()))
NN = (((1,), (0,)), ((), ()))


def round_up(value, unit):
    return -(-value // unit) * unit


def vmem_spec():
    return pl.BlockSpec(memory_space=pltpu.VMEM)


def smem_spec():
    return pl.BlockSpec(memory_space=pltpu.SMEM)


def call(kernel, out_shape, flops=0, limit=VMEM_LIMIT, **options):
    return pl.pallas_call(
        kernel,
        out_shape=out_shape,
        compiler_params=pltpu.CompilerParams(vmem_limit_bytes=limit),
        cost_estimate=pl.CostEstimate(flops=flops, bytes_accessed=0, transcendentals=0),
        **options,
    )


def bf16_rows(count, width):
    return jax.ShapeDtypeStruct((count, width), jnp.bfloat16)


def as_mask(values):
    return values.astype(jnp.float32).astype(jnp.bfloat16)


def split_rows(values, out_refs, spare=None, note=None):
    size, width = out_refs[0].shape
    for turn, out_ref in enumerate(out_refs):
        part = values[turn * size : (turn + 1) * size]
        if note is not None:
            row = lax.broadcasted_iota(jnp.int32, (size, width), 0)
            part = jnp.where(row == spare, note, part)
        out_ref[...] = part.astype(jnp.bfloat16)


def join_rows(refs):
    return jnp.concatenate([ref[...].astype(jnp.float32) for ref in refs], axis=0)


def rms_scale(values, gain):
    values = values.astype(jnp.float32)
    scale = lax.rsqrt(jnp.mean(values * values, axis=-1, keepdims=True) + EPSILON)
    return (values * scale * gain).astype(jnp.bfloat16)


def expert_column(ids, frame_count):
    pairs = ids.shape[0]
    square = jnp.concatenate(
        [ids.astype(jnp.float32), jnp.full((LANES - pairs, LANES), -1.0, jnp.float32)], axis=0
    )
    turned = jnp.transpose(square, (1, 0)).astype(jnp.int32)
    return jnp.concatenate([turned[:frame_count, p : p + 1] for p in range(pairs)], axis=0)


def placement(column, member, experts, capacity):
    count = column.shape[0]
    shifted = column - member
    relative = jnp.where(shifted < 0, shifted + experts, shifted)
    lane = lax.broadcasted_iota(jnp.int32, (count, LANES), 1)
    one_hot = (lane == relative).astype(jnp.float32)
    before = lax.broadcasted_iota(jnp.int32, (count, count), 1) <= lax.broadcasted_iota(
        jnp.int32, (count, count), 0
    )
    rank = lax.dot_general(
        as_mask(before), one_hot.astype(jnp.bfloat16), NN, preferred_element_type=jnp.float32
    )
    start = (lane * capacity - 1).astype(jnp.float32)
    slots = jnp.sum(one_hot * (rank + start), axis=1, keepdims=True).astype(jnp.int32)
    places = lax.broadcasted_iota(jnp.int32, (count, experts * capacity), 1)
    return (places == slots).astype(jnp.float32)


def scatter_rows(rows, ids, member, experts, capacity, frame_count, out_refs):
    count = rows.shape[0]
    chosen = placement(expert_column(ids, frame_count), member, experts, capacity)
    tall = round_up(count, LANES)
    if tall > count:
        chosen = jnp.concatenate(
            [chosen, jnp.zeros((tall - count, chosen.shape[1]), jnp.float32)], axis=0
        )
    pick = jnp.transpose(chosen, (1, 0))[:, :count].astype(jnp.bfloat16)
    placed = lax.dot_general(pick, rows, NN, preferred_element_type=jnp.float32)
    split_rows(placed, out_refs)


def combine_rows(rows, returned, ids, table, member, experts, capacity, frame_count):
    column = expert_column(ids, frame_count)
    pick = placement(column, member, experts, capacity).astype(jnp.bfloat16)
    normed = rms_scale(rows, table[:1])
    router = jnp.concatenate(
        [table[8:], jnp.zeros((LANES + 8 - table.shape[0], rows.shape[1]), jnp.float32)], axis=0
    ).astype(jnp.bfloat16)
    logits = lax.dot_general(normed, router, NT, preferred_element_type=jnp.float32)
    lane = lax.broadcasted_iota(jnp.int32, logits.shape, 1)
    gate = jax.nn.sigmoid(jnp.sum(jnp.where(lane == column, logits, 0.0), axis=1, keepdims=True))
    stacked = join_rows(returned).astype(jnp.bfloat16)
    mixed = lax.dot_general(pick, stacked, NN, preferred_element_type=jnp.float32)
    return (rows.astype(jnp.float32) + gate * mixed).astype(jnp.bfloat16)


def dispatch(rows, ids, member, experts, capacity, frame_count):
    width = rows.shape[1]

    def kernel(member_ref, rows_ref, ids_ref, *out_refs):
        scatter_rows(
            rows_ref[...], ids_ref[...], member_ref[0], experts, capacity, frame_count, out_refs
        )

    return call(
        kernel,
        tuple(bf16_rows(capacity, width) for _ in range(experts)),
        1 << 27,
        in_specs=[smem_spec()] + [vmem_spec()] * 2,
        out_specs=tuple(vmem_spec() for _ in range(experts)),
    )(member, rows, ids)


def pick_table(pick_ref, tables):
    if len(tables) == 1:
        return tables[0][...]
    return jnp.where(pick_ref[0] == 1, tables[0][...], tables[1][...])


def run_expert(received, tables, own, other, pick_own, spare, note):
    count = len(received)
    capacity, width = received[0].shape
    others, choices = len(other), len(tables)
    noted = [] if note is None else [note]

    def kernel(pick_ref, in_ref, out_weight_ref, *refs):
        table_refs, refs = refs[:choices], refs[choices:]
        other_refs, refs = refs[: 2 * others], refs[2 * others :]
        received_refs, refs = refs[:count], refs[count:]
        out_refs = refs[len(noted) :]

        def work(pieces):
            gain = pick_table(pick_ref, table_refs)[:1]
            normed = rms_scale(join_rows(received_refs), gain)
            total = None
            for weight_in, weight_out in pieces:
                hidden = lax.dot_general(
                    normed, weight_in[...], NN, preferred_element_type=jnp.float32
                )
                active = (hidden / (1.0 + jnp.exp(-hidden))).astype(jnp.bfloat16)
                part = lax.dot_general(
                    active, weight_out[...], NN, preferred_element_type=jnp.float32
                )
                total = part if total is None else total + part
            split_rows(total, out_refs, spare, refs[0][...] if noted else None)

        if others == 0:
            work([(in_ref, out_weight_ref)])
            return

        @pl.when(pick_ref[0] == 1)
        def _():
            work([(in_ref, out_weight_ref)])

        @pl.when(pick_ref[0] != 1)
        def _():
            work([(other_refs[2 * i], other_refs[2 * i + 1]) for i in range(others)])

    flat = [weight for pair in other for weight in pair]
    return call(
        kernel,
        tuple(bf16_rows(capacity, width) for _ in range(count)),
        4 * count * capacity * width * own[0].shape[1],
        in_specs=[smem_spec()] + [vmem_spec()] * (2 + choices + 2 * others + count + len(noted)),
        out_specs=tuple(vmem_spec() for _ in range(count)),
    )(pick_own, *own, *tables, *flat, *received, *noted)


def combine_and_dispatch(
    rows, returned, ids, tables, pick_own, next_ids, member, experts, capacity, frame_count
):
    width = rows.shape[1]
    choices = len(tables)

    def kernel(member_ref, pick_ref, rows_ref, ids_ref, next_ref, *refs):
        table_refs, refs = refs[:choices], refs[choices:]
        returned_refs, x_ref, out_refs = refs[:experts], refs[experts], refs[experts + 1 :]
        mixed = combine_rows(
            rows_ref[...],
            returned_refs,
            ids_ref[...],
            pick_table(pick_ref, table_refs),
            member_ref[0],
            experts,
            capacity,
            frame_count,
        )
        x_ref[...] = mixed
        scatter_rows(
            mixed, next_ref[...], member_ref[0], experts, capacity, frame_count, out_refs
        )

    shapes = (bf16_rows(*rows.shape),) + tuple(
        bf16_rows(capacity, width) for _ in range(experts)
    )
    result = call(
        kernel,
        shapes,
        1 << 28,
        in_specs=[smem_spec()] * 2 + [vmem_spec()] * (3 + choices + experts),
        out_specs=tuple(vmem_spec() for _ in shapes),
    )(member, pick_own, rows, ids, next_ids, *tables, *returned)
    return result[0], result[1:]


def combine_and_norm(
    rows, returned, ids, tables, pick_own, head_gain, member, experts, capacity, frame_count
):
    choices = len(tables)

    def kernel(member_ref, pick_ref, rows_ref, ids_ref, head_ref, *refs):
        table_refs, refs = refs[:choices], refs[choices:]
        final = combine_rows(
            rows_ref[...],
            refs[:experts],
            ids_ref[...],
            pick_table(pick_ref, table_refs),
            member_ref[0],
            experts,
            capacity,
            frame_count,
        )
        refs[experts][...] = rms_scale(final, head_ref[...])

    return call(
        kernel,
        bf16_rows(*rows.shape),
        1 << 28,
        in_specs=[smem_spec()] * 2 + [vmem_spec()] * (3 + choices + experts),
        out_specs=vmem_spec(),
    )(member, pick_own, rows, ids, head_gain, *tables, *returned)


def half_weights(core, weight_in, weight_out):
    width, hidden = weight_in.shape
    half = hidden // 2

    def kernel(core_ref, in_ref, out_ref, half_in, half_out, sems):
        start = pl.multiple_of(core_ref[0] * half, half)
        copies = (
            pltpu.make_async_copy(in_ref.at[:, pl.ds(start, half)], half_in, sems.at[0]),
            pltpu.make_async_copy(out_ref.at[pl.ds(start, half)], half_out, sems.at[1]),
        )
        for copy in copies:
            copy.start()
        for copy in copies:
            copy.wait()

    return call(
        kernel,
        (bf16_rows(width, half), bf16_rows(half, width)),
        1 << 20,
        in_specs=[smem_spec()] + [pl.BlockSpec(memory_space=pl.ANY)] * 2,
        out_specs=(vmem_spec(), vmem_spec()),
        scratch_shapes=[pltpu.SemaphoreType.DMA((2,))],
    )(core, weight_in, weight_out)


def block_list(shard):
    return [(i, min(BLOCK_ROWS, shard - i)) for i in range(0, shard, BLOCK_ROWS)]


def label_rows(weight, notes, member, pairs, spare, label_max, line):
    shard, width = weight.shape
    sources = len(notes)
    utterances = sources * pairs
    entries = utterances * COLS

    def kernel(member_ref, weight_ref, *refs):
        note_refs = refs[:sources]
        out_ref, places_ref, names_ref, turned_ref = refs[sources:]
        place = member_ref[0]
        found = []
        for ref in note_refs:
            row = ref[...].astype(jnp.float32)[spare : spare + 1]
            found.append((row[:, :LANES] * LANES + row[:, LANES : 2 * LANES]).astype(jnp.int32))
        if line:
            low = place < 2
            found = [
                found[0],
                jnp.where(low, found[1], found[3]),
                found[2],
                jnp.where(low, found[3], found[1]),
            ]
        names_ref[...] = jnp.zeros(names_ref.shape, jnp.int32)
        for slot in range(sources):
            for pair in range(pairs):
                row = slot * pairs + pair
                names_ref[row : row + 1, :COLS] = found[slot][:, pair * COLS : (pair + 1) * COLS]
        lane = lax.broadcasted_iota(jnp.int32, (utterances, LANES), 1)
        named = jnp.where(lane < label_max, names_ref[...], jnp.where(lane == label_max, 0, -1))
        local = named - place * shard
        local = jnp.where((named >= 0) & (local >= 0) & (local < shard), local, -1)
        square = jnp.concatenate(
            [
                local.astype(jnp.float32),
                jnp.full((LANES - utterances, LANES), -1.0, jnp.float32),
            ],
            axis=0,
        )
        turned = jnp.transpose(square, (1, 0))
        for utterance in range(utterances):
            turned_ref[utterance * COLS : (utterance + 1) * COLS] = jnp.broadcast_to(
                turned[:COLS, utterance : utterance + 1], (COLS, LANES)
            )
        places = turned_ref[:, :1].astype(jnp.int32)
        places_ref[...] = jnp.transpose(turned_ref[...], (1, 0))[:1].astype(jnp.int32)
        total = jnp.zeros((entries, width), jnp.float32)
        for first, size in block_list(shard):
            entry = first + lax.broadcasted_iota(jnp.int32, (entries, size), 1)
            total = total + lax.dot_general(
                as_mask(entry == places),
                weight_ref[first : first + size],
                NN,
                preferred_element_type=jnp.float32,
            )
        out_ref[...] = total.astype(jnp.bfloat16)

    return call(
        kernel,
        (
            bf16_rows(entries, width),
            jax.ShapeDtypeStruct((1, entries), jnp.int32),
            jax.ShapeDtypeStruct((utterances, LANES), jnp.int32),
        ),
        2 * shard * entries * width,
        LARGE_LIMIT,
        in_specs=[smem_spec()] + [vmem_spec()] * (1 + sources),
        out_specs=tuple(vmem_spec() for _ in range(3)),
        scratch_shapes=[pltpu.VMEM((entries, LANES), jnp.float32)],
    )(member, weight, *notes)


def head_logits(
    fill, first_slot, count, pieces, member, weight, label_weight, frame_count
):
    given = len(pieces)
    span, width = pieces[0].shape
    row_count = count * span
    shard = weight.shape[0]
    height = round_up(shard, BLOCK_ROWS)
    entries = row_count // frame_count * COLS
    first_entry = first_slot * entries // count

    def kernel(member_ref, weight_ref, label_ref, *refs):
        piece_refs = refs[:given]
        logits_ref, rows_ref, stats_ref = refs[given:]

        def put(slot, piece_ref):
            rows_ref[slot * span : (slot + 1) * span] = piece_ref[...]

        def put_if(condition, slot, piece_ref):
            @pl.when(condition)
            def _():
                put(slot, piece_ref)

        fill(member_ref[0], piece_refs, put, put_if)
        peak = jnp.full((1, row_count), LOG_ZERO, jnp.float32)
        total = jnp.zeros((1, row_count), jnp.float32)
        for first, size in block_list(shard):
            logits = lax.dot_general(
                weight_ref[first : first + size],
                rows_ref[...],
                NT,
                preferred_element_type=jnp.float32,
            )
            logits_ref[first : first + size] = logits
            before = peak
            peak = jnp.maximum(before, jnp.max(logits, axis=0, keepdims=True))
            total = total * jnp.exp(before - peak) + jnp.sum(
                jnp.exp(logits - peak), axis=0, keepdims=True
            )
        if height > shard:
            logits_ref[shard:] = jnp.full((height - shard, row_count), LOG_ZERO, jnp.float32)
        crossed = lax.dot_general(
            label_ref[first_entry : first_entry + entries],
            rows_ref[...],
            NT,
            preferred_element_type=jnp.float32,
        )
        owner = lax.broadcasted_iota(jnp.int32, (COLS, row_count), 1) // frame_count
        picked = jnp.zeros((COLS, row_count), jnp.float32)
        for utterance in range(entries // COLS):
            part = crossed[utterance * COLS : (utterance + 1) * COLS]
            picked = picked + jnp.where(owner == utterance, part, 0.0)
        place = lax.broadcasted_iota(jnp.int32, (COLS, row_count), 0)
        stats = jnp.where(place == PEAK, peak, picked)
        stats = jnp.where(place == TOTAL, total, stats)
        for slot in range(count):
            stats_ref[slot] = stats[:, slot * span : (slot + 1) * span]

    return call(
        kernel,
        (
            jax.ShapeDtypeStruct((height, row_count), jnp.float32),
            bf16_rows(row_count, width),
            jax.ShapeDtypeStruct((count, COLS, span), jnp.float32),
        ),
        2 * height * row_count * width,
        LARGE_LIMIT,
        in_specs=[smem_spec()] + [vmem_spec()] * (2 + given),
        out_specs=tuple(vmem_spec() for _ in range(3)),
    )(member, weight, label_weight, *pieces)


def fill_near(place, piece_refs, put, put_if):
    value_ref, left_ref, right_ref = piece_refs
    put(0, value_ref)
    put_if(place < 2, 1, left_ref)
    put_if(place >= 2, 1, right_ref)


def fill_far(place, piece_refs, put, put_if):
    left_far, right_far, left_end, right_end, left_ref, right_ref = piece_refs
    put_if(place < 2, 0, left_far)
    put_if(place >= 2, 0, right_far)
    put_if(place == 0, 1, left_end)
    put_if(place == 3, 1, right_end)
    put_if(place == 1, 1, right_ref)
    put_if(place == 2, 1, left_ref)


def fill_all(place, piece_refs, put, put_if):
    for slot, piece_ref in enumerate(piece_refs):
        put(slot, piece_ref)


def log_add(first, second):
    peak = jnp.maximum(first, second)
    return peak + jnp.log(jnp.exp(first - peak) + jnp.exp(second - peak))


def log_add3(first, second, third):
    peak = jnp.maximum(jnp.maximum(first, second), third)
    return peak + jnp.log(
        jnp.exp(first - peak) + jnp.exp(second - peak) + jnp.exp(third - peak)
    )


def ctc_pass(stats, slots, notes, frame_count, label_max, kept):
    calls, sources = len(stats), len(stats[0])
    each, _, span = stats[0][0].shape
    count = calls * each
    row_count = count * span
    utterances = notes.shape[0]
    entries = utterances * COLS
    tall = round_up(span, LANES)

    def kernel(slots_ref, notes_ref, *refs):
        (
            out_ref,
            high_ref,
            low_ref,
            loss_ref,
            turn_ref,
            emission_ref,
            emit_blank,
            emit_label,
            blank_fwd,
            label_fwd,
            blank_bwd,
            label_bwd,
            occupancy_ref,
        ) = refs[calls * sources :]
        place = lax.broadcasted_iota(jnp.int32, (COLS, span), 0)
        turn_ref[...] = jnp.zeros(turn_ref.shape, jnp.float32)
        for slot in range(count):
            found = []
            for k in range(sources):
                where = slots_ref[k * count + slot]
                part = refs[k][where % each]
                for other in range(1, calls):
                    later = refs[other * sources + k][where % each]
                    part = jnp.where(where >= other * each, later, part)
                found.append(part)
            joined = found[0]
            peak = found[0][PEAK : PEAK + 1]
            for other in found[1:]:
                joined = joined + other
                peak = jnp.maximum(peak, other[PEAK : PEAK + 1])
            total = jnp.zeros((1, span), jnp.float32)
            for other in found:
                total = total + other[TOTAL : TOTAL + 1] * jnp.exp(other[PEAK : PEAK + 1] - peak)
            log_total = peak + jnp.log(total)
            turn_ref[:COLS, :span] = jnp.where(place == TOTAL, log_total, joined - log_total)
            emission_ref[slot * span : (slot + 1) * span] = jnp.transpose(turn_ref[...], (1, 0))[
                :span
            ]

        lane = lax.broadcasted_iota(jnp.int32, (utterances, LANES), 1)
        is_label = lane < label_max
        is_blank = lane <= label_max
        names = jnp.where(is_label, notes_ref[...], 0)
        earlier = pltpu.roll(names, 1, 1)
        skip = is_label & (lane >= 1) & (names != 0) & (names != earlier)
        later = pltpu.roll(names, LANES - 1, 1)
        skip_next = (lane < label_max - 1) & (later != 0) & (later != names)
        frames = notes_ref[:, label_max : label_max + 1]
        counts = notes_ref[:, label_max + 1 : label_max + 2]
        ends_blank = jnp.where(lane == counts, 0.0, LOG_ZERO)
        ends_label = jnp.where(lane == counts - 1, 0.0, LOG_ZERO)

        def spread(step, carry):
            row = emission_ref[pl.ds(step, utterances, stride=frame_count), :]
            blank = jnp.sum(jnp.where(lane == label_max, row, 0.0), axis=1, keepdims=True)
            emit_blank[step] = jnp.where(is_blank, blank, LOG_ZERO)
            emit_label[step] = jnp.where(is_label, row, LOG_ZERO)
            return carry

        lax.fori_loop(0, frame_count, spread, 0, unroll=16)

        def advance(step, carry):
            fwd_blank, fwd_label, bwd_blank, bwd_label = carry
            moved = jnp.where(lane == 0, LOG_ZERO, pltpu.roll(fwd_label, 1, 1))
            new_blank = log_add(fwd_blank, moved) + emit_blank[step]
            new_label = (
                log_add3(fwd_label, fwd_blank, jnp.where(skip, moved, LOG_ZERO))
                + emit_label[step]
            )
            alive = step < frames
            fwd_blank = jnp.where(alive, new_blank, fwd_blank)
            fwd_label = jnp.where(alive, new_label, fwd_label)
            blank_fwd[step] = fwd_blank
            label_fwd[step] = fwd_label

            back = frame_count - 1 - step
            out_blank = bwd_blank + emit_blank[back + 1]
            out_label = bwd_label + emit_label[back + 1]
            next_blank = pltpu.roll(out_blank, LANES - 1, 1)
            next_label = jnp.where(skip_next, pltpu.roll(out_label, LANES - 1, 1), LOG_ZERO)
            ended = back >= frames - 1
            bwd_blank = jnp.where(ended, ends_blank, log_add(out_blank, out_label))
            bwd_label = jnp.where(
                ended, ends_label, log_add3(out_label, next_blank, next_label)
            )
            blank_bwd[back] = bwd_blank
            label_bwd[back] = bwd_label
            return (fwd_blank, fwd_label, bwd_blank, bwd_label)

        first_blank = jnp.where(lane == 0, emit_blank[0], LOG_ZERO)
        first_label = jnp.where(lane == 0, emit_label[0], LOG_ZERO)
        blank_fwd[0] = first_blank
        label_fwd[0] = first_label
        blank_bwd[frame_count - 1] = ends_blank
        label_bwd[frame_count - 1] = ends_label
        fwd_blank, fwd_label, _, _ = lax.fori_loop(
            1, frame_count, advance, (first_blank, first_label, ends_blank, ends_label), unroll=4
        )
        end_state = jnp.sum(jnp.where(lane == counts, fwd_blank, 0.0), axis=1, keepdims=True)
        near_state = jnp.sum(jnp.where(lane == counts - 1, fwd_label, 0.0), axis=1, keepdims=True)
        log_like = log_add(end_state, near_state)
        turned_losses = jnp.transpose(jnp.broadcast_to(-log_like, (utterances, LANES)), (1, 0))
        loss_ref[...] = turned_losses[:1, :kept]

        def occupy(step, carry):
            blank = jnp.exp(blank_fwd[step] + blank_bwd[step] - log_like)
            label = jnp.exp(label_fwd[step] + label_bwd[step] - log_like)
            blank = jnp.sum(jnp.where(is_blank, blank, 0.0), axis=1, keepdims=True)
            label = jnp.where(is_label, label, 0.0)
            whole = blank + jnp.sum(label, axis=1, keepdims=True)
            filled = jnp.where(lane == label_max, blank, label)
            filled = jnp.where(lane == WHOLE, whole, filled)
            filled = jnp.where(step < frames, -filled, 0.0)
            row = emission_ref[pl.ds(step, utterances, stride=frame_count), :]
            occupancy_ref[pl.ds(step, utterances, stride=frame_count), :] = jnp.where(
                lane == TOTAL, row, filled
            )
            return carry

        lax.fori_loop(0, frame_count, occupy, 0, unroll=16)
        turned = jnp.transpose(occupancy_ref[...], (1, 0))[:COLS]
        out_ref[...] = turned
        row_place = lax.broadcasted_iota(jnp.int32, (COLS, row_count), 0)
        owner = lax.broadcasted_iota(jnp.int32, (COLS, row_count), 1) // frame_count
        source = jnp.where(row_place < WHOLE, turned, 0.0)
        for utterance in range(utterances):
            part = jnp.where(owner == utterance, source, 0.0)
            high = part.astype(jnp.bfloat16)
            high_ref[utterance * COLS : (utterance + 1) * COLS] = high
            low_ref[utterance * COLS : (utterance + 1) * COLS] = (
                part - high.astype(jnp.float32)
            ).astype(jnp.bfloat16)

    held = pltpu.VMEM((frame_count, utterances, LANES), jnp.float32)
    table = pltpu.VMEM((row_count, LANES), jnp.float32)
    return call(
        kernel,
        (
            jax.ShapeDtypeStruct((COLS, row_count), jnp.float32),
            bf16_rows(entries, row_count),
            bf16_rows(entries, row_count),
            jax.ShapeDtypeStruct((1, kept), jnp.float32),
        ),
        1 << 26,
        in_specs=[smem_spec()] + [vmem_spec()] * (1 + calls * sources),
        out_specs=tuple(vmem_spec() for _ in range(4)),
        scratch_shapes=[pltpu.VMEM((LANES, tall), jnp.float32), table]
        + [held] * 6
        + [table],
    )(slots, notes, *[value for group in stats for value in group])


def head_gradient(logits, rows, occupancy, high, low, places, order, outputs, each):
    count = len(logits)
    row_count, width = rows[0].shape
    entries = places.shape[1]
    blocks = outputs * each

    def kernel(order_ref, *refs):
        logits_refs, rows_refs = refs[:count], refs[count : 2 * count]
        occupancy_ref, high_ref, low_ref, places_ref = refs[2 * count : 2 * count + 4]
        out_refs = refs[2 * count + 4 :]
        for block in range(blocks):
            start = pl.multiple_of(order_ref[block] * BLOCK_ROWS, BLOCK_ROWS)
            entry = start + lax.broadcasted_iota(jnp.int32, (BLOCK_ROWS, entries), 0)
            select = as_mask(entry == places_ref[...])
            total = None
            for g in range(count):
                lanes = slice(g * row_count, (g + 1) * row_count)
                scattered = lax.dot_general(
                    select, high_ref[:, lanes], NN, preferred_element_type=jnp.float32
                ) + lax.dot_general(
                    select, low_ref[:, lanes], NN, preferred_element_type=jnp.float32
                )
                whole = occupancy_ref[WHOLE : WHOLE + 1, lanes]
                log_total = occupancy_ref[TOTAL : TOTAL + 1, lanes]
                values = logits_refs[g][pl.ds(start, BLOCK_ROWS), :]
                grad = (scattered - jnp.exp(values - log_total) * whole).astype(jnp.bfloat16)
                part = lax.dot_general(
                    grad, rows_refs[g][...], NN, preferred_element_type=jnp.float32
                )
                total = part if total is None else total + part
            out_refs[block // each][
                block % each * BLOCK_ROWS : (block % each + 1) * BLOCK_ROWS
            ] = total.astype(jnp.bfloat16)

    return call(
        kernel,
        tuple(bf16_rows(each * BLOCK_ROWS, width) for _ in range(outputs)),
        2 * blocks * BLOCK_ROWS * count * row_count * (width + 2 * entries),
        LARGE_LIMIT,
        in_specs=[smem_spec()] + [vmem_spec()] * (2 * count + 4),
        out_specs=tuple(vmem_spec() for _ in range(outputs)),
    )(order, *logits, *rows, occupancy, high, low, places)


def assemble(pieces, offsets, height, whole=None):
    count = len(pieces)
    part, width = pieces[0].shape
    short = height % part
    started = [] if whole is None else [whole]

    def kernel(offsets_ref, *refs):
        out_ref, sems = refs[count + len(started) :]

        def each(act):
            for index in range(count):
                offset = pl.multiple_of(offsets_ref[index], part)

                @pl.when(offset + part <= height)
                def _():
                    act(
                        pltpu.make_async_copy(
                            refs[index], out_ref.at[pl.ds(offset, part)], sems.at[index]
                        )
                    )

                if short:

                    @pl.when(offset + part > height)
                    def _():
                        act(
                            pltpu.make_async_copy(
                                refs[index].at[pl.ds(0, short)],
                                out_ref.at[pl.ds(height - short, short)],
                                sems.at[index],
                            )
                        )

        each(lambda copy: copy.start())
        each(lambda copy: copy.wait())

    anywhere = pl.BlockSpec(memory_space=pl.ANY)
    return call(
        kernel,
        bf16_rows(height, width),
        in_specs=[smem_spec()] + [vmem_spec()] * count + [anywhere] * len(started),
        out_specs=anywhere,
        scratch_shapes=[pltpu.SemaphoreType.DMA((count,))],
        input_output_aliases={} if whole is None else {1 + count: 0},
    )(offsets, *pieces, *started)


def swap(value, axis):
    return lax.ppermute(value, axis, [(0, 1), (1, 0)])


def rotate(value, axis, by):
    count = lax.axis_size(axis)
    return lax.ppermute(value, axis, [(i, (i + by) % count) for i in range(count)])


def after(value, *others):
    return lax.optimization_barrier((value,) + others)[0]


def line_near(value):
    left = lax.ppermute(value, "expert", [(1, 0), (2, 1), (3, 2)])
    right = lax.ppermute(value, "expert", [(0, 1), (1, 2), (2, 3)])
    return left, right


def line_far(left, right):
    return (
        lax.ppermute(left, "expert", [(1, 0), (2, 1)]),
        lax.ppermute(right, "expert", [(1, 2), (2, 3)]),
    )


def line_end(left_far, right_far):
    return (
        lax.ppermute(left_far, "expert", [(1, 0)]),
        lax.ppermute(right_far, "expert", [(2, 3)]),
    )


LINE_ORDER = np.array([[0, 1, 2, 3], [1, 2, 3, 0], [2, 1, 0, 3], [3, 2, 1, 0]])


def slot_orders(count):
    return LINE_ORDER if count == 4 else np.tile(np.arange(count), (count, 1))


def slot_tables(count):
    orders = slot_orders(count)
    tables = np.zeros((count, count, count), np.int32)
    for member in range(count):
        for k in range(count):
            source = (member + k) % count
            for slot in range(count):
                tables[member, k, slot] = list(orders[source]).index(orders[member][slot])
    return tables.reshape(count, count * count)


def wide(ref, start, size):
    return ref[pl.ds(start, size), :].astype(jnp.float32)


def sum_sent(own, came, places):
    height, width = own.shape
    part = height // 4

    def kernel(places_ref, own_ref, came_ref, *out_refs):
        section, outer = places_ref[0], places_ref[1]
        starts = (
            (1 - outer) * part,
            outer * part,
            (2 + 1 - section) * part,
            (2 + section) * part,
        )
        for start, out_ref in zip(starts, out_refs):
            start = pl.multiple_of(start, part)
            out_ref[...] = (wide(own_ref, start, part) + wide(came_ref, start, part)).astype(
                jnp.bfloat16
            )

    return call(
        kernel,
        tuple(bf16_rows(part, width) for _ in range(4)),
        1 << 20,
        in_specs=[smem_spec()] + [vmem_spec()] * 2,
        out_specs=tuple(vmem_spec() for _ in range(4)),
    )(places, own, came)


def sum_kept(own, came, arrived, places, keep):
    height, width = own.shape
    part = height // 4
    count = len(arrived) // 2

    def kernel(places_ref, own_ref, came_ref, *refs):
        section, outer = places_ref[0], places_ref[1]
        if not keep:
            section, outer = 1 - section, 1 - outer
        for side, start in enumerate((outer * part, (2 + section) * part)):
            start = pl.multiple_of(start, part)
            total = wide(own_ref, start, part) + wide(came_ref, start, part)
            for ref in refs[side * count : (side + 1) * count]:
                total = total + ref[...].astype(jnp.float32)
            refs[2 * count + side][...] = total.astype(jnp.bfloat16)

    return call(
        kernel,
        (bf16_rows(part, width), bf16_rows(part, width)),
        1 << 20,
        in_specs=[smem_spec()] + [vmem_spec()] * (2 + 2 * count),
        out_specs=(vmem_spec(), vmem_spec()),
    )(places, own, came, *arrived)


def per_device(
    frames,
    norm_gain,
    router,
    w_in,
    w_out,
    routing,
    head_gain,
    head_weight,
    frame_lengths,
    labels,
    label_lengths,
):
    sections = lax.axis_size("section")
    section_id = lax.axis_index("section")
    group_size = lax.axis_size("expert")
    member = lax.axis_index("expert")
    outer_size = lax.axis_size("dpo")
    inner_size = lax.axis_size("dpi")
    core = lax.axis_index("dpi")
    micro, utt_dev, frame_count, width = frames.shape
    label_max = labels.shape[2]
    experts = w_in.shape[1] * group_size
    pair_count = micro * utt_dev
    per_section = pair_count // sections
    first_pair = section_id * per_section
    share = (utt_dev * frame_count * 9 + 8 * experts - 1) // (8 * experts)
    filled = share * -(-per_section // utt_dev)
    capacity = round_up(filled + 1, 8)
    span = per_section * frame_count
    member_ref = member.astype(jnp.int32).reshape(1)

    def mine_of(value):
        return lax.dynamic_slice_in_dim(value, first_pair, per_section, 0)

    def exchange(blocks, sign):
        return [blocks[0]] + [
            rotate(blocks[k], "expert", sign * k) for k in range(1, group_size)
        ]

    def lanes_of(ids):
        return jnp.pad(mine_of(ids), ((0, 0), (0, LANES - frame_count)), constant_values=-1)

    current = lax.dynamic_slice_in_dim(
        frames.reshape(pair_count * frame_count, width), first_pair * frame_count, span, 0
    )
    own_ids = routing.reshape(pair_count, frame_count)
    paired = sections == 2 and inner_size == 2
    if paired:
        other_ids = swap(own_ids, "section")
        all_ids = [
            jnp.where(section_id == layer, own_ids, other_ids) for layer in range(sections)
        ]
    else:
        all_ids = lax.all_gather(own_ids, "section")
    layer_ids = [lanes_of(all_ids[layer]) for layer in range(sections)]
    own_table = jnp.concatenate(
        [
            norm_gain,
            jnp.zeros((7, width), jnp.float32),
            jnp.transpose(router[0]).astype(jnp.float32),
            jnp.zeros((round_up(experts, 8) - experts, width), jnp.float32),
        ],
        axis=0,
    )
    own = (w_in[0, 0], w_out[0, 0])
    layers = []
    if paired:
        other_table = swap(own_table, "section")
        sent_in, sent_out = half_weights(core.astype(jnp.int32).reshape(1), *own)
        came_in = swap(sent_in, "section")
        came_out = swap(sent_out, "section")
    else:
        all_tables = lax.all_gather(own_table, "section")
        all_in = lax.all_gather(own[0], "section")
        all_out = lax.all_gather(own[1], "section")
        for layer in range(sections):
            chosen = (all_in[layer], all_out[layer])
            layers.append(((all_tables[layer],), chosen, [], jnp.ones((1,), jnp.int32)))

    outgoing = dispatch(current, layer_ids[0], member_ref, experts, capacity, frame_count)
    received = exchange(outgoing, 1)
    if paired:
        (came_in, came_out), received = lax.optimization_barrier(((came_in, came_out), received))
        other = [(came_in, came_out), (swap(came_in, "dpi"), swap(came_out, "dpi"))]
        for layer in range(sections):
            mine = (section_id == layer).astype(jnp.int32).reshape(1)
            layers.append(((own_table, other_table), own, other, mine))

    labels, frame_lengths, label_lengths = lax.optimization_barrier(
        (labels, frame_lengths, label_lengths, outgoing[0])
    )[:3]
    notes = jnp.concatenate(
        [
            mine_of(labels.reshape(pair_count, label_max)),
            mine_of(frame_lengths.reshape(pair_count, 1)),
            mine_of(label_lengths.reshape(pair_count, 1)),
        ],
        axis=1,
    )
    notes = jnp.pad(notes, ((0, 0), (0, COLS - label_max - 2))).reshape(1, per_section * COLS)
    notes = jnp.pad(notes, ((0, 0), (0, LANES - per_section * COLS)))
    notes = jnp.concatenate([notes // LANES, notes % LANES], axis=1).astype(jnp.float32)
    notes = jnp.pad(notes, ((0, 0), (0, width - 2 * LANES)))
    shard = head_weight.shape[1]
    weight_rows = jnp.transpose(head_weight)
    line = group_size == 4
    tables = jnp.asarray(slot_tables(group_size))
    slots = lax.dynamic_index_in_dim(tables, member, 0, keepdims=False)
    outer = lax.axis_index("dpo")
    blocks = -(-shard // BLOCK_ROWS)
    tree = paired and outer_size == 2 and blocks == 8

    def pair_of(side, first, second):
        return [side * 4 + first, side * 4 + 2 + second]

    def offset_of(side, s, y):
        base = side * 4 * BLOCK_ROWS
        part = BLOCK_ROWS // 2
        return [
            base + s * BLOCK_ROWS + y * part,
            base + 2 * BLOCK_ROWS + y * BLOCK_ROWS + s * part,
        ]

    def whole_numbers(values):
        return jnp.stack([jnp.asarray(value, jnp.int32) for value in values])

    here, there = (section_id, outer), (1 - section_id, 1 - outer)
    sibling_order = whole_numbers(pair_of(1 - core, *there) + pair_of(1 - core, *here))
    sent_order = whole_numbers(pair_of(core, *there))
    kept_order = whole_numbers(pair_of(core, *here))
    chip_place = whole_numbers(here)
    first_offsets, last_offsets = [], offset_of(core, *there) + offset_of(1 - core, *there)
    for side in (core, 1 - core):
        for s, y in (here, (section_id, 1 - outer), (1 - section_id, outer)):
            first_offsets += offset_of(side, s, y)
    first_offsets, last_offsets = whole_numbers(first_offsets), whole_numbers(last_offsets)
    early = (
        notes,
        slots,
        head_gain.reshape(1, width),
        layer_ids[1:],
        sibling_order,
        sent_order,
        kept_order,
        chip_place,
        first_offsets,
        last_offsets,
    )
    early, received = lax.optimization_barrier((early, received))
    notes, slots, head_row, later_ids, sibling_order, sent_order = early[:6]
    kept_order, chip_place, first_offsets, last_offsets = early[6:]
    layer_ids = [layer_ids[0]] + list(later_ids)

    for layer in range(sections):
        choices, weights, others, pick_own = layers[layer]
        note = notes if layer == 0 else None
        done = run_expert(received, choices, weights, others, pick_own, filled, note)
        returned = exchange(done, -1)
        if layer == 0:
            found = returned
            if not line:
                stacked = jnp.stack(returned)
                found = [
                    lax.dynamic_index_in_dim(stacked, (k - member) % group_size, 0, keepdims=False)
                    for k in range(group_size)
                ]
        if layer < sections - 1:
            current, outgoing = combine_and_dispatch(
                current,
                returned,
                layer_ids[layer],
                choices,
                pick_own,
                layer_ids[layer + 1],
                member_ref,
                experts,
                capacity,
                frame_count,
            )
            received = exchange(outgoing, 1)
            if layer == 0:
                found = [after(found[0], current)] + list(found[1:])
                label_weight, places, names = label_rows(
                    weight_rows, found, member_ref, per_section, filled, label_max, line
                )
                received, label_weight = lax.optimization_barrier((received, label_weight))
        else:
            normed = combine_and_norm(
                current,
                returned,
                layer_ids[layer],
                choices,
                pick_own,
                head_row,
                member_ref,
                experts,
                capacity,
                frame_count,
            )

    def logits_of(fill, first, count, pieces):
        return head_logits(
            fill, first, count, pieces, member_ref, weight_rows, label_weight, frame_count
        )

    if line:
        left, right = line_near(normed)
        far = line_far(left, right)
        heads = [logits_of(fill_near, 0, 2, [normed, left, right])]
        far, heads[0] = lax.optimization_barrier((far, heads[0]))
        end = line_end(*far)
        heads.append(logits_of(fill_far, 2, 2, [*far, *end, left, right]))
        found = [
            [head[2]] + [rotate(head[2], "expert", -k) for k in range(1, group_size)]
            for head in heads
        ]
    else:
        gathered = lax.all_gather(normed, "expert")
        pieces = [gathered[k] for k in range(group_size)]
        heads = [logits_of(fill_all, 0, group_size, pieces)]
        gathered = lax.all_gather(heads[0][2], "expert")
        found = [
            [
                lax.dynamic_index_in_dim(gathered, (member + k) % group_size, 0, keepdims=False)
                for k in range(group_size)
            ]
        ]
    kept_losses = per_section if line else group_size * per_section
    occupancy, high, low, losses = ctc_pass(
        found, slots, names, frame_count, label_max, kept_losses
    )
    if not line:
        losses = lax.dynamic_slice(losses, (0, member * per_section), (1, per_section))
    losses = jnp.transpose(losses)

    def gradient(order, outputs, each):
        return head_gradient(
            [head[0] for head in heads],
            [head[1] for head in heads],
            occupancy,
            high,
            low,
            places,
            order,
            outputs,
            each,
        )

    if tree:
        sibling_sent, sibling_kept = gradient(sibling_order, 2, 2)
        came_sent, came_kept = swap(sibling_sent, "dpi"), swap(sibling_kept, "dpi")
        own_sent = gradient(after(sent_order, sibling_sent), 1, 2)[0]
        a_far, a_near, b_far, b_near = sum_sent(own_sent, came_sent, chip_place)
        kept_order = after(kept_order, a_far)
        a_far, b_far = swap(a_far, "section"), swap(b_far, "dpo")
        a_near, b_near = swap(a_near, "section"), swap(b_near, "dpo")
        own_kept = gradient(kept_order, 1, 2)[0]
        a_on, b_on = sum_kept(own_kept, came_kept, [a_far, b_far], chip_place, False)
        a_in, b_in = swap(a_on, "dpo"), swap(b_on, "section")
        a, b = sum_kept(own_kept, came_kept, [a_near, a_in, b_near, b_in], chip_place, True)
        a_y, b_x = swap(a, "dpo"), swap(b, "section")
        b_y, a_x = swap(b, "dpo"), swap(a, "section")
        a_xy, b_xy = swap(a_y, "section"), swap(b_x, "dpo")
        b_y, a_x = lax.optimization_barrier((b_y, a_x, a_xy, b_xy))[:2]
        mine = [a, b, a_y, b_y, a_x, b_x]
        theirs = [swap(value, "dpi") for value in mine]
        whole = assemble(mine + theirs, first_offsets, shard)
        last = [a_xy, b_xy, swap(a_xy, "dpi"), swap(b_xy, "dpi")]
        whole = assemble(last, last_offsets, shard, whole)
    else:
        partial = gradient(jnp.arange(blocks, dtype=jnp.int32), 1, blocks)[0][:shard]
        whole = lax.psum(partial.astype(jnp.float32), ("section", "dpo", "dpi")).astype(
            jnp.bfloat16
        )
    return (losses, jnp.transpose(whole))


def solution(mesh):
    sections, group_size, spread = (mesh.shape[name] for name in ("section", "expert", "dp"))
    inner = 2 if spread % 2 == 0 else 1
    split = Mesh(
        mesh.devices.reshape(sections, group_size, spread // inner, inner),
        ("section", "expert", "dpo", "dpi"),
    )
    block = ("expert", "dpo", "dpi")
    placed = (
        P(None, block, None, None),
        P("section", None),
        P("section", None, None),
        P("section", "expert", None, None),
        P("section", "expert", None, None),
        P("section", None, block, None, None),
        P(),
        P(None, "expert"),
        P(None, block),
        P(None, block, None),
        P(None, block),
    )
    return jax.shard_map(
        per_device,
        mesh=split,
        in_specs=placed,
        out_specs=(P("section", block), P(None, "expert")),
        check_vma=False,
    )
```

```python
import jax
import jax.numpy as jnp
import numpy as np
from jax import lax
from jax.experimental import pallas as pl
from jax.experimental.pallas import tpu as pltpu
from jax.sharding import Mesh, PartitionSpec as P

EPSILON = 1e-06
LOG_ZERO = -1e30
VMEM_LIMIT = 12 * 1024 * 1024
LARGE_LIMIT = 24 * 1024 * 1024
LANES = 128
COLS = 16
PEAK, TOTAL, WHOLE = COLS - 3, COLS - 2, COLS - 3
BLOCK_ROWS = 256
NT = (((1,), (1,)), ((), ()))
NN = (((1,), (0,)), ((), ()))


def round_up(value, unit):
    return -(-value // unit) * unit


def vmem_spec():
    return pl.BlockSpec(memory_space=pltpu.VMEM)


def smem_spec():
    return pl.BlockSpec(memory_space=pltpu.SMEM)


def call(kernel, out_shape, flops=0, limit=VMEM_LIMIT, **options):
    return pl.pallas_call(
        kernel,
        out_shape=out_shape,
        compiler_params=pltpu.CompilerParams(vmem_limit_bytes=limit),
        cost_estimate=pl.CostEstimate(flops=flops, bytes_accessed=0, transcendentals=0),
        **options,
    )


def bf16_rows(count, width):
    return jax.ShapeDtypeStruct((count, width), jnp.bfloat16)


def as_mask(values):
    return values.astype(jnp.float32).astype(jnp.bfloat16)


def split_rows(values, out_refs, spare=None, note=None):
    size, width = out_refs[0].shape
    for turn, out_ref in enumerate(out_refs):
        part = values[turn * size : (turn + 1) * size]
        if note is not None:
            row = lax.broadcasted_iota(jnp.int32, (size, width), 0)
            part = jnp.where(row == spare, note, part)
        out_ref[...] = part.astype(jnp.bfloat16)


def join_rows(refs):
    return jnp.concatenate([ref[...].astype(jnp.float32) for ref in refs], axis=0)


def rms_scale(values, gain):
    values = values.astype(jnp.float32)
    scale = lax.rsqrt(jnp.mean(values * values, axis=-1, keepdims=True) + EPSILON)
    return (values * scale * gain).astype(jnp.bfloat16)


def expert_column(ids, frame_count):
    pairs = ids.shape[0]
    square = jnp.concatenate(
        [ids.astype(jnp.float32), jnp.full((LANES - pairs, LANES), -1.0, jnp.float32)], axis=0
    )
    turned = jnp.transpose(square, (1, 0)).astype(jnp.int32)
    return jnp.concatenate([turned[:frame_count, p : p + 1] for p in range(pairs)], axis=0)


def placement(column, member, experts, capacity):
    count = column.shape[0]
    relative = column ^ member
    lane = lax.broadcasted_iota(jnp.int32, (count, LANES), 1)
    one_hot = (lane == relative).astype(jnp.float32)
    before = lax.broadcasted_iota(jnp.int32, (count, count), 1) <= lax.broadcasted_iota(
        jnp.int32, (count, count), 0
    )
    rank = lax.dot_general(
        as_mask(before), one_hot.astype(jnp.bfloat16), NN, preferred_element_type=jnp.float32
    )
    start = (lane * capacity - 1).astype(jnp.float32)
    slots = jnp.sum(one_hot * (rank + start), axis=1, keepdims=True).astype(jnp.int32)
    places = lax.broadcasted_iota(jnp.int32, (count, experts * capacity), 1)
    return (places == slots).astype(jnp.float32)


def scatter_rows(rows, ids, member, experts, capacity, frame_count, out_refs):
    count = rows.shape[0]
    chosen = placement(expert_column(ids, frame_count), member, experts, capacity)
    tall = round_up(count, LANES)
    if tall > count:
        chosen = jnp.concatenate(
            [chosen, jnp.zeros((tall - count, chosen.shape[1]), jnp.float32)], axis=0
        )
    pick = jnp.transpose(chosen, (1, 0))[:, :count].astype(jnp.bfloat16)
    placed = lax.dot_general(pick, rows, NN, preferred_element_type=jnp.float32)
    split_rows(placed, out_refs)


def combine_rows(rows, returned, ids, table, member, experts, capacity, frame_count):
    column = expert_column(ids, frame_count)
    pick = placement(column, member, experts, capacity).astype(jnp.bfloat16)
    normed = rms_scale(rows, table[:1])
    router = jnp.concatenate(
        [table[8:], jnp.zeros((LANES + 8 - table.shape[0], rows.shape[1]), jnp.float32)], axis=0
    ).astype(jnp.bfloat16)
    logits = lax.dot_general(normed, router, NT, preferred_element_type=jnp.float32)
    lane = lax.broadcasted_iota(jnp.int32, logits.shape, 1)
    gate = jax.nn.sigmoid(jnp.sum(jnp.where(lane == column, logits, 0.0), axis=1, keepdims=True))
    stacked = join_rows(returned).astype(jnp.bfloat16)
    mixed = lax.dot_general(pick, stacked, NN, preferred_element_type=jnp.float32)
    return (rows.astype(jnp.float32) + gate * mixed).astype(jnp.bfloat16)


def dispatch(rows, ids, member, experts, capacity, frame_count):
    width = rows.shape[1]

    def kernel(member_ref, rows_ref, ids_ref, *out_refs):
        scatter_rows(
            rows_ref[...], ids_ref[...], member_ref[0], experts, capacity, frame_count, out_refs
        )

    return call(
        kernel,
        tuple(bf16_rows(capacity, width) for _ in range(experts)),
        1 << 27,
        in_specs=[smem_spec()] + [vmem_spec()] * 2,
        out_specs=tuple(vmem_spec() for _ in range(experts)),
    )(member, rows, ids)


def pick_table(pick_ref, tables):
    if len(tables) == 1:
        return tables[0][...]
    return jnp.where(pick_ref[0] == 1, tables[0][...], tables[1][...])


def run_expert(received, tables, own, other, pick_own, spare, note):
    count = len(received)
    capacity, width = received[0].shape
    others, choices = len(other), len(tables)
    noted = [] if note is None else [note]

    def kernel(pick_ref, in_ref, out_weight_ref, *refs):
        table_refs, refs = refs[:choices], refs[choices:]
        other_refs, refs = refs[: 2 * others], refs[2 * others :]
        received_refs, refs = refs[:count], refs[count:]
        out_refs = refs[len(noted) :]

        def work(pieces):
            gain = pick_table(pick_ref, table_refs)[:1]
            normed = rms_scale(join_rows(received_refs), gain)
            total = None
            for weight_in, weight_out in pieces:
                hidden = lax.dot_general(
                    normed, weight_in[...], NN, preferred_element_type=jnp.float32
                )
                active = (hidden / (1.0 + jnp.exp(-hidden))).astype(jnp.bfloat16)
                part = lax.dot_general(
                    active, weight_out[...], NN, preferred_element_type=jnp.float32
                )
                total = part if total is None else total + part
            split_rows(total, out_refs, spare, refs[0][...] if noted else None)

        if others == 0:
            work([(in_ref, out_weight_ref)])
            return

        @pl.when(pick_ref[0] == 1)
        def _():
            work([(in_ref, out_weight_ref)])

        @pl.when(pick_ref[0] != 1)
        def _():
            work([(other_refs[2 * i], other_refs[2 * i + 1]) for i in range(others)])

    flat = [weight for pair in other for weight in pair]
    return call(
        kernel,
        tuple(bf16_rows(capacity, width) for _ in range(count)),
        4 * count * capacity * width * own[0].shape[1],
        in_specs=[smem_spec()] + [vmem_spec()] * (2 + choices + 2 * others + count + len(noted)),
        out_specs=tuple(vmem_spec() for _ in range(count)),
    )(pick_own, *own, *tables, *flat, *received, *noted)


def combine_and_dispatch(
    rows, returned, ids, tables, pick_own, next_ids, member, experts, capacity, frame_count
):
    width = rows.shape[1]
    choices = len(tables)

    def kernel(member_ref, pick_ref, rows_ref, ids_ref, next_ref, *refs):
        table_refs, refs = refs[:choices], refs[choices:]
        returned_refs, x_ref, out_refs = refs[:experts], refs[experts], refs[experts + 1 :]
        mixed = combine_rows(
            rows_ref[...],
            returned_refs,
            ids_ref[...],
            pick_table(pick_ref, table_refs),
            member_ref[0],
            experts,
            capacity,
            frame_count,
        )
        x_ref[...] = mixed
        scatter_rows(
            mixed, next_ref[...], member_ref[0], experts, capacity, frame_count, out_refs
        )

    shapes = (bf16_rows(*rows.shape),) + tuple(
        bf16_rows(capacity, width) for _ in range(experts)
    )
    result = call(
        kernel,
        shapes,
        1 << 28,
        in_specs=[smem_spec()] * 2 + [vmem_spec()] * (3 + choices + experts),
        out_specs=tuple(vmem_spec() for _ in shapes),
    )(member, pick_own, rows, ids, next_ids, *tables, *returned)
    return result[0], result[1:]


def combine_and_norm(
    rows, returned, ids, tables, pick_own, head_gain, member, experts, capacity, frame_count
):
    choices = len(tables)

    def kernel(member_ref, pick_ref, rows_ref, ids_ref, head_ref, *refs):
        table_refs, refs = refs[:choices], refs[choices:]
        final = combine_rows(
            rows_ref[...],
            refs[:experts],
            ids_ref[...],
            pick_table(pick_ref, table_refs),
            member_ref[0],
            experts,
            capacity,
            frame_count,
        )
        refs[experts][...] = rms_scale(final, head_ref[...])

    return call(
        kernel,
        bf16_rows(*rows.shape),
        1 << 28,
        in_specs=[smem_spec()] * 2 + [vmem_spec()] * (3 + choices + experts),
        out_specs=vmem_spec(),
    )(member, pick_own, rows, ids, head_gain, *tables, *returned)


def half_weights(core, weight_in, weight_out):
    width, hidden = weight_in.shape
    half = hidden // 2

    def kernel(core_ref, in_ref, out_ref, half_in, half_out, sems):
        start = pl.multiple_of(core_ref[0] * half, half)
        copies = (
            pltpu.make_async_copy(in_ref.at[:, pl.ds(start, half)], half_in, sems.at[0]),
            pltpu.make_async_copy(out_ref.at[pl.ds(start, half)], half_out, sems.at[1]),
        )
        for copy in copies:
            copy.start()
        for copy in copies:
            copy.wait()

    return call(
        kernel,
        (bf16_rows(width, half), bf16_rows(half, width)),
        1 << 20,
        in_specs=[smem_spec()] + [pl.BlockSpec(memory_space=pl.ANY)] * 2,
        out_specs=(vmem_spec(), vmem_spec()),
        scratch_shapes=[pltpu.SemaphoreType.DMA((2,))],
    )(core, weight_in, weight_out)


def block_list(shard):
    return [(i, min(BLOCK_ROWS, shard - i)) for i in range(0, shard, BLOCK_ROWS)]


def label_rows(weight, notes, member, pairs, spare, label_max, line):
    shard, width = weight.shape
    sources = len(notes)
    utterances = sources * pairs
    entries = utterances * COLS

    def kernel(member_ref, weight_ref, *refs):
        note_refs = refs[:sources]
        out_ref, places_ref, names_ref, turned_ref = refs[sources:]
        place = member_ref[0]
        found = []
        for ref in note_refs:
            row = ref[...].astype(jnp.float32)[spare : spare + 1]
            found.append((row[:, :LANES] * LANES + row[:, LANES : 2 * LANES]).astype(jnp.int32))
        if line:
            ends = (place == 0) | (place == 3)
            found = [
                found[0],
                found[1],
                jnp.where(ends, found[2], found[3]),
                jnp.where(ends, found[3], found[2]),
            ]
        names_ref[...] = jnp.zeros(names_ref.shape, jnp.int32)
        for slot in range(sources):
            for pair in range(pairs):
                row = slot * pairs + pair
                names_ref[row : row + 1, :COLS] = found[slot][:, pair * COLS : (pair + 1) * COLS]
        lane = lax.broadcasted_iota(jnp.int32, (utterances, LANES), 1)
        named = jnp.where(lane < label_max, names_ref[...], jnp.where(lane == label_max, 0, -1))
        local = named - place * shard
        local = jnp.where((named >= 0) & (local >= 0) & (local < shard), local, -1)
        square = jnp.concatenate(
            [
                local.astype(jnp.float32),
                jnp.full((LANES - utterances, LANES), -1.0, jnp.float32),
            ],
            axis=0,
        )
        turned = jnp.transpose(square, (1, 0))
        for utterance in range(utterances):
            turned_ref[utterance * COLS : (utterance + 1) * COLS] = jnp.broadcast_to(
                turned[:COLS, utterance : utterance + 1], (COLS, LANES)
            )
        places = turned_ref[:, :1].astype(jnp.int32)
        places_ref[...] = jnp.transpose(turned_ref[...], (1, 0))[:1].astype(jnp.int32)
        total = jnp.zeros((entries, width), jnp.float32)
        for first, size in block_list(shard):
            entry = first + lax.broadcasted_iota(jnp.int32, (entries, size), 1)
            total = total + lax.dot_general(
                as_mask(entry == places),
                weight_ref[first : first + size],
                NN,
                preferred_element_type=jnp.float32,
            )
        out_ref[...] = total.astype(jnp.bfloat16)

    return call(
        kernel,
        (
            bf16_rows(entries, width),
            jax.ShapeDtypeStruct((1, entries), jnp.int32),
            jax.ShapeDtypeStruct((utterances, LANES), jnp.int32),
        ),
        2 * shard * entries * width,
        LARGE_LIMIT,
        in_specs=[smem_spec()] + [vmem_spec()] * (1 + sources),
        out_specs=tuple(vmem_spec() for _ in range(3)),
        scratch_shapes=[pltpu.VMEM((entries, LANES), jnp.float32)],
    )(member, weight, *notes)


def head_logits(
    fill, first_slot, count, pieces, member, weight, label_weight, frame_count
):
    given = len(pieces)
    span, width = pieces[0].shape
    row_count = count * span
    shard = weight.shape[0]
    height = round_up(shard, BLOCK_ROWS)
    entries = row_count // frame_count * COLS
    first_entry = first_slot * entries // count

    def kernel(member_ref, weight_ref, label_ref, *refs):
        piece_refs = refs[:given]
        logits_ref, rows_ref, stats_ref = refs[given:]

        def put(slot, piece_ref):
            rows_ref[slot * span : (slot + 1) * span] = piece_ref[...]

        def put_if(condition, slot, piece_ref):
            @pl.when(condition)
            def _():
                put(slot, piece_ref)

        fill(member_ref[0], piece_refs, put, put_if)
        peak = jnp.full((1, row_count), LOG_ZERO, jnp.float32)
        total = jnp.zeros((1, row_count), jnp.float32)
        for first, size in block_list(shard):
            logits = lax.dot_general(
                weight_ref[first : first + size],
                rows_ref[...],
                NT,
                preferred_element_type=jnp.float32,
            )
            logits_ref[first : first + size] = logits
            before = peak
            peak = jnp.maximum(before, jnp.max(logits, axis=0, keepdims=True))
            total = total * jnp.exp(before - peak) + jnp.sum(
                jnp.exp(logits - peak), axis=0, keepdims=True
            )
        if height > shard:
            logits_ref[shard:] = jnp.full((height - shard, row_count), LOG_ZERO, jnp.float32)
        crossed = lax.dot_general(
            label_ref[first_entry : first_entry + entries],
            rows_ref[...],
            NT,
            preferred_element_type=jnp.float32,
        )
        owner = lax.broadcasted_iota(jnp.int32, (COLS, row_count), 1) // frame_count
        picked = jnp.zeros((COLS, row_count), jnp.float32)
        for utterance in range(entries // COLS):
            part = crossed[utterance * COLS : (utterance + 1) * COLS]
            picked = picked + jnp.where(owner == utterance, part, 0.0)
        place = lax.broadcasted_iota(jnp.int32, (COLS, row_count), 0)
        stats = jnp.where(place == PEAK, peak, picked)
        stats = jnp.where(place == TOTAL, total, stats)
        for slot in range(count):
            stats_ref[slot] = stats[:, slot * span : (slot + 1) * span]

    return call(
        kernel,
        (
            jax.ShapeDtypeStruct((height, row_count), jnp.float32),
            bf16_rows(row_count, width),
            jax.ShapeDtypeStruct((count, COLS, span), jnp.float32),
        ),
        2 * height * row_count * width,
        LARGE_LIMIT,
        in_specs=[smem_spec()] + [vmem_spec()] * (2 + given),
        out_specs=tuple(vmem_spec() for _ in range(3)),
    )(member, weight, label_weight, *pieces)


def fill_far(place, piece_refs, put, put_if):
    middle, outward, far, last = piece_refs
    ends = (place == 0) | (place == 3)
    put_if(ends, 0, outward)
    put_if(ends, 1, last)
    put_if((place == 1) | (place == 2), 0, middle)
    put_if((place == 1) | (place == 2), 1, far)


def fill_all(place, piece_refs, put, put_if):
    for slot, piece_ref in enumerate(piece_refs):
        put(slot, piece_ref)


def log_add(first, second):
    peak = jnp.maximum(first, second)
    return peak + jnp.log(jnp.exp(first - peak) + jnp.exp(second - peak))


def log_add3(first, second, third):
    peak = jnp.maximum(jnp.maximum(first, second), third)
    return peak + jnp.log(
        jnp.exp(first - peak) + jnp.exp(second - peak) + jnp.exp(third - peak)
    )


def ctc_pass(stats, slots, notes, frame_count, label_max, kept):
    calls, sources = len(stats), len(stats[0])
    each, _, span = stats[0][0].shape
    count = calls * each
    row_count = count * span
    utterances = notes.shape[0]
    entries = utterances * COLS
    tall = round_up(span, LANES)

    def kernel(slots_ref, notes_ref, *refs):
        (
            out_ref,
            high_ref,
            low_ref,
            loss_ref,
            turn_ref,
            emission_ref,
            emit_blank,
            emit_label,
            blank_fwd,
            label_fwd,
            blank_bwd,
            label_bwd,
            occupancy_ref,
        ) = refs[calls * sources :]
        place = lax.broadcasted_iota(jnp.int32, (COLS, span), 0)
        turn_ref[...] = jnp.zeros(turn_ref.shape, jnp.float32)
        for slot in range(count):
            found = []
            for k in range(sources):
                where = slots_ref[k * count + slot]
                part = refs[k][where % each]
                for other in range(1, calls):
                    later = refs[other * sources + k][where % each]
                    part = jnp.where(where >= other * each, later, part)
                found.append(part)
            joined = found[0]
            peak = found[0][PEAK : PEAK + 1]
            for other in found[1:]:
                joined = joined + other
                peak = jnp.maximum(peak, other[PEAK : PEAK + 1])
            total = jnp.zeros((1, span), jnp.float32)
            for other in found:
                total = total + other[TOTAL : TOTAL + 1] * jnp.exp(other[PEAK : PEAK + 1] - peak)
            log_total = peak + jnp.log(total)
            turn_ref[:COLS, :span] = jnp.where(place == TOTAL, log_total, joined - log_total)
            emission_ref[slot * span : (slot + 1) * span] = jnp.transpose(turn_ref[...], (1, 0))[
                :span
            ]

        lane = lax.broadcasted_iota(jnp.int32, (utterances, LANES), 1)
        is_label = lane < label_max
        is_blank = lane <= label_max
        names = jnp.where(is_label, notes_ref[...], 0)
        earlier = pltpu.roll(names, 1, 1)
        skip = is_label & (lane >= 1) & (names != 0) & (names != earlier)
        later = pltpu.roll(names, LANES - 1, 1)
        skip_next = (lane < label_max - 1) & (later != 0) & (later != names)
        frames = notes_ref[:, label_max : label_max + 1]
        counts = notes_ref[:, label_max + 1 : label_max + 2]
        ends_blank = jnp.where(lane == counts, 0.0, LOG_ZERO)
        ends_label = jnp.where(lane == counts - 1, 0.0, LOG_ZERO)

        def spread(step, carry):
            row = emission_ref[pl.ds(step, utterances, stride=frame_count), :]
            blank = jnp.sum(jnp.where(lane == label_max, row, 0.0), axis=1, keepdims=True)
            emit_blank[step] = jnp.where(is_blank, blank, LOG_ZERO)
            emit_label[step] = jnp.where(is_label, row, LOG_ZERO)
            return carry

        lax.fori_loop(0, frame_count, spread, 0, unroll=16)

        def advance(step, carry):
            fwd_blank, fwd_label, bwd_blank, bwd_label = carry
            moved = jnp.where(lane == 0, LOG_ZERO, pltpu.roll(fwd_label, 1, 1))
            new_blank = log_add(fwd_blank, moved) + emit_blank[step]
            new_label = (
                log_add3(fwd_label, fwd_blank, jnp.where(skip, moved, LOG_ZERO))
                + emit_label[step]
            )
            alive = step < frames
            fwd_blank = jnp.where(alive, new_blank, fwd_blank)
            fwd_label = jnp.where(alive, new_label, fwd_label)
            blank_fwd[step] = fwd_blank
            label_fwd[step] = fwd_label

            back = frame_count - 1 - step
            out_blank = bwd_blank + emit_blank[back + 1]
            out_label = bwd_label + emit_label[back + 1]
            next_blank = pltpu.roll(out_blank, LANES - 1, 1)
            next_label = jnp.where(skip_next, pltpu.roll(out_label, LANES - 1, 1), LOG_ZERO)
            ended = back >= frames - 1
            bwd_blank = jnp.where(ended, ends_blank, log_add(out_blank, out_label))
            bwd_label = jnp.where(
                ended, ends_label, log_add3(out_label, next_blank, next_label)
            )
            blank_bwd[back] = bwd_blank
            label_bwd[back] = bwd_label
            return (fwd_blank, fwd_label, bwd_blank, bwd_label)

        first_blank = jnp.where(lane == 0, emit_blank[0], LOG_ZERO)
        first_label = jnp.where(lane == 0, emit_label[0], LOG_ZERO)
        blank_fwd[0] = first_blank
        label_fwd[0] = first_label
        blank_bwd[frame_count - 1] = ends_blank
        label_bwd[frame_count - 1] = ends_label
        fwd_blank, fwd_label, _, _ = lax.fori_loop(
            1, frame_count, advance, (first_blank, first_label, ends_blank, ends_label), unroll=4
        )
        end_state = jnp.sum(jnp.where(lane == counts, fwd_blank, 0.0), axis=1, keepdims=True)
        near_state = jnp.sum(jnp.where(lane == counts - 1, fwd_label, 0.0), axis=1, keepdims=True)
        log_like = log_add(end_state, near_state)
        turned_losses = jnp.transpose(jnp.broadcast_to(-log_like, (utterances, LANES)), (1, 0))
        loss_ref[...] = turned_losses[:1, :kept]

        def occupy(step, carry):
            blank = jnp.exp(blank_fwd[step] + blank_bwd[step] - log_like)
            label = jnp.exp(label_fwd[step] + label_bwd[step] - log_like)
            blank = jnp.sum(jnp.where(is_blank, blank, 0.0), axis=1, keepdims=True)
            label = jnp.where(is_label, label, 0.0)
            whole = blank + jnp.sum(label, axis=1, keepdims=True)
            filled = jnp.where(lane == label_max, blank, label)
            filled = jnp.where(lane == WHOLE, whole, filled)
            filled = jnp.where(step < frames, -filled, 0.0)
            row = emission_ref[pl.ds(step, utterances, stride=frame_count), :]
            occupancy_ref[pl.ds(step, utterances, stride=frame_count), :] = jnp.where(
                lane == TOTAL, row, filled
            )
            return carry

        lax.fori_loop(0, frame_count, occupy, 0, unroll=16)
        turned = jnp.transpose(occupancy_ref[...], (1, 0))[:COLS]
        out_ref[...] = turned
        row_place = lax.broadcasted_iota(jnp.int32, (COLS, row_count), 0)
        owner = lax.broadcasted_iota(jnp.int32, (COLS, row_count), 1) // frame_count
        source = jnp.where(row_place < WHOLE, turned, 0.0)
        for utterance in range(utterances):
            part = jnp.where(owner == utterance, source, 0.0)
            high = part.astype(jnp.bfloat16)
            high_ref[utterance * COLS : (utterance + 1) * COLS] = high
            low_ref[utterance * COLS : (utterance + 1) * COLS] = (
                part - high.astype(jnp.float32)
            ).astype(jnp.bfloat16)

    held = pltpu.VMEM((frame_count, utterances, LANES), jnp.float32)
    table = pltpu.VMEM((row_count, LANES), jnp.float32)
    return call(
        kernel,
        (
            jax.ShapeDtypeStruct((COLS, row_count), jnp.float32),
            bf16_rows(entries, row_count),
            bf16_rows(entries, row_count),
            jax.ShapeDtypeStruct((1, kept), jnp.float32),
        ),
        1 << 26,
        in_specs=[smem_spec()] + [vmem_spec()] * (1 + calls * sources),
        out_specs=tuple(vmem_spec() for _ in range(4)),
        scratch_shapes=[pltpu.VMEM((LANES, tall), jnp.float32), table]
        + [held] * 6
        + [table],
    )(slots, notes, *[value for group in stats for value in group])


def head_gradient(logits, rows, occupancy, high, low, places, order, outputs, each):
    count = len(logits)
    row_count, width = rows[0].shape
    entries = places.shape[1]
    blocks = outputs * each

    def kernel(order_ref, *refs):
        logits_refs, rows_refs = refs[:count], refs[count : 2 * count]
        occupancy_ref, high_ref, low_ref, places_ref = refs[2 * count : 2 * count + 4]
        out_refs = refs[2 * count + 4 :]
        for block in range(blocks):
            start = pl.multiple_of(order_ref[block] * BLOCK_ROWS, BLOCK_ROWS)
            entry = start + lax.broadcasted_iota(jnp.int32, (BLOCK_ROWS, entries), 0)
            select = as_mask(entry == places_ref[...])
            total = None
            for g in range(count):
                lanes = slice(g * row_count, (g + 1) * row_count)
                scattered = lax.dot_general(
                    select, high_ref[:, lanes], NN, preferred_element_type=jnp.float32
                ) + lax.dot_general(
                    select, low_ref[:, lanes], NN, preferred_element_type=jnp.float32
                )
                whole = occupancy_ref[WHOLE : WHOLE + 1, lanes]
                log_total = occupancy_ref[TOTAL : TOTAL + 1, lanes]
                values = logits_refs[g][pl.ds(start, BLOCK_ROWS), :]
                grad = (scattered - jnp.exp(values - log_total) * whole).astype(jnp.bfloat16)
                part = lax.dot_general(
                    grad, rows_refs[g][...], NN, preferred_element_type=jnp.float32
                )
                total = part if total is None else total + part
            out_refs[block // each][
                block % each * BLOCK_ROWS : (block % each + 1) * BLOCK_ROWS
            ] = total.astype(jnp.bfloat16)

    return call(
        kernel,
        tuple(bf16_rows(each * BLOCK_ROWS, width) for _ in range(outputs)),
        2 * blocks * BLOCK_ROWS * count * row_count * (width + 2 * entries),
        LARGE_LIMIT,
        in_specs=[smem_spec()] + [vmem_spec()] * (2 * count + 4),
        out_specs=tuple(vmem_spec() for _ in range(outputs)),
    )(order, *logits, *rows, occupancy, high, low, places)


def assemble(pieces, offsets, height, whole=None):
    count = len(pieces)
    part, width = pieces[0].shape
    short = height % part
    started = [] if whole is None else [whole]

    def kernel(offsets_ref, *refs):
        out_ref, sems = refs[count + len(started) :]

        def each(act):
            for index in range(count):
                offset = pl.multiple_of(offsets_ref[index], part)

                @pl.when(offset + part <= height)
                def _():
                    act(
                        pltpu.make_async_copy(
                            refs[index], out_ref.at[pl.ds(offset, part)], sems.at[index]
                        )
                    )

                if short:

                    @pl.when(offset + part > height)
                    def _():
                        act(
                            pltpu.make_async_copy(
                                refs[index].at[pl.ds(0, short)],
                                out_ref.at[pl.ds(height - short, short)],
                                sems.at[index],
                            )
                        )

        each(lambda copy: copy.start())
        each(lambda copy: copy.wait())

    anywhere = pl.BlockSpec(memory_space=pl.ANY)
    return call(
        kernel,
        bf16_rows(height, width),
        in_specs=[smem_spec()] + [vmem_spec()] * count + [anywhere] * len(started),
        out_specs=anywhere,
        scratch_shapes=[pltpu.SemaphoreType.DMA((count,))],
        input_output_aliases={} if whole is None else {1 + count: 0},
    )(offsets, *pieces, *started)


def swap(value, axis):
    return lax.ppermute(value, axis, [(0, 1), (1, 0)])


def crossed(value, axis, by):
    count = lax.axis_size(axis)
    return lax.ppermute(value, axis, [(i, i ^ by) for i in range(count)])


def after(value, *others):
    return lax.optimization_barrier((value,) + others)[0]


LINE_ORDER = np.array([[0, 1, 2, 3], [1, 0, 2, 3], [2, 3, 1, 0], [3, 2, 1, 0]])
MIDDLE = [(1, 2), (2, 1)]
OUTWARD = [(1, 0), (2, 3)]


def slot_orders(count):
    return LINE_ORDER if count == 4 else np.tile(np.arange(count), (count, 1))


def slot_tables(count):
    orders = slot_orders(count)
    tables = np.zeros((count, count, count), np.int32)
    for member in range(count):
        for k in range(count):
            source = member ^ k
            for slot in range(count):
                tables[member, k, slot] = list(orders[source]).index(orders[member][slot])
    return tables.reshape(count, count * count)


def wide(ref, start, size):
    return ref[pl.ds(start, size), :].astype(jnp.float32)


def sum_sent(own, came, places):
    height, width = own.shape
    part = height // 4

    def kernel(places_ref, own_ref, came_ref, *out_refs):
        section, outer = places_ref[0], places_ref[1]
        starts = (
            (1 - outer) * part,
            outer * part,
            (2 + 1 - section) * part,
            (2 + section) * part,
        )
        for start, out_ref in zip(starts, out_refs):
            start = pl.multiple_of(start, part)
            out_ref[...] = (wide(own_ref, start, part) + wide(came_ref, start, part)).astype(
                jnp.bfloat16
            )

    return call(
        kernel,
        tuple(bf16_rows(part, width) for _ in range(4)),
        1 << 20,
        in_specs=[smem_spec()] + [vmem_spec()] * 2,
        out_specs=tuple(vmem_spec() for _ in range(4)),
    )(places, own, came)


def sum_kept(own, came, arrived, places, keep):
    height, width = own.shape
    part = height // 4
    count = len(arrived) // 2

    def kernel(places_ref, own_ref, came_ref, *refs):
        section, outer = places_ref[0], places_ref[1]
        if not keep:
            section, outer = 1 - section, 1 - outer
        for side, start in enumerate((outer * part, (2 + section) * part)):
            start = pl.multiple_of(start, part)
            total = wide(own_ref, start, part) + wide(came_ref, start, part)
            for ref in refs[side * count : (side + 1) * count]:
                total = total + ref[...].astype(jnp.float32)
            refs[2 * count + side][...] = total.astype(jnp.bfloat16)

    return call(
        kernel,
        (bf16_rows(part, width), bf16_rows(part, width)),
        1 << 20,
        in_specs=[smem_spec()] + [vmem_spec()] * (2 + 2 * count),
        out_specs=(vmem_spec(), vmem_spec()),
    )(places, own, came, *arrived)


def per_device(
    frames,
    norm_gain,
    router,
    w_in,
    w_out,
    routing,
    head_gain,
    head_weight,
    frame_lengths,
    labels,
    label_lengths,
):
    sections = lax.axis_size("section")
    section_id = lax.axis_index("section")
    group_size = lax.axis_size("expert")
    member = lax.axis_index("expert")
    outer_size = lax.axis_size("dpo")
    inner_size = lax.axis_size("dpi")
    core = lax.axis_index("dpi")
    micro, utt_dev, frame_count, width = frames.shape
    label_max = labels.shape[2]
    experts = w_in.shape[1] * group_size
    pair_count = micro * utt_dev
    per_section = pair_count // sections
    first_pair = section_id * per_section
    share = (utt_dev * frame_count * 9 + 8 * experts - 1) // (8 * experts)
    filled = share * -(-per_section // utt_dev)
    capacity = round_up(filled + 1, 8)
    span = per_section * frame_count
    member_ref = member.astype(jnp.int32).reshape(1)

    def mine_of(value):
        return lax.dynamic_slice_in_dim(value, first_pair, per_section, 0)

    def exchange(blocks):
        return [blocks[0]] + [crossed(blocks[k], "expert", k) for k in range(1, group_size)]

    def lanes_of(ids):
        return jnp.pad(mine_of(ids), ((0, 0), (0, LANES - frame_count)), constant_values=-1)

    current = lax.dynamic_slice_in_dim(
        frames.reshape(pair_count * frame_count, width), first_pair * frame_count, span, 0
    )
    own_ids = routing.reshape(pair_count, frame_count)
    paired = sections == 2 and inner_size == 2
    if paired:
        other_ids = swap(own_ids, "section")
        all_ids = [
            jnp.where(section_id == layer, own_ids, other_ids) for layer in range(sections)
        ]
    else:
        all_ids = lax.all_gather(own_ids, "section")
    layer_ids = [lanes_of(all_ids[layer]) for layer in range(sections)]
    own_table = jnp.concatenate(
        [
            norm_gain,
            jnp.zeros((7, width), jnp.float32),
            jnp.transpose(router[0]).astype(jnp.float32),
            jnp.zeros((round_up(experts, 8) - experts, width), jnp.float32),
        ],
        axis=0,
    )
    own = (w_in[0, 0], w_out[0, 0])
    layers = []
    if paired:
        other_table = swap(own_table, "section")
        sent_in, sent_out = half_weights(core.astype(jnp.int32).reshape(1), *own)
        came_in = swap(sent_in, "section")
        came_out = swap(sent_out, "section")
    else:
        all_tables = lax.all_gather(own_table, "section")
        all_in = lax.all_gather(own[0], "section")
        all_out = lax.all_gather(own[1], "section")
        for layer in range(sections):
            chosen = (all_in[layer], all_out[layer])
            layers.append(((all_tables[layer],), chosen, [], jnp.ones((1,), jnp.int32)))

    outgoing = dispatch(current, layer_ids[0], member_ref, experts, capacity, frame_count)
    received = exchange(outgoing)
    if paired:
        (came_in, came_out), received = lax.optimization_barrier(((came_in, came_out), received))
        other = [(came_in, came_out), (swap(came_in, "dpi"), swap(came_out, "dpi"))]
        for layer in range(sections):
            mine = (section_id == layer).astype(jnp.int32).reshape(1)
            layers.append(((own_table, other_table), own, other, mine))

    labels, frame_lengths, label_lengths = lax.optimization_barrier(
        (labels, frame_lengths, label_lengths, outgoing[0])
    )[:3]
    notes = jnp.concatenate(
        [
            mine_of(labels.reshape(pair_count, label_max)),
            mine_of(frame_lengths.reshape(pair_count, 1)),
            mine_of(label_lengths.reshape(pair_count, 1)),
        ],
        axis=1,
    )
    notes = jnp.pad(notes, ((0, 0), (0, COLS - label_max - 2))).reshape(1, per_section * COLS)
    notes = jnp.pad(notes, ((0, 0), (0, LANES - per_section * COLS)))
    notes = jnp.concatenate([notes // LANES, notes % LANES], axis=1).astype(jnp.float32)
    notes = jnp.pad(notes, ((0, 0), (0, width - 2 * LANES)))
    shard = head_weight.shape[1]
    weight_rows = jnp.transpose(head_weight)
    line = group_size == 4
    tables = jnp.asarray(slot_tables(group_size))
    slots = lax.dynamic_index_in_dim(tables, member, 0, keepdims=False)
    outer = lax.axis_index("dpo")
    blocks = -(-shard // BLOCK_ROWS)
    tree = paired and outer_size == 2 and blocks == 8

    def pair_of(side, first, second):
        return [side * 4 + first, side * 4 + 2 + second]

    def offset_of(side, s, y):
        base = side * 4 * BLOCK_ROWS
        part = BLOCK_ROWS // 2
        return [
            base + s * BLOCK_ROWS + y * part,
            base + 2 * BLOCK_ROWS + y * BLOCK_ROWS + s * part,
        ]

    def whole_numbers(values):
        return jnp.stack([jnp.asarray(value, jnp.int32) for value in values])

    here, there = (section_id, outer), (1 - section_id, 1 - outer)
    sibling_order = whole_numbers(pair_of(1 - core, *there) + pair_of(1 - core, *here))
    sent_order = whole_numbers(pair_of(core, *there))
    kept_order = whole_numbers(pair_of(core, *here))
    chip_place = whole_numbers(here)
    first_offsets, last_offsets = [], offset_of(core, *there) + offset_of(1 - core, *there)
    for side in (core, 1 - core):
        for s, y in (here, (section_id, 1 - outer), (1 - section_id, outer)):
            first_offsets += offset_of(side, s, y)
    first_offsets, last_offsets = whole_numbers(first_offsets), whole_numbers(last_offsets)
    early = (
        notes,
        slots,
        head_gain.reshape(1, width),
        layer_ids[1:],
        sibling_order,
        sent_order,
        kept_order,
        chip_place,
        first_offsets,
        last_offsets,
    )
    early, received = lax.optimization_barrier((early, received))
    notes, slots, head_row, later_ids, sibling_order, sent_order = early[:6]
    kept_order, chip_place, first_offsets, last_offsets = early[6:]
    layer_ids = [layer_ids[0]] + list(later_ids)

    for layer in range(sections):
        choices, weights, others, pick_own = layers[layer]
        note = notes if layer == 0 else None
        done = run_expert(received, choices, weights, others, pick_own, filled, note)
        returned = exchange(done)
        if layer == 0:
            found = returned
            if not line:
                stacked = jnp.stack(returned)
                found = [
                    lax.dynamic_index_in_dim(stacked, member ^ k, 0, keepdims=False)
                    for k in range(group_size)
                ]
        if layer < sections - 1:
            current, outgoing = combine_and_dispatch(
                current,
                returned,
                layer_ids[layer],
                choices,
                pick_own,
                layer_ids[layer + 1],
                member_ref,
                experts,
                capacity,
                frame_count,
            )
            received = exchange(outgoing)
            if layer == 0:
                found = [after(found[0], current)] + list(found[1:])
                label_weight, places, names = label_rows(
                    weight_rows, found, member_ref, per_section, filled, label_max, line
                )
                received, label_weight = lax.optimization_barrier((received, label_weight))
        else:
            normed = combine_and_norm(
                current,
                returned,
                layer_ids[layer],
                choices,
                pick_own,
                head_row,
                member_ref,
                experts,
                capacity,
                frame_count,
            )

    def logits_of(fill, first, count, pieces):
        return head_logits(
            fill, first, count, pieces, member_ref, weight_rows, label_weight, frame_count
        )

    def stats_of(stats):
        first = crossed(stats, "expert", 1)
        return [stats, first, crossed(stats, "expert", 2), crossed(first, "expert", 2)]

    if line:
        beside = crossed(normed, "expert", 1)
        middle = lax.ppermute(normed, "expert", MIDDLE)
        far = lax.ppermute(beside, "expert", MIDDLE)
        outward = lax.ppermute(middle, "expert", OUTWARD)
        heads = [logits_of(fill_all, 0, 2, [normed, beside])]
        held, heads[0] = lax.optimization_barrier((far, heads[0]))
        last = lax.ppermute(held, "expert", OUTWARD)
        found = [stats_of(heads[0][2])]
        middle, found[0] = lax.optimization_barrier((middle, found[0]))
        heads.append(logits_of(fill_far, 2, 2, [middle, outward, held, last]))
        found.append(stats_of(heads[1][2]))
    else:
        gathered = lax.all_gather(normed, "expert")
        pieces = [gathered[k] for k in range(group_size)]
        heads = [logits_of(fill_all, 0, group_size, pieces)]
        gathered = lax.all_gather(heads[0][2], "expert")
        found = [
            [
                lax.dynamic_index_in_dim(gathered, member ^ k, 0, keepdims=False)
                for k in range(group_size)
            ]
        ]
    kept_losses = per_section if line else group_size * per_section
    occupancy, high, low, losses = ctc_pass(
        found, slots, names, frame_count, label_max, kept_losses
    )
    if not line:
        losses = lax.dynamic_slice(losses, (0, member * per_section), (1, per_section))
    losses = jnp.transpose(losses)

    def gradient(order, outputs, each):
        return head_gradient(
            [head[0] for head in heads],
            [head[1] for head in heads],
            occupancy,
            high,
            low,
            places,
            order,
            outputs,
            each,
        )

    if tree:
        sibling_sent, sibling_kept = gradient(sibling_order, 2, 2)
        came_sent, came_kept = swap(sibling_sent, "dpi"), swap(sibling_kept, "dpi")
        own_sent = gradient(after(sent_order, sibling_sent), 1, 2)[0]
        a_far, a_near, b_far, b_near = sum_sent(own_sent, came_sent, chip_place)
        kept_order = after(kept_order, a_far)
        a_far, b_far = swap(a_far, "section"), swap(b_far, "dpo")
        a_near, b_near = swap(a_near, "section"), swap(b_near, "dpo")
        own_kept = gradient(kept_order, 1, 2)[0]
        a_on, b_on = sum_kept(own_kept, came_kept, [a_far, b_far], chip_place, False)
        a_in, b_in = swap(a_on, "dpo"), swap(b_on, "section")
        a, b = sum_kept(own_kept, came_kept, [a_near, a_in, b_near, b_in], chip_place, True)
        a_y, b_x = swap(a, "dpo"), swap(b, "section")
        b_y, a_x = swap(b, "dpo"), swap(a, "section")
        a_xy, b_xy = swap(a_y, "section"), swap(b_x, "dpo")
        b_y, a_x = lax.optimization_barrier((b_y, a_x, a_xy, b_xy))[:2]
        mine = [a, b, a_y, b_y, a_x, b_x]
        theirs = [swap(value, "dpi") for value in mine]
        whole = assemble(mine + theirs, first_offsets, shard)
        last = [a_xy, b_xy, swap(a_xy, "dpi"), swap(b_xy, "dpi")]
        whole = assemble(last, last_offsets, shard, whole)
    else:
        partial = gradient(jnp.arange(blocks, dtype=jnp.int32), 1, blocks)[0][:shard]
        whole = lax.psum(partial.astype(jnp.float32), ("section", "dpo", "dpi")).astype(
            jnp.bfloat16
        )
    return (losses, jnp.transpose(whole))


def solution(mesh):
    sections, group_size, spread = (mesh.shape[name] for name in ("section", "expert", "dp"))
    inner = 2 if spread % 2 == 0 else 1
    split = Mesh(
        mesh.devices.reshape(sections, group_size, spread // inner, inner),
        ("section", "expert", "dpo", "dpi"),
    )
    block = ("expert", "dpo", "dpi")
    placed = (
        P(None, block, None, None),
        P("section", None),
        P("section", None, None),
        P("section", "expert", None, None),
        P("section", "expert", None, None),
        P("section", None, block, None, None),
        P(),
        P(None, "expert"),
        P(None, block),
        P(None, block, None),
        P(None, block),
    )
    return jax.shard_map(
        per_device,
        mesh=split,
        in_specs=placed,
        out_specs=(P("section", block), P(None, "expert")),
        check_vma=False,
    )
```

```python
import jax
import jax.numpy as jnp
import numpy as np
from jax import lax
from jax.experimental import pallas as pl
from jax.experimental.pallas import tpu as pltpu
from jax.sharding import Mesh, PartitionSpec as P

EPSILON = 1e-06
LOG_ZERO = -1e30
VMEM_LIMIT = 12 * 1024 * 1024
LARGE_LIMIT = 24 * 1024 * 1024
LANES = 128
COLS = 16
PEAK, TOTAL, WHOLE = COLS - 3, COLS - 2, COLS - 3
BLOCK_ROWS = 256
NT = (((1,), (1,)), ((), ()))
NN = (((1,), (0,)), ((), ()))


def round_up(value, unit):
    return -(-value // unit) * unit


def vmem_spec():
    return pl.BlockSpec(memory_space=pltpu.VMEM)


def smem_spec():
    return pl.BlockSpec(memory_space=pltpu.SMEM)


def call(kernel, out_shape, flops=0, limit=VMEM_LIMIT, **options):
    return pl.pallas_call(
        kernel,
        out_shape=out_shape,
        compiler_params=pltpu.CompilerParams(vmem_limit_bytes=limit),
        cost_estimate=pl.CostEstimate(flops=flops, bytes_accessed=0, transcendentals=0),
        **options,
    )


def bf16_rows(count, width):
    return jax.ShapeDtypeStruct((count, width), jnp.bfloat16)


def as_mask(values):
    return values.astype(jnp.float32).astype(jnp.bfloat16)


def split_rows(values, out_refs, spare=None, note=None):
    size, width = out_refs[0].shape
    for turn, out_ref in enumerate(out_refs):
        part = values[turn * size : (turn + 1) * size]
        if note is not None:
            row = lax.broadcasted_iota(jnp.int32, (size, width), 0)
            part = jnp.where(row == spare, note, part)
        out_ref[...] = part.astype(jnp.bfloat16)


def join_rows(refs):
    return jnp.concatenate([ref[...].astype(jnp.float32) for ref in refs], axis=0)


def rms_scale(values, gain):
    values = values.astype(jnp.float32)
    scale = lax.rsqrt(jnp.mean(values * values, axis=-1, keepdims=True) + EPSILON)
    return (values * scale * gain).astype(jnp.bfloat16)


def expert_column(ids, frame_count):
    pairs = ids.shape[0]
    square = jnp.concatenate(
        [ids.astype(jnp.float32), jnp.full((LANES - pairs, LANES), -1.0, jnp.float32)], axis=0
    )
    turned = jnp.transpose(square, (1, 0)).astype(jnp.int32)
    return jnp.concatenate([turned[:frame_count, p : p + 1] for p in range(pairs)], axis=0)


def placement(column, member, experts, capacity):
    count = column.shape[0]
    relative = column ^ member
    lane = lax.broadcasted_iota(jnp.int32, (count, LANES), 1)
    one_hot = (lane == relative).astype(jnp.float32)
    before = lax.broadcasted_iota(jnp.int32, (count, count), 1) <= lax.broadcasted_iota(
        jnp.int32, (count, count), 0
    )
    rank = lax.dot_general(
        as_mask(before), one_hot.astype(jnp.bfloat16), NN, preferred_element_type=jnp.float32
    )
    start = (lane * capacity - 1).astype(jnp.float32)
    slots = jnp.sum(one_hot * (rank + start), axis=1, keepdims=True).astype(jnp.int32)
    places = lax.broadcasted_iota(jnp.int32, (count, experts * capacity), 1)
    return (places == slots).astype(jnp.float32)


def scatter_rows(rows, ids, member, experts, capacity, frame_count, out_refs):
    count = rows.shape[0]
    chosen = placement(expert_column(ids, frame_count), member, experts, capacity)
    tall = round_up(count, LANES)
    if tall > count:
        chosen = jnp.concatenate(
            [chosen, jnp.zeros((tall - count, chosen.shape[1]), jnp.float32)], axis=0
        )
    pick = jnp.transpose(chosen, (1, 0))[:, :count].astype(jnp.bfloat16)
    placed = lax.dot_general(pick, rows, NN, preferred_element_type=jnp.float32)
    split_rows(placed, out_refs)


def combine_rows(rows, returned, ids, table, member, experts, capacity, frame_count):
    column = expert_column(ids, frame_count)
    pick = placement(column, member, experts, capacity).astype(jnp.bfloat16)
    normed = rms_scale(rows, table[:1])
    router = jnp.concatenate(
        [table[8:], jnp.zeros((LANES + 8 - table.shape[0], rows.shape[1]), jnp.float32)], axis=0
    ).astype(jnp.bfloat16)
    logits = lax.dot_general(normed, router, NT, preferred_element_type=jnp.float32)
    lane = lax.broadcasted_iota(jnp.int32, logits.shape, 1)
    gate = jax.nn.sigmoid(jnp.sum(jnp.where(lane == column, logits, 0.0), axis=1, keepdims=True))
    stacked = join_rows(returned).astype(jnp.bfloat16)
    mixed = lax.dot_general(pick, stacked, NN, preferred_element_type=jnp.float32)
    return (rows.astype(jnp.float32) + gate * mixed).astype(jnp.bfloat16)


def dispatch(rows, ids, member, experts, capacity, frame_count):
    width = rows.shape[1]

    def kernel(member_ref, rows_ref, ids_ref, *out_refs):
        scatter_rows(
            rows_ref[...], ids_ref[...], member_ref[0], experts, capacity, frame_count, out_refs
        )

    return call(
        kernel,
        tuple(bf16_rows(capacity, width) for _ in range(experts)),
        1 << 27,
        in_specs=[smem_spec()] + [vmem_spec()] * 2,
        out_specs=tuple(vmem_spec() for _ in range(experts)),
    )(member, rows, ids)


def pick_table(pick_ref, tables):
    if len(tables) == 1:
        return tables[0][...]
    return jnp.where(pick_ref[0] == 1, tables[0][...], tables[1][...])


def run_expert(received, tables, own, other, pick_own, spare, note):
    count = len(received)
    capacity, width = received[0].shape
    others, choices = len(other), len(tables)
    noted = [] if note is None else [note]

    def kernel(pick_ref, in_ref, out_weight_ref, *refs):
        table_refs, refs = refs[:choices], refs[choices:]
        other_refs, refs = refs[: 2 * others], refs[2 * others :]
        received_refs, refs = refs[:count], refs[count:]
        out_refs = refs[len(noted) :]

        def work(pieces):
            gain = pick_table(pick_ref, table_refs)[:1]
            normed = rms_scale(join_rows(received_refs), gain)
            total = None
            for weight_in, weight_out in pieces:
                hidden = lax.dot_general(
                    normed, weight_in[...], NN, preferred_element_type=jnp.float32
                )
                active = (hidden / (1.0 + jnp.exp(-hidden))).astype(jnp.bfloat16)
                part = lax.dot_general(
                    active, weight_out[...], NN, preferred_element_type=jnp.float32
                )
                total = part if total is None else total + part
            split_rows(total, out_refs, spare, refs[0][...] if noted else None)

        if others == 0:
            work([(in_ref, out_weight_ref)])
            return

        @pl.when(pick_ref[0] == 1)
        def _():
            work([(in_ref, out_weight_ref)])

        @pl.when(pick_ref[0] != 1)
        def _():
            work([(other_refs[2 * i], other_refs[2 * i + 1]) for i in range(others)])

    flat = [weight for pair in other for weight in pair]
    return call(
        kernel,
        tuple(bf16_rows(capacity, width) for _ in range(count)),
        4 * count * capacity * width * own[0].shape[1],
        in_specs=[smem_spec()] + [vmem_spec()] * (2 + choices + 2 * others + count + len(noted)),
        out_specs=tuple(vmem_spec() for _ in range(count)),
    )(pick_own, *own, *tables, *flat, *received, *noted)


def combine_and_dispatch(
    rows, returned, ids, tables, pick_own, next_ids, member, experts, capacity, frame_count
):
    width = rows.shape[1]
    choices = len(tables)

    def kernel(member_ref, pick_ref, rows_ref, ids_ref, next_ref, *refs):
        table_refs, refs = refs[:choices], refs[choices:]
        returned_refs, x_ref, out_refs = refs[:experts], refs[experts], refs[experts + 1 :]
        mixed = combine_rows(
            rows_ref[...],
            returned_refs,
            ids_ref[...],
            pick_table(pick_ref, table_refs),
            member_ref[0],
            experts,
            capacity,
            frame_count,
        )
        x_ref[...] = mixed
        scatter_rows(
            mixed, next_ref[...], member_ref[0], experts, capacity, frame_count, out_refs
        )

    shapes = (bf16_rows(*rows.shape),) + tuple(
        bf16_rows(capacity, width) for _ in range(experts)
    )
    result = call(
        kernel,
        shapes,
        1 << 28,
        in_specs=[smem_spec()] * 2 + [vmem_spec()] * (3 + choices + experts),
        out_specs=tuple(vmem_spec() for _ in shapes),
    )(member, pick_own, rows, ids, next_ids, *tables, *returned)
    return result[0], result[1:]


def combine_and_norm(
    rows, returned, ids, tables, pick_own, head_gain, member, experts, capacity, frame_count
):
    choices = len(tables)

    def kernel(member_ref, pick_ref, rows_ref, ids_ref, head_ref, *refs):
        table_refs, refs = refs[:choices], refs[choices:]
        final = combine_rows(
            rows_ref[...],
            refs[:experts],
            ids_ref[...],
            pick_table(pick_ref, table_refs),
            member_ref[0],
            experts,
            capacity,
            frame_count,
        )
        refs[experts][...] = rms_scale(final, head_ref[...])

    return call(
        kernel,
        bf16_rows(*rows.shape),
        1 << 28,
        in_specs=[smem_spec()] * 2 + [vmem_spec()] * (3 + choices + experts),
        out_specs=vmem_spec(),
    )(member, pick_own, rows, ids, head_gain, *tables, *returned)


def half_weights(core, weight_in, weight_out):
    width, hidden = weight_in.shape
    half = hidden // 2

    def kernel(core_ref, in_ref, out_ref, half_in, half_out, sems):
        start = pl.multiple_of(core_ref[0] * half, half)
        copies = (
            pltpu.make_async_copy(in_ref.at[:, pl.ds(start, half)], half_in, sems.at[0]),
            pltpu.make_async_copy(out_ref.at[pl.ds(start, half)], half_out, sems.at[1]),
        )
        for copy in copies:
            copy.start()
        for copy in copies:
            copy.wait()

    return call(
        kernel,
        (bf16_rows(width, half), bf16_rows(half, width)),
        1 << 20,
        in_specs=[smem_spec()] + [pl.BlockSpec(memory_space=pl.ANY)] * 2,
        out_specs=(vmem_spec(), vmem_spec()),
        scratch_shapes=[pltpu.SemaphoreType.DMA((2,))],
    )(core, weight_in, weight_out)


def block_list(shard):
    return [(i, min(BLOCK_ROWS, shard - i)) for i in range(0, shard, BLOCK_ROWS)]


def label_rows(weight, notes, member, pairs, spare, label_max, line):
    shard, width = weight.shape
    sources = len(notes)
    utterances = sources * pairs
    entries = utterances * COLS

    def kernel(member_ref, weight_ref, *refs):
        note_refs = refs[:sources]
        out_ref, places_ref, names_ref, turned_ref = refs[sources:]
        place = member_ref[0]
        found = []
        for ref in note_refs:
            row = ref[...].astype(jnp.float32)[spare : spare + 1]
            found.append((row[:, :LANES] * LANES + row[:, LANES : 2 * LANES]).astype(jnp.int32))
        if line:
            ends = (place == 0) | (place == 3)
            found = [
                found[0],
                found[1],
                jnp.where(ends, found[2], found[3]),
                jnp.where(ends, found[3], found[2]),
            ]
        names_ref[...] = jnp.zeros(names_ref.shape, jnp.int32)
        for slot in range(sources):
            for pair in range(pairs):
                row = slot * pairs + pair
                names_ref[row : row + 1, :COLS] = found[slot][:, pair * COLS : (pair + 1) * COLS]
        lane = lax.broadcasted_iota(jnp.int32, (utterances, LANES), 1)
        named = jnp.where(lane < label_max, names_ref[...], jnp.where(lane == label_max, 0, -1))
        local = named - place * shard
        local = jnp.where((named >= 0) & (local >= 0) & (local < shard), local, -1)
        square = jnp.concatenate(
            [
                local.astype(jnp.float32),
                jnp.full((LANES - utterances, LANES), -1.0, jnp.float32),
            ],
            axis=0,
        )
        turned = jnp.transpose(square, (1, 0))
        for utterance in range(utterances):
            turned_ref[utterance * COLS : (utterance + 1) * COLS] = jnp.broadcast_to(
                turned[:COLS, utterance : utterance + 1], (COLS, LANES)
            )
        places = turned_ref[:, :1].astype(jnp.int32)
        places_ref[...] = jnp.transpose(turned_ref[...], (1, 0))[:1].astype(jnp.int32)
        total = jnp.zeros((entries, width), jnp.float32)
        for first, size in block_list(shard):
            entry = first + lax.broadcasted_iota(jnp.int32, (entries, size), 1)
            total = total + lax.dot_general(
                as_mask(entry == places),
                weight_ref[first : first + size],
                NN,
                preferred_element_type=jnp.float32,
            )
        out_ref[...] = total.astype(jnp.bfloat16)

    return call(
        kernel,
        (
            bf16_rows(entries, width),
            jax.ShapeDtypeStruct((1, entries), jnp.int32),
            jax.ShapeDtypeStruct((utterances, LANES), jnp.int32),
        ),
        2 * shard * entries * width,
        LARGE_LIMIT,
        in_specs=[smem_spec()] + [vmem_spec()] * (1 + sources),
        out_specs=tuple(vmem_spec() for _ in range(3)),
        scratch_shapes=[pltpu.VMEM((entries, LANES), jnp.float32)],
    )(member, weight, *notes)


def head_logits(
    fill, first_slot, count, pieces, member, weight, label_weight, frame_count, earlier=None
):
    given = len(pieces)
    span, width = pieces[0].shape
    row_count = count * span
    shard = weight.shape[0]
    height = round_up(shard, BLOCK_ROWS)
    entries = row_count // frame_count * COLS
    first_entry = first_slot * entries // count
    others = [] if earlier is None else [earlier]
    ahead = 0 if earlier is None else earlier.shape[0]

    def kernel(member_ref, weight_ref, label_ref, *refs):
        piece_refs = refs[:given]
        logits_ref, rows_ref, stats_ref = refs[given + len(others) :]

        def put(slot, piece_ref):
            rows_ref[slot * span : (slot + 1) * span] = piece_ref[...]

        def put_if(condition, slot, piece_ref):
            @pl.when(condition)
            def _():
                put(slot, piece_ref)

        fill(member_ref[0], piece_refs, put, put_if)
        peak = jnp.full((1, row_count), LOG_ZERO, jnp.float32)
        total = jnp.zeros((1, row_count), jnp.float32)
        for first, size in block_list(shard):
            logits = lax.dot_general(
                weight_ref[first : first + size],
                rows_ref[...],
                NT,
                preferred_element_type=jnp.float32,
            )
            logits_ref[first : first + size] = logits
            before = peak
            peak = jnp.maximum(before, jnp.max(logits, axis=0, keepdims=True))
            total = total * jnp.exp(before - peak) + jnp.sum(
                jnp.exp(logits - peak), axis=0, keepdims=True
            )
        if height > shard:
            logits_ref[shard:] = jnp.full((height - shard, row_count), LOG_ZERO, jnp.float32)
        crossed = lax.dot_general(
            label_ref[first_entry : first_entry + entries],
            rows_ref[...],
            NT,
            preferred_element_type=jnp.float32,
        )
        owner = lax.broadcasted_iota(jnp.int32, (COLS, row_count), 1) // frame_count
        picked = jnp.zeros((COLS, row_count), jnp.float32)
        for utterance in range(entries // COLS):
            part = crossed[utterance * COLS : (utterance + 1) * COLS]
            picked = picked + jnp.where(owner == utterance, part, 0.0)
        place = lax.broadcasted_iota(jnp.int32, (COLS, row_count), 0)
        stats = jnp.where(place == PEAK, peak, picked)
        stats = jnp.where(place == TOTAL, total, stats)
        for slot in range(ahead):
            stats_ref[slot] = refs[given][slot]
        for slot in range(count):
            stats_ref[ahead + slot] = stats[:, slot * span : (slot + 1) * span]

    return call(
        kernel,
        (
            jax.ShapeDtypeStruct((height, row_count), jnp.float32),
            bf16_rows(row_count, width),
            jax.ShapeDtypeStruct((ahead + count, COLS, span), jnp.float32),
        ),
        2 * height * row_count * width,
        LARGE_LIMIT,
        in_specs=[smem_spec()] + [vmem_spec()] * (2 + given + len(others)),
        out_specs=tuple(vmem_spec() for _ in range(3)),
    )(member, weight, label_weight, *pieces, *others)


def fill_far(place, piece_refs, put, put_if):
    middle, outward, far, last = piece_refs
    ends = (place == 0) | (place == 3)
    put_if(ends, 0, outward)
    put_if(ends, 1, last)
    put_if((place == 1) | (place == 2), 0, middle)
    put_if((place == 1) | (place == 2), 1, far)


def fill_all(place, piece_refs, put, put_if):
    for slot, piece_ref in enumerate(piece_refs):
        put(slot, piece_ref)


def log_add(first, second):
    peak = jnp.maximum(first, second)
    return peak + jnp.log(jnp.exp(first - peak) + jnp.exp(second - peak))


def log_add3(first, second, third):
    peak = jnp.maximum(jnp.maximum(first, second), third)
    return peak + jnp.log(
        jnp.exp(first - peak) + jnp.exp(second - peak) + jnp.exp(third - peak)
    )


def ctc_pass(stats, slots, notes, frame_count, label_max, kept):
    calls, sources = len(stats), len(stats[0])
    each, _, span = stats[0][0].shape
    count = calls * each
    row_count = count * span
    utterances = notes.shape[0]
    entries = utterances * COLS
    tall = round_up(span, LANES)

    def kernel(slots_ref, notes_ref, *refs):
        (
            out_ref,
            high_ref,
            low_ref,
            loss_ref,
            turn_ref,
            emission_ref,
            emit_blank,
            emit_label,
            blank_fwd,
            label_fwd,
            blank_bwd,
            label_bwd,
            occupancy_ref,
        ) = refs[calls * sources :]
        place = lax.broadcasted_iota(jnp.int32, (COLS, span), 0)
        turn_ref[...] = jnp.zeros(turn_ref.shape, jnp.float32)
        for slot in range(count):
            found = []
            for k in range(sources):
                where = slots_ref[k * count + slot]
                part = refs[k][where % each]
                for other in range(1, calls):
                    later = refs[other * sources + k][where % each]
                    part = jnp.where(where >= other * each, later, part)
                found.append(part)
            joined = found[0]
            peak = found[0][PEAK : PEAK + 1]
            for other in found[1:]:
                joined = joined + other
                peak = jnp.maximum(peak, other[PEAK : PEAK + 1])
            total = jnp.zeros((1, span), jnp.float32)
            for other in found:
                total = total + other[TOTAL : TOTAL + 1] * jnp.exp(other[PEAK : PEAK + 1] - peak)
            log_total = peak + jnp.log(total)
            turn_ref[:COLS, :span] = jnp.where(place == TOTAL, log_total, joined - log_total)
            emission_ref[slot * span : (slot + 1) * span] = jnp.transpose(turn_ref[...], (1, 0))[
                :span
            ]

        lane = lax.broadcasted_iota(jnp.int32, (utterances, LANES), 1)
        is_label = lane < label_max
        is_blank = lane <= label_max
        names = jnp.where(is_label, notes_ref[...], 0)
        earlier = pltpu.roll(names, 1, 1)
        skip = is_label & (lane >= 1) & (names != 0) & (names != earlier)
        later = pltpu.roll(names, LANES - 1, 1)
        skip_next = (lane < label_max - 1) & (later != 0) & (later != names)
        frames = notes_ref[:, label_max : label_max + 1]
        counts = notes_ref[:, label_max + 1 : label_max + 2]
        ends_blank = jnp.where(lane == counts, 0.0, LOG_ZERO)
        ends_label = jnp.where(lane == counts - 1, 0.0, LOG_ZERO)

        def spread(step, carry):
            row = emission_ref[pl.ds(step, utterances, stride=frame_count), :]
            blank = jnp.sum(jnp.where(lane == label_max, row, 0.0), axis=1, keepdims=True)
            emit_blank[step] = jnp.where(is_blank, blank, LOG_ZERO)
            emit_label[step] = jnp.where(is_label, row, LOG_ZERO)
            return carry

        lax.fori_loop(0, frame_count, spread, 0, unroll=16)

        def advance(step, carry):
            fwd_blank, fwd_label, bwd_blank, bwd_label = carry
            moved = jnp.where(lane == 0, LOG_ZERO, pltpu.roll(fwd_label, 1, 1))
            new_blank = log_add(fwd_blank, moved) + emit_blank[step]
            new_label = (
                log_add3(fwd_label, fwd_blank, jnp.where(skip, moved, LOG_ZERO))
                + emit_label[step]
            )
            alive = step < frames
            fwd_blank = jnp.where(alive, new_blank, fwd_blank)
            fwd_label = jnp.where(alive, new_label, fwd_label)
            blank_fwd[step] = fwd_blank
            label_fwd[step] = fwd_label

            back = frame_count - 1 - step
            out_blank = bwd_blank + emit_blank[back + 1]
            out_label = bwd_label + emit_label[back + 1]
            next_blank = pltpu.roll(out_blank, LANES - 1, 1)
            next_label = jnp.where(skip_next, pltpu.roll(out_label, LANES - 1, 1), LOG_ZERO)
            ended = back >= frames - 1
            bwd_blank = jnp.where(ended, ends_blank, log_add(out_blank, out_label))
            bwd_label = jnp.where(
                ended, ends_label, log_add3(out_label, next_blank, next_label)
            )
            blank_bwd[back] = bwd_blank
            label_bwd[back] = bwd_label
            return (fwd_blank, fwd_label, bwd_blank, bwd_label)

        first_blank = jnp.where(lane == 0, emit_blank[0], LOG_ZERO)
        first_label = jnp.where(lane == 0, emit_label[0], LOG_ZERO)
        blank_fwd[0] = first_blank
        label_fwd[0] = first_label
        blank_bwd[frame_count - 1] = ends_blank
        label_bwd[frame_count - 1] = ends_label
        fwd_blank, fwd_label, _, _ = lax.fori_loop(
            1, frame_count, advance, (first_blank, first_label, ends_blank, ends_label), unroll=4
        )
        end_state = jnp.sum(jnp.where(lane == counts, fwd_blank, 0.0), axis=1, keepdims=True)
        near_state = jnp.sum(jnp.where(lane == counts - 1, fwd_label, 0.0), axis=1, keepdims=True)
        log_like = log_add(end_state, near_state)
        turned_losses = jnp.transpose(jnp.broadcast_to(-log_like, (utterances, LANES)), (1, 0))
        loss_ref[...] = turned_losses[:1, :kept]

        def occupy(step, carry):
            blank = jnp.exp(blank_fwd[step] + blank_bwd[step] - log_like)
            label = jnp.exp(label_fwd[step] + label_bwd[step] - log_like)
            blank = jnp.sum(jnp.where(is_blank, blank, 0.0), axis=1, keepdims=True)
            label = jnp.where(is_label, label, 0.0)
            whole = blank + jnp.sum(label, axis=1, keepdims=True)
            filled = jnp.where(lane == label_max, blank, label)
            filled = jnp.where(lane == WHOLE, whole, filled)
            filled = jnp.where(step < frames, -filled, 0.0)
            row = emission_ref[pl.ds(step, utterances, stride=frame_count), :]
            occupancy_ref[pl.ds(step, utterances, stride=frame_count), :] = jnp.where(
                lane == TOTAL, row, filled
            )
            return carry

        lax.fori_loop(0, frame_count, occupy, 0, unroll=16)
        turned = jnp.transpose(occupancy_ref[...], (1, 0))[:COLS]
        out_ref[...] = turned
        row_place = lax.broadcasted_iota(jnp.int32, (COLS, row_count), 0)
        owner = lax.broadcasted_iota(jnp.int32, (COLS, row_count), 1) // frame_count
        source = jnp.where(row_place < WHOLE, turned, 0.0)
        for utterance in range(utterances):
            part = jnp.where(owner == utterance, source, 0.0)
            high = part.astype(jnp.bfloat16)
            high_ref[utterance * COLS : (utterance + 1) * COLS] = high
            low_ref[utterance * COLS : (utterance + 1) * COLS] = (
                part - high.astype(jnp.float32)
            ).astype(jnp.bfloat16)

    held = pltpu.VMEM((frame_count, utterances, LANES), jnp.float32)
    table = pltpu.VMEM((row_count, LANES), jnp.float32)
    return call(
        kernel,
        (
            jax.ShapeDtypeStruct((COLS, row_count), jnp.float32),
            bf16_rows(entries, row_count),
            bf16_rows(entries, row_count),
            jax.ShapeDtypeStruct((1, kept), jnp.float32),
        ),
        1 << 26,
        in_specs=[smem_spec()] + [vmem_spec()] * (1 + calls * sources),
        out_specs=tuple(vmem_spec() for _ in range(4)),
        scratch_shapes=[pltpu.VMEM((LANES, tall), jnp.float32), table]
        + [held] * 6
        + [table],
    )(slots, notes, *[value for group in stats for value in group])


def head_gradient(logits, rows, occupancy, high, low, places, order, outputs, each):
    count = len(logits)
    row_count, width = rows[0].shape
    entries = places.shape[1]
    blocks = outputs * each

    def kernel(order_ref, *refs):
        logits_refs, rows_refs = refs[:count], refs[count : 2 * count]
        occupancy_ref, high_ref, low_ref, places_ref = refs[2 * count : 2 * count + 4]
        out_refs = refs[2 * count + 4 :]
        for block in range(blocks):
            start = pl.multiple_of(order_ref[block] * BLOCK_ROWS, BLOCK_ROWS)
            entry = start + lax.broadcasted_iota(jnp.int32, (BLOCK_ROWS, entries), 0)
            select = as_mask(entry == places_ref[...])
            total = None
            for g in range(count):
                lanes = slice(g * row_count, (g + 1) * row_count)
                scattered = lax.dot_general(
                    select, high_ref[:, lanes], NN, preferred_element_type=jnp.float32
                ) + lax.dot_general(
                    select, low_ref[:, lanes], NN, preferred_element_type=jnp.float32
                )
                whole = occupancy_ref[WHOLE : WHOLE + 1, lanes]
                log_total = occupancy_ref[TOTAL : TOTAL + 1, lanes]
                values = logits_refs[g][pl.ds(start, BLOCK_ROWS), :]
                grad = (scattered - jnp.exp(values - log_total) * whole).astype(jnp.bfloat16)
                part = lax.dot_general(
                    grad, rows_refs[g][...], NN, preferred_element_type=jnp.float32
                )
                total = part if total is None else total + part
            out_refs[block // each][
                block % each * BLOCK_ROWS : (block % each + 1) * BLOCK_ROWS
            ] = total.astype(jnp.bfloat16)

    return call(
        kernel,
        tuple(bf16_rows(each * BLOCK_ROWS, width) for _ in range(outputs)),
        2 * blocks * BLOCK_ROWS * count * row_count * (width + 2 * entries),
        LARGE_LIMIT,
        in_specs=[smem_spec()] + [vmem_spec()] * (2 * count + 4),
        out_specs=tuple(vmem_spec() for _ in range(outputs)),
    )(order, *logits, *rows, occupancy, high, low, places)


def assemble(pieces, offsets, height, whole=None):
    count = len(pieces)
    part, width = pieces[0].shape
    short = height % part
    started = [] if whole is None else [whole]

    def kernel(offsets_ref, *refs):
        out_ref, sems = refs[count + len(started) :]

        def each(act):
            for index in range(count):
                offset = pl.multiple_of(offsets_ref[index], part)

                @pl.when(offset + part <= height)
                def _():
                    act(
                        pltpu.make_async_copy(
                            refs[index], out_ref.at[pl.ds(offset, part)], sems.at[index]
                        )
                    )

                if short:

                    @pl.when(offset + part > height)
                    def _():
                        act(
                            pltpu.make_async_copy(
                                refs[index].at[pl.ds(0, short)],
                                out_ref.at[pl.ds(height - short, short)],
                                sems.at[index],
                            )
                        )

        each(lambda copy: copy.start())
        each(lambda copy: copy.wait())

    anywhere = pl.BlockSpec(memory_space=pl.ANY)
    return call(
        kernel,
        bf16_rows(height, width),
        in_specs=[smem_spec()] + [vmem_spec()] * count + [anywhere] * len(started),
        out_specs=anywhere,
        scratch_shapes=[pltpu.SemaphoreType.DMA((count,))],
        input_output_aliases={} if whole is None else {1 + count: 0},
    )(offsets, *pieces, *started)


def swap(value, axis):
    return lax.ppermute(value, axis, [(0, 1), (1, 0)])


def crossed(value, axis, by):
    count = lax.axis_size(axis)
    return lax.ppermute(value, axis, [(i, i ^ by) for i in range(count)])


def after(value, *others):
    return lax.optimization_barrier((value,) + others)[0]


LINE_ORDER = np.array([[0, 1, 2, 3], [1, 0, 2, 3], [2, 3, 1, 0], [3, 2, 1, 0]])
MIDDLE = [(1, 2), (2, 1)]
OUTWARD = [(1, 0), (2, 3)]


def slot_orders(count):
    return LINE_ORDER if count == 4 else np.tile(np.arange(count), (count, 1))


def slot_tables(count):
    orders = slot_orders(count)
    tables = np.zeros((count, count, count), np.int32)
    for member in range(count):
        for k in range(count):
            source = member ^ k
            for slot in range(count):
                tables[member, k, slot] = list(orders[source]).index(orders[member][slot])
    return tables.reshape(count, count * count)


def wide(ref, start, size):
    return ref[pl.ds(start, size), :].astype(jnp.float32)


def sum_sent(own, came, places):
    height, width = own.shape
    part = height // 4

    def kernel(places_ref, own_ref, came_ref, *out_refs):
        section, outer = places_ref[0], places_ref[1]
        starts = (
            (1 - outer) * part,
            outer * part,
            (2 + 1 - section) * part,
            (2 + section) * part,
        )
        for start, out_ref in zip(starts, out_refs):
            start = pl.multiple_of(start, part)
            out_ref[...] = (wide(own_ref, start, part) + wide(came_ref, start, part)).astype(
                jnp.bfloat16
            )

    return call(
        kernel,
        tuple(bf16_rows(part, width) for _ in range(4)),
        1 << 20,
        in_specs=[smem_spec()] + [vmem_spec()] * 2,
        out_specs=tuple(vmem_spec() for _ in range(4)),
    )(places, own, came)


def sum_kept(own, came, arrived, places, keep):
    height, width = own.shape
    part = height // 4
    count = len(arrived) // 2

    def kernel(places_ref, own_ref, came_ref, *refs):
        section, outer = places_ref[0], places_ref[1]
        if not keep:
            section, outer = 1 - section, 1 - outer
        for side, start in enumerate((outer * part, (2 + section) * part)):
            start = pl.multiple_of(start, part)
            total = wide(own_ref, start, part) + wide(came_ref, start, part)
            for ref in refs[side * count : (side + 1) * count]:
                total = total + ref[...].astype(jnp.float32)
            refs[2 * count + side][...] = total.astype(jnp.bfloat16)

    return call(
        kernel,
        (bf16_rows(part, width), bf16_rows(part, width)),
        1 << 20,
        in_specs=[smem_spec()] + [vmem_spec()] * (2 + 2 * count),
        out_specs=(vmem_spec(), vmem_spec()),
    )(places, own, came, *arrived)


def per_device(
    frames,
    norm_gain,
    router,
    w_in,
    w_out,
    routing,
    head_gain,
    head_weight,
    frame_lengths,
    labels,
    label_lengths,
):
    sections = lax.axis_size("section")
    section_id = lax.axis_index("section")
    group_size = lax.axis_size("expert")
    member = lax.axis_index("expert")
    outer_size = lax.axis_size("dpo")
    inner_size = lax.axis_size("dpi")
    core = lax.axis_index("dpi")
    micro, utt_dev, frame_count, width = frames.shape
    label_max = labels.shape[2]
    experts = w_in.shape[1] * group_size
    pair_count = micro * utt_dev
    per_section = pair_count // sections
    first_pair = section_id * per_section
    share = (utt_dev * frame_count * 9 + 8 * experts - 1) // (8 * experts)
    filled = share * -(-per_section // utt_dev)
    capacity = round_up(filled + 1, 8)
    span = per_section * frame_count
    member_ref = member.astype(jnp.int32).reshape(1)

    def mine_of(value):
        return lax.dynamic_slice_in_dim(value, first_pair, per_section, 0)

    def exchange(blocks):
        return [blocks[0]] + [crossed(blocks[k], "expert", k) for k in range(1, group_size)]

    def lanes_of(ids):
        return jnp.pad(mine_of(ids), ((0, 0), (0, LANES - frame_count)), constant_values=-1)

    current = lax.dynamic_slice_in_dim(
        frames.reshape(pair_count * frame_count, width), first_pair * frame_count, span, 0
    )
    own_ids = routing.reshape(pair_count, frame_count)
    paired = sections == 2 and inner_size == 2
    if paired:
        other_ids = swap(own_ids, "section")
        all_ids = [
            jnp.where(section_id == layer, own_ids, other_ids) for layer in range(sections)
        ]
    else:
        all_ids = lax.all_gather(own_ids, "section")
    layer_ids = [lanes_of(all_ids[layer]) for layer in range(sections)]
    own_table = jnp.concatenate(
        [
            norm_gain,
            jnp.zeros((7, width), jnp.float32),
            jnp.transpose(router[0]).astype(jnp.float32),
            jnp.zeros((round_up(experts, 8) - experts, width), jnp.float32),
        ],
        axis=0,
    )
    own = (w_in[0, 0], w_out[0, 0])
    layers = []
    if paired:
        other_table = swap(own_table, "section")
    else:
        all_tables = lax.all_gather(own_table, "section")
        all_in = lax.all_gather(own[0], "section")
        all_out = lax.all_gather(own[1], "section")
        for layer in range(sections):
            chosen = (all_in[layer], all_out[layer])
            layers.append(((all_tables[layer],), chosen, [], jnp.ones((1,), jnp.int32)))

    outgoing = dispatch(current, layer_ids[0], member_ref, experts, capacity, frame_count)
    received = exchange(outgoing)
    if paired:
        sent_in, sent_out = half_weights(
            after(core.astype(jnp.int32).reshape(1), outgoing[0]), *own
        )
        came_in = swap(sent_in, "section")
        came_out = swap(sent_out, "section")
        came_in, came_out = lax.optimization_barrier((came_in, came_out, received))[:2]
        other = [(came_in, came_out), (swap(came_in, "dpi"), swap(came_out, "dpi"))]
        for layer in range(sections):
            mine = (section_id == layer).astype(jnp.int32).reshape(1)
            layers.append(((own_table, other_table), own, other, mine))

    labels, frame_lengths, label_lengths = lax.optimization_barrier(
        (labels, frame_lengths, label_lengths, outgoing[0])
    )[:3]
    notes = jnp.concatenate(
        [
            mine_of(labels.reshape(pair_count, label_max)),
            mine_of(frame_lengths.reshape(pair_count, 1)),
            mine_of(label_lengths.reshape(pair_count, 1)),
        ],
        axis=1,
    )
    notes = jnp.pad(notes, ((0, 0), (0, COLS - label_max - 2))).reshape(1, per_section * COLS)
    notes = jnp.pad(notes, ((0, 0), (0, LANES - per_section * COLS)))
    notes = jnp.concatenate([notes // LANES, notes % LANES], axis=1).astype(jnp.float32)
    notes = jnp.pad(notes, ((0, 0), (0, width - 2 * LANES)))
    shard = head_weight.shape[1]
    weight_rows = jnp.transpose(head_weight)
    line = group_size == 4
    tables = jnp.asarray(slot_tables(group_size))
    slots = lax.dynamic_index_in_dim(tables, member, 0, keepdims=False)
    outer = lax.axis_index("dpo")
    blocks = -(-shard // BLOCK_ROWS)
    tree = paired and outer_size == 2 and blocks == 8

    def pair_of(side, first, second):
        return [side * 4 + first, side * 4 + 2 + second]

    def offset_of(side, s, y):
        base = side * 4 * BLOCK_ROWS
        part = BLOCK_ROWS // 2
        return [
            base + s * BLOCK_ROWS + y * part,
            base + 2 * BLOCK_ROWS + y * BLOCK_ROWS + s * part,
        ]

    def whole_numbers(values):
        return jnp.stack([jnp.asarray(value, jnp.int32) for value in values])

    here, there = (section_id, outer), (1 - section_id, 1 - outer)
    sibling_order = whole_numbers(pair_of(1 - core, *there) + pair_of(1 - core, *here))
    sent_order = whole_numbers(pair_of(core, *there))
    kept_order = whole_numbers(pair_of(core, *here))
    chip_place = whole_numbers(here)
    first_offsets, last_offsets = [], offset_of(core, *there) + offset_of(1 - core, *there)
    for side in (core, 1 - core):
        for s, y in (here, (section_id, 1 - outer), (1 - section_id, outer)):
            first_offsets += offset_of(side, s, y)
    first_offsets, last_offsets = whole_numbers(first_offsets), whole_numbers(last_offsets)
    early = (
        notes,
        slots,
        head_gain.reshape(1, width),
        layer_ids[1:],
        sibling_order,
        sent_order,
        kept_order,
        chip_place,
        first_offsets,
        last_offsets,
    )
    early, received = lax.optimization_barrier((early, received))
    notes, slots, head_row, later_ids, sibling_order, sent_order = early[:6]
    kept_order, chip_place, first_offsets, last_offsets = early[6:]
    layer_ids = [layer_ids[0]] + list(later_ids)

    for layer in range(sections):
        choices, weights, others, pick_own = layers[layer]
        note = notes if layer == 0 else None
        done = run_expert(received, choices, weights, others, pick_own, filled, note)
        returned = exchange(done)
        if layer == 0:
            found = returned
            if not line:
                stacked = jnp.stack(returned)
                found = [
                    lax.dynamic_index_in_dim(stacked, member ^ k, 0, keepdims=False)
                    for k in range(group_size)
                ]
        if layer < sections - 1:
            current, outgoing = combine_and_dispatch(
                current,
                returned,
                layer_ids[layer],
                choices,
                pick_own,
                layer_ids[layer + 1],
                member_ref,
                experts,
                capacity,
                frame_count,
            )
            received = exchange(outgoing)
            if layer == 0:
                found = [after(found[0], current)] + list(found[1:])
                label_weight, places, names = label_rows(
                    weight_rows, found, member_ref, per_section, filled, label_max, line
                )
                received, label_weight = lax.optimization_barrier((received, label_weight))
        else:
            normed = combine_and_norm(
                current,
                returned,
                layer_ids[layer],
                choices,
                pick_own,
                head_row,
                member_ref,
                experts,
                capacity,
                frame_count,
            )

    def logits_of(fill, first, count, pieces, earlier=None):
        return head_logits(
            fill, first, count, pieces, member_ref, weight_rows, label_weight, frame_count, earlier
        )

    def stats_of(stats):
        first = crossed(stats, "expert", 1)
        return [stats, first, crossed(stats, "expert", 2), crossed(first, "expert", 2)]

    if line:
        beside = crossed(normed, "expert", 1)
        middle = lax.ppermute(normed, "expert", MIDDLE)
        far = lax.ppermute(beside, "expert", MIDDLE)
        outward = lax.ppermute(middle, "expert", OUTWARD)
        heads = [logits_of(fill_all, 0, 2, [normed, beside])]
        held, heads[0] = lax.optimization_barrier((far, heads[0]))
        last = lax.ppermute(held, "expert", OUTWARD)
        heads.append(logits_of(fill_far, 2, 2, [middle, outward, held, last], heads[0][2]))
        found = [stats_of(heads[1][2])]
    else:
        gathered = lax.all_gather(normed, "expert")
        pieces = [gathered[k] for k in range(group_size)]
        heads = [logits_of(fill_all, 0, group_size, pieces)]
        gathered = lax.all_gather(heads[0][2], "expert")
        found = [
            [
                lax.dynamic_index_in_dim(gathered, member ^ k, 0, keepdims=False)
                for k in range(group_size)
            ]
        ]
    kept_losses = per_section if line else group_size * per_section
    occupancy, high, low, losses = ctc_pass(
        found, slots, names, frame_count, label_max, kept_losses
    )
    if not line:
        losses = lax.dynamic_slice(losses, (0, member * per_section), (1, per_section))
    losses = jnp.transpose(losses)

    def gradient(order, outputs, each):
        return head_gradient(
            [head[0] for head in heads],
            [head[1] for head in heads],
            occupancy,
            high,
            low,
            places,
            order,
            outputs,
            each,
        )

    if tree:
        sibling_sent, sibling_kept = gradient(sibling_order, 2, 2)
        came_sent, came_kept = swap(sibling_sent, "dpi"), swap(sibling_kept, "dpi")
        own_sent = gradient(after(sent_order, sibling_sent), 1, 2)[0]
        a_far, a_near, b_far, b_near = sum_sent(own_sent, came_sent, chip_place)
        kept_order = after(kept_order, a_far)
        a_far, b_far = swap(a_far, "section"), swap(b_far, "dpo")
        a_near, b_near = swap(a_near, "section"), swap(b_near, "dpo")
        own_kept = gradient(kept_order, 1, 2)[0]
        a_on, b_on = sum_kept(own_kept, came_kept, [a_far, b_far], chip_place, False)
        a_in, b_in = swap(a_on, "dpo"), swap(b_on, "section")
        a, b = sum_kept(own_kept, came_kept, [a_near, a_in, b_near, b_in], chip_place, True)
        a_y, b_x = swap(a, "dpo"), swap(b, "section")
        b_y, a_x = swap(b, "dpo"), swap(a, "section")
        a_xy, b_xy = swap(a_y, "section"), swap(b_x, "dpo")
        b_y, a_x = lax.optimization_barrier((b_y, a_x, a_xy, b_xy))[:2]
        mine = [a, b, a_y, b_y, a_x, b_x]
        theirs = [swap(value, "dpi") for value in mine]
        whole = assemble(mine + theirs, first_offsets, shard)
        last = [a_xy, b_xy, swap(a_xy, "dpi"), swap(b_xy, "dpi")]
        whole = assemble(last, last_offsets, shard, whole)
    else:
        partial = gradient(jnp.arange(blocks, dtype=jnp.int32), 1, blocks)[0][:shard]
        whole = lax.psum(partial.astype(jnp.float32), ("section", "dpo", "dpi")).astype(
            jnp.bfloat16
        )
    return (losses, jnp.transpose(whole))


def solution(mesh):
    sections, group_size, spread = (mesh.shape[name] for name in ("section", "expert", "dp"))
    inner = 2 if spread % 2 == 0 else 1
    split = Mesh(
        mesh.devices.reshape(sections, group_size, spread // inner, inner),
        ("section", "expert", "dpo", "dpi"),
    )
    block = ("expert", "dpo", "dpi")
    placed = (
        P(None, block, None, None),
        P("section", None),
        P("section", None, None),
        P("section", "expert", None, None),
        P("section", "expert", None, None),
        P("section", None, block, None, None),
        P(),
        P(None, "expert"),
        P(None, block),
        P(None, block, None),
        P(None, block),
    )
    return jax.shard_map(
        per_device,
        mesh=split,
        in_specs=placed,
        out_specs=(P("section", block), P(None, "expert")),
        check_vma=False,
    )
```

```python
import jax
import jax.numpy as jnp
import numpy as np
from jax import lax
from jax.experimental import pallas as pl
from jax.experimental.pallas import tpu as pltpu
from jax.sharding import Mesh, PartitionSpec as P

EPSILON = 1e-06
LOG_ZERO = -1e30
VMEM_LIMIT = 12 * 1024 * 1024
LARGE_LIMIT = 24 * 1024 * 1024
LANES = 128
COLS = 16
PEAK, TOTAL, WHOLE = COLS - 3, COLS - 2, COLS - 3
BLOCK_ROWS = 256
NT = (((1,), (1,)), ((), ()))
NN = (((1,), (0,)), ((), ()))


def round_up(value, unit):
    return -(-value // unit) * unit


def vmem_spec():
    return pl.BlockSpec(memory_space=pltpu.VMEM)


def smem_spec():
    return pl.BlockSpec(memory_space=pltpu.SMEM)


def call(kernel, out_shape, flops=0, limit=VMEM_LIMIT, **options):
    return pl.pallas_call(
        kernel,
        out_shape=out_shape,
        compiler_params=pltpu.CompilerParams(vmem_limit_bytes=limit),
        cost_estimate=pl.CostEstimate(flops=flops, bytes_accessed=0, transcendentals=0),
        **options,
    )


def bf16_rows(count, width):
    return jax.ShapeDtypeStruct((count, width), jnp.bfloat16)


def as_mask(values):
    return values.astype(jnp.float32).astype(jnp.bfloat16)


def split_rows(values, out_refs, spare=None, note=None):
    size, width = out_refs[0].shape
    for turn, out_ref in enumerate(out_refs):
        part = values[turn * size : (turn + 1) * size]
        if note is not None:
            row = lax.broadcasted_iota(jnp.int32, (size, width), 0)
            part = jnp.where(row == spare, note, part)
        out_ref[...] = part.astype(jnp.bfloat16)


def join_rows(refs):
    return jnp.concatenate([ref[...].astype(jnp.float32) for ref in refs], axis=0)


def rms_scale(values, gain):
    values = values.astype(jnp.float32)
    scale = lax.rsqrt(jnp.mean(values * values, axis=-1, keepdims=True) + EPSILON)
    return (values * scale * gain).astype(jnp.bfloat16)


def expert_column(ids, frame_count):
    pairs = ids.shape[0]
    square = jnp.concatenate(
        [ids.astype(jnp.float32), jnp.full((LANES - pairs, LANES), -1.0, jnp.float32)], axis=0
    )
    turned = jnp.transpose(square, (1, 0)).astype(jnp.int32)
    return jnp.concatenate([turned[:frame_count, p : p + 1] for p in range(pairs)], axis=0)


def placement(column, member, experts, capacity):
    count = column.shape[0]
    relative = column ^ member
    lane = lax.broadcasted_iota(jnp.int32, (count, LANES), 1)
    one_hot = (lane == relative).astype(jnp.float32)
    before = lax.broadcasted_iota(jnp.int32, (count, count), 1) <= lax.broadcasted_iota(
        jnp.int32, (count, count), 0
    )
    rank = lax.dot_general(
        as_mask(before), one_hot.astype(jnp.bfloat16), NN, preferred_element_type=jnp.float32
    )
    start = (lane * capacity - 1).astype(jnp.float32)
    slots = jnp.sum(one_hot * (rank + start), axis=1, keepdims=True).astype(jnp.int32)
    places = lax.broadcasted_iota(jnp.int32, (count, experts * capacity), 1)
    return (places == slots).astype(jnp.float32)


def scatter_rows(rows, ids, member, experts, capacity, frame_count, out_refs):
    count = rows.shape[0]
    chosen = placement(expert_column(ids, frame_count), member, experts, capacity)
    tall = round_up(count, LANES)
    if tall > count:
        chosen = jnp.concatenate(
            [chosen, jnp.zeros((tall - count, chosen.shape[1]), jnp.float32)], axis=0
        )
    pick = jnp.transpose(chosen, (1, 0))[:, :count].astype(jnp.bfloat16)
    placed = lax.dot_general(pick, rows, NN, preferred_element_type=jnp.float32)
    split_rows(placed, out_refs)


def combine_rows(rows, returned, ids, table, member, experts, capacity, frame_count):
    column = expert_column(ids, frame_count)
    pick = placement(column, member, experts, capacity).astype(jnp.bfloat16)
    normed = rms_scale(rows, table[:1])
    router = jnp.concatenate(
        [table[8:], jnp.zeros((LANES + 8 - table.shape[0], rows.shape[1]), jnp.float32)], axis=0
    ).astype(jnp.bfloat16)
    logits = lax.dot_general(normed, router, NT, preferred_element_type=jnp.float32)
    lane = lax.broadcasted_iota(jnp.int32, logits.shape, 1)
    gate = jax.nn.sigmoid(jnp.sum(jnp.where(lane == column, logits, 0.0), axis=1, keepdims=True))
    stacked = join_rows(returned).astype(jnp.bfloat16)
    mixed = lax.dot_general(pick, stacked, NN, preferred_element_type=jnp.float32)
    return (rows.astype(jnp.float32) + gate * mixed).astype(jnp.bfloat16)


def dispatch(rows, ids, member, experts, capacity, frame_count):
    width = rows.shape[1]

    def kernel(member_ref, rows_ref, ids_ref, *out_refs):
        scatter_rows(
            rows_ref[...], ids_ref[...], member_ref[0], experts, capacity, frame_count, out_refs
        )

    return call(
        kernel,
        tuple(bf16_rows(capacity, width) for _ in range(experts)),
        1 << 27,
        in_specs=[smem_spec()] + [vmem_spec()] * 2,
        out_specs=tuple(vmem_spec() for _ in range(experts)),
    )(member, rows, ids)


def pick_table(pick_ref, tables):
    if len(tables) == 1:
        return tables[0][...]
    return jnp.where(pick_ref[0] == 1, tables[0][...], tables[1][...])


def run_expert(received, tables, own, other, pick_own, spare, note):
    count = len(received)
    capacity, width = received[0].shape
    others, choices = len(other), len(tables)
    noted = [] if note is None else [note]

    def kernel(pick_ref, in_ref, out_weight_ref, *refs):
        table_refs, refs = refs[:choices], refs[choices:]
        other_refs, refs = refs[: 2 * others], refs[2 * others :]
        received_refs, refs = refs[:count], refs[count:]
        out_refs = refs[len(noted) :]

        def work(pieces):
            gain = pick_table(pick_ref, table_refs)[:1]
            normed = rms_scale(join_rows(received_refs), gain)
            total = None
            for weight_in, weight_out in pieces:
                hidden = lax.dot_general(
                    normed, weight_in[...], NN, preferred_element_type=jnp.float32
                )
                active = (hidden / (1.0 + jnp.exp(-hidden))).astype(jnp.bfloat16)
                part = lax.dot_general(
                    active, weight_out[...], NN, preferred_element_type=jnp.float32
                )
                total = part if total is None else total + part
            split_rows(total, out_refs, spare, refs[0][...] if noted else None)

        if others == 0:
            work([(in_ref, out_weight_ref)])
            return

        @pl.when(pick_ref[0] == 1)
        def _():
            work([(in_ref, out_weight_ref)])

        @pl.when(pick_ref[0] != 1)
        def _():
            work([(other_refs[2 * i], other_refs[2 * i + 1]) for i in range(others)])

    flat = [weight for pair in other for weight in pair]
    return call(
        kernel,
        tuple(bf16_rows(capacity, width) for _ in range(count)),
        4 * count * capacity * width * own[0].shape[1],
        in_specs=[smem_spec()] + [vmem_spec()] * (2 + choices + 2 * others + count + len(noted)),
        out_specs=tuple(vmem_spec() for _ in range(count)),
    )(pick_own, *own, *tables, *flat, *received, *noted)


def combine_and_dispatch(
    rows, returned, ids, tables, pick_own, next_ids, member, experts, capacity, frame_count
):
    width = rows.shape[1]
    choices = len(tables)

    def kernel(member_ref, pick_ref, rows_ref, ids_ref, next_ref, *refs):
        table_refs, refs = refs[:choices], refs[choices:]
        returned_refs, x_ref, out_refs = refs[:experts], refs[experts], refs[experts + 1 :]
        mixed = combine_rows(
            rows_ref[...],
            returned_refs,
            ids_ref[...],
            pick_table(pick_ref, table_refs),
            member_ref[0],
            experts,
            capacity,
            frame_count,
        )
        x_ref[...] = mixed
        scatter_rows(
            mixed, next_ref[...], member_ref[0], experts, capacity, frame_count, out_refs
        )

    shapes = (bf16_rows(*rows.shape),) + tuple(
        bf16_rows(capacity, width) for _ in range(experts)
    )
    result = call(
        kernel,
        shapes,
        1 << 28,
        in_specs=[smem_spec()] * 2 + [vmem_spec()] * (3 + choices + experts),
        out_specs=tuple(vmem_spec() for _ in shapes),
    )(member, pick_own, rows, ids, next_ids, *tables, *returned)
    return result[0], result[1:]


def combine_and_norm(
    rows, returned, ids, tables, pick_own, head_gain, member, experts, capacity, frame_count
):
    choices = len(tables)

    def kernel(member_ref, pick_ref, rows_ref, ids_ref, head_ref, *refs):
        table_refs, refs = refs[:choices], refs[choices:]
        final = combine_rows(
            rows_ref[...],
            refs[:experts],
            ids_ref[...],
            pick_table(pick_ref, table_refs),
            member_ref[0],
            experts,
            capacity,
            frame_count,
        )
        refs[experts][...] = rms_scale(final, head_ref[...])

    return call(
        kernel,
        bf16_rows(*rows.shape),
        1 << 28,
        in_specs=[smem_spec()] * 2 + [vmem_spec()] * (3 + choices + experts),
        out_specs=vmem_spec(),
    )(member, pick_own, rows, ids, head_gain, *tables, *returned)


def half_weights(core, weight_in, weight_out):
    width, hidden = weight_in.shape
    half = hidden // 2

    def kernel(core_ref, in_ref, out_ref, half_in, half_out, sems):
        start = pl.multiple_of(core_ref[0] * half, half)
        copies = (
            pltpu.make_async_copy(in_ref.at[:, pl.ds(start, half)], half_in, sems.at[0]),
            pltpu.make_async_copy(out_ref.at[pl.ds(start, half)], half_out, sems.at[1]),
        )
        for copy in copies:
            copy.start()
        for copy in copies:
            copy.wait()

    return call(
        kernel,
        (bf16_rows(width, half), bf16_rows(half, width)),
        1 << 20,
        in_specs=[smem_spec()] + [pl.BlockSpec(memory_space=pl.ANY)] * 2,
        out_specs=(vmem_spec(), vmem_spec()),
        scratch_shapes=[pltpu.SemaphoreType.DMA((2,))],
    )(core, weight_in, weight_out)


def block_list(shard):
    return [(i, min(BLOCK_ROWS, shard - i)) for i in range(0, shard, BLOCK_ROWS)]


def label_rows(weight, notes, member, groups, pairs, spare, label_max, line):
    shard, width = weight.shape
    sources = len(notes)
    utterances = sources * groups * pairs
    entries = utterances * COLS

    def kernel(member_ref, weight_ref, *refs):
        note_refs = refs[:sources]
        out_ref, places_ref, names_ref, turned_ref = refs[sources:]
        place = member_ref[0]
        found = []
        for ref in note_refs:
            row = ref[...].astype(jnp.float32)[spare : spare + 1]
            found.append((row[:, :LANES] * LANES + row[:, LANES : 2 * LANES]).astype(jnp.int32))
        if line:
            ends = (place == 0) | (place == 3)
            found = [
                found[0],
                found[1],
                jnp.where(ends, found[2], found[3]),
                jnp.where(ends, found[3], found[2]),
            ]
        names_ref[...] = jnp.zeros(names_ref.shape, jnp.int32)
        for slot in range(sources):
            for pair in range(groups * pairs):
                row = (pair // pairs * sources + slot) * pairs + pair % pairs
                names_ref[row : row + 1, :COLS] = found[slot][:, pair * COLS : (pair + 1) * COLS]
        lane = lax.broadcasted_iota(jnp.int32, (utterances, LANES), 1)
        named = jnp.where(lane < label_max, names_ref[...], jnp.where(lane == label_max, 0, -1))
        local = named - place * shard
        local = jnp.where((named >= 0) & (local >= 0) & (local < shard), local, -1)
        square = jnp.concatenate(
            [
                local.astype(jnp.float32),
                jnp.full((LANES - utterances, LANES), -1.0, jnp.float32),
            ],
            axis=0,
        )
        turned = jnp.transpose(square, (1, 0))
        for utterance in range(utterances):
            turned_ref[utterance * COLS : (utterance + 1) * COLS] = jnp.broadcast_to(
                turned[:COLS, utterance : utterance + 1], (COLS, LANES)
            )
        places = turned_ref[:, :1].astype(jnp.int32)
        places_ref[...] = jnp.transpose(turned_ref[...], (1, 0))[:1].astype(jnp.int32)
        total = jnp.zeros((entries, width), jnp.float32)
        for first, size in block_list(shard):
            entry = first + lax.broadcasted_iota(jnp.int32, (entries, size), 1)
            total = total + lax.dot_general(
                as_mask(entry == places),
                weight_ref[first : first + size],
                NN,
                preferred_element_type=jnp.float32,
            )
        out_ref[...] = total.astype(jnp.bfloat16)

    return call(
        kernel,
        (
            bf16_rows(entries, width),
            jax.ShapeDtypeStruct((1, entries), jnp.int32),
            jax.ShapeDtypeStruct((utterances, LANES), jnp.int32),
        ),
        2 * shard * entries * width,
        LARGE_LIMIT,
        in_specs=[smem_spec()] + [vmem_spec()] * (1 + sources),
        out_specs=tuple(vmem_spec() for _ in range(3)),
        scratch_shapes=[pltpu.VMEM((entries, LANES), jnp.float32)],
    )(member, weight, *notes)


def head_logits(
    fill, first_slot, count, pieces, member, weight, label_weight, frame_count, earlier=None
):
    given = len(pieces)
    span, width = pieces[0].shape
    row_count = count * span
    shard = weight.shape[0]
    height = round_up(shard, BLOCK_ROWS)
    entries = row_count // frame_count * COLS
    first_entry = first_slot * entries // count
    others = [] if earlier is None else [earlier]
    ahead = 0 if earlier is None else earlier.shape[0]

    def kernel(member_ref, weight_ref, label_ref, *refs):
        piece_refs = refs[:given]
        logits_ref, rows_ref, stats_ref = refs[given + len(others) :]

        def put(slot, piece_ref):
            rows_ref[slot * span : (slot + 1) * span] = piece_ref[...]

        def put_if(condition, slot, piece_ref):
            @pl.when(condition)
            def _():
                put(slot, piece_ref)

        fill(member_ref[0], piece_refs, put, put_if)
        peak = jnp.full((1, row_count), LOG_ZERO, jnp.float32)
        total = jnp.zeros((1, row_count), jnp.float32)
        for first, size in block_list(shard):
            logits = lax.dot_general(
                weight_ref[first : first + size],
                rows_ref[...],
                NT,
                preferred_element_type=jnp.float32,
            )
            logits_ref[first : first + size] = logits
            before = peak
            peak = jnp.maximum(before, jnp.max(logits, axis=0, keepdims=True))
            total = total * jnp.exp(before - peak) + jnp.sum(
                jnp.exp(logits - peak), axis=0, keepdims=True
            )
        if height > shard:
            logits_ref[shard:] = jnp.full((height - shard, row_count), LOG_ZERO, jnp.float32)
        crossed = lax.dot_general(
            label_ref[first_entry : first_entry + entries],
            rows_ref[...],
            NT,
            preferred_element_type=jnp.float32,
        )
        owner = lax.broadcasted_iota(jnp.int32, (COLS, row_count), 1) // frame_count
        picked = jnp.zeros((COLS, row_count), jnp.float32)
        for utterance in range(entries // COLS):
            part = crossed[utterance * COLS : (utterance + 1) * COLS]
            picked = picked + jnp.where(owner == utterance, part, 0.0)
        place = lax.broadcasted_iota(jnp.int32, (COLS, row_count), 0)
        stats = jnp.where(place == PEAK, peak, picked)
        stats = jnp.where(place == TOTAL, total, stats)
        for slot in range(ahead):
            stats_ref[slot] = refs[given][slot]
        for slot in range(count):
            stats_ref[ahead + slot] = stats[:, slot * span : (slot + 1) * span]

    return call(
        kernel,
        (
            jax.ShapeDtypeStruct((height, row_count), jnp.float32),
            bf16_rows(row_count, width),
            jax.ShapeDtypeStruct((ahead + count, COLS, span), jnp.float32),
        ),
        2 * height * row_count * width,
        LARGE_LIMIT,
        in_specs=[smem_spec()] + [vmem_spec()] * (2 + given + len(others)),
        out_specs=tuple(vmem_spec() for _ in range(3)),
    )(member, weight, label_weight, *pieces, *others)


def fill_line(place, piece_refs, put, put_if):
    own, beside, middle, outward, far, last = piece_refs
    ends = (place == 0) | (place == 3)
    inner = (place == 1) | (place == 2)
    put(0, own)
    put(1, beside)
    put_if(ends, 2, outward)
    put_if(ends, 3, last)
    put_if(inner, 2, middle)
    put_if(inner, 3, far)


def fill_all(place, piece_refs, put, put_if):
    for slot, piece_ref in enumerate(piece_refs):
        put(slot, piece_ref)


def log_add(first, second):
    peak = jnp.maximum(first, second)
    return peak + jnp.log(jnp.exp(first - peak) + jnp.exp(second - peak))


def log_add3(first, second, third):
    peak = jnp.maximum(jnp.maximum(first, second), third)
    return peak + jnp.log(
        jnp.exp(first - peak) + jnp.exp(second - peak) + jnp.exp(third - peak)
    )


def ctc_pass(stats, slots, notes, frame_count, label_max, parts, kept):
    calls, sources = len(stats), len(stats[0])
    each, _, span = stats[0][0].shape
    count = calls * each
    row_count = count * span
    utterances = notes.shape[0]
    entries = utterances * COLS
    tall = round_up(span, LANES)

    def kernel(slots_ref, notes_ref, *refs):
        (
            out_ref,
            high_ref,
            low_ref,
            loss_ref,
            turn_ref,
            emission_ref,
            emit_blank,
            emit_label,
            blank_fwd,
            label_fwd,
            blank_bwd,
            label_bwd,
            occupancy_ref,
        ) = refs[calls * sources :]
        place = lax.broadcasted_iota(jnp.int32, (COLS, span), 0)
        turn_ref[...] = jnp.zeros(turn_ref.shape, jnp.float32)
        for slot in range(count):
            found = []
            for k in range(sources):
                where = slots_ref[k * count + slot]
                part = refs[k][where % each]
                for other in range(1, calls):
                    later = refs[other * sources + k][where % each]
                    part = jnp.where(where >= other * each, later, part)
                found.append(part)
            joined = found[0]
            peak = found[0][PEAK : PEAK + 1]
            for other in found[1:]:
                joined = joined + other
                peak = jnp.maximum(peak, other[PEAK : PEAK + 1])
            total = jnp.zeros((1, span), jnp.float32)
            for other in found:
                total = total + other[TOTAL : TOTAL + 1] * jnp.exp(other[PEAK : PEAK + 1] - peak)
            log_total = peak + jnp.log(total)
            turn_ref[:COLS, :span] = jnp.where(place == TOTAL, log_total, joined - log_total)
            emission_ref[slot * span : (slot + 1) * span] = jnp.transpose(turn_ref[...], (1, 0))[
                :span
            ]

        lane = lax.broadcasted_iota(jnp.int32, (utterances, LANES), 1)
        is_label = lane < label_max
        is_blank = lane <= label_max
        names = jnp.where(is_label, notes_ref[...], 0)
        earlier = pltpu.roll(names, 1, 1)
        skip = is_label & (lane >= 1) & (names != 0) & (names != earlier)
        later = pltpu.roll(names, LANES - 1, 1)
        skip_next = (lane < label_max - 1) & (later != 0) & (later != names)
        frames = notes_ref[:, label_max : label_max + 1]
        counts = notes_ref[:, label_max + 1 : label_max + 2]
        ends_blank = jnp.where(lane == counts, 0.0, LOG_ZERO)
        ends_label = jnp.where(lane == counts - 1, 0.0, LOG_ZERO)

        def spread(step, carry):
            row = emission_ref[pl.ds(step, utterances, stride=frame_count), :]
            blank = jnp.sum(jnp.where(lane == label_max, row, 0.0), axis=1, keepdims=True)
            emit_blank[step] = jnp.where(is_blank, blank, LOG_ZERO)
            emit_label[step] = jnp.where(is_label, row, LOG_ZERO)
            return carry

        lax.fori_loop(0, frame_count, spread, 0, unroll=16)

        def advance(step, carry):
            fwd_blank, fwd_label, bwd_blank, bwd_label = carry
            moved = jnp.where(lane == 0, LOG_ZERO, pltpu.roll(fwd_label, 1, 1))
            new_blank = log_add(fwd_blank, moved) + emit_blank[step]
            new_label = (
                log_add3(fwd_label, fwd_blank, jnp.where(skip, moved, LOG_ZERO))
                + emit_label[step]
            )
            alive = step < frames
            fwd_blank = jnp.where(alive, new_blank, fwd_blank)
            fwd_label = jnp.where(alive, new_label, fwd_label)
            blank_fwd[step] = fwd_blank
            label_fwd[step] = fwd_label

            back = frame_count - 1 - step
            out_blank = bwd_blank + emit_blank[back + 1]
            out_label = bwd_label + emit_label[back + 1]
            next_blank = pltpu.roll(out_blank, LANES - 1, 1)
            next_label = jnp.where(skip_next, pltpu.roll(out_label, LANES - 1, 1), LOG_ZERO)
            ended = back >= frames - 1
            bwd_blank = jnp.where(ended, ends_blank, log_add(out_blank, out_label))
            bwd_label = jnp.where(
                ended, ends_label, log_add3(out_label, next_blank, next_label)
            )
            blank_bwd[back] = bwd_blank
            label_bwd[back] = bwd_label
            return (fwd_blank, fwd_label, bwd_blank, bwd_label)

        first_blank = jnp.where(lane == 0, emit_blank[0], LOG_ZERO)
        first_label = jnp.where(lane == 0, emit_label[0], LOG_ZERO)
        blank_fwd[0] = first_blank
        label_fwd[0] = first_label
        blank_bwd[frame_count - 1] = ends_blank
        label_bwd[frame_count - 1] = ends_label
        fwd_blank, fwd_label, _, _ = lax.fori_loop(
            1, frame_count, advance, (first_blank, first_label, ends_blank, ends_label), unroll=4
        )
        end_state = jnp.sum(jnp.where(lane == counts, fwd_blank, 0.0), axis=1, keepdims=True)
        near_state = jnp.sum(jnp.where(lane == counts - 1, fwd_label, 0.0), axis=1, keepdims=True)
        log_like = log_add(end_state, near_state)
        turned_losses = jnp.transpose(jnp.broadcast_to(-log_like, (utterances, LANES)), (1, 0))
        for part in range(parts):
            first = part * utterances // parts
            loss_ref[:, part * kept : (part + 1) * kept] = turned_losses[:1, first : first + kept]

        def occupy(step, carry):
            blank = jnp.exp(blank_fwd[step] + blank_bwd[step] - log_like)
            label = jnp.exp(label_fwd[step] + label_bwd[step] - log_like)
            blank = jnp.sum(jnp.where(is_blank, blank, 0.0), axis=1, keepdims=True)
            label = jnp.where(is_label, label, 0.0)
            whole = blank + jnp.sum(label, axis=1, keepdims=True)
            filled = jnp.where(lane == label_max, blank, label)
            filled = jnp.where(lane == WHOLE, whole, filled)
            filled = jnp.where(step < frames, -filled, 0.0)
            row = emission_ref[pl.ds(step, utterances, stride=frame_count), :]
            occupancy_ref[pl.ds(step, utterances, stride=frame_count), :] = jnp.where(
                lane == TOTAL, row, filled
            )
            return carry

        lax.fori_loop(0, frame_count, occupy, 0, unroll=16)
        turned = jnp.transpose(occupancy_ref[...], (1, 0))[:COLS]
        out_ref[...] = turned
        row_place = lax.broadcasted_iota(jnp.int32, (COLS, row_count), 0)
        owner = lax.broadcasted_iota(jnp.int32, (COLS, row_count), 1) // frame_count
        source = jnp.where(row_place < WHOLE, turned, 0.0)
        for utterance in range(utterances):
            part = jnp.where(owner == utterance, source, 0.0)
            high = part.astype(jnp.bfloat16)
            high_ref[utterance * COLS : (utterance + 1) * COLS] = high
            low_ref[utterance * COLS : (utterance + 1) * COLS] = (
                part - high.astype(jnp.float32)
            ).astype(jnp.bfloat16)

    held = pltpu.VMEM((frame_count, utterances, LANES), jnp.float32)
    table = pltpu.VMEM((row_count, LANES), jnp.float32)
    return call(
        kernel,
        (
            jax.ShapeDtypeStruct((COLS, row_count), jnp.float32),
            bf16_rows(entries, row_count),
            bf16_rows(entries, row_count),
            jax.ShapeDtypeStruct((1, parts * kept), jnp.float32),
        ),
        1 << 26,
        in_specs=[smem_spec()] + [vmem_spec()] * (1 + calls * sources),
        out_specs=tuple(vmem_spec() for _ in range(4)),
        scratch_shapes=[pltpu.VMEM((LANES, tall), jnp.float32), table]
        + [held] * 6
        + [table],
    )(slots, notes, *[value for group in stats for value in group])


def head_gradient(logits, rows, occupancy, high, low, places, order, outputs, each):
    count = len(logits)
    row_count, width = rows[0].shape
    entries = places.shape[1]
    blocks = outputs * each

    def kernel(order_ref, *refs):
        logits_refs, rows_refs = refs[:count], refs[count : 2 * count]
        occupancy_ref, high_ref, low_ref, places_ref = refs[2 * count : 2 * count + 4]
        out_refs = refs[2 * count + 4 :]
        for block in range(blocks):
            start = pl.multiple_of(order_ref[block] * BLOCK_ROWS, BLOCK_ROWS)
            entry = start + lax.broadcasted_iota(jnp.int32, (BLOCK_ROWS, entries), 0)
            select = as_mask(entry == places_ref[...])
            total = None
            for g in range(count):
                lanes = slice(g * row_count, (g + 1) * row_count)
                scattered = lax.dot_general(
                    select, high_ref[:, lanes], NN, preferred_element_type=jnp.float32
                ) + lax.dot_general(
                    select, low_ref[:, lanes], NN, preferred_element_type=jnp.float32
                )
                whole = occupancy_ref[WHOLE : WHOLE + 1, lanes]
                log_total = occupancy_ref[TOTAL : TOTAL + 1, lanes]
                values = logits_refs[g][pl.ds(start, BLOCK_ROWS), :]
                grad = (scattered - jnp.exp(values - log_total) * whole).astype(jnp.bfloat16)
                part = lax.dot_general(
                    grad, rows_refs[g][...], NN, preferred_element_type=jnp.float32
                )
                total = part if total is None else total + part
            out_refs[block // each][
                block % each * BLOCK_ROWS : (block % each + 1) * BLOCK_ROWS
            ] = total.astype(jnp.bfloat16)

    return call(
        kernel,
        tuple(bf16_rows(each * BLOCK_ROWS, width) for _ in range(outputs)),
        2 * blocks * BLOCK_ROWS * count * row_count * (width + 2 * entries),
        LARGE_LIMIT,
        in_specs=[smem_spec()] + [vmem_spec()] * (2 * count + 4),
        out_specs=tuple(vmem_spec() for _ in range(outputs)),
    )(order, *logits, *rows, occupancy, high, low, places)


def assemble(pieces, offsets, height, whole=None):
    count = len(pieces)
    part, width = pieces[0].shape
    short = height % part
    started = [] if whole is None else [whole]

    def kernel(offsets_ref, *refs):
        out_ref, sems = refs[count + len(started) :]

        def each(act):
            for index in range(count):
                offset = pl.multiple_of(offsets_ref[index], part)

                @pl.when(offset + part <= height)
                def _():
                    act(
                        pltpu.make_async_copy(
                            refs[index], out_ref.at[pl.ds(offset, part)], sems.at[index]
                        )
                    )

                if short:

                    @pl.when(offset + part > height)
                    def _():
                        act(
                            pltpu.make_async_copy(
                                refs[index].at[pl.ds(0, short)],
                                out_ref.at[pl.ds(height - short, short)],
                                sems.at[index],
                            )
                        )

        each(lambda copy: copy.start())
        each(lambda copy: copy.wait())

    anywhere = pl.BlockSpec(memory_space=pl.ANY)
    return call(
        kernel,
        bf16_rows(height, width),
        in_specs=[smem_spec()] + [vmem_spec()] * count + [anywhere] * len(started),
        out_specs=anywhere,
        scratch_shapes=[pltpu.SemaphoreType.DMA((count,))],
        input_output_aliases={} if whole is None else {1 + count: 0},
    )(offsets, *pieces, *started)


def swap(value, axis):
    return lax.ppermute(value, axis, [(0, 1), (1, 0)])


def crossed(value, axis, by):
    count = lax.axis_size(axis)
    return lax.ppermute(value, axis, [(i, i ^ by) for i in range(count)])


def after(value, *others):
    return lax.optimization_barrier((value,) + others)[0]


LINE_ORDER = np.array([[0, 1, 2, 3], [1, 0, 2, 3], [2, 3, 1, 0], [3, 2, 1, 0]])
MIDDLE = [(1, 2), (2, 1)]
OUTWARD = [(1, 0), (2, 3)]


def slot_orders(count):
    return LINE_ORDER if count == 4 else np.tile(np.arange(count), (count, 1))


def slot_tables(count, groups):
    orders = slot_orders(count)
    tables = np.zeros((count, count, count), np.int32)
    for member in range(count):
        for k in range(count):
            source = member ^ k
            for slot in range(count):
                tables[member, k, slot] = list(orders[source]).index(orders[member][slot])
    tables = np.concatenate([tables + g * count for g in range(groups)], axis=2)
    return tables.reshape(count, groups * count * count)


def wide(ref, start, size):
    return ref[pl.ds(start, size), :].astype(jnp.float32)


def sum_sent(own, came, places):
    height, width = own.shape
    part = height // 4

    def kernel(places_ref, own_ref, came_ref, *out_refs):
        section, outer = places_ref[0], places_ref[1]
        starts = (
            (1 - outer) * part,
            outer * part,
            (2 + 1 - section) * part,
            (2 + section) * part,
        )
        for start, out_ref in zip(starts, out_refs):
            start = pl.multiple_of(start, part)
            out_ref[...] = (wide(own_ref, start, part) + wide(came_ref, start, part)).astype(
                jnp.bfloat16
            )

    return call(
        kernel,
        tuple(bf16_rows(part, width) for _ in range(4)),
        1 << 20,
        in_specs=[smem_spec()] + [vmem_spec()] * 2,
        out_specs=tuple(vmem_spec() for _ in range(4)),
    )(places, own, came)


def sum_kept(own, came, arrived, places, keep):
    height, width = own.shape
    part = height // 4
    count = len(arrived) // 2

    def kernel(places_ref, own_ref, came_ref, *refs):
        section, outer = places_ref[0], places_ref[1]
        if not keep:
            section, outer = 1 - section, 1 - outer
        for side, start in enumerate((outer * part, (2 + section) * part)):
            start = pl.multiple_of(start, part)
            total = wide(own_ref, start, part) + wide(came_ref, start, part)
            for ref in refs[side * count : (side + 1) * count]:
                total = total + ref[...].astype(jnp.float32)
            refs[2 * count + side][...] = total.astype(jnp.bfloat16)

    return call(
        kernel,
        (bf16_rows(part, width), bf16_rows(part, width)),
        1 << 20,
        in_specs=[smem_spec()] + [vmem_spec()] * (2 + 2 * count),
        out_specs=(vmem_spec(), vmem_spec()),
    )(places, own, came, *arrived)


def per_device(
    frames,
    norm_gain,
    router,
    w_in,
    w_out,
    routing,
    head_gain,
    head_weight,
    frame_lengths,
    labels,
    label_lengths,
):
    sections = lax.axis_size("section")
    section_id = lax.axis_index("section")
    group_size = lax.axis_size("expert")
    member = lax.axis_index("expert")
    outer_size = lax.axis_size("dpo")
    inner_size = lax.axis_size("dpi")
    core = lax.axis_index("dpi")
    micro, utt_dev, frame_count, width = frames.shape
    label_max = labels.shape[2]
    experts = w_in.shape[1] * group_size
    pair_count = micro * utt_dev
    per_section = pair_count // sections
    first_pair = section_id * per_section
    share = (utt_dev * frame_count * 9 + 8 * experts - 1) // (8 * experts)
    group_count = 2 if per_section % (2 * utt_dev) == 0 else 1
    group_pairs = per_section // group_count
    filled = share * -(-group_pairs // utt_dev)
    capacity = round_up(filled + 1, 8)
    span = group_pairs * frame_count
    member_ref = member.astype(jnp.int32).reshape(1)

    def mine_of(value):
        return lax.dynamic_slice_in_dim(value, first_pair, per_section, 0)

    def exchange(blocks):
        return [blocks[0]] + [crossed(blocks[k], "expert", k) for k in range(1, group_size)]

    def lanes_of(ids):
        ids = jnp.pad(mine_of(ids), ((0, 0), (0, LANES - frame_count)), constant_values=-1)
        return [ids[g * group_pairs : (g + 1) * group_pairs] for g in range(group_count)]

    flat_frames = frames.reshape(pair_count * frame_count, width)
    current = [
        lax.dynamic_slice_in_dim(flat_frames, first_pair * frame_count + g * span, span, 0)
        for g in range(group_count)
    ]
    own_ids = routing.reshape(pair_count, frame_count)
    paired = sections == 2 and inner_size == 2
    if paired:
        other_ids = swap(own_ids, "section")
        all_ids = [
            jnp.where(section_id == layer, own_ids, other_ids) for layer in range(sections)
        ]
    else:
        all_ids = lax.all_gather(own_ids, "section")
    layer_ids = [lanes_of(all_ids[layer]) for layer in range(sections)]
    own_table = jnp.concatenate(
        [
            norm_gain,
            jnp.zeros((7, width), jnp.float32),
            jnp.transpose(router[0]).astype(jnp.float32),
            jnp.zeros((round_up(experts, 8) - experts, width), jnp.float32),
        ],
        axis=0,
    )
    own = (w_in[0, 0], w_out[0, 0])
    layers = []
    if paired:
        other_table = swap(own_table, "section")
    else:
        all_tables = lax.all_gather(own_table, "section")
        all_in = lax.all_gather(own[0], "section")
        all_out = lax.all_gather(own[1], "section")
        for layer in range(sections):
            chosen = (all_in[layer], all_out[layer])
            layers.append(((all_tables[layer],), chosen, [], jnp.ones((1,), jnp.int32)))

    outgoing = [
        dispatch(current[g], layer_ids[0][g], member_ref, experts, capacity, frame_count)
        for g in range(group_count)
    ]
    received = [exchange(blocks) for blocks in outgoing]
    if paired:
        sent_in, sent_out = half_weights(
            after(core.astype(jnp.int32).reshape(1), outgoing[0][0]), *own
        )
        came_in = swap(sent_in, "section")
        came_out = swap(sent_out, "section")
        came_in, came_out = lax.optimization_barrier((came_in, came_out, received))[:2]
        other = [(came_in, came_out), (swap(came_in, "dpi"), swap(came_out, "dpi"))]
        for layer in range(sections):
            mine = (section_id == layer).astype(jnp.int32).reshape(1)
            layers.append(((own_table, other_table), own, other, mine))

    labels, frame_lengths, label_lengths = lax.optimization_barrier(
        (labels, frame_lengths, label_lengths, outgoing[-1][0])
    )[:3]
    notes = jnp.concatenate(
        [
            mine_of(labels.reshape(pair_count, label_max)),
            mine_of(frame_lengths.reshape(pair_count, 1)),
            mine_of(label_lengths.reshape(pair_count, 1)),
        ],
        axis=1,
    )
    notes = jnp.pad(notes, ((0, 0), (0, COLS - label_max - 2))).reshape(1, per_section * COLS)
    notes = jnp.pad(notes, ((0, 0), (0, LANES - per_section * COLS)))
    notes = jnp.concatenate([notes // LANES, notes % LANES], axis=1).astype(jnp.float32)
    notes = jnp.pad(notes, ((0, 0), (0, width - 2 * LANES)))
    shard = head_weight.shape[1]
    weight_rows = jnp.transpose(head_weight)
    line = group_size == 4
    tables = jnp.asarray(slot_tables(group_size, group_count))
    slots = lax.dynamic_index_in_dim(tables, member, 0, keepdims=False)
    outer = lax.axis_index("dpo")
    blocks = -(-shard // BLOCK_ROWS)
    tree = paired and outer_size == 2 and blocks == 8

    def pair_of(side, first, second):
        return [side * 4 + first, side * 4 + 2 + second]

    def offset_of(side, s, y):
        base = side * 4 * BLOCK_ROWS
        part = BLOCK_ROWS // 2
        return [
            base + s * BLOCK_ROWS + y * part,
            base + 2 * BLOCK_ROWS + y * BLOCK_ROWS + s * part,
        ]

    def whole_numbers(values):
        return jnp.stack([jnp.asarray(value, jnp.int32) for value in values])

    here, there = (section_id, outer), (1 - section_id, 1 - outer)
    sibling_order = whole_numbers(pair_of(1 - core, *there) + pair_of(1 - core, *here))
    sent_order = whole_numbers(pair_of(core, *there))
    kept_order = whole_numbers(pair_of(core, *here))
    chip_place = whole_numbers(here)
    first_offsets, last_offsets = [], offset_of(core, *there) + offset_of(1 - core, *there)
    for side in (core, 1 - core):
        for s, y in (here, (section_id, 1 - outer), (1 - section_id, outer)):
            first_offsets += offset_of(side, s, y)
    first_offsets, last_offsets = whole_numbers(first_offsets), whole_numbers(last_offsets)
    early = (
        notes,
        slots,
        head_gain.reshape(1, width),
        layer_ids[1:],
        sibling_order,
        sent_order,
        kept_order,
        chip_place,
        first_offsets,
        last_offsets,
    )
    early, received = lax.optimization_barrier((early, received))
    notes, slots, head_row, later_ids, sibling_order, sent_order = early[:6]
    kept_order, chip_place, first_offsets, last_offsets = early[6:]
    layer_ids = [layer_ids[0]] + list(later_ids)

    def tied(value, others, g):
        marks = [other for i, other in enumerate(others) if i != g]
        return after(value, *marks) if marks else value

    normed, marks = [], []
    for layer in range(sections):
        choices, weights, others, pick_own = layers[layer]
        done = [
            run_expert(
                received[g],
                choices,
                weights,
                others,
                tied(pick_own, marks, g),
                filled,
                notes if layer == 0 and g == 0 else None,
            )
            for g in range(group_count)
        ]
        returned = [exchange(parts) for parts in done]
        marks = [parts[0] for parts in done]
        tokens = [tied(member_ref, marks, g) for g in range(group_count)]
        sizes = (experts, capacity, frame_count)
        if layer < sections - 1:
            made = [
                combine_and_dispatch(
                    current[g],
                    returned[g],
                    layer_ids[layer][g],
                    choices,
                    pick_own,
                    layer_ids[layer + 1][g],
                    tokens[g],
                    *sizes,
                )
                for g in range(group_count)
            ]
            current = [pair[0] for pair in made]
            received = [exchange(pair[1]) for pair in made]
            marks = current
        else:
            normed = [
                combine_and_norm(
                    current[g],
                    returned[g],
                    layer_ids[layer][g],
                    choices,
                    pick_own,
                    head_row,
                    tokens[g],
                    *sizes,
                )
                for g in range(group_count)
            ]
        if layer == 0:
            found = list(returned[0])
            if not line:
                stacked = jnp.stack(found)
                found = [
                    lax.dynamic_index_in_dim(stacked, member ^ k, 0, keepdims=False)
                    for k in range(group_size)
                ]
            label_weight, places, names = label_rows(
                weight_rows, found, member_ref, group_count, group_pairs, filled, label_max, line
            )

    def logits_of(fill, first, count, pieces, earlier=None):
        return head_logits(
            fill, first, count, pieces, member_ref, weight_rows, label_weight, frame_count, earlier
        )

    def stats_of(stats):
        first = crossed(stats, "expert", 1)
        return [stats, first, crossed(stats, "expert", 2), crossed(first, "expert", 2)]

    heads, found = [], []
    for g in range(group_count):
        if line:
            beside = crossed(normed[g], "expert", 1)
            middle = lax.ppermute(normed[g], "expert", MIDDLE)
            far = lax.ppermute(beside, "expert", MIDDLE)
            outward = lax.ppermute(middle, "expert", OUTWARD)
            last = lax.ppermute(far, "expert", OUTWARD)
            pieces = [normed[g], beside, middle, outward, far, last]
            heads.append(logits_of(fill_line, g * group_size, group_size, pieces))
            found.append(stats_of(heads[g][2]))
        else:
            gathered = lax.all_gather(normed[g], "expert")
            pieces = [gathered[k] for k in range(group_size)]
            heads.append(logits_of(fill_all, g * group_size, group_size, pieces))
            gathered = lax.all_gather(heads[g][2], "expert")
            found.append(
                [
                    lax.dynamic_index_in_dim(gathered, member ^ k, 0, keepdims=False)
                    for k in range(group_size)
                ]
            )
    kept_losses = group_pairs if line else group_size * group_pairs
    occupancy, high, low, losses = ctc_pass(
        found, slots, names, frame_count, label_max, group_count, kept_losses
    )
    if not line:
        pairs = losses.reshape(group_count, group_size, group_pairs)
        losses = lax.dynamic_index_in_dim(pairs, member, 1).reshape(1, per_section)
    losses = jnp.transpose(losses)

    def gradient(order, outputs, each):
        return head_gradient(
            [head[0] for head in heads],
            [head[1] for head in heads],
            occupancy,
            high,
            low,
            places,
            order,
            outputs,
            each,
        )

    if tree:
        sibling_sent, sibling_kept = gradient(sibling_order, 2, 2)
        came_sent, came_kept = swap(sibling_sent, "dpi"), swap(sibling_kept, "dpi")
        own_sent = gradient(after(sent_order, sibling_sent), 1, 2)[0]
        a_far, a_near, b_far, b_near = sum_sent(own_sent, came_sent, chip_place)
        kept_order = after(kept_order, a_far)
        a_far, b_far = swap(a_far, "section"), swap(b_far, "dpo")
        a_near, b_near = swap(a_near, "section"), swap(b_near, "dpo")
        own_kept = gradient(kept_order, 1, 2)[0]
        a_on, b_on = sum_kept(own_kept, came_kept, [a_far, b_far], chip_place, False)
        a_in, b_in = swap(a_on, "dpo"), swap(b_on, "section")
        a, b = sum_kept(own_kept, came_kept, [a_near, a_in, b_near, b_in], chip_place, True)
        a_y, b_x = swap(a, "dpo"), swap(b, "section")
        b_y, a_x = swap(b, "dpo"), swap(a, "section")
        a_xy, b_xy = swap(a_y, "section"), swap(b_x, "dpo")
        b_y, a_x = lax.optimization_barrier((b_y, a_x, a_xy, b_xy))[:2]
        mine = [a, b, a_y, b_y, a_x, b_x]
        theirs = [swap(value, "dpi") for value in mine]
        whole = assemble(mine + theirs, first_offsets, shard)
        last = [a_xy, b_xy, swap(a_xy, "dpi"), swap(b_xy, "dpi")]
        whole = assemble(last, last_offsets, shard, whole)
    else:
        partial = gradient(jnp.arange(blocks, dtype=jnp.int32), 1, blocks)[0][:shard]
        whole = lax.psum(partial.astype(jnp.float32), ("section", "dpo", "dpi")).astype(
            jnp.bfloat16
        )
    return (losses, jnp.transpose(whole))


def solution(mesh):
    sections, group_size, spread = (mesh.shape[name] for name in ("section", "expert", "dp"))
    inner = 2 if spread % 2 == 0 else 1
    split = Mesh(
        mesh.devices.reshape(sections, group_size, spread // inner, inner),
        ("section", "expert", "dpo", "dpi"),
    )
    block = ("expert", "dpo", "dpi")
    placed = (
        P(None, block, None, None),
        P("section", None),
        P("section", None, None),
        P("section", "expert", None, None),
        P("section", "expert", None, None),
        P("section", None, block, None, None),
        P(),
        P(None, "expert"),
        P(None, block),
        P(None, block, None),
        P(None, block),
    )
    return jax.shard_map(
        per_device,
        mesh=split,
        in_specs=placed,
        out_specs=(P("section", block), P(None, "expert")),
        check_vma=False,
    )
```

```python
import jax
import jax.numpy as jnp
import numpy as np
from jax import lax
from jax.experimental import pallas as pl
from jax.experimental.pallas import tpu as pltpu
from jax.sharding import Mesh, PartitionSpec as P

EPSILON = 1e-06
LOG_ZERO = -1e30
VMEM_LIMIT = 12 * 1024 * 1024
LARGE_LIMIT = 24 * 1024 * 1024
LANES = 128
COLS = 16
PEAK, TOTAL, WHOLE = COLS - 3, COLS - 2, COLS - 3
BLOCK_ROWS = 256
NT = (((1,), (1,)), ((), ()))
NN = (((1,), (0,)), ((), ()))


def round_up(value, unit):
    return -(-value // unit) * unit


def vmem_spec():
    return pl.BlockSpec(memory_space=pltpu.VMEM)


def smem_spec():
    return pl.BlockSpec(memory_space=pltpu.SMEM)


def call(kernel, out_shape, flops=0, limit=VMEM_LIMIT, **options):
    return pl.pallas_call(
        kernel,
        out_shape=out_shape,
        compiler_params=pltpu.CompilerParams(vmem_limit_bytes=limit),
        cost_estimate=pl.CostEstimate(flops=flops, bytes_accessed=0, transcendentals=0),
        **options,
    )


def bf16_rows(count, width):
    return jax.ShapeDtypeStruct((count, width), jnp.bfloat16)


def as_mask(values):
    return values.astype(jnp.float32).astype(jnp.bfloat16)


def split_rows(values, out_refs, spare=None, note=None):
    size, width = out_refs[0].shape
    for turn, out_ref in enumerate(out_refs):
        part = values[turn * size : (turn + 1) * size]
        if note is not None:
            row = lax.broadcasted_iota(jnp.int32, (size, width), 0)
            part = jnp.where(row == spare, note, part)
        out_ref[...] = part.astype(jnp.bfloat16)


def join_rows(refs):
    return jnp.concatenate([ref[...].astype(jnp.float32) for ref in refs], axis=0)


def rms_scale(values, gain):
    values = values.astype(jnp.float32)
    scale = lax.rsqrt(jnp.mean(values * values, axis=-1, keepdims=True) + EPSILON)
    return (values * scale * gain).astype(jnp.bfloat16)


def expert_column(ids, frame_count):
    pairs = ids.shape[0]
    square = jnp.concatenate(
        [ids.astype(jnp.float32), jnp.full((LANES - pairs, LANES), -1.0, jnp.float32)], axis=0
    )
    turned = jnp.transpose(square, (1, 0)).astype(jnp.int32)
    return jnp.concatenate([turned[:frame_count, p : p + 1] for p in range(pairs)], axis=0)


def placement(column, member, experts, capacity):
    count = column.shape[0]
    relative = column ^ member
    lane = lax.broadcasted_iota(jnp.int32, (count, LANES), 1)
    one_hot = (lane == relative).astype(jnp.float32)
    before = lax.broadcasted_iota(jnp.int32, (count, count), 1) <= lax.broadcasted_iota(
        jnp.int32, (count, count), 0
    )
    rank = lax.dot_general(
        as_mask(before), one_hot.astype(jnp.bfloat16), NN, preferred_element_type=jnp.float32
    )
    start = (lane * capacity - 1).astype(jnp.float32)
    slots = jnp.sum(one_hot * (rank + start), axis=1, keepdims=True).astype(jnp.int32)
    places = lax.broadcasted_iota(jnp.int32, (count, experts * capacity), 1)
    return (places == slots).astype(jnp.float32)


def scatter_rows(rows, ids, member, experts, capacity, frame_count, out_refs):
    count = rows.shape[0]
    chosen = placement(expert_column(ids, frame_count), member, experts, capacity)
    tall = round_up(count, LANES)
    if tall > count:
        chosen = jnp.concatenate(
            [chosen, jnp.zeros((tall - count, chosen.shape[1]), jnp.float32)], axis=0
        )
    pick = jnp.transpose(chosen, (1, 0))[:, :count].astype(jnp.bfloat16)
    placed = lax.dot_general(pick, rows, NN, preferred_element_type=jnp.float32)
    split_rows(placed, out_refs)


def combine_rows(rows, returned, ids, table, member, experts, capacity, frame_count):
    column = expert_column(ids, frame_count)
    pick = placement(column, member, experts, capacity).astype(jnp.bfloat16)
    normed = rms_scale(rows, table[:1])
    router = jnp.concatenate(
        [table[8:], jnp.zeros((LANES + 8 - table.shape[0], rows.shape[1]), jnp.float32)], axis=0
    ).astype(jnp.bfloat16)
    logits = lax.dot_general(normed, router, NT, preferred_element_type=jnp.float32)
    lane = lax.broadcasted_iota(jnp.int32, logits.shape, 1)
    gate = jax.nn.sigmoid(jnp.sum(jnp.where(lane == column, logits, 0.0), axis=1, keepdims=True))
    stacked = join_rows(returned).astype(jnp.bfloat16)
    mixed = lax.dot_general(pick, stacked, NN, preferred_element_type=jnp.float32)
    return (rows.astype(jnp.float32) + gate * mixed).astype(jnp.bfloat16)


def dispatch(rows, ids, member, experts, capacity, frame_count):
    width = rows.shape[1]

    def kernel(member_ref, rows_ref, ids_ref, *out_refs):
        scatter_rows(
            rows_ref[...], ids_ref[...], member_ref[0], experts, capacity, frame_count, out_refs
        )

    return call(
        kernel,
        tuple(bf16_rows(capacity, width) for _ in range(experts)),
        1 << 27,
        in_specs=[smem_spec()] + [vmem_spec()] * 2,
        out_specs=tuple(vmem_spec() for _ in range(experts)),
    )(member, rows, ids)


def pick_table(pick_ref, tables):
    if len(tables) == 1:
        return tables[0][...]
    return jnp.where(pick_ref[0] == 1, tables[0][...], tables[1][...])


def note_row(first_ref, labels_ref, frames_ref, counts_ref, pairs, width):
    utt_dev, label_max = labels_ref.shape[1:]
    lane = lax.broadcasted_iota(jnp.int32, (1, width), 1)
    row = jnp.zeros((1, width), jnp.int32)
    for pair in range(pairs):
        index = first_ref[0] + pair
        micro, utt = index // utt_dev, index % utt_dev
        values = [labels_ref[micro, utt, c] for c in range(label_max)]
        values += [frames_ref[utt, micro], counts_ref[utt, micro]]
        for c, value in enumerate(values):
            row = jnp.where(lane == pair * COLS + c, value // LANES, row)
            row = jnp.where(lane == LANES + pair * COLS + c, value % LANES, row)
    return row.astype(jnp.float32)


def run_expert(received, tables, own, other, pick_own, spare, note, pairs):
    count = len(received)
    capacity, width = received[0].shape
    others, choices = len(other), len(tables)
    noted = [] if note is None else list(note)

    def kernel(pick_ref, in_ref, out_weight_ref, *refs):
        table_refs, refs = refs[:choices], refs[choices:]
        other_refs, refs = refs[: 2 * others], refs[2 * others :]
        received_refs, refs = refs[:count], refs[count:]
        out_refs = refs[len(noted) :]

        def work(pieces):
            gain = pick_table(pick_ref, table_refs)[:1]
            normed = rms_scale(join_rows(received_refs), gain)
            total = None
            for weight_in, weight_out in pieces:
                hidden = lax.dot_general(
                    normed, weight_in[...], NN, preferred_element_type=jnp.float32
                )
                active = (hidden / (1.0 + jnp.exp(-hidden))).astype(jnp.bfloat16)
                part = lax.dot_general(
                    active, weight_out[...], NN, preferred_element_type=jnp.float32
                )
                total = part if total is None else total + part
            row = note_row(*refs[: len(noted)], pairs, width) if noted else None
            split_rows(total, out_refs, spare, row)

        if others == 0:
            work([(in_ref, out_weight_ref)])
            return

        @pl.when(pick_ref[0] == 1)
        def _():
            work([(in_ref, out_weight_ref)])

        @pl.when(pick_ref[0] != 1)
        def _():
            work([(other_refs[2 * i], other_refs[2 * i + 1]) for i in range(others)])

    flat = [weight for pair in other for weight in pair]
    return call(
        kernel,
        tuple(bf16_rows(capacity, width) for _ in range(count)),
        4 * count * capacity * width * own[0].shape[1],
        in_specs=[smem_spec()] + [vmem_spec()] * (2 + choices + 2 * others + count)
        + [smem_spec()] * len(noted),
        out_specs=tuple(vmem_spec() for _ in range(count)),
    )(pick_own, *own, *tables, *flat, *received, *noted)


def combine_and_dispatch(
    rows, returned, ids, tables, pick_own, next_ids, member, experts, capacity, frame_count
):
    width = rows.shape[1]
    choices = len(tables)

    def kernel(member_ref, pick_ref, rows_ref, ids_ref, next_ref, *refs):
        table_refs, refs = refs[:choices], refs[choices:]
        returned_refs, x_ref, out_refs = refs[:experts], refs[experts], refs[experts + 1 :]
        mixed = combine_rows(
            rows_ref[...],
            returned_refs,
            ids_ref[...],
            pick_table(pick_ref, table_refs),
            member_ref[0],
            experts,
            capacity,
            frame_count,
        )
        x_ref[...] = mixed
        scatter_rows(
            mixed, next_ref[...], member_ref[0], experts, capacity, frame_count, out_refs
        )

    shapes = (bf16_rows(*rows.shape),) + tuple(
        bf16_rows(capacity, width) for _ in range(experts)
    )
    result = call(
        kernel,
        shapes,
        1 << 28,
        in_specs=[smem_spec()] * 2 + [vmem_spec()] * (3 + choices + experts),
        out_specs=tuple(vmem_spec() for _ in shapes),
    )(member, pick_own, rows, ids, next_ids, *tables, *returned)
    return result[0], result[1:]


def combine_and_norm(
    rows, returned, ids, tables, pick_own, head_gain, member, experts, capacity, frame_count
):
    choices = len(tables)

    def kernel(member_ref, pick_ref, rows_ref, ids_ref, head_ref, *refs):
        table_refs, refs = refs[:choices], refs[choices:]
        final = combine_rows(
            rows_ref[...],
            refs[:experts],
            ids_ref[...],
            pick_table(pick_ref, table_refs),
            member_ref[0],
            experts,
            capacity,
            frame_count,
        )
        refs[experts][...] = rms_scale(final, head_ref[...])

    return call(
        kernel,
        bf16_rows(*rows.shape),
        1 << 28,
        in_specs=[smem_spec()] * 2 + [vmem_spec()] * (3 + choices + experts),
        out_specs=vmem_spec(),
    )(member, pick_own, rows, ids, head_gain, *tables, *returned)


def half_weights(core, weight_in, weight_out):
    width, hidden = weight_in.shape
    half = hidden // 2

    def kernel(core_ref, in_ref, out_ref, half_in, half_out, sems):
        start = pl.multiple_of(core_ref[0] * half, half)
        copies = (
            pltpu.make_async_copy(in_ref.at[:, pl.ds(start, half)], half_in, sems.at[0]),
            pltpu.make_async_copy(out_ref.at[pl.ds(start, half)], half_out, sems.at[1]),
        )
        for copy in copies:
            copy.start()
        for copy in copies:
            copy.wait()

    return call(
        kernel,
        (bf16_rows(width, half), bf16_rows(half, width)),
        1 << 20,
        in_specs=[smem_spec()] + [pl.BlockSpec(memory_space=pl.ANY)] * 2,
        out_specs=(vmem_spec(), vmem_spec()),
        scratch_shapes=[pltpu.SemaphoreType.DMA((2,))],
    )(core, weight_in, weight_out)


def block_list(shard):
    return [(i, min(BLOCK_ROWS, shard - i)) for i in range(0, shard, BLOCK_ROWS)]


def label_rows(weight, notes, member, groups, pairs, spare, label_max, line):
    shard, width = weight.shape
    sources = len(notes)
    utterances = sources * groups * pairs
    entries = utterances * COLS

    def kernel(member_ref, weight_ref, *refs):
        note_refs = refs[:sources]
        out_ref, places_ref, names_ref, turned_ref = refs[sources:]
        place = member_ref[0]
        found = []
        for ref in note_refs:
            row = ref[...].astype(jnp.float32)[spare : spare + 1]
            found.append((row[:, :LANES] * LANES + row[:, LANES : 2 * LANES]).astype(jnp.int32))
        if line:
            ends = (place == 0) | (place == 3)
            found = [
                found[0],
                found[1],
                jnp.where(ends, found[2], found[3]),
                jnp.where(ends, found[3], found[2]),
            ]
        names_ref[...] = jnp.zeros(names_ref.shape, jnp.int32)
        for slot in range(sources):
            for pair in range(groups * pairs):
                row = (pair // pairs * sources + slot) * pairs + pair % pairs
                names_ref[row : row + 1, :COLS] = found[slot][:, pair * COLS : (pair + 1) * COLS]
        lane = lax.broadcasted_iota(jnp.int32, (utterances, LANES), 1)
        named = jnp.where(lane < label_max, names_ref[...], jnp.where(lane == label_max, 0, -1))
        local = named - place * shard
        local = jnp.where((named >= 0) & (local >= 0) & (local < shard), local, -1)
        square = jnp.concatenate(
            [
                local.astype(jnp.float32),
                jnp.full((LANES - utterances, LANES), -1.0, jnp.float32),
            ],
            axis=0,
        )
        turned = jnp.transpose(square, (1, 0))
        for utterance in range(utterances):
            turned_ref[utterance * COLS : (utterance + 1) * COLS] = jnp.broadcast_to(
                turned[:COLS, utterance : utterance + 1], (COLS, LANES)
            )
        places = turned_ref[:, :1].astype(jnp.int32)
        places_ref[...] = jnp.transpose(turned_ref[...], (1, 0))[:1].astype(jnp.int32)
        total = jnp.zeros((entries, width), jnp.float32)
        for first, size in block_list(shard):
            entry = first + lax.broadcasted_iota(jnp.int32, (entries, size), 1)
            total = total + lax.dot_general(
                as_mask(entry == places),
                weight_ref[first : first + size],
                NN,
                preferred_element_type=jnp.float32,
            )
        out_ref[...] = total.astype(jnp.bfloat16)

    return call(
        kernel,
        (
            bf16_rows(entries, width),
            jax.ShapeDtypeStruct((1, entries), jnp.int32),
            jax.ShapeDtypeStruct((utterances, LANES), jnp.int32),
        ),
        2 * shard * entries * width,
        LARGE_LIMIT,
        in_specs=[smem_spec()] + [vmem_spec()] * (1 + sources),
        out_specs=tuple(vmem_spec() for _ in range(3)),
        scratch_shapes=[pltpu.VMEM((entries, LANES), jnp.float32)],
    )(member, weight, *notes)


def head_logits(
    fill, first_slot, count, pieces, member, weight, label_weight, frame_count, earlier=None
):
    given = len(pieces)
    span, width = pieces[0].shape
    row_count = count * span
    shard = weight.shape[0]
    height = round_up(shard, BLOCK_ROWS)
    entries = row_count // frame_count * COLS
    first_entry = first_slot * entries // count
    others = [] if earlier is None else [earlier]
    ahead = 0 if earlier is None else earlier.shape[0]

    def kernel(member_ref, weight_ref, label_ref, *refs):
        piece_refs = refs[:given]
        logits_ref, rows_ref, stats_ref = refs[given + len(others) :]

        def put(slot, piece_ref):
            rows_ref[slot * span : (slot + 1) * span] = piece_ref[...]

        def put_if(condition, slot, piece_ref):
            @pl.when(condition)
            def _():
                put(slot, piece_ref)

        fill(member_ref[0], piece_refs, put, put_if)
        peak = jnp.full((1, row_count), LOG_ZERO, jnp.float32)
        total = jnp.zeros((1, row_count), jnp.float32)
        for first, size in block_list(shard):
            logits = lax.dot_general(
                weight_ref[first : first + size],
                rows_ref[...],
                NT,
                preferred_element_type=jnp.float32,
            )
            logits_ref[first : first + size] = logits
            before = peak
            peak = jnp.maximum(before, jnp.max(logits, axis=0, keepdims=True))
            total = total * jnp.exp(before - peak) + jnp.sum(
                jnp.exp(logits - peak), axis=0, keepdims=True
            )
        if height > shard:
            logits_ref[shard:] = jnp.full((height - shard, row_count), LOG_ZERO, jnp.float32)
        crossed = lax.dot_general(
            label_ref[first_entry : first_entry + entries],
            rows_ref[...],
            NT,
            preferred_element_type=jnp.float32,
        )
        owner = lax.broadcasted_iota(jnp.int32, (COLS, row_count), 1) // frame_count
        picked = jnp.zeros((COLS, row_count), jnp.float32)
        for utterance in range(entries // COLS):
            part = crossed[utterance * COLS : (utterance + 1) * COLS]
            picked = picked + jnp.where(owner == utterance, part, 0.0)
        place = lax.broadcasted_iota(jnp.int32, (COLS, row_count), 0)
        stats = jnp.where(place == PEAK, peak, picked)
        stats = jnp.where(place == TOTAL, total, stats)
        for slot in range(ahead):
            stats_ref[slot] = refs[given][slot]
        for slot in range(count):
            stats_ref[ahead + slot] = stats[:, slot * span : (slot + 1) * span]

    return call(
        kernel,
        (
            jax.ShapeDtypeStruct((height, row_count), jnp.float32),
            bf16_rows(row_count, width),
            jax.ShapeDtypeStruct((ahead + count, COLS, span), jnp.float32),
        ),
        2 * height * row_count * width,
        LARGE_LIMIT,
        in_specs=[smem_spec()] + [vmem_spec()] * (2 + given + len(others)),
        out_specs=tuple(vmem_spec() for _ in range(3)),
    )(member, weight, label_weight, *pieces, *others)


def fill_line(place, piece_refs, put, put_if):
    own, beside, middle, outward, far, last = piece_refs
    ends = (place == 0) | (place == 3)
    inner = (place == 1) | (place == 2)
    put(0, own)
    put(1, beside)
    put_if(ends, 2, outward)
    put_if(ends, 3, last)
    put_if(inner, 2, middle)
    put_if(inner, 3, far)


def fill_all(place, piece_refs, put, put_if):
    for slot, piece_ref in enumerate(piece_refs):
        put(slot, piece_ref)


def log_add(first, second):
    peak = jnp.maximum(first, second)
    return peak + jnp.log(jnp.exp(first - peak) + jnp.exp(second - peak))


def log_add3(first, second, third):
    peak = jnp.maximum(jnp.maximum(first, second), third)
    return peak + jnp.log(
        jnp.exp(first - peak) + jnp.exp(second - peak) + jnp.exp(third - peak)
    )


def ctc_pass(stats, slots, notes, frame_count, label_max, parts, kept):
    calls, sources = len(stats), len(stats[0])
    each, _, span = stats[0][0].shape
    count = calls * each
    row_count = count * span
    utterances = notes.shape[0]
    entries = utterances * COLS
    tall = round_up(span, LANES)

    def kernel(slots_ref, notes_ref, *refs):
        (
            out_ref,
            high_ref,
            low_ref,
            loss_ref,
            turn_ref,
            emission_ref,
            emit_blank,
            emit_label,
            blank_fwd,
            label_fwd,
            blank_bwd,
            label_bwd,
            occupancy_ref,
        ) = refs[calls * sources :]
        place = lax.broadcasted_iota(jnp.int32, (COLS, span), 0)
        turn_ref[...] = jnp.zeros(turn_ref.shape, jnp.float32)
        for slot in range(count):
            found = []
            for k in range(sources):
                where = slots_ref[k * count + slot]
                part = refs[k][where % each]
                for other in range(1, calls):
                    later = refs[other * sources + k][where % each]
                    part = jnp.where(where >= other * each, later, part)
                found.append(part)
            joined = found[0]
            peak = found[0][PEAK : PEAK + 1]
            for other in found[1:]:
                joined = joined + other
                peak = jnp.maximum(peak, other[PEAK : PEAK + 1])
            total = jnp.zeros((1, span), jnp.float32)
            for other in found:
                total = total + other[TOTAL : TOTAL + 1] * jnp.exp(other[PEAK : PEAK + 1] - peak)
            log_total = peak + jnp.log(total)
            turn_ref[:COLS, :span] = jnp.where(place == TOTAL, log_total, joined - log_total)
            emission_ref[slot * span : (slot + 1) * span] = jnp.transpose(turn_ref[...], (1, 0))[
                :span
            ]

        lane = lax.broadcasted_iota(jnp.int32, (utterances, LANES), 1)
        is_label = lane < label_max
        is_blank = lane <= label_max
        names = jnp.where(is_label, notes_ref[...], 0)
        earlier = pltpu.roll(names, 1, 1)
        skip = is_label & (lane >= 1) & (names != 0) & (names != earlier)
        later = pltpu.roll(names, LANES - 1, 1)
        skip_next = (lane < label_max - 1) & (later != 0) & (later != names)
        frames = notes_ref[:, label_max : label_max + 1]
        counts = notes_ref[:, label_max + 1 : label_max + 2]
        ends_blank = jnp.where(lane == counts, 0.0, LOG_ZERO)
        ends_label = jnp.where(lane == counts - 1, 0.0, LOG_ZERO)

        def spread(step, carry):
            row = emission_ref[pl.ds(step, utterances, stride=frame_count), :]
            blank = jnp.sum(jnp.where(lane == label_max, row, 0.0), axis=1, keepdims=True)
            emit_blank[step] = jnp.where(is_blank, blank, LOG_ZERO)
            emit_label[step] = jnp.where(is_label, row, LOG_ZERO)
            return carry

        lax.fori_loop(0, frame_count, spread, 0, unroll=16)

        def advance(step, carry):
            fwd_blank, fwd_label, bwd_blank, bwd_label = carry
            moved = jnp.where(lane == 0, LOG_ZERO, pltpu.roll(fwd_label, 1, 1))
            new_blank = log_add(fwd_blank, moved) + emit_blank[step]
            new_label = (
                log_add3(fwd_label, fwd_blank, jnp.where(skip, moved, LOG_ZERO))
                + emit_label[step]
            )
            alive = step < frames
            fwd_blank = jnp.where(alive, new_blank, fwd_blank)
            fwd_label = jnp.where(alive, new_label, fwd_label)
            blank_fwd[step] = fwd_blank
            label_fwd[step] = fwd_label

            back = frame_count - 1 - step
            out_blank = bwd_blank + emit_blank[back + 1]
            out_label = bwd_label + emit_label[back + 1]
            next_blank = pltpu.roll(out_blank, LANES - 1, 1)
            next_label = jnp.where(skip_next, pltpu.roll(out_label, LANES - 1, 1), LOG_ZERO)
            ended = back >= frames - 1
            bwd_blank = jnp.where(ended, ends_blank, log_add(out_blank, out_label))
            bwd_label = jnp.where(
                ended, ends_label, log_add3(out_label, next_blank, next_label)
            )
            blank_bwd[back] = bwd_blank
            label_bwd[back] = bwd_label
            return (fwd_blank, fwd_label, bwd_blank, bwd_label)

        first_blank = jnp.where(lane == 0, emit_blank[0], LOG_ZERO)
        first_label = jnp.where(lane == 0, emit_label[0], LOG_ZERO)
        blank_fwd[0] = first_blank
        label_fwd[0] = first_label
        blank_bwd[frame_count - 1] = ends_blank
        label_bwd[frame_count - 1] = ends_label
        fwd_blank, fwd_label, _, _ = lax.fori_loop(
            1, frame_count, advance, (first_blank, first_label, ends_blank, ends_label), unroll=4
        )
        end_state = jnp.sum(jnp.where(lane == counts, fwd_blank, 0.0), axis=1, keepdims=True)
        near_state = jnp.sum(jnp.where(lane == counts - 1, fwd_label, 0.0), axis=1, keepdims=True)
        log_like = log_add(end_state, near_state)
        turned_losses = jnp.transpose(jnp.broadcast_to(-log_like, (utterances, LANES)), (1, 0))
        for part in range(parts):
            first = part * utterances // parts
            loss_ref[:, part * kept : (part + 1) * kept] = turned_losses[:1, first : first + kept]

        def occupy(step, carry):
            blank = jnp.exp(blank_fwd[step] + blank_bwd[step] - log_like)
            label = jnp.exp(label_fwd[step] + label_bwd[step] - log_like)
            blank = jnp.sum(jnp.where(is_blank, blank, 0.0), axis=1, keepdims=True)
            label = jnp.where(is_label, label, 0.0)
            whole = blank + jnp.sum(label, axis=1, keepdims=True)
            filled = jnp.where(lane == label_max, blank, label)
            filled = jnp.where(lane == WHOLE, whole, filled)
            filled = jnp.where(step < frames, -filled, 0.0)
            row = emission_ref[pl.ds(step, utterances, stride=frame_count), :]
            occupancy_ref[pl.ds(step, utterances, stride=frame_count), :] = jnp.where(
                lane == TOTAL, row, filled
            )
            return carry

        lax.fori_loop(0, frame_count, occupy, 0, unroll=16)
        turned = jnp.transpose(occupancy_ref[...], (1, 0))[:COLS]
        out_ref[...] = turned
        row_place = lax.broadcasted_iota(jnp.int32, (COLS, row_count), 0)
        owner = lax.broadcasted_iota(jnp.int32, (COLS, row_count), 1) // frame_count
        source = jnp.where(row_place < WHOLE, turned, 0.0)
        for utterance in range(utterances):
            part = jnp.where(owner == utterance, source, 0.0)
            high = part.astype(jnp.bfloat16)
            high_ref[utterance * COLS : (utterance + 1) * COLS] = high
            low_ref[utterance * COLS : (utterance + 1) * COLS] = (
                part - high.astype(jnp.float32)
            ).astype(jnp.bfloat16)

    held = pltpu.VMEM((frame_count, utterances, LANES), jnp.float32)
    table = pltpu.VMEM((row_count, LANES), jnp.float32)
    return call(
        kernel,
        (
            jax.ShapeDtypeStruct((COLS, row_count), jnp.float32),
            bf16_rows(entries, row_count),
            bf16_rows(entries, row_count),
            jax.ShapeDtypeStruct((1, parts * kept), jnp.float32),
        ),
        1 << 26,
        in_specs=[smem_spec()] + [vmem_spec()] * (1 + calls * sources),
        out_specs=tuple(vmem_spec() for _ in range(4)),
        scratch_shapes=[pltpu.VMEM((LANES, tall), jnp.float32), table]
        + [held] * 6
        + [table],
    )(slots, notes, *[value for group in stats for value in group])


def head_gradient(logits, rows, occupancy, high, low, places, order, outputs, each):
    count = len(logits)
    row_count, width = rows[0].shape
    entries = places.shape[1]
    blocks = outputs * each

    def kernel(order_ref, *refs):
        logits_refs, rows_refs = refs[:count], refs[count : 2 * count]
        occupancy_ref, high_ref, low_ref, places_ref = refs[2 * count : 2 * count + 4]
        out_refs = refs[2 * count + 4 :]
        for block in range(blocks):
            start = pl.multiple_of(order_ref[block] * BLOCK_ROWS, BLOCK_ROWS)
            entry = start + lax.broadcasted_iota(jnp.int32, (BLOCK_ROWS, entries), 0)
            select = as_mask(entry == places_ref[...])
            total = None
            for g in range(count):
                lanes = slice(g * row_count, (g + 1) * row_count)
                scattered = lax.dot_general(
                    select, high_ref[:, lanes], NN, preferred_element_type=jnp.float32
                ) + lax.dot_general(
                    select, low_ref[:, lanes], NN, preferred_element_type=jnp.float32
                )
                whole = occupancy_ref[WHOLE : WHOLE + 1, lanes]
                log_total = occupancy_ref[TOTAL : TOTAL + 1, lanes]
                values = logits_refs[g][pl.ds(start, BLOCK_ROWS), :]
                grad = (scattered - jnp.exp(values - log_total) * whole).astype(jnp.bfloat16)
                part = lax.dot_general(
                    grad, rows_refs[g][...], NN, preferred_element_type=jnp.float32
                )
                total = part if total is None else total + part
            out_refs[block // each][
                block % each * BLOCK_ROWS : (block % each + 1) * BLOCK_ROWS
            ] = total.astype(jnp.bfloat16)

    return call(
        kernel,
        tuple(bf16_rows(each * BLOCK_ROWS, width) for _ in range(outputs)),
        2 * blocks * BLOCK_ROWS * count * row_count * (width + 2 * entries),
        LARGE_LIMIT,
        in_specs=[smem_spec()] + [vmem_spec()] * (2 * count + 4),
        out_specs=tuple(vmem_spec() for _ in range(outputs)),
    )(order, *logits, *rows, occupancy, high, low, places)


def assemble(pieces, offsets, height, whole=None):
    count = len(pieces)
    part, width = pieces[0].shape
    short = height % part
    started = [] if whole is None else [whole]

    def kernel(offsets_ref, *refs):
        out_ref, sems = refs[count + len(started) :]

        def each(act):
            for index in range(count):
                offset = pl.multiple_of(offsets_ref[index], part)

                @pl.when(offset + part <= height)
                def _():
                    act(
                        pltpu.make_async_copy(
                            refs[index], out_ref.at[pl.ds(offset, part)], sems.at[index]
                        )
                    )

                if short:

                    @pl.when(offset + part > height)
                    def _():
                        act(
                            pltpu.make_async_copy(
                                refs[index].at[pl.ds(0, short)],
                                out_ref.at[pl.ds(height - short, short)],
                                sems.at[index],
                            )
                        )

        each(lambda copy: copy.start())
        each(lambda copy: copy.wait())

    anywhere = pl.BlockSpec(memory_space=pl.ANY)
    return call(
        kernel,
        bf16_rows(height, width),
        in_specs=[smem_spec()] + [vmem_spec()] * count + [anywhere] * len(started),
        out_specs=anywhere,
        scratch_shapes=[pltpu.SemaphoreType.DMA((count,))],
        input_output_aliases={} if whole is None else {1 + count: 0},
    )(offsets, *pieces, *started)


def swap(value, axis):
    return lax.ppermute(value, axis, [(0, 1), (1, 0)])


def crossed(value, axis, by):
    count = lax.axis_size(axis)
    return lax.ppermute(value, axis, [(i, i ^ by) for i in range(count)])


def after(value, *others):
    return lax.optimization_barrier((value,) + others)[0]


LINE_ORDER = np.array([[0, 1, 2, 3], [1, 0, 2, 3], [2, 3, 1, 0], [3, 2, 1, 0]])
MIDDLE = [(1, 2), (2, 1)]
OUTWARD = [(1, 0), (2, 3)]


def slot_orders(count):
    return LINE_ORDER if count == 4 else np.tile(np.arange(count), (count, 1))


def slot_tables(count, groups):
    orders = slot_orders(count)
    tables = np.zeros((count, count, count), np.int32)
    for member in range(count):
        for k in range(count):
            source = member ^ k
            for slot in range(count):
                tables[member, k, slot] = list(orders[source]).index(orders[member][slot])
    tables = np.concatenate([tables + g * count for g in range(groups)], axis=2)
    return tables.reshape(count, groups * count * count)


def wide(ref, start, size):
    return ref[pl.ds(start, size), :].astype(jnp.float32)


def sum_sent(own, came, places):
    height, width = own.shape
    part = height // 4

    def kernel(places_ref, own_ref, came_ref, *out_refs):
        section, outer = places_ref[0], places_ref[1]
        starts = (
            (1 - outer) * part,
            outer * part,
            (2 + 1 - section) * part,
            (2 + section) * part,
        )
        for start, out_ref in zip(starts, out_refs):
            start = pl.multiple_of(start, part)
            out_ref[...] = (wide(own_ref, start, part) + wide(came_ref, start, part)).astype(
                jnp.bfloat16
            )

    return call(
        kernel,
        tuple(bf16_rows(part, width) for _ in range(4)),
        1 << 20,
        in_specs=[smem_spec()] + [vmem_spec()] * 2,
        out_specs=tuple(vmem_spec() for _ in range(4)),
    )(places, own, came)


def sum_kept(own, came, arrived, places, keep):
    height, width = own.shape
    part = height // 4
    count = len(arrived) // 2

    def kernel(places_ref, own_ref, came_ref, *refs):
        section, outer = places_ref[0], places_ref[1]
        if not keep:
            section, outer = 1 - section, 1 - outer
        for side, start in enumerate((outer * part, (2 + section) * part)):
            start = pl.multiple_of(start, part)
            total = wide(own_ref, start, part) + wide(came_ref, start, part)
            for ref in refs[side * count : (side + 1) * count]:
                total = total + ref[...].astype(jnp.float32)
            refs[2 * count + side][...] = total.astype(jnp.bfloat16)

    return call(
        kernel,
        (bf16_rows(part, width), bf16_rows(part, width)),
        1 << 20,
        in_specs=[smem_spec()] + [vmem_spec()] * (2 + 2 * count),
        out_specs=(vmem_spec(), vmem_spec()),
    )(places, own, came, *arrived)


def per_device(
    frames,
    norm_gain,
    router,
    w_in,
    w_out,
    routing,
    head_gain,
    head_weight,
    frame_lengths,
    labels,
    label_lengths,
):
    sections = lax.axis_size("section")
    section_id = lax.axis_index("section")
    group_size = lax.axis_size("expert")
    member = lax.axis_index("expert")
    outer_size = lax.axis_size("dpo")
    inner_size = lax.axis_size("dpi")
    core = lax.axis_index("dpi")
    micro, utt_dev, frame_count, width = frames.shape
    label_max = labels.shape[2]
    experts = w_in.shape[1] * group_size
    pair_count = micro * utt_dev
    per_section = pair_count // sections
    first_pair = section_id * per_section
    share = (utt_dev * frame_count * 9 + 8 * experts - 1) // (8 * experts)
    group_count = 2 if per_section % (2 * utt_dev) == 0 else 1
    group_pairs = per_section // group_count
    filled = share * -(-group_pairs // utt_dev)
    capacity = round_up(filled + 1, 8)
    span = group_pairs * frame_count
    member_ref = member.astype(jnp.int32).reshape(1)

    def mine_of(value):
        return lax.dynamic_slice_in_dim(value, first_pair, per_section, 0)

    def exchange(blocks):
        return [blocks[0]] + [crossed(blocks[k], "expert", k) for k in range(1, group_size)]

    def lanes_of(ids):
        ids = jnp.pad(mine_of(ids), ((0, 0), (0, LANES - frame_count)), constant_values=-1)
        return [ids[g * group_pairs : (g + 1) * group_pairs] for g in range(group_count)]

    flat_frames = frames.reshape(pair_count * frame_count, width)
    current = [
        lax.dynamic_slice_in_dim(flat_frames, first_pair * frame_count + g * span, span, 0)
        for g in range(group_count)
    ]
    own_ids = routing.reshape(pair_count, frame_count)
    paired = sections == 2 and inner_size == 2
    if paired:
        other_ids = swap(own_ids, "section")
        all_ids = [
            jnp.where(section_id == layer, own_ids, other_ids) for layer in range(sections)
        ]
    else:
        all_ids = lax.all_gather(own_ids, "section")
    layer_ids = [lanes_of(all_ids[layer]) for layer in range(sections)]
    own_table = jnp.concatenate(
        [
            norm_gain,
            jnp.zeros((7, width), jnp.float32),
            jnp.transpose(router[0]).astype(jnp.float32),
            jnp.zeros((round_up(experts, 8) - experts, width), jnp.float32),
        ],
        axis=0,
    )
    own = (w_in[0, 0], w_out[0, 0])
    layers = []
    if paired:
        other_table = swap(own_table, "section")
    else:
        all_tables = lax.all_gather(own_table, "section")
        all_in = lax.all_gather(own[0], "section")
        all_out = lax.all_gather(own[1], "section")
        for layer in range(sections):
            chosen = (all_in[layer], all_out[layer])
            layers.append(((all_tables[layer],), chosen, [], jnp.ones((1,), jnp.int32)))

    outgoing = [
        dispatch(current[g], layer_ids[0][g], member_ref, experts, capacity, frame_count)
        for g in range(group_count)
    ]
    received = [exchange(blocks) for blocks in outgoing]
    if paired:
        sent_in, sent_out = half_weights(
            after(core.astype(jnp.int32).reshape(1), outgoing[0][0]), *own
        )
        came_in = swap(sent_in, "section")
        came_out = swap(sent_out, "section")
        came_in, came_out = lax.optimization_barrier((came_in, came_out, received))[:2]
        other = [(came_in, came_out), (swap(came_in, "dpi"), swap(came_out, "dpi"))]
        for layer in range(sections):
            mine = (section_id == layer).astype(jnp.int32).reshape(1)
            layers.append(((own_table, other_table), own, other, mine))

    notes = (
        first_pair.astype(jnp.int32).reshape(1),
        labels,
        jnp.transpose(frame_lengths),
        jnp.transpose(label_lengths),
    )
    shard = head_weight.shape[1]
    weight_rows = jnp.transpose(head_weight)
    line = group_size == 4
    tables = jnp.asarray(slot_tables(group_size, group_count))
    slots = lax.dynamic_index_in_dim(tables, member, 0, keepdims=False)
    outer = lax.axis_index("dpo")
    blocks = -(-shard // BLOCK_ROWS)
    tree = paired and outer_size == 2 and blocks == 8

    def pair_of(side, first, second):
        return [side * 4 + first, side * 4 + 2 + second]

    def offset_of(side, s, y):
        base = side * 4 * BLOCK_ROWS
        part = BLOCK_ROWS // 2
        return [
            base + s * BLOCK_ROWS + y * part,
            base + 2 * BLOCK_ROWS + y * BLOCK_ROWS + s * part,
        ]

    def whole_numbers(values):
        return jnp.stack([jnp.asarray(value, jnp.int32) for value in values])

    here, there = (section_id, outer), (1 - section_id, 1 - outer)
    sibling_order = whole_numbers(pair_of(1 - core, *there) + pair_of(1 - core, *here))
    sent_order = whole_numbers(pair_of(core, *there))
    kept_order = whole_numbers(pair_of(core, *here))
    chip_place = whole_numbers(here)
    first_offsets, last_offsets = [], offset_of(core, *there) + offset_of(1 - core, *there)
    for side in (core, 1 - core):
        for s, y in (here, (section_id, 1 - outer), (1 - section_id, outer)):
            first_offsets += offset_of(side, s, y)
    first_offsets, last_offsets = whole_numbers(first_offsets), whole_numbers(last_offsets)
    early = (
        slots,
        head_gain.reshape(1, width),
        layer_ids[1:],
        sibling_order,
        sent_order,
        kept_order,
        chip_place,
        first_offsets,
        last_offsets,
    )
    early, received = lax.optimization_barrier((early, received))
    slots, head_row, later_ids, sibling_order, sent_order, kept_order = early[:6]
    chip_place, first_offsets, last_offsets = early[6:]
    layer_ids = [layer_ids[0]] + list(later_ids)

    def tied(value, others, g):
        marks = [other for i, other in enumerate(others) if i != g]
        return after(value, *marks) if marks else value

    normed, marks = [], []
    for layer in range(sections):
        choices, weights, others, pick_own = layers[layer]
        done = [
            run_expert(
                received[g],
                choices,
                weights,
                others,
                tied(pick_own, marks, g),
                filled,
                notes if layer == 0 and g == 0 else None,
                per_section,
            )
            for g in range(group_count)
        ]
        returned = [exchange(parts) for parts in done]
        marks = [parts[0] for parts in done]
        tokens = [tied(member_ref, marks, g) for g in range(group_count)]
        sizes = (experts, capacity, frame_count)
        if layer < sections - 1:
            made = [
                combine_and_dispatch(
                    current[g],
                    returned[g],
                    layer_ids[layer][g],
                    choices,
                    pick_own,
                    layer_ids[layer + 1][g],
                    tokens[g],
                    *sizes,
                )
                for g in range(group_count)
            ]
            current = [pair[0] for pair in made]
            received = [exchange(pair[1]) for pair in made]
            marks = current
        else:
            normed = [
                combine_and_norm(
                    current[g],
                    returned[g],
                    layer_ids[layer][g],
                    choices,
                    pick_own,
                    head_row,
                    tokens[g],
                    *sizes,
                )
                for g in range(group_count)
            ]
        if layer == 0:
            found = list(returned[0])
            if not line:
                stacked = jnp.stack(found)
                found = [
                    lax.dynamic_index_in_dim(stacked, member ^ k, 0, keepdims=False)
                    for k in range(group_size)
                ]
            label_weight, places, names = label_rows(
                weight_rows, found, member_ref, group_count, group_pairs, filled, label_max, line
            )

    def logits_of(fill, first, count, pieces, earlier=None):
        return head_logits(
            fill, first, count, pieces, member_ref, weight_rows, label_weight, frame_count, earlier
        )

    def stats_of(stats):
        first = crossed(stats, "expert", 1)
        return [stats, first, crossed(stats, "expert", 2), crossed(first, "expert", 2)]

    heads, found = [], []
    for g in range(group_count):
        if line:
            beside = crossed(normed[g], "expert", 1)
            middle = lax.ppermute(normed[g], "expert", MIDDLE)
            beside, middle = lax.optimization_barrier((beside, middle, normed[-1]))[:2]
            far = lax.ppermute(beside, "expert", MIDDLE)
            outward = lax.ppermute(middle, "expert", OUTWARD)
            if g > 0:
                far = after(far, heads[0][2])
            last = lax.ppermute(far, "expert", OUTWARD)
            pieces = [normed[g], beside, middle, outward, far, last]
            earlier = heads[-1][2] if heads else None
            heads.append(logits_of(fill_line, g * group_size, group_size, pieces, earlier))
        else:
            gathered = lax.all_gather(normed[g], "expert")
            pieces = [gathered[k] for k in range(group_size)]
            heads.append(logits_of(fill_all, g * group_size, group_size, pieces))
            gathered = lax.all_gather(heads[g][2], "expert")
            found.append(
                [
                    lax.dynamic_index_in_dim(gathered, member ^ k, 0, keepdims=False)
                    for k in range(group_size)
                ]
            )
    if line:
        found = [stats_of(heads[-1][2])]
    kept_losses = group_pairs if line else group_size * group_pairs
    occupancy, high, low, losses = ctc_pass(
        found, slots, names, frame_count, label_max, group_count, kept_losses
    )
    if not line:
        pairs = losses.reshape(group_count, group_size, group_pairs)
        losses = lax.dynamic_index_in_dim(pairs, member, 1).reshape(1, per_section)
    losses = jnp.transpose(losses)

    def gradient(order, outputs, each):
        return head_gradient(
            [head[0] for head in heads],
            [head[1] for head in heads],
            occupancy,
            high,
            low,
            places,
            order,
            outputs,
            each,
        )

    if tree:
        sibling_sent, sibling_kept = gradient(sibling_order, 2, 2)
        came_sent, came_kept = swap(sibling_sent, "dpi"), swap(sibling_kept, "dpi")
        own_sent = gradient(after(sent_order, sibling_sent), 1, 2)[0]
        a_far, a_near, b_far, b_near = sum_sent(own_sent, came_sent, chip_place)
        kept_order = after(kept_order, a_far)
        a_far, b_far = swap(a_far, "section"), swap(b_far, "dpo")
        a_near, b_near = swap(a_near, "section"), swap(b_near, "dpo")
        own_kept = gradient(kept_order, 1, 2)[0]
        a_on, b_on = sum_kept(own_kept, came_kept, [a_far, b_far], chip_place, False)
        a_in, b_in = swap(a_on, "dpo"), swap(b_on, "section")
        a, b = sum_kept(own_kept, came_kept, [a_near, a_in, b_near, b_in], chip_place, True)
        a_y, b_x = swap(a, "dpo"), swap(b, "section")
        b_y, a_x = swap(b, "dpo"), swap(a, "section")
        a_xy, b_xy = swap(a_y, "section"), swap(b_x, "dpo")
        b_y, a_x = lax.optimization_barrier((b_y, a_x, a_xy, b_xy))[:2]
        mine = [a, b, a_y, b_y, a_x, b_x]
        theirs = [swap(value, "dpi") for value in mine]
        whole = assemble(mine + theirs, first_offsets, shard)
        last = [a_xy, b_xy, swap(a_xy, "dpi"), swap(b_xy, "dpi")]
        whole = assemble(last, last_offsets, shard, whole)
    else:
        partial = gradient(jnp.arange(blocks, dtype=jnp.int32), 1, blocks)[0][:shard]
        whole = lax.psum(partial.astype(jnp.float32), ("section", "dpo", "dpi")).astype(
            jnp.bfloat16
        )
    return (losses, jnp.transpose(whole))


def solution(mesh):
    sections, group_size, spread = (mesh.shape[name] for name in ("section", "expert", "dp"))
    inner = 2 if spread % 2 == 0 else 1
    split = Mesh(
        mesh.devices.reshape(sections, group_size, spread // inner, inner),
        ("section", "expert", "dpo", "dpi"),
    )
    block = ("expert", "dpo", "dpi")
    placed = (
        P(None, block, None, None),
        P("section", None),
        P("section", None, None),
        P("section", "expert", None, None),
        P("section", "expert", None, None),
        P("section", None, block, None, None),
        P(),
        P(None, "expert"),
        P(None, block),
        P(None, block, None),
        P(None, block),
    )
    return jax.shard_map(
        per_device,
        mesh=split,
        in_specs=placed,
        out_specs=(P("section", block), P(None, "expert")),
        check_vma=False,
    )
```

```python
import jax
import jax.numpy as jnp
import numpy as np
from jax import lax
from jax.experimental import pallas as pl
from jax.experimental.pallas import tpu as pltpu
from jax.sharding import Mesh, PartitionSpec as P

EPSILON = 1e-06
LOG_ZERO = -1e30
VMEM_LIMIT = 12 * 1024 * 1024
LARGE_LIMIT = 24 * 1024 * 1024
LANES = 128
COLS = 16
PEAK, TOTAL, WHOLE = COLS - 3, COLS - 2, COLS - 3
BLOCK_ROWS = 256
NT = (((1,), (1,)), ((), ()))
NN = (((1,), (0,)), ((), ()))


def round_up(value, unit):
    return -(-value // unit) * unit


def vmem_spec():
    return pl.BlockSpec(memory_space=pltpu.VMEM)


def smem_spec():
    return pl.BlockSpec(memory_space=pltpu.SMEM)


def call(kernel, out_shape, flops=0, limit=VMEM_LIMIT, **options):
    return pl.pallas_call(
        kernel,
        out_shape=out_shape,
        compiler_params=pltpu.CompilerParams(vmem_limit_bytes=limit),
        cost_estimate=pl.CostEstimate(flops=flops, bytes_accessed=0, transcendentals=0),
        **options,
    )


def bf16_rows(count, width):
    return jax.ShapeDtypeStruct((count, width), jnp.bfloat16)


def as_mask(values):
    return values.astype(jnp.float32).astype(jnp.bfloat16)


def split_rows(values, out_refs, spare=None, note=None):
    size, width = out_refs[0].shape
    for turn, out_ref in enumerate(out_refs):
        part = values[turn * size : (turn + 1) * size]
        if note is not None:
            row = lax.broadcasted_iota(jnp.int32, (size, width), 0)
            part = jnp.where(row == spare, note, part)
        out_ref[...] = part.astype(jnp.bfloat16)


def join_rows(refs):
    return jnp.concatenate([ref[...].astype(jnp.float32) for ref in refs], axis=0)


def rms_scale(values, gain):
    values = values.astype(jnp.float32)
    scale = lax.rsqrt(jnp.mean(values * values, axis=-1, keepdims=True) + EPSILON)
    return (values * scale * gain).astype(jnp.bfloat16)


def expert_column(ids, frame_count):
    pairs = ids.shape[0]
    square = jnp.concatenate(
        [ids.astype(jnp.float32), jnp.full((LANES - pairs, LANES), -1.0, jnp.float32)], axis=0
    )
    turned = jnp.transpose(square, (1, 0)).astype(jnp.int32)
    return jnp.concatenate([turned[:frame_count, p : p + 1] for p in range(pairs)], axis=0)


def placement(column, member, experts, capacity):
    count = column.shape[0]
    relative = column ^ member
    lane = lax.broadcasted_iota(jnp.int32, (count, LANES), 1)
    one_hot = (lane == relative).astype(jnp.float32)
    before = lax.broadcasted_iota(jnp.int32, (count, count), 1) <= lax.broadcasted_iota(
        jnp.int32, (count, count), 0
    )
    rank = lax.dot_general(
        as_mask(before), one_hot.astype(jnp.bfloat16), NN, preferred_element_type=jnp.float32
    )
    start = (lane * capacity - 1).astype(jnp.float32)
    slots = jnp.sum(one_hot * (rank + start), axis=1, keepdims=True).astype(jnp.int32)
    places = lax.broadcasted_iota(jnp.int32, (count, experts * capacity), 1)
    return (places == slots).astype(jnp.float32)


def scatter_rows(rows, ids, member, experts, capacity, frame_count, out_refs):
    count = rows.shape[0]
    chosen = placement(expert_column(ids, frame_count), member, experts, capacity)
    tall = round_up(count, LANES)
    if tall > count:
        chosen = jnp.concatenate(
            [chosen, jnp.zeros((tall - count, chosen.shape[1]), jnp.float32)], axis=0
        )
    pick = jnp.transpose(chosen, (1, 0))[:, :count].astype(jnp.bfloat16)
    placed = lax.dot_general(pick, rows, NN, preferred_element_type=jnp.float32)
    split_rows(placed, out_refs)


def combine_rows(rows, returned, ids, table, member, experts, capacity, frame_count):
    column = expert_column(ids, frame_count)
    pick = placement(column, member, experts, capacity).astype(jnp.bfloat16)
    normed = rms_scale(rows, table[:1])
    router = jnp.concatenate(
        [table[8:], jnp.zeros((LANES + 8 - table.shape[0], rows.shape[1]), jnp.float32)], axis=0
    ).astype(jnp.bfloat16)
    logits = lax.dot_general(normed, router, NT, preferred_element_type=jnp.float32)
    lane = lax.broadcasted_iota(jnp.int32, logits.shape, 1)
    gate = jax.nn.sigmoid(jnp.sum(jnp.where(lane == column, logits, 0.0), axis=1, keepdims=True))
    stacked = join_rows(returned).astype(jnp.bfloat16)
    mixed = lax.dot_general(pick, stacked, NN, preferred_element_type=jnp.float32)
    return (rows.astype(jnp.float32) + gate * mixed).astype(jnp.bfloat16)


def dispatch(rows, ids, member, experts, capacity, frame_count):
    width = rows.shape[1]

    def kernel(member_ref, rows_ref, ids_ref, *out_refs):
        scatter_rows(
            rows_ref[...], ids_ref[...], member_ref[0], experts, capacity, frame_count, out_refs
        )

    return call(
        kernel,
        tuple(bf16_rows(capacity, width) for _ in range(experts)),
        1 << 27,
        in_specs=[smem_spec()] + [vmem_spec()] * 2,
        out_specs=tuple(vmem_spec() for _ in range(experts)),
    )(member, rows, ids)


def pick_table(pick_ref, tables):
    if len(tables) == 1:
        return tables[0][...]
    return jnp.where(pick_ref[0] == 1, tables[0][...], tables[1][...])


def note_row(first_ref, labels_ref, frames_ref, counts_ref, pairs, width):
    utt_dev, label_max = labels_ref.shape[1:]
    lane = lax.broadcasted_iota(jnp.int32, (1, width), 1)
    row = jnp.zeros((1, width), jnp.int32)
    for pair in range(pairs):
        index = first_ref[0] + pair
        micro, utt = index // utt_dev, index % utt_dev
        values = [labels_ref[micro, utt, c] for c in range(label_max)]
        values += [frames_ref[utt, micro], counts_ref[utt, micro]]
        for c, value in enumerate(values):
            row = jnp.where(lane == pair * COLS + c, value // LANES, row)
            row = jnp.where(lane == LANES + pair * COLS + c, value % LANES, row)
    return row.astype(jnp.float32)


def run_expert(received, tables, own, other, pick_own, spare, note, pairs):
    count = len(received)
    capacity, width = received[0].shape
    others, choices = len(other), len(tables)
    noted = [] if note is None else list(note)

    def kernel(pick_ref, in_ref, out_weight_ref, *refs):
        table_refs, refs = refs[:choices], refs[choices:]
        other_refs, refs = refs[: 2 * others], refs[2 * others :]
        received_refs, refs = refs[:count], refs[count:]
        out_refs = refs[len(noted) :]

        def work(pieces):
            gain = pick_table(pick_ref, table_refs)[:1]
            normed = rms_scale(join_rows(received_refs), gain)
            total = None
            for weight_in, weight_out in pieces:
                hidden = lax.dot_general(
                    normed, weight_in[...], NN, preferred_element_type=jnp.float32
                )
                active = (hidden / (1.0 + jnp.exp(-hidden))).astype(jnp.bfloat16)
                part = lax.dot_general(
                    active, weight_out[...], NN, preferred_element_type=jnp.float32
                )
                total = part if total is None else total + part
            row = note_row(*refs[: len(noted)], pairs, width) if noted else None
            split_rows(total, out_refs, spare, row)

        if others == 0:
            work([(in_ref, out_weight_ref)])
            return

        @pl.when(pick_ref[0] == 1)
        def _():
            work([(in_ref, out_weight_ref)])

        @pl.when(pick_ref[0] != 1)
        def _():
            work([(other_refs[2 * i], other_refs[2 * i + 1]) for i in range(others)])

    flat = [weight for pair in other for weight in pair]
    return call(
        kernel,
        tuple(bf16_rows(capacity, width) for _ in range(count)),
        4 * count * capacity * width * own[0].shape[1],
        in_specs=[smem_spec()] + [vmem_spec()] * (2 + choices + 2 * others + count)
        + [smem_spec()] * len(noted),
        out_specs=tuple(vmem_spec() for _ in range(count)),
    )(pick_own, *own, *tables, *flat, *received, *noted)


def combine_and_dispatch(
    rows, returned, ids, tables, pick_own, next_ids, member, experts, capacity, frame_count
):
    width = rows.shape[1]
    choices = len(tables)

    def kernel(member_ref, pick_ref, rows_ref, ids_ref, next_ref, *refs):
        table_refs, refs = refs[:choices], refs[choices:]
        returned_refs, x_ref, out_refs = refs[:experts], refs[experts], refs[experts + 1 :]
        mixed = combine_rows(
            rows_ref[...],
            returned_refs,
            ids_ref[...],
            pick_table(pick_ref, table_refs),
            member_ref[0],
            experts,
            capacity,
            frame_count,
        )
        x_ref[...] = mixed
        scatter_rows(
            mixed, next_ref[...], member_ref[0], experts, capacity, frame_count, out_refs
        )

    shapes = (bf16_rows(*rows.shape),) + tuple(
        bf16_rows(capacity, width) for _ in range(experts)
    )
    result = call(
        kernel,
        shapes,
        1 << 28,
        in_specs=[smem_spec()] * 2 + [vmem_spec()] * (3 + choices + experts),
        out_specs=tuple(vmem_spec() for _ in shapes),
    )(member, pick_own, rows, ids, next_ids, *tables, *returned)
    return result[0], result[1:]


def combine_and_norm(
    rows, returned, ids, tables, pick_own, head_gain, member, experts, capacity, frame_count
):
    choices = len(tables)

    def kernel(member_ref, pick_ref, rows_ref, ids_ref, head_ref, *refs):
        table_refs, refs = refs[:choices], refs[choices:]
        final = combine_rows(
            rows_ref[...],
            refs[:experts],
            ids_ref[...],
            pick_table(pick_ref, table_refs),
            member_ref[0],
            experts,
            capacity,
            frame_count,
        )
        refs[experts][...] = rms_scale(final, head_ref[...])

    return call(
        kernel,
        bf16_rows(*rows.shape),
        1 << 28,
        in_specs=[smem_spec()] * 2 + [vmem_spec()] * (3 + choices + experts),
        out_specs=vmem_spec(),
    )(member, pick_own, rows, ids, head_gain, *tables, *returned)


def half_weights(core, weight_in, weight_out):
    width, hidden = weight_in.shape
    half = hidden // 2

    def kernel(core_ref, in_ref, out_ref, half_in, half_out, sems):
        start = pl.multiple_of(core_ref[0] * half, half)
        copies = (
            pltpu.make_async_copy(in_ref.at[:, pl.ds(start, half)], half_in, sems.at[0]),
            pltpu.make_async_copy(out_ref.at[pl.ds(start, half)], half_out, sems.at[1]),
        )
        for copy in copies:
            copy.start()
        for copy in copies:
            copy.wait()

    return call(
        kernel,
        (bf16_rows(width, half), bf16_rows(half, width)),
        1 << 20,
        in_specs=[smem_spec()] + [pl.BlockSpec(memory_space=pl.ANY)] * 2,
        out_specs=(vmem_spec(), vmem_spec()),
        scratch_shapes=[pltpu.SemaphoreType.DMA((2,))],
    )(core, weight_in, weight_out)


def block_list(shard):
    return [(i, min(BLOCK_ROWS, shard - i)) for i in range(0, shard, BLOCK_ROWS)]


def label_rows(weight, notes, member, groups, pairs, spare, label_max, line):
    shard, width = weight.shape
    sources = len(notes)
    utterances = sources * groups * pairs
    entries = utterances * COLS

    def kernel(member_ref, weight_ref, *refs):
        note_refs = refs[:sources]
        out_ref, places_ref, names_ref, turned_ref = refs[sources:]
        place = member_ref[0]
        found = []
        for ref in note_refs:
            row = ref[...].astype(jnp.float32)[spare : spare + 1]
            found.append((row[:, :LANES] * LANES + row[:, LANES : 2 * LANES]).astype(jnp.int32))
        if line:
            ends = (place == 0) | (place == 3)
            found = [
                found[0],
                found[1],
                jnp.where(ends, found[2], found[3]),
                jnp.where(ends, found[3], found[2]),
            ]
        names_ref[...] = jnp.zeros(names_ref.shape, jnp.int32)
        for slot in range(sources):
            for pair in range(groups * pairs):
                row = (pair // pairs * sources + slot) * pairs + pair % pairs
                names_ref[row : row + 1, :COLS] = found[slot][:, pair * COLS : (pair + 1) * COLS]
        lane = lax.broadcasted_iota(jnp.int32, (utterances, LANES), 1)
        named = jnp.where(lane < label_max, names_ref[...], jnp.where(lane == label_max, 0, -1))
        local = named - place * shard
        local = jnp.where((named >= 0) & (local >= 0) & (local < shard), local, -1)
        square = jnp.concatenate(
            [
                local.astype(jnp.float32),
                jnp.full((LANES - utterances, LANES), -1.0, jnp.float32),
            ],
            axis=0,
        )
        turned = jnp.transpose(square, (1, 0))
        for utterance in range(utterances):
            turned_ref[utterance * COLS : (utterance + 1) * COLS] = jnp.broadcast_to(
                turned[:COLS, utterance : utterance + 1], (COLS, LANES)
            )
        places = turned_ref[:, :1].astype(jnp.int32)
        places_ref[...] = jnp.transpose(turned_ref[...], (1, 0))[:1].astype(jnp.int32)
        total = jnp.zeros((entries, width), jnp.float32)
        for first, size in block_list(shard):
            entry = first + lax.broadcasted_iota(jnp.int32, (entries, size), 1)
            total = total + lax.dot_general(
                as_mask(entry == places),
                weight_ref[first : first + size],
                NN,
                preferred_element_type=jnp.float32,
            )
        out_ref[...] = total.astype(jnp.bfloat16)

    return call(
        kernel,
        (
            bf16_rows(entries, width),
            jax.ShapeDtypeStruct((1, entries), jnp.int32),
            jax.ShapeDtypeStruct((utterances, LANES), jnp.int32),
        ),
        2 * shard * entries * width,
        LARGE_LIMIT,
        in_specs=[smem_spec()] + [vmem_spec()] * (1 + sources),
        out_specs=tuple(vmem_spec() for _ in range(3)),
        scratch_shapes=[pltpu.VMEM((entries, LANES), jnp.float32)],
    )(member, weight, *notes)


def head_logits(
    fill, first_slot, count, pieces, member, weight, label_weight, frame_count, earlier=None
):
    given = len(pieces)
    span, width = pieces[0].shape
    row_count = count * span
    shard = weight.shape[0]
    height = round_up(shard, BLOCK_ROWS)
    entries = row_count // frame_count * COLS
    first_entry = first_slot * entries // count
    others = [] if earlier is None else [earlier]
    ahead = 0 if earlier is None else earlier.shape[0]

    def kernel(member_ref, weight_ref, label_ref, *refs):
        piece_refs = refs[:given]
        logits_ref, rows_ref, stats_ref = refs[given + len(others) :]

        def put(slot, piece_ref):
            rows_ref[slot * span : (slot + 1) * span] = piece_ref[...]

        def put_if(condition, slot, piece_ref):
            @pl.when(condition)
            def _():
                put(slot, piece_ref)

        fill(member_ref[0], piece_refs, put, put_if)
        peak = jnp.full((1, row_count), LOG_ZERO, jnp.float32)
        total = jnp.zeros((1, row_count), jnp.float32)
        for first, size in block_list(shard):
            logits = lax.dot_general(
                weight_ref[first : first + size],
                rows_ref[...],
                NT,
                preferred_element_type=jnp.float32,
            )
            logits_ref[first : first + size] = logits
            before = peak
            peak = jnp.maximum(before, jnp.max(logits, axis=0, keepdims=True))
            total = total * jnp.exp(before - peak) + jnp.sum(
                jnp.exp(logits - peak), axis=0, keepdims=True
            )
        if height > shard:
            logits_ref[shard:] = jnp.full((height - shard, row_count), LOG_ZERO, jnp.float32)
        crossed = lax.dot_general(
            label_ref[first_entry : first_entry + entries],
            rows_ref[...],
            NT,
            preferred_element_type=jnp.float32,
        )
        owner = lax.broadcasted_iota(jnp.int32, (COLS, row_count), 1) // frame_count
        picked = jnp.zeros((COLS, row_count), jnp.float32)
        for utterance in range(entries // COLS):
            part = crossed[utterance * COLS : (utterance + 1) * COLS]
            picked = picked + jnp.where(owner == utterance, part, 0.0)
        place = lax.broadcasted_iota(jnp.int32, (COLS, row_count), 0)
        stats = jnp.where(place == PEAK, peak, picked)
        stats = jnp.where(place == TOTAL, total, stats)
        for slot in range(ahead):
            stats_ref[slot] = refs[given][slot]
        for slot in range(count):
            stats_ref[ahead + slot] = stats[:, slot * span : (slot + 1) * span]

    return call(
        kernel,
        (
            jax.ShapeDtypeStruct((height, row_count), jnp.float32),
            bf16_rows(row_count, width),
            jax.ShapeDtypeStruct((ahead + count, COLS, span), jnp.float32),
        ),
        2 * height * row_count * width,
        LARGE_LIMIT,
        in_specs=[smem_spec()] + [vmem_spec()] * (2 + given + len(others)),
        out_specs=tuple(vmem_spec() for _ in range(3)),
    )(member, weight, label_weight, *pieces, *others)


def fill_line(place, piece_refs, put, put_if):
    own, beside, middle, outward, far, last = piece_refs
    ends = (place == 0) | (place == 3)
    inner = (place == 1) | (place == 2)
    put(0, own)
    put(1, beside)
    put_if(ends, 2, outward)
    put_if(ends, 3, last)
    put_if(inner, 2, middle)
    put_if(inner, 3, far)


def fill_all(place, piece_refs, put, put_if):
    for slot, piece_ref in enumerate(piece_refs):
        put(slot, piece_ref)


def log_add(first, second):
    peak = jnp.maximum(first, second)
    return peak + jnp.log(jnp.exp(first - peak) + jnp.exp(second - peak))


def log_add3(first, second, third):
    peak = jnp.maximum(jnp.maximum(first, second), third)
    return peak + jnp.log(
        jnp.exp(first - peak) + jnp.exp(second - peak) + jnp.exp(third - peak)
    )


def ctc_pass(stats, slots, notes, frame_count, label_max, parts, kept):
    calls, sources = len(stats), len(stats[0])
    each, _, span = stats[0][0].shape
    count = calls * each
    row_count = count * span
    utterances = notes.shape[0]
    entries = utterances * COLS
    tall = round_up(span, LANES)

    def kernel(slots_ref, notes_ref, *refs):
        (
            out_ref,
            high_ref,
            low_ref,
            loss_ref,
            turn_ref,
            emission_ref,
            emit_blank,
            emit_label,
            blank_fwd,
            label_fwd,
            blank_bwd,
            label_bwd,
            occupancy_ref,
        ) = refs[calls * sources :]
        place = lax.broadcasted_iota(jnp.int32, (COLS, span), 0)
        turn_ref[...] = jnp.zeros(turn_ref.shape, jnp.float32)
        for slot in range(count):
            found = []
            for k in range(sources):
                where = slots_ref[k * count + slot]
                part = refs[k][where % each]
                for other in range(1, calls):
                    later = refs[other * sources + k][where % each]
                    part = jnp.where(where >= other * each, later, part)
                found.append(part)
            joined = found[0]
            peak = found[0][PEAK : PEAK + 1]
            for other in found[1:]:
                joined = joined + other
                peak = jnp.maximum(peak, other[PEAK : PEAK + 1])
            total = jnp.zeros((1, span), jnp.float32)
            for other in found:
                total = total + other[TOTAL : TOTAL + 1] * jnp.exp(other[PEAK : PEAK + 1] - peak)
            log_total = peak + jnp.log(total)
            turn_ref[:COLS, :span] = jnp.where(place == TOTAL, log_total, joined - log_total)
            emission_ref[slot * span : (slot + 1) * span] = jnp.transpose(turn_ref[...], (1, 0))[
                :span
            ]

        lane = lax.broadcasted_iota(jnp.int32, (utterances, LANES), 1)
        is_label = lane < label_max
        is_blank = lane <= label_max
        names = jnp.where(is_label, notes_ref[...], 0)
        earlier = pltpu.roll(names, 1, 1)
        skip = is_label & (lane >= 1) & (names != 0) & (names != earlier)
        later = pltpu.roll(names, LANES - 1, 1)
        skip_next = (lane < label_max - 1) & (later != 0) & (later != names)
        frames = notes_ref[:, label_max : label_max + 1]
        counts = notes_ref[:, label_max + 1 : label_max + 2]
        ends_blank = jnp.where(lane == counts, 0.0, LOG_ZERO)
        ends_label = jnp.where(lane == counts - 1, 0.0, LOG_ZERO)

        def spread(step, carry):
            row = emission_ref[pl.ds(step, utterances, stride=frame_count), :]
            blank = jnp.sum(jnp.where(lane == label_max, row, 0.0), axis=1, keepdims=True)
            emit_blank[step] = jnp.where(is_blank, blank, LOG_ZERO)
            emit_label[step] = jnp.where(is_label, row, LOG_ZERO)
            return carry

        lax.fori_loop(0, frame_count, spread, 0, unroll=16)

        def advance(step, carry):
            fwd_blank, fwd_label, bwd_blank, bwd_label = carry
            moved = jnp.where(lane == 0, LOG_ZERO, pltpu.roll(fwd_label, 1, 1))
            new_blank = log_add(fwd_blank, moved) + emit_blank[step]
            new_label = (
                log_add3(fwd_label, fwd_blank, jnp.where(skip, moved, LOG_ZERO))
                + emit_label[step]
            )
            alive = step < frames
            fwd_blank = jnp.where(alive, new_blank, fwd_blank)
            fwd_label = jnp.where(alive, new_label, fwd_label)
            blank_fwd[step] = fwd_blank
            label_fwd[step] = fwd_label

            back = frame_count - 1 - step
            out_blank = bwd_blank + emit_blank[back + 1]
            out_label = bwd_label + emit_label[back + 1]
            next_blank = pltpu.roll(out_blank, LANES - 1, 1)
            next_label = jnp.where(skip_next, pltpu.roll(out_label, LANES - 1, 1), LOG_ZERO)
            ended = back >= frames - 1
            bwd_blank = jnp.where(ended, ends_blank, log_add(out_blank, out_label))
            bwd_label = jnp.where(
                ended, ends_label, log_add3(out_label, next_blank, next_label)
            )
            blank_bwd[back] = bwd_blank
            label_bwd[back] = bwd_label
            return (fwd_blank, fwd_label, bwd_blank, bwd_label)

        first_blank = jnp.where(lane == 0, emit_blank[0], LOG_ZERO)
        first_label = jnp.where(lane == 0, emit_label[0], LOG_ZERO)
        blank_fwd[0] = first_blank
        label_fwd[0] = first_label
        blank_bwd[frame_count - 1] = ends_blank
        label_bwd[frame_count - 1] = ends_label
        fwd_blank, fwd_label, _, _ = lax.fori_loop(
            1, frame_count, advance, (first_blank, first_label, ends_blank, ends_label), unroll=4
        )
        end_state = jnp.sum(jnp.where(lane == counts, fwd_blank, 0.0), axis=1, keepdims=True)
        near_state = jnp.sum(jnp.where(lane == counts - 1, fwd_label, 0.0), axis=1, keepdims=True)
        log_like = log_add(end_state, near_state)
        turned_losses = jnp.transpose(jnp.broadcast_to(-log_like, (utterances, LANES)), (1, 0))
        for part in range(parts):
            first = part * utterances // parts
            loss_ref[:, part * kept : (part + 1) * kept] = turned_losses[:1, first : first + kept]

        def occupy(step, carry):
            blank = jnp.exp(blank_fwd[step] + blank_bwd[step] - log_like)
            label = jnp.exp(label_fwd[step] + label_bwd[step] - log_like)
            blank = jnp.sum(jnp.where(is_blank, blank, 0.0), axis=1, keepdims=True)
            label = jnp.where(is_label, label, 0.0)
            whole = blank + jnp.sum(label, axis=1, keepdims=True)
            filled = jnp.where(lane == label_max, blank, label)
            filled = jnp.where(lane == WHOLE, whole, filled)
            filled = jnp.where(step < frames, -filled, 0.0)
            row = emission_ref[pl.ds(step, utterances, stride=frame_count), :]
            occupancy_ref[pl.ds(step, utterances, stride=frame_count), :] = jnp.where(
                lane == TOTAL, row, filled
            )
            return carry

        lax.fori_loop(0, frame_count, occupy, 0, unroll=16)
        turned = jnp.transpose(occupancy_ref[...], (1, 0))[:COLS]
        out_ref[...] = turned
        row_place = lax.broadcasted_iota(jnp.int32, (COLS, row_count), 0)
        owner = lax.broadcasted_iota(jnp.int32, (COLS, row_count), 1) // frame_count
        source = jnp.where(row_place < WHOLE, turned, 0.0)
        for utterance in range(utterances):
            part = jnp.where(owner == utterance, source, 0.0)
            high = part.astype(jnp.bfloat16)
            high_ref[utterance * COLS : (utterance + 1) * COLS] = high
            low_ref[utterance * COLS : (utterance + 1) * COLS] = (
                part - high.astype(jnp.float32)
            ).astype(jnp.bfloat16)

    held = pltpu.VMEM((frame_count, utterances, LANES), jnp.float32)
    table = pltpu.VMEM((row_count, LANES), jnp.float32)
    return call(
        kernel,
        (
            jax.ShapeDtypeStruct((COLS, row_count), jnp.float32),
            bf16_rows(entries, row_count),
            bf16_rows(entries, row_count),
            jax.ShapeDtypeStruct((1, parts * kept), jnp.float32),
        ),
        1 << 26,
        in_specs=[smem_spec()] + [vmem_spec()] * (1 + calls * sources),
        out_specs=tuple(vmem_spec() for _ in range(4)),
        scratch_shapes=[pltpu.VMEM((LANES, tall), jnp.float32), table]
        + [held] * 6
        + [table],
    )(slots, notes, *[value for group in stats for value in group])


def head_gradient(logits, rows, occupancy, high, low, places, order, outputs, each):
    count = len(logits)
    row_count, width = rows[0].shape
    entries = places.shape[1]
    blocks = outputs * each

    def kernel(order_ref, *refs):
        logits_refs, rows_refs = refs[:count], refs[count : 2 * count]
        occupancy_ref, high_ref, low_ref, places_ref = refs[2 * count : 2 * count + 4]
        out_refs = refs[2 * count + 4 :]
        for block in range(blocks):
            start = pl.multiple_of(order_ref[block] * BLOCK_ROWS, BLOCK_ROWS)
            entry = start + lax.broadcasted_iota(jnp.int32, (BLOCK_ROWS, entries), 0)
            select = as_mask(entry == places_ref[...])
            total = None
            for g in range(count):
                lanes = slice(g * row_count, (g + 1) * row_count)
                scattered = lax.dot_general(
                    select, high_ref[:, lanes], NN, preferred_element_type=jnp.float32
                ) + lax.dot_general(
                    select, low_ref[:, lanes], NN, preferred_element_type=jnp.float32
                )
                whole = occupancy_ref[WHOLE : WHOLE + 1, lanes]
                log_total = occupancy_ref[TOTAL : TOTAL + 1, lanes]
                values = logits_refs[g][pl.ds(start, BLOCK_ROWS), :]
                grad = (scattered - jnp.exp(values - log_total) * whole).astype(jnp.bfloat16)
                part = lax.dot_general(
                    grad, rows_refs[g][...], NN, preferred_element_type=jnp.float32
                )
                total = part if total is None else total + part
            out_refs[block // each][
                block % each * BLOCK_ROWS : (block % each + 1) * BLOCK_ROWS
            ] = total.astype(jnp.bfloat16)

    return call(
        kernel,
        tuple(bf16_rows(each * BLOCK_ROWS, width) for _ in range(outputs)),
        2 * blocks * BLOCK_ROWS * count * row_count * (width + 2 * entries),
        LARGE_LIMIT,
        in_specs=[smem_spec()] + [vmem_spec()] * (2 * count + 4),
        out_specs=tuple(vmem_spec() for _ in range(outputs)),
    )(order, *logits, *rows, occupancy, high, low, places)


def assemble(pieces, offsets, height, whole=None):
    count = len(pieces)
    part, width = pieces[0].shape
    short = height % part
    started = [] if whole is None else [whole]

    def kernel(offsets_ref, *refs):
        out_ref, sems = refs[count + len(started) :]

        def each(act):
            for index in range(count):
                offset = pl.multiple_of(offsets_ref[index], part)

                @pl.when(offset + part <= height)
                def _():
                    act(
                        pltpu.make_async_copy(
                            refs[index], out_ref.at[pl.ds(offset, part)], sems.at[index]
                        )
                    )

                if short:

                    @pl.when(offset + part > height)
                    def _():
                        act(
                            pltpu.make_async_copy(
                                refs[index].at[pl.ds(0, short)],
                                out_ref.at[pl.ds(height - short, short)],
                                sems.at[index],
                            )
                        )

        each(lambda copy: copy.start())
        each(lambda copy: copy.wait())

    anywhere = pl.BlockSpec(memory_space=pl.ANY)
    return call(
        kernel,
        bf16_rows(height, width),
        in_specs=[smem_spec()] + [vmem_spec()] * count + [anywhere] * len(started),
        out_specs=anywhere,
        scratch_shapes=[pltpu.SemaphoreType.DMA((count,))],
        input_output_aliases={} if whole is None else {1 + count: 0},
    )(offsets, *pieces, *started)


def swap(value, axis):
    return lax.ppermute(value, axis, [(0, 1), (1, 0)])


def crossed(value, axis, by):
    count = lax.axis_size(axis)
    return lax.ppermute(value, axis, [(i, i ^ by) for i in range(count)])


def after(value, *others):
    return lax.optimization_barrier((value,) + others)[0]


LINE_ORDER = np.array([[0, 1, 2, 3], [1, 0, 2, 3], [2, 3, 1, 0], [3, 2, 1, 0]])
MIDDLE = [(1, 2), (2, 1)]
OUTWARD = [(1, 0), (2, 3)]


def slot_orders(count):
    return LINE_ORDER if count == 4 else np.tile(np.arange(count), (count, 1))


def slot_tables(count, groups):
    orders = slot_orders(count)
    tables = np.zeros((count, count, count), np.int32)
    for member in range(count):
        for k in range(count):
            source = member ^ k
            for slot in range(count):
                tables[member, k, slot] = list(orders[source]).index(orders[member][slot])
    tables = np.concatenate([tables + g * count for g in range(groups)], axis=2)
    return tables.reshape(count, groups * count * count)


def wide(ref, start, size):
    return ref[pl.ds(start, size), :].astype(jnp.float32)


def sum_sent(own, came, places):
    height, width = own.shape
    part = height // 4

    def kernel(places_ref, own_ref, came_ref, *out_refs):
        section, outer = places_ref[0], places_ref[1]
        starts = (
            (1 - outer) * part,
            outer * part,
            (2 + 1 - section) * part,
            (2 + section) * part,
        )
        for start, out_ref in zip(starts, out_refs):
            start = pl.multiple_of(start, part)
            out_ref[...] = (wide(own_ref, start, part) + wide(came_ref, start, part)).astype(
                jnp.bfloat16
            )

    return call(
        kernel,
        tuple(bf16_rows(part, width) for _ in range(4)),
        1 << 20,
        in_specs=[smem_spec()] + [vmem_spec()] * 2,
        out_specs=tuple(vmem_spec() for _ in range(4)),
    )(places, own, came)


def sum_kept(own, came, arrived, places, keep):
    height, width = own.shape
    part = height // 4
    count = len(arrived) // 2

    def kernel(places_ref, own_ref, came_ref, *refs):
        section, outer = places_ref[0], places_ref[1]
        if not keep:
            section, outer = 1 - section, 1 - outer
        for side, start in enumerate((outer * part, (2 + section) * part)):
            start = pl.multiple_of(start, part)
            total = wide(own_ref, start, part) + wide(came_ref, start, part)
            for ref in refs[side * count : (side + 1) * count]:
                total = total + ref[...].astype(jnp.float32)
            refs[2 * count + side][...] = total.astype(jnp.bfloat16)

    return call(
        kernel,
        (bf16_rows(part, width), bf16_rows(part, width)),
        1 << 20,
        in_specs=[smem_spec()] + [vmem_spec()] * (2 + 2 * count),
        out_specs=(vmem_spec(), vmem_spec()),
    )(places, own, came, *arrived)


def per_device(
    frames,
    norm_gain,
    router,
    w_in,
    w_out,
    routing,
    head_gain,
    head_weight,
    frame_lengths,
    labels,
    label_lengths,
):
    sections = lax.axis_size("section")
    section_id = lax.axis_index("section")
    group_size = lax.axis_size("expert")
    member = lax.axis_index("expert")
    outer_size = lax.axis_size("dpo")
    inner_size = lax.axis_size("dpi")
    core = lax.axis_index("dpi")
    micro, utt_dev, frame_count, width = frames.shape
    label_max = labels.shape[2]
    experts = w_in.shape[1] * group_size
    pair_count = micro * utt_dev
    per_section = pair_count // sections
    first_pair = section_id * per_section
    share = (utt_dev * frame_count * 9 + 8 * experts - 1) // (8 * experts)
    group_count = 2 if per_section % (2 * utt_dev) == 0 else 1
    group_pairs = per_section // group_count
    filled = share * -(-group_pairs // utt_dev)
    capacity = round_up(filled + 1, 8)
    span = group_pairs * frame_count
    member_ref = member.astype(jnp.int32).reshape(1)

    def mine_of(value):
        return lax.dynamic_slice_in_dim(value, first_pair, per_section, 0)

    def exchange(blocks):
        return [blocks[0]] + [crossed(blocks[k], "expert", k) for k in range(1, group_size)]

    def lanes_of(ids):
        ids = jnp.pad(mine_of(ids), ((0, 0), (0, LANES - frame_count)), constant_values=-1)
        return [ids[g * group_pairs : (g + 1) * group_pairs] for g in range(group_count)]

    flat_frames = frames.reshape(pair_count * frame_count, width)
    current = [
        lax.dynamic_slice_in_dim(flat_frames, first_pair * frame_count + g * span, span, 0)
        for g in range(group_count)
    ]
    own_ids = routing.reshape(pair_count, frame_count)
    paired = sections == 2 and inner_size == 2
    if paired:
        other_ids = swap(own_ids, "section")
        all_ids = [
            jnp.where(section_id == layer, own_ids, other_ids) for layer in range(sections)
        ]
    else:
        all_ids = lax.all_gather(own_ids, "section")
    layer_ids = [lanes_of(all_ids[layer]) for layer in range(sections)]
    own_table = jnp.concatenate(
        [
            norm_gain,
            jnp.zeros((7, width), jnp.float32),
            jnp.transpose(router[0]).astype(jnp.float32),
            jnp.zeros((round_up(experts, 8) - experts, width), jnp.float32),
        ],
        axis=0,
    )
    own = (w_in[0, 0], w_out[0, 0])
    layers = []
    if paired:
        other_table = swap(own_table, "section")
    else:
        all_tables = lax.all_gather(own_table, "section")
        all_in = lax.all_gather(own[0], "section")
        all_out = lax.all_gather(own[1], "section")
        for layer in range(sections):
            chosen = (all_in[layer], all_out[layer])
            layers.append(((all_tables[layer],), chosen, [], jnp.ones((1,), jnp.int32)))

    outgoing = [
        dispatch(current[g], layer_ids[0][g], member_ref, experts, capacity, frame_count)
        for g in range(group_count)
    ]
    received = [exchange(blocks) for blocks in outgoing]
    if paired:
        sent_in, sent_out = half_weights(
            after(core.astype(jnp.int32).reshape(1), outgoing[0][0]), *own
        )
        came_in = swap(sent_in, "section")
        came_out = swap(sent_out, "section")
        came_in, came_out = lax.optimization_barrier((came_in, came_out, received))[:2]
        other = [(came_in, came_out), (swap(came_in, "dpi"), swap(came_out, "dpi"))]
        for layer in range(sections):
            mine = (section_id == layer).astype(jnp.int32).reshape(1)
            layers.append(((own_table, other_table), own, other, mine))

    notes = (
        first_pair.astype(jnp.int32).reshape(1),
        labels,
        jnp.transpose(frame_lengths),
        jnp.transpose(label_lengths),
    )
    shard = head_weight.shape[1]
    weight_rows = jnp.transpose(head_weight)
    line = group_size == 4
    tables = jnp.asarray(slot_tables(group_size, group_count))
    slots = lax.dynamic_index_in_dim(tables, member, 0, keepdims=False)
    outer = lax.axis_index("dpo")
    blocks = -(-shard // BLOCK_ROWS)
    tree = paired and outer_size == 2 and blocks == 8

    def pair_of(side, first, second):
        return [side * 4 + first, side * 4 + 2 + second]

    def offset_of(side, s, y):
        base = side * 4 * BLOCK_ROWS
        part = BLOCK_ROWS // 2
        return [
            base + s * BLOCK_ROWS + y * part,
            base + 2 * BLOCK_ROWS + y * BLOCK_ROWS + s * part,
        ]

    def whole_numbers(values):
        return jnp.stack([jnp.asarray(value, jnp.int32) for value in values])

    here, there = (section_id, outer), (1 - section_id, 1 - outer)
    sibling_order = whole_numbers(pair_of(1 - core, *there) + pair_of(1 - core, *here))
    sent_order = whole_numbers(pair_of(core, *there))
    kept_order = whole_numbers(pair_of(core, *here))
    chip_place = whole_numbers(here)
    first_offsets, last_offsets = [], offset_of(core, *there) + offset_of(1 - core, *there)
    for side in (core, 1 - core):
        for s, y in (here, (section_id, 1 - outer), (1 - section_id, outer)):
            first_offsets += offset_of(side, s, y)
    first_offsets, last_offsets = whole_numbers(first_offsets), whole_numbers(last_offsets)
    early = (
        slots,
        head_gain.reshape(1, width),
        layer_ids[1:],
        sibling_order,
        sent_order,
        kept_order,
        chip_place,
        first_offsets,
        last_offsets,
    )
    early, received = lax.optimization_barrier((early, received))
    slots, head_row, later_ids, sibling_order, sent_order, kept_order = early[:6]
    chip_place, first_offsets, last_offsets = early[6:]
    layer_ids = [layer_ids[0]] + list(later_ids)

    def tied(value, others, g):
        marks = [other for i, other in enumerate(others) if i != g]
        return after(value, *marks) if marks else value

    normed, marks = [], []
    for layer in range(sections):
        choices, weights, others, pick_own = layers[layer]
        done = [
            run_expert(
                received[g],
                choices,
                weights,
                others,
                tied(pick_own, marks, g),
                filled,
                notes if layer == 0 and g == 0 else None,
                per_section,
            )
            for g in range(group_count)
        ]
        returned = [exchange(parts) for parts in done]
        marks = [parts[0] for parts in done]
        tokens = [tied(member_ref, marks, g) for g in range(group_count)]
        if layer == sections - 1 and group_count > 1:
            tokens[-1] = after(tokens[-1], label_weight)
        sizes = (experts, capacity, frame_count)
        if layer < sections - 1:
            made = [
                combine_and_dispatch(
                    current[g],
                    returned[g],
                    layer_ids[layer][g],
                    choices,
                    pick_own,
                    layer_ids[layer + 1][g],
                    tokens[g],
                    *sizes,
                )
                for g in range(group_count)
            ]
            current = [pair[0] for pair in made]
            received = [exchange(pair[1]) for pair in made]
            marks = current
        else:
            normed = [
                combine_and_norm(
                    current[g],
                    returned[g],
                    layer_ids[layer][g],
                    choices,
                    pick_own,
                    head_row,
                    tokens[g],
                    *sizes,
                )
                for g in range(group_count)
            ]
        if layer == 0:
            found = list(returned[0])
            if not line:
                stacked = jnp.stack(found)
                found = [
                    lax.dynamic_index_in_dim(stacked, member ^ k, 0, keepdims=False)
                    for k in range(group_size)
                ]
            label_weight, places, names = label_rows(
                weight_rows, found, member_ref, group_count, group_pairs, filled, label_max, line
            )

    def logits_of(fill, first, count, pieces, earlier=None):
        return head_logits(
            fill, first, count, pieces, member_ref, weight_rows, label_weight, frame_count, earlier
        )

    def stats_of(stats):
        first = crossed(stats, "expert", 1)
        return [stats, first, crossed(stats, "expert", 2), crossed(first, "expert", 2)]

    heads, found = [], []
    for g in range(group_count):
        if line:
            beside = crossed(normed[g], "expert", 1)
            middle = lax.ppermute(normed[g], "expert", MIDDLE)
            beside, middle = lax.optimization_barrier((beside, middle, normed[-1]))[:2]
            far = lax.ppermute(beside, "expert", MIDDLE)
            outward = lax.ppermute(middle, "expert", OUTWARD)
            if g > 0:
                far = after(far, heads[0][2])
            last = lax.ppermute(far, "expert", OUTWARD)
            pieces = [normed[g], beside, middle, outward, far, last]
            earlier = heads[-1][2] if heads else None
            heads.append(logits_of(fill_line, g * group_size, group_size, pieces, earlier))
        else:
            gathered = lax.all_gather(normed[g], "expert")
            pieces = [gathered[k] for k in range(group_size)]
            heads.append(logits_of(fill_all, g * group_size, group_size, pieces))
            gathered = lax.all_gather(heads[g][2], "expert")
            found.append(
                [
                    lax.dynamic_index_in_dim(gathered, member ^ k, 0, keepdims=False)
                    for k in range(group_size)
                ]
            )
    if line:
        found = [stats_of(heads[-1][2])]
    kept_losses = group_pairs if line else group_size * group_pairs
    occupancy, high, low, losses = ctc_pass(
        found, slots, names, frame_count, label_max, group_count, kept_losses
    )
    if not line:
        pairs = losses.reshape(group_count, group_size, group_pairs)
        losses = lax.dynamic_index_in_dim(pairs, member, 1).reshape(1, per_section)
    losses = jnp.transpose(losses)

    def gradient(order, outputs, each):
        return head_gradient(
            [head[0] for head in heads],
            [head[1] for head in heads],
            occupancy,
            high,
            low,
            places,
            order,
            outputs,
            each,
        )

    if tree:
        sibling_sent, sibling_kept = gradient(sibling_order, 2, 2)
        came_sent, came_kept = swap(sibling_sent, "dpi"), swap(sibling_kept, "dpi")
        own_sent = gradient(after(sent_order, sibling_sent), 1, 2)[0]
        a_far, a_near, b_far, b_near = sum_sent(own_sent, came_sent, chip_place)
        kept_order = after(kept_order, a_far)
        a_far, b_far = swap(a_far, "section"), swap(b_far, "dpo")
        a_near, b_near = swap(a_near, "section"), swap(b_near, "dpo")
        own_kept = gradient(kept_order, 1, 2)[0]
        a_on, b_on = sum_kept(own_kept, came_kept, [a_far, b_far], chip_place, False)
        a_in, b_in = swap(a_on, "dpo"), swap(b_on, "section")
        a, b = sum_kept(own_kept, came_kept, [a_near, a_in, b_near, b_in], chip_place, True)
        a_y, b_x = swap(a, "dpo"), swap(b, "section")
        b_y, a_x = swap(b, "dpo"), swap(a, "section")
        a_xy, b_xy = swap(a_y, "section"), swap(b_x, "dpo")
        b_y, a_x = lax.optimization_barrier((b_y, a_x, a_xy, b_xy))[:2]
        mine = [a, b, a_y, b_y, a_x, b_x]
        theirs = [swap(value, "dpi") for value in mine]
        whole = assemble(mine + theirs, first_offsets, shard)
        last = [a_xy, b_xy, swap(a_xy, "dpi"), swap(b_xy, "dpi")]
        whole = assemble(last, last_offsets, shard, whole)
    else:
        partial = gradient(jnp.arange(blocks, dtype=jnp.int32), 1, blocks)[0][:shard]
        whole = lax.psum(partial.astype(jnp.float32), ("section", "dpo", "dpi")).astype(
            jnp.bfloat16
        )
    return (losses, jnp.transpose(whole))


def solution(mesh):
    sections, group_size, spread = (mesh.shape[name] for name in ("section", "expert", "dp"))
    inner = 2 if spread % 2 == 0 else 1
    split = Mesh(
        mesh.devices.reshape(sections, group_size, spread // inner, inner),
        ("section", "expert", "dpo", "dpi"),
    )
    block = ("expert", "dpo", "dpi")
    placed = (
        P(None, block, None, None),
        P("section", None),
        P("section", None, None),
        P("section", "expert", None, None),
        P("section", "expert", None, None),
        P("section", None, block, None, None),
        P(),
        P(None, "expert"),
        P(None, block),
        P(None, block, None),
        P(None, block),
    )
    return jax.shard_map(
        per_device,
        mesh=split,
        in_specs=placed,
        out_specs=(P("section", block), P(None, "expert")),
        check_vma=False,
    )
```

```python
import jax
import jax.numpy as jnp
import numpy as np
from jax import lax
from jax.experimental import pallas as pl
from jax.experimental.pallas import tpu as pltpu
from jax.sharding import Mesh, PartitionSpec as P

EPSILON = 1e-06
LOG_ZERO = -1e30
VMEM_LIMIT = 12 * 1024 * 1024
LARGE_LIMIT = 24 * 1024 * 1024
LANES = 128
COLS = 16
PEAK, TOTAL, WHOLE = COLS - 3, COLS - 2, COLS - 3
BLOCK_ROWS = 256
NT = (((1,), (1,)), ((), ()))
NN = (((1,), (0,)), ((), ()))


def round_up(value, unit):
    return -(-value // unit) * unit


def vmem_spec():
    return pl.BlockSpec(memory_space=pltpu.VMEM)


def smem_spec():
    return pl.BlockSpec(memory_space=pltpu.SMEM)


def call(kernel, out_shape, flops=0, limit=VMEM_LIMIT, **options):
    return pl.pallas_call(
        kernel,
        out_shape=out_shape,
        compiler_params=pltpu.CompilerParams(vmem_limit_bytes=limit),
        cost_estimate=pl.CostEstimate(flops=flops, bytes_accessed=0, transcendentals=0),
        **options,
    )


def bf16_rows(count, width):
    return jax.ShapeDtypeStruct((count, width), jnp.bfloat16)


def as_mask(values):
    return values.astype(jnp.float32).astype(jnp.bfloat16)


def split_rows(values, out_refs, spare=None, note=None):
    size, width = out_refs[0].shape
    for turn, out_ref in enumerate(out_refs):
        part = values[turn * size : (turn + 1) * size]
        if note is not None:
            row = lax.broadcasted_iota(jnp.int32, (size, width), 0)
            part = jnp.where(row == spare, note, part)
        out_ref[...] = part.astype(jnp.bfloat16)


def join_rows(refs):
    return jnp.concatenate([ref[...].astype(jnp.float32) for ref in refs], axis=0)


def rms_scale(values, gain):
    values = values.astype(jnp.float32)
    scale = lax.rsqrt(jnp.mean(values * values, axis=-1, keepdims=True) + EPSILON)
    return (values * scale * gain).astype(jnp.bfloat16)


def expert_column(ids, frame_count):
    pairs = ids.shape[0]
    square = jnp.concatenate(
        [ids.astype(jnp.float32), jnp.full((LANES - pairs, LANES), -1.0, jnp.float32)], axis=0
    )
    turned = jnp.transpose(square, (1, 0)).astype(jnp.int32)
    return jnp.concatenate([turned[:frame_count, p : p + 1] for p in range(pairs)], axis=0)


def placement(column, member, experts, capacity):
    count = column.shape[0]
    relative = column ^ member
    lane = lax.broadcasted_iota(jnp.int32, (count, LANES), 1)
    one_hot = (lane == relative).astype(jnp.float32)
    before = lax.broadcasted_iota(jnp.int32, (count, count), 1) <= lax.broadcasted_iota(
        jnp.int32, (count, count), 0
    )
    rank = lax.dot_general(
        as_mask(before), one_hot.astype(jnp.bfloat16), NN, preferred_element_type=jnp.float32
    )
    start = (lane * capacity - 1).astype(jnp.float32)
    slots = jnp.sum(one_hot * (rank + start), axis=1, keepdims=True).astype(jnp.int32)
    places = lax.broadcasted_iota(jnp.int32, (count, experts * capacity), 1)
    return (places == slots).astype(jnp.float32)


def scatter_rows(rows, ids, member, experts, capacity, frame_count, out_refs):
    count = rows.shape[0]
    chosen = placement(expert_column(ids, frame_count), member, experts, capacity)
    tall = round_up(count, LANES)
    if tall > count:
        chosen = jnp.concatenate(
            [chosen, jnp.zeros((tall - count, chosen.shape[1]), jnp.float32)], axis=0
        )
    pick = jnp.transpose(chosen, (1, 0))[:, :count].astype(jnp.bfloat16)
    placed = lax.dot_general(pick, rows, NN, preferred_element_type=jnp.float32)
    split_rows(placed, out_refs)


def combine_rows(rows, returned, ids, table, member, experts, capacity, frame_count):
    column = expert_column(ids, frame_count)
    pick = placement(column, member, experts, capacity).astype(jnp.bfloat16)
    normed = rms_scale(rows, table[:1])
    router = jnp.concatenate(
        [table[8:], jnp.zeros((LANES + 8 - table.shape[0], rows.shape[1]), jnp.float32)], axis=0
    ).astype(jnp.bfloat16)
    logits = lax.dot_general(normed, router, NT, preferred_element_type=jnp.float32)
    lane = lax.broadcasted_iota(jnp.int32, logits.shape, 1)
    gate = jax.nn.sigmoid(jnp.sum(jnp.where(lane == column, logits, 0.0), axis=1, keepdims=True))
    stacked = join_rows(returned).astype(jnp.bfloat16)
    mixed = lax.dot_general(pick, stacked, NN, preferred_element_type=jnp.float32)
    return (rows.astype(jnp.float32) + gate * mixed).astype(jnp.bfloat16)


def dispatch(rows, ids, member, experts, capacity, frame_count):
    width = rows.shape[1]

    def kernel(member_ref, rows_ref, ids_ref, *out_refs):
        scatter_rows(
            rows_ref[...], ids_ref[...], member_ref[0], experts, capacity, frame_count, out_refs
        )

    return call(
        kernel,
        tuple(bf16_rows(capacity, width) for _ in range(experts)),
        1 << 27,
        in_specs=[smem_spec()] + [vmem_spec()] * 2,
        out_specs=tuple(vmem_spec() for _ in range(experts)),
    )(member, rows, ids)


def pick_table(pick_ref, tables):
    if len(tables) == 1:
        return tables[0][...]
    return jnp.where(pick_ref[0] == 1, tables[0][...], tables[1][...])


def note_row(first_ref, labels_ref, frames_ref, counts_ref, pairs, width):
    utt_dev, label_max = labels_ref.shape[1:]
    lane = lax.broadcasted_iota(jnp.int32, (1, width), 1)
    row = jnp.zeros((1, width), jnp.int32)
    for pair in range(pairs):
        index = first_ref[0] + pair
        micro, utt = index // utt_dev, index % utt_dev
        values = [labels_ref[micro, utt, c] for c in range(label_max)]
        values += [frames_ref[utt, micro], counts_ref[utt, micro]]
        for c, value in enumerate(values):
            row = jnp.where(lane == pair * COLS + c, value // LANES, row)
            row = jnp.where(lane == LANES + pair * COLS + c, value % LANES, row)
    return row.astype(jnp.float32)


def run_expert(received, tables, own, other, pick_own, spare, note, pairs):
    count = len(received)
    capacity, width = received[0].shape
    others, choices = len(other), len(tables)
    noted = [] if note is None else list(note)

    def kernel(pick_ref, in_ref, out_weight_ref, *refs):
        table_refs, refs = refs[:choices], refs[choices:]
        other_refs, refs = refs[: 2 * others], refs[2 * others :]
        received_refs, refs = refs[:count], refs[count:]
        out_refs = refs[len(noted) :]

        def work(pieces):
            gain = pick_table(pick_ref, table_refs)[:1]
            normed = rms_scale(join_rows(received_refs), gain)
            total = None
            for weight_in, weight_out in pieces:
                hidden = lax.dot_general(
                    normed, weight_in[...], NN, preferred_element_type=jnp.float32
                )
                active = (hidden / (1.0 + jnp.exp(-hidden))).astype(jnp.bfloat16)
                part = lax.dot_general(
                    active, weight_out[...], NN, preferred_element_type=jnp.float32
                )
                total = part if total is None else total + part
            row = note_row(*refs[: len(noted)], pairs, width) if noted else None
            split_rows(total, out_refs, spare, row)

        if others == 0:
            work([(in_ref, out_weight_ref)])
            return

        @pl.when(pick_ref[0] == 1)
        def _():
            work([(in_ref, out_weight_ref)])

        @pl.when(pick_ref[0] != 1)
        def _():
            work([(other_refs[2 * i], other_refs[2 * i + 1]) for i in range(others)])

    flat = [weight for pair in other for weight in pair]
    return call(
        kernel,
        tuple(bf16_rows(capacity, width) for _ in range(count)),
        4 * count * capacity * width * own[0].shape[1],
        in_specs=[smem_spec()] + [vmem_spec()] * (2 + choices + 2 * others + count)
        + [smem_spec()] * len(noted),
        out_specs=tuple(vmem_spec() for _ in range(count)),
    )(pick_own, *own, *tables, *flat, *received, *noted)


def combine_and_dispatch(
    rows, returned, ids, tables, pick_own, next_ids, member, experts, capacity, frame_count
):
    width = rows.shape[1]
    choices = len(tables)

    def kernel(member_ref, pick_ref, rows_ref, ids_ref, next_ref, *refs):
        table_refs, refs = refs[:choices], refs[choices:]
        returned_refs, x_ref, out_refs = refs[:experts], refs[experts], refs[experts + 1 :]
        mixed = combine_rows(
            rows_ref[...],
            returned_refs,
            ids_ref[...],
            pick_table(pick_ref, table_refs),
            member_ref[0],
            experts,
            capacity,
            frame_count,
        )
        x_ref[...] = mixed
        scatter_rows(
            mixed, next_ref[...], member_ref[0], experts, capacity, frame_count, out_refs
        )

    shapes = (bf16_rows(*rows.shape),) + tuple(
        bf16_rows(capacity, width) for _ in range(experts)
    )
    result = call(
        kernel,
        shapes,
        1 << 28,
        in_specs=[smem_spec()] * 2 + [vmem_spec()] * (3 + choices + experts),
        out_specs=tuple(vmem_spec() for _ in shapes),
    )(member, pick_own, rows, ids, next_ids, *tables, *returned)
    return result[0], result[1:]


def combine_and_norm(
    rows, returned, ids, tables, pick_own, head_gain, member, experts, capacity, frame_count
):
    choices = len(tables)

    def kernel(member_ref, pick_ref, rows_ref, ids_ref, head_ref, *refs):
        table_refs, refs = refs[:choices], refs[choices:]
        final = combine_rows(
            rows_ref[...],
            refs[:experts],
            ids_ref[...],
            pick_table(pick_ref, table_refs),
            member_ref[0],
            experts,
            capacity,
            frame_count,
        )
        refs[experts][...] = rms_scale(final, head_ref[...])

    return call(
        kernel,
        bf16_rows(*rows.shape),
        1 << 28,
        in_specs=[smem_spec()] * 2 + [vmem_spec()] * (3 + choices + experts),
        out_specs=vmem_spec(),
    )(member, pick_own, rows, ids, head_gain, *tables, *returned)


def half_weights(core, weight_in, weight_out):
    width, hidden = weight_in.shape
    half = hidden // 2

    def kernel(core_ref, in_ref, out_ref, half_in, half_out, sems):
        start = pl.multiple_of(core_ref[0] * half, half)
        copies = (
            pltpu.make_async_copy(in_ref.at[:, pl.ds(start, half)], half_in, sems.at[0]),
            pltpu.make_async_copy(out_ref.at[pl.ds(start, half)], half_out, sems.at[1]),
        )
        for copy in copies:
            copy.start()
        for copy in copies:
            copy.wait()

    return call(
        kernel,
        (bf16_rows(width, half), bf16_rows(half, width)),
        1 << 20,
        in_specs=[smem_spec()] + [pl.BlockSpec(memory_space=pl.ANY)] * 2,
        out_specs=(vmem_spec(), vmem_spec()),
        scratch_shapes=[pltpu.SemaphoreType.DMA((2,))],
    )(core, weight_in, weight_out)


def block_list(shard):
    return [(i, min(BLOCK_ROWS, shard - i)) for i in range(0, shard, BLOCK_ROWS)]


def label_rows(weight, notes, member, groups, pairs, spare, label_max, line):
    shard, width = weight.shape
    sources = len(notes)
    utterances = sources * groups * pairs
    entries = utterances * COLS

    def kernel(member_ref, weight_ref, *refs):
        note_refs = refs[:sources]
        out_ref, places_ref, names_ref, turned_ref = refs[sources:]
        place = member_ref[0]
        found = []
        for ref in note_refs:
            row = ref[...].astype(jnp.float32)[spare : spare + 1]
            found.append((row[:, :LANES] * LANES + row[:, LANES : 2 * LANES]).astype(jnp.int32))
        if line:
            ends = (place == 0) | (place == 3)
            found = [
                found[0],
                found[1],
                jnp.where(ends, found[2], found[3]),
                jnp.where(ends, found[3], found[2]),
            ]
        names_ref[...] = jnp.zeros(names_ref.shape, jnp.int32)
        for slot in range(sources):
            for pair in range(groups * pairs):
                row = (pair // pairs * sources + slot) * pairs + pair % pairs
                names_ref[row : row + 1, :COLS] = found[slot][:, pair * COLS : (pair + 1) * COLS]
        lane = lax.broadcasted_iota(jnp.int32, (utterances, LANES), 1)
        named = jnp.where(lane < label_max, names_ref[...], jnp.where(lane == label_max, 0, -1))
        local = named - place * shard
        local = jnp.where((named >= 0) & (local >= 0) & (local < shard), local, -1)
        square = jnp.concatenate(
            [
                local.astype(jnp.float32),
                jnp.full((LANES - utterances, LANES), -1.0, jnp.float32),
            ],
            axis=0,
        )
        turned = jnp.transpose(square, (1, 0))
        for utterance in range(utterances):
            turned_ref[utterance * COLS : (utterance + 1) * COLS] = jnp.broadcast_to(
                turned[:COLS, utterance : utterance + 1], (COLS, LANES)
            )
        places = turned_ref[:, :1].astype(jnp.int32)
        places_ref[...] = jnp.transpose(turned_ref[...], (1, 0))[:1].astype(jnp.int32)
        total = jnp.zeros((entries, width), jnp.float32)
        for first, size in block_list(shard):
            entry = first + lax.broadcasted_iota(jnp.int32, (entries, size), 1)
            total = total + lax.dot_general(
                as_mask(entry == places),
                weight_ref[first : first + size],
                NN,
                preferred_element_type=jnp.float32,
            )
        out_ref[...] = total.astype(jnp.bfloat16)

    return call(
        kernel,
        (
            bf16_rows(entries, width),
            jax.ShapeDtypeStruct((1, entries), jnp.int32),
            jax.ShapeDtypeStruct((utterances, LANES), jnp.int32),
        ),
        2 * shard * entries * width,
        LARGE_LIMIT,
        in_specs=[smem_spec()] + [vmem_spec()] * (1 + sources),
        out_specs=tuple(vmem_spec() for _ in range(3)),
        scratch_shapes=[pltpu.VMEM((entries, LANES), jnp.float32)],
    )(member, weight, *notes)


def head_logits(
    fill, first_slot, count, pieces, member, weight, label_weight, frame_count, earlier=None
):
    given = len(pieces)
    span, width = pieces[0].shape
    row_count = count * span
    shard = weight.shape[0]
    height = round_up(shard, BLOCK_ROWS)
    entries = row_count // frame_count * COLS
    first_entry = first_slot * entries // count
    others = [] if earlier is None else [earlier]
    ahead = 0 if earlier is None else earlier.shape[0]

    def kernel(member_ref, weight_ref, label_ref, *refs):
        piece_refs = refs[:given]
        logits_ref, rows_ref, stats_ref = refs[given + len(others) :]

        def put(slot, piece_ref):
            rows_ref[slot * span : (slot + 1) * span] = piece_ref[...]

        def put_if(condition, slot, piece_ref):
            @pl.when(condition)
            def _():
                put(slot, piece_ref)

        fill(member_ref[0], piece_refs, put, put_if)
        peak = jnp.full((1, row_count), LOG_ZERO, jnp.float32)
        total = jnp.zeros((1, row_count), jnp.float32)
        for first, size in block_list(shard):
            logits = lax.dot_general(
                weight_ref[first : first + size],
                rows_ref[...],
                NT,
                preferred_element_type=jnp.float32,
            )
            logits_ref[first : first + size] = logits
            before = peak
            peak = jnp.maximum(before, jnp.max(logits, axis=0, keepdims=True))
            total = total * jnp.exp(before - peak) + jnp.sum(
                jnp.exp(logits - peak), axis=0, keepdims=True
            )
        if height > shard:
            logits_ref[shard:] = jnp.full((height - shard, row_count), LOG_ZERO, jnp.float32)
        crossed = lax.dot_general(
            label_ref[first_entry : first_entry + entries],
            rows_ref[...],
            NT,
            preferred_element_type=jnp.float32,
        )
        owner = lax.broadcasted_iota(jnp.int32, (COLS, row_count), 1) // frame_count
        picked = jnp.zeros((COLS, row_count), jnp.float32)
        for utterance in range(entries // COLS):
            part = crossed[utterance * COLS : (utterance + 1) * COLS]
            picked = picked + jnp.where(owner == utterance, part, 0.0)
        place = lax.broadcasted_iota(jnp.int32, (COLS, row_count), 0)
        stats = jnp.where(place == PEAK, peak, picked)
        stats = jnp.where(place == TOTAL, total, stats)
        for slot in range(ahead):
            stats_ref[slot] = refs[given][slot]
        for slot in range(count):
            stats_ref[ahead + slot] = stats[:, slot * span : (slot + 1) * span]

    return call(
        kernel,
        (
            jax.ShapeDtypeStruct((height, row_count), jnp.float32),
            bf16_rows(row_count, width),
            jax.ShapeDtypeStruct((ahead + count, COLS, span), jnp.float32),
        ),
        2 * height * row_count * width,
        LARGE_LIMIT,
        in_specs=[smem_spec()] + [vmem_spec()] * (2 + given + len(others)),
        out_specs=tuple(vmem_spec() for _ in range(3)),
    )(member, weight, label_weight, *pieces, *others)


def fill_line(place, piece_refs, put, put_if):
    own, beside, middle, outward, far, last = piece_refs
    ends = (place == 0) | (place == 3)
    inner = (place == 1) | (place == 2)
    put(0, own)
    put(1, beside)
    put_if(ends, 2, outward)
    put_if(ends, 3, last)
    put_if(inner, 2, middle)
    put_if(inner, 3, far)


def fill_all(place, piece_refs, put, put_if):
    for slot, piece_ref in enumerate(piece_refs):
        put(slot, piece_ref)


def log_add(first, second):
    peak = jnp.maximum(first, second)
    return peak + jnp.log(jnp.exp(first - peak) + jnp.exp(second - peak))


def log_add3(first, second, third):
    peak = jnp.maximum(jnp.maximum(first, second), third)
    return peak + jnp.log(
        jnp.exp(first - peak) + jnp.exp(second - peak) + jnp.exp(third - peak)
    )


def ctc_pass(stats, slots, notes, frame_count, label_max, parts, kept):
    calls, sources = len(stats), len(stats[0])
    each, _, span = stats[0][0].shape
    count = calls * each
    row_count = count * span
    utterances = notes.shape[0]
    entries = utterances * COLS
    tall = round_up(span, LANES)

    def kernel(slots_ref, notes_ref, *refs):
        (
            out_ref,
            high_ref,
            low_ref,
            loss_ref,
            turn_ref,
            emission_ref,
            emit_blank,
            emit_label,
            blank_fwd,
            label_fwd,
            blank_bwd,
            label_bwd,
            occupancy_ref,
        ) = refs[calls * sources :]
        place = lax.broadcasted_iota(jnp.int32, (COLS, span), 0)
        turn_ref[...] = jnp.zeros(turn_ref.shape, jnp.float32)
        for slot in range(count):
            found = []
            for k in range(sources):
                where = slots_ref[k * count + slot]
                part = refs[k][where % each]
                for other in range(1, calls):
                    later = refs[other * sources + k][where % each]
                    part = jnp.where(where >= other * each, later, part)
                found.append(part)
            joined = found[0]
            peak = found[0][PEAK : PEAK + 1]
            for other in found[1:]:
                joined = joined + other
                peak = jnp.maximum(peak, other[PEAK : PEAK + 1])
            total = jnp.zeros((1, span), jnp.float32)
            for other in found:
                total = total + other[TOTAL : TOTAL + 1] * jnp.exp(other[PEAK : PEAK + 1] - peak)
            log_total = peak + jnp.log(total)
            turn_ref[:COLS, :span] = jnp.where(place == TOTAL, log_total, joined - log_total)
            emission_ref[slot * span : (slot + 1) * span] = jnp.transpose(turn_ref[...], (1, 0))[
                :span
            ]

        lane = lax.broadcasted_iota(jnp.int32, (utterances, LANES), 1)
        is_label = lane < label_max
        is_blank = lane <= label_max
        names = jnp.where(is_label, notes_ref[...], 0)
        earlier = pltpu.roll(names, 1, 1)
        skip = is_label & (lane >= 1) & (names != 0) & (names != earlier)
        later = pltpu.roll(names, LANES - 1, 1)
        skip_next = (lane < label_max - 1) & (later != 0) & (later != names)
        frames = notes_ref[:, label_max : label_max + 1]
        counts = notes_ref[:, label_max + 1 : label_max + 2]
        ends_blank = jnp.where(lane == counts, 0.0, LOG_ZERO)
        ends_label = jnp.where(lane == counts - 1, 0.0, LOG_ZERO)

        def spread(step, carry):
            row = emission_ref[pl.ds(step, utterances, stride=frame_count), :]
            blank = jnp.sum(jnp.where(lane == label_max, row, 0.0), axis=1, keepdims=True)
            emit_blank[step] = jnp.where(is_blank, blank, LOG_ZERO)
            emit_label[step] = jnp.where(is_label, row, LOG_ZERO)
            return carry

        lax.fori_loop(0, frame_count, spread, 0, unroll=16)

        def advance(step, carry):
            fwd_blank, fwd_label, bwd_blank, bwd_label = carry
            moved = jnp.where(lane == 0, LOG_ZERO, pltpu.roll(fwd_label, 1, 1))
            new_blank = log_add(fwd_blank, moved) + emit_blank[step]
            new_label = (
                log_add3(fwd_label, fwd_blank, jnp.where(skip, moved, LOG_ZERO))
                + emit_label[step]
            )
            alive = step < frames
            fwd_blank = jnp.where(alive, new_blank, fwd_blank)
            fwd_label = jnp.where(alive, new_label, fwd_label)
            blank_fwd[step] = fwd_blank
            label_fwd[step] = fwd_label

            back = frame_count - 1 - step
            out_blank = bwd_blank + emit_blank[back + 1]
            out_label = bwd_label + emit_label[back + 1]
            next_blank = pltpu.roll(out_blank, LANES - 1, 1)
            next_label = jnp.where(skip_next, pltpu.roll(out_label, LANES - 1, 1), LOG_ZERO)
            ended = back >= frames - 1
            bwd_blank = jnp.where(ended, ends_blank, log_add(out_blank, out_label))
            bwd_label = jnp.where(
                ended, ends_label, log_add3(out_label, next_blank, next_label)
            )
            blank_bwd[back] = bwd_blank
            label_bwd[back] = bwd_label
            return (fwd_blank, fwd_label, bwd_blank, bwd_label)

        first_blank = jnp.where(lane == 0, emit_blank[0], LOG_ZERO)
        first_label = jnp.where(lane == 0, emit_label[0], LOG_ZERO)
        blank_fwd[0] = first_blank
        label_fwd[0] = first_label
        blank_bwd[frame_count - 1] = ends_blank
        label_bwd[frame_count - 1] = ends_label
        fwd_blank, fwd_label, _, _ = lax.fori_loop(
            1, frame_count, advance, (first_blank, first_label, ends_blank, ends_label), unroll=4
        )
        end_state = jnp.sum(jnp.where(lane == counts, fwd_blank, 0.0), axis=1, keepdims=True)
        near_state = jnp.sum(jnp.where(lane == counts - 1, fwd_label, 0.0), axis=1, keepdims=True)
        log_like = log_add(end_state, near_state)
        turned_losses = jnp.transpose(jnp.broadcast_to(-log_like, (utterances, LANES)), (1, 0))
        for part in range(parts):
            first = part * utterances // parts
            loss_ref[:, part * kept : (part + 1) * kept] = turned_losses[:1, first : first + kept]

        def occupy(step, carry):
            blank = jnp.exp(blank_fwd[step] + blank_bwd[step] - log_like)
            label = jnp.exp(label_fwd[step] + label_bwd[step] - log_like)
            blank = jnp.sum(jnp.where(is_blank, blank, 0.0), axis=1, keepdims=True)
            label = jnp.where(is_label, label, 0.0)
            whole = blank + jnp.sum(label, axis=1, keepdims=True)
            filled = jnp.where(lane == label_max, blank, label)
            filled = jnp.where(lane == WHOLE, whole, filled)
            filled = jnp.where(step < frames, -filled, 0.0)
            row = emission_ref[pl.ds(step, utterances, stride=frame_count), :]
            occupancy_ref[pl.ds(step, utterances, stride=frame_count), :] = jnp.where(
                lane == TOTAL, row, filled
            )
            return carry

        lax.fori_loop(0, frame_count, occupy, 0, unroll=16)
        turned = jnp.transpose(occupancy_ref[...], (1, 0))[:COLS]
        out_ref[...] = turned
        row_place = lax.broadcasted_iota(jnp.int32, (COLS, row_count), 0)
        owner = lax.broadcasted_iota(jnp.int32, (COLS, row_count), 1) // frame_count
        source = jnp.where(row_place < WHOLE, turned, 0.0)
        for utterance in range(utterances):
            part = jnp.where(owner == utterance, source, 0.0)
            high = part.astype(jnp.bfloat16)
            high_ref[utterance * COLS : (utterance + 1) * COLS] = high
            low_ref[utterance * COLS : (utterance + 1) * COLS] = (
                part - high.astype(jnp.float32)
            ).astype(jnp.bfloat16)

    held = pltpu.VMEM((frame_count, utterances, LANES), jnp.float32)
    table = pltpu.VMEM((row_count, LANES), jnp.float32)
    return call(
        kernel,
        (
            jax.ShapeDtypeStruct((COLS, row_count), jnp.float32),
            bf16_rows(entries, row_count),
            bf16_rows(entries, row_count),
            jax.ShapeDtypeStruct((1, parts * kept), jnp.float32),
        ),
        1 << 26,
        in_specs=[smem_spec()] + [vmem_spec()] * (1 + calls * sources),
        out_specs=tuple(vmem_spec() for _ in range(4)),
        scratch_shapes=[pltpu.VMEM((LANES, tall), jnp.float32), table]
        + [held] * 6
        + [table],
    )(slots, notes, *[value for group in stats for value in group])


def head_gradient(logits, rows, occupancy, high, low, places, order, outputs, each):
    count = len(logits)
    row_count, width = rows[0].shape
    entries = places.shape[1]
    blocks = outputs * each

    def kernel(order_ref, *refs):
        logits_refs, rows_refs = refs[:count], refs[count : 2 * count]
        occupancy_ref, high_ref, low_ref, places_ref = refs[2 * count : 2 * count + 4]
        out_refs = refs[2 * count + 4 :]
        for block in range(blocks):
            start = pl.multiple_of(order_ref[block] * BLOCK_ROWS, BLOCK_ROWS)
            entry = start + lax.broadcasted_iota(jnp.int32, (BLOCK_ROWS, entries), 0)
            select = as_mask(entry == places_ref[...])
            total = None
            for g in range(count):
                lanes = slice(g * row_count, (g + 1) * row_count)
                scattered = lax.dot_general(
                    select, high_ref[:, lanes], NN, preferred_element_type=jnp.float32
                ) + lax.dot_general(
                    select, low_ref[:, lanes], NN, preferred_element_type=jnp.float32
                )
                whole = occupancy_ref[WHOLE : WHOLE + 1, lanes]
                log_total = occupancy_ref[TOTAL : TOTAL + 1, lanes]
                values = logits_refs[g][pl.ds(start, BLOCK_ROWS), :]
                grad = (scattered - jnp.exp(values - log_total) * whole).astype(jnp.bfloat16)
                part = lax.dot_general(
                    grad, rows_refs[g][...], NN, preferred_element_type=jnp.float32
                )
                total = part if total is None else total + part
            out_refs[block // each][
                block % each * BLOCK_ROWS : (block % each + 1) * BLOCK_ROWS
            ] = total.astype(jnp.bfloat16)

    return call(
        kernel,
        tuple(bf16_rows(each * BLOCK_ROWS, width) for _ in range(outputs)),
        2 * blocks * BLOCK_ROWS * count * row_count * (width + 2 * entries),
        LARGE_LIMIT,
        in_specs=[smem_spec()] + [vmem_spec()] * (2 * count + 4),
        out_specs=tuple(vmem_spec() for _ in range(outputs)),
    )(order, *logits, *rows, occupancy, high, low, places)


def assemble(pieces, offsets, height, whole=None):
    count = len(pieces)
    part, width = pieces[0].shape
    short = height % part
    started = [] if whole is None else [whole]

    def kernel(offsets_ref, *refs):
        out_ref, sems = refs[count + len(started) :]

        def each(act):
            for index in range(count):
                offset = pl.multiple_of(offsets_ref[index], part)

                @pl.when(offset + part <= height)
                def _():
                    act(
                        pltpu.make_async_copy(
                            refs[index], out_ref.at[pl.ds(offset, part)], sems.at[index]
                        )
                    )

                if short:

                    @pl.when(offset + part > height)
                    def _():
                        act(
                            pltpu.make_async_copy(
                                refs[index].at[pl.ds(0, short)],
                                out_ref.at[pl.ds(height - short, short)],
                                sems.at[index],
                            )
                        )

        each(lambda copy: copy.start())
        each(lambda copy: copy.wait())

    anywhere = pl.BlockSpec(memory_space=pl.ANY)
    return call(
        kernel,
        bf16_rows(height, width),
        in_specs=[smem_spec()] + [vmem_spec()] * count + [anywhere] * len(started),
        out_specs=anywhere,
        scratch_shapes=[pltpu.SemaphoreType.DMA((count,))],
        input_output_aliases={} if whole is None else {1 + count: 0},
    )(offsets, *pieces, *started)


def swap(value, axis):
    return lax.ppermute(value, axis, [(0, 1), (1, 0)])


def crossed(value, axis, by):
    count = lax.axis_size(axis)
    return lax.ppermute(value, axis, [(i, i ^ by) for i in range(count)])


def after(value, *others):
    return lax.optimization_barrier((value,) + others)[0]


LINE_ORDER = np.array([[0, 1, 2, 3], [1, 0, 2, 3], [2, 3, 1, 0], [3, 2, 1, 0]])
MIDDLE = [(1, 2), (2, 1)]
OUTWARD = [(1, 0), (2, 3)]


def slot_orders(count):
    return LINE_ORDER if count == 4 else np.tile(np.arange(count), (count, 1))


def slot_tables(count, groups):
    orders = slot_orders(count)
    tables = np.zeros((count, count, count), np.int32)
    for member in range(count):
        for k in range(count):
            source = member ^ k
            for slot in range(count):
                tables[member, k, slot] = list(orders[source]).index(orders[member][slot])
    tables = np.concatenate([tables + g * count for g in range(groups)], axis=2)
    return tables.reshape(count, groups * count * count)


def wide(ref, start, size):
    return ref[pl.ds(start, size), :].astype(jnp.float32)


def sum_sent(own, came, places):
    height, width = own.shape
    part = height // 4

    def kernel(places_ref, own_ref, came_ref, *out_refs):
        section, outer = places_ref[0], places_ref[1]
        starts = (
            (1 - outer) * part,
            outer * part,
            (2 + 1 - section) * part,
            (2 + section) * part,
        )
        for start, out_ref in zip(starts, out_refs):
            start = pl.multiple_of(start, part)
            out_ref[...] = (wide(own_ref, start, part) + wide(came_ref, start, part)).astype(
                jnp.bfloat16
            )

    return call(
        kernel,
        tuple(bf16_rows(part, width) for _ in range(4)),
        1 << 20,
        in_specs=[smem_spec()] + [vmem_spec()] * 2,
        out_specs=tuple(vmem_spec() for _ in range(4)),
    )(places, own, came)


def sum_kept(own, came, arrived, places, keep):
    height, width = own.shape
    part = height // 4
    count = len(arrived) // 2

    def kernel(places_ref, own_ref, came_ref, *refs):
        section, outer = places_ref[0], places_ref[1]
        if not keep:
            section, outer = 1 - section, 1 - outer
        for side, start in enumerate((outer * part, (2 + section) * part)):
            start = pl.multiple_of(start, part)
            total = wide(own_ref, start, part) + wide(came_ref, start, part)
            for ref in refs[side * count : (side + 1) * count]:
                total = total + ref[...].astype(jnp.float32)
            refs[2 * count + side][...] = total.astype(jnp.bfloat16)

    return call(
        kernel,
        (bf16_rows(part, width), bf16_rows(part, width)),
        1 << 20,
        in_specs=[smem_spec()] + [vmem_spec()] * (2 + 2 * count),
        out_specs=(vmem_spec(), vmem_spec()),
    )(places, own, came, *arrived)


def per_device(
    frames,
    norm_gain,
    router,
    w_in,
    w_out,
    routing,
    head_gain,
    head_weight,
    frame_lengths,
    labels,
    label_lengths,
):
    sections = lax.axis_size("section")
    section_id = lax.axis_index("section")
    group_size = lax.axis_size("expert")
    member = lax.axis_index("expert")
    outer_size = lax.axis_size("dpo")
    inner_size = lax.axis_size("dpi")
    core = lax.axis_index("dpi")
    micro, utt_dev, frame_count, width = frames.shape
    label_max = labels.shape[2]
    experts = w_in.shape[1] * group_size
    pair_count = micro * utt_dev
    per_section = pair_count // sections
    first_pair = section_id * per_section
    share = (utt_dev * frame_count * 9 + 8 * experts - 1) // (8 * experts)
    group_count = 2 if per_section % (2 * utt_dev) == 0 else 1
    group_pairs = per_section // group_count
    filled = share * -(-group_pairs // utt_dev)
    capacity = round_up(filled + 1, 8)
    span = group_pairs * frame_count
    member_ref = member.astype(jnp.int32).reshape(1)

    def mine_of(value):
        return lax.dynamic_slice_in_dim(value, first_pair, per_section, 0)

    def exchange(blocks):
        return [blocks[0]] + [crossed(blocks[k], "expert", k) for k in range(1, group_size)]

    def lanes_of(ids):
        ids = jnp.pad(mine_of(ids), ((0, 0), (0, LANES - frame_count)), constant_values=-1)
        return [ids[g * group_pairs : (g + 1) * group_pairs] for g in range(group_count)]

    flat_frames = frames.reshape(pair_count * frame_count, width)
    current = [
        lax.dynamic_slice_in_dim(flat_frames, first_pair * frame_count + g * span, span, 0)
        for g in range(group_count)
    ]
    own_ids = routing.reshape(pair_count, frame_count)
    paired = sections == 2 and inner_size == 2
    if paired:
        other_ids = swap(own_ids, "section")
        all_ids = [
            jnp.where(section_id == layer, own_ids, other_ids) for layer in range(sections)
        ]
    else:
        all_ids = lax.all_gather(own_ids, "section")
    layer_ids = [lanes_of(all_ids[layer]) for layer in range(sections)]
    own_table = jnp.concatenate(
        [
            norm_gain,
            jnp.zeros((7, width), jnp.float32),
            jnp.transpose(router[0]).astype(jnp.float32),
            jnp.zeros((round_up(experts, 8) - experts, width), jnp.float32),
        ],
        axis=0,
    )
    own = (w_in[0, 0], w_out[0, 0])
    layers = []
    if paired:
        other_table = swap(own_table, "section")
    else:
        all_tables = lax.all_gather(own_table, "section")
        all_in = lax.all_gather(own[0], "section")
        all_out = lax.all_gather(own[1], "section")
        for layer in range(sections):
            chosen = (all_in[layer], all_out[layer])
            layers.append(((all_tables[layer],), chosen, [], jnp.ones((1,), jnp.int32)))

    outgoing = [
        dispatch(current[g], layer_ids[0][g], member_ref, experts, capacity, frame_count)
        for g in range(group_count)
    ]
    received = [exchange(blocks) for blocks in outgoing]
    if paired:
        sent_in, sent_out = half_weights(
            after(core.astype(jnp.int32).reshape(1), outgoing[0][0]), *own
        )
        came_in = swap(sent_in, "section")
        came_out = swap(sent_out, "section")
        came_in, came_out = lax.optimization_barrier((came_in, came_out, received))[:2]
        other = [(came_in, came_out), (swap(came_in, "dpi"), swap(came_out, "dpi"))]
        for layer in range(sections):
            mine = (section_id == layer).astype(jnp.int32).reshape(1)
            layers.append(((own_table, other_table), own, other, mine))

    notes = (
        first_pair.astype(jnp.int32).reshape(1),
        labels,
        jnp.transpose(frame_lengths),
        jnp.transpose(label_lengths),
    )
    shard = head_weight.shape[1]
    weight_rows = jnp.transpose(head_weight)
    line = group_size == 4
    tables = jnp.asarray(slot_tables(group_size, group_count))
    slots = lax.dynamic_index_in_dim(tables, member, 0, keepdims=False)
    outer = lax.axis_index("dpo")
    blocks = -(-shard // BLOCK_ROWS)
    tree = paired and outer_size == 2 and blocks == 8

    def pair_of(side, first, second):
        return [side * 4 + first, side * 4 + 2 + second]

    def offset_of(side, s, y):
        base = side * 4 * BLOCK_ROWS
        part = BLOCK_ROWS // 2
        return [
            base + s * BLOCK_ROWS + y * part,
            base + 2 * BLOCK_ROWS + y * BLOCK_ROWS + s * part,
        ]

    def whole_numbers(values):
        return jnp.stack([jnp.asarray(value, jnp.int32) for value in values])

    here, there = (section_id, outer), (1 - section_id, 1 - outer)
    sibling_order = whole_numbers(pair_of(1 - core, *there) + pair_of(1 - core, *here))
    sent_order = whole_numbers(pair_of(core, *there))
    kept_order = whole_numbers(pair_of(core, *here))
    chip_place = whole_numbers(here)
    first_offsets, last_offsets = [], []
    for side in (core, 1 - core):
        near_y = offset_of(side, section_id, 1 - outer)
        near_x = offset_of(side, 1 - section_id, outer)
        first_offsets += offset_of(side, *here) + [near_y[0], near_x[1]]
        last_offsets += [near_y[1], near_x[0]] + offset_of(side, *there)
    first_offsets, last_offsets = whole_numbers(first_offsets), whole_numbers(last_offsets)
    early = (
        slots,
        head_gain.reshape(1, width),
        layer_ids[1:],
        sibling_order,
        sent_order,
        kept_order,
        chip_place,
        first_offsets,
        last_offsets,
    )
    early, received = lax.optimization_barrier((early, received))
    slots, head_row, later_ids, sibling_order, sent_order, kept_order = early[:6]
    chip_place, first_offsets, last_offsets = early[6:]
    layer_ids = [layer_ids[0]] + list(later_ids)

    def tied(value, others, g):
        marks = [other for i, other in enumerate(others) if i != g]
        return after(value, *marks) if marks else value

    normed, marks = [], []
    for layer in range(sections):
        choices, weights, others, pick_own = layers[layer]
        done = [
            run_expert(
                received[g],
                choices,
                weights,
                others,
                tied(pick_own, marks, g),
                filled,
                notes if layer == 0 and g == 0 else None,
                per_section,
            )
            for g in range(group_count)
        ]
        returned = [exchange(parts) for parts in done]
        marks = [parts[0] for parts in done]
        tokens = [tied(member_ref, marks, g) for g in range(group_count)]
        if layer == sections - 1 and group_count > 1:
            tokens[-1] = after(tokens[-1], label_weight)
        sizes = (experts, capacity, frame_count)
        if layer < sections - 1:
            made = [
                combine_and_dispatch(
                    current[g],
                    returned[g],
                    layer_ids[layer][g],
                    choices,
                    pick_own,
                    layer_ids[layer + 1][g],
                    tokens[g],
                    *sizes,
                )
                for g in range(group_count)
            ]
            current = [pair[0] for pair in made]
            received = [exchange(pair[1]) for pair in made]
            marks = current
        else:
            normed = [
                combine_and_norm(
                    current[g],
                    returned[g],
                    layer_ids[layer][g],
                    choices,
                    pick_own,
                    head_row,
                    tokens[g],
                    *sizes,
                )
                for g in range(group_count)
            ]
        if layer == 0:
            found = list(returned[0])
            if not line:
                stacked = jnp.stack(found)
                found = [
                    lax.dynamic_index_in_dim(stacked, member ^ k, 0, keepdims=False)
                    for k in range(group_size)
                ]
            label_weight, places, names = label_rows(
                weight_rows, found, member_ref, group_count, group_pairs, filled, label_max, line
            )

    def logits_of(fill, first, count, pieces, earlier=None):
        return head_logits(
            fill, first, count, pieces, member_ref, weight_rows, label_weight, frame_count, earlier
        )

    def stats_of(stats):
        first = crossed(stats, "expert", 1)
        return [stats, first, crossed(stats, "expert", 2), crossed(first, "expert", 2)]

    heads, found = [], []
    for g in range(group_count):
        if line:
            beside = crossed(normed[g], "expert", 1)
            middle = lax.ppermute(normed[g], "expert", MIDDLE)
            beside, middle = lax.optimization_barrier((beside, middle, normed[-1]))[:2]
            far = lax.ppermute(beside, "expert", MIDDLE)
            outward = lax.ppermute(middle, "expert", OUTWARD)
            if g > 0:
                far = after(far, heads[0][2])
            last = lax.ppermute(far, "expert", OUTWARD)
            pieces = [normed[g], beside, middle, outward, far, last]
            earlier = heads[-1][2] if heads else None
            heads.append(logits_of(fill_line, g * group_size, group_size, pieces, earlier))
        else:
            gathered = lax.all_gather(normed[g], "expert")
            pieces = [gathered[k] for k in range(group_size)]
            heads.append(logits_of(fill_all, g * group_size, group_size, pieces))
            gathered = lax.all_gather(heads[g][2], "expert")
            found.append(
                [
                    lax.dynamic_index_in_dim(gathered, member ^ k, 0, keepdims=False)
                    for k in range(group_size)
                ]
            )
    if line:
        found = [stats_of(heads[-1][2])]
    kept_losses = group_pairs if line else group_size * group_pairs
    occupancy, high, low, losses = ctc_pass(
        found, slots, names, frame_count, label_max, group_count, kept_losses
    )
    if not line:
        pairs = losses.reshape(group_count, group_size, group_pairs)
        losses = lax.dynamic_index_in_dim(pairs, member, 1).reshape(1, per_section)
    losses = jnp.transpose(losses)

    def gradient(order, outputs, each):
        return head_gradient(
            [head[0] for head in heads],
            [head[1] for head in heads],
            occupancy,
            high,
            low,
            places,
            order,
            outputs,
            each,
        )

    if tree:
        sibling_sent, sibling_kept = gradient(sibling_order, 2, 2)
        came_sent, came_kept = swap(sibling_sent, "dpi"), swap(sibling_kept, "dpi")
        own_sent = gradient(after(sent_order, sibling_sent), 1, 2)[0]
        a_far, a_near, b_far, b_near = sum_sent(own_sent, came_sent, chip_place)
        kept_order = after(kept_order, a_far)
        a_far, b_far = swap(a_far, "section"), swap(b_far, "dpo")
        a_near, b_near = swap(a_near, "section"), swap(b_near, "dpo")
        own_kept = gradient(kept_order, 1, 2)[0]
        a_on, b_on = sum_kept(own_kept, came_kept, [a_far, b_far], chip_place, False)
        a_in, b_in = swap(a_on, "dpo"), swap(b_on, "section")
        a, b = sum_kept(own_kept, came_kept, [a_near, a_in, b_near, b_in], chip_place, True)
        a_y, b_x = swap(a, "dpo"), swap(b, "section")
        b_y, a_x = swap(b, "dpo"), swap(a, "section")
        a_xy, b_xy = swap(a_y, "section"), swap(b_x, "dpo")
        b_y, a_x = lax.optimization_barrier((b_y, a_x, a_xy, b_xy))[:2]
        mine = [a, b, a_y, b_x]
        theirs = [swap(value, "dpi") for value in mine]
        whole = assemble(mine + theirs, first_offsets, shard)
        mine = [b_y, a_x, a_xy, b_xy]
        theirs = [swap(value, "dpi") for value in mine]
        whole = assemble(mine + theirs, last_offsets, shard, whole)
    else:
        partial = gradient(jnp.arange(blocks, dtype=jnp.int32), 1, blocks)[0][:shard]
        whole = lax.psum(partial.astype(jnp.float32), ("section", "dpo", "dpi")).astype(
            jnp.bfloat16
        )
    return (losses, jnp.transpose(whole))


def solution(mesh):
    sections, group_size, spread = (mesh.shape[name] for name in ("section", "expert", "dp"))
    inner = 2 if spread % 2 == 0 else 1
    split = Mesh(
        mesh.devices.reshape(sections, group_size, spread // inner, inner),
        ("section", "expert", "dpo", "dpi"),
    )
    block = ("expert", "dpo", "dpi")
    placed = (
        P(None, block, None, None),
        P("section", None),
        P("section", None, None),
        P("section", "expert", None, None),
        P("section", "expert", None, None),
        P("section", None, block, None, None),
        P(),
        P(None, "expert"),
        P(None, block),
        P(None, block, None),
        P(None, block),
    )
    return jax.shard_map(
        per_device,
        mesh=split,
        in_specs=placed,
        out_specs=(P("section", block), P(None, "expert")),
        check_vma=False,
    )
```

```python
import jax
import jax.numpy as jnp
import numpy as np
from jax import lax
from jax.experimental import pallas as pl
from jax.experimental.pallas import tpu as pltpu
from jax.sharding import Mesh, PartitionSpec as P

EPSILON = 1e-06
LOG_ZERO = -1e30
VMEM_LIMIT = 12 * 1024 * 1024
LARGE_LIMIT = 24 * 1024 * 1024
LANES = 128
COLS = 16
PEAK, TOTAL, WHOLE = COLS - 3, COLS - 2, COLS - 3
BLOCK_ROWS = 256
NT = (((1,), (1,)), ((), ()))
NN = (((1,), (0,)), ((), ()))


def round_up(value, unit):
    return -(-value // unit) * unit


def vmem_spec():
    return pl.BlockSpec(memory_space=pltpu.VMEM)


def smem_spec():
    return pl.BlockSpec(memory_space=pltpu.SMEM)


def call(kernel, out_shape, flops=0, limit=VMEM_LIMIT, **options):
    return pl.pallas_call(
        kernel,
        out_shape=out_shape,
        compiler_params=pltpu.CompilerParams(vmem_limit_bytes=limit),
        cost_estimate=pl.CostEstimate(flops=flops, bytes_accessed=0, transcendentals=0),
        **options,
    )


def bf16_rows(count, width):
    return jax.ShapeDtypeStruct((count, width), jnp.bfloat16)


def as_mask(values):
    return values.astype(jnp.float32).astype(jnp.bfloat16)


def split_rows(values, out_refs, spare=None, note=None):
    size, width = out_refs[0].shape
    for turn, out_ref in enumerate(out_refs):
        part = values[turn * size : (turn + 1) * size]
        if note is not None:
            row = lax.broadcasted_iota(jnp.int32, (size, width), 0)
            part = jnp.where(row == spare, note, part)
        out_ref[...] = part.astype(jnp.bfloat16)


def join_rows(refs):
    return jnp.concatenate([ref[...].astype(jnp.float32) for ref in refs], axis=0)


def rms_scale(values, gain):
    values = values.astype(jnp.float32)
    scale = lax.rsqrt(jnp.mean(values * values, axis=-1, keepdims=True) + EPSILON)
    return (values * scale * gain).astype(jnp.bfloat16)


def expert_column(ids, frame_count):
    pairs = ids.shape[0]
    square = jnp.concatenate(
        [ids.astype(jnp.float32), jnp.full((LANES - pairs, LANES), -1.0, jnp.float32)], axis=0
    )
    turned = jnp.transpose(square, (1, 0)).astype(jnp.int32)
    return jnp.concatenate([turned[:frame_count, p : p + 1] for p in range(pairs)], axis=0)


def placement(column, member, experts, capacity):
    count = column.shape[0]
    relative = column ^ member
    lane = lax.broadcasted_iota(jnp.int32, (count, LANES), 1)
    one_hot = (lane == relative).astype(jnp.float32)
    before = lax.broadcasted_iota(jnp.int32, (count, count), 1) <= lax.broadcasted_iota(
        jnp.int32, (count, count), 0
    )
    rank = lax.dot_general(
        as_mask(before), one_hot.astype(jnp.bfloat16), NN, preferred_element_type=jnp.float32
    )
    start = (lane * capacity - 1).astype(jnp.float32)
    slots = jnp.sum(one_hot * (rank + start), axis=1, keepdims=True).astype(jnp.int32)
    places = lax.broadcasted_iota(jnp.int32, (count, experts * capacity), 1)
    return (places == slots).astype(jnp.float32)


def scatter_rows(rows, ids, member, experts, capacity, frame_count, out_refs):
    count = rows.shape[0]
    chosen = placement(expert_column(ids, frame_count), member, experts, capacity)
    tall = round_up(count, LANES)
    if tall > count:
        chosen = jnp.concatenate(
            [chosen, jnp.zeros((tall - count, chosen.shape[1]), jnp.float32)], axis=0
        )
    pick = jnp.transpose(chosen, (1, 0))[:, :count].astype(jnp.bfloat16)
    placed = lax.dot_general(pick, rows, NN, preferred_element_type=jnp.float32)
    split_rows(placed, out_refs)


def combine_rows(rows, returned, ids, table, member, experts, capacity, frame_count):
    column = expert_column(ids, frame_count)
    pick = placement(column, member, experts, capacity).astype(jnp.bfloat16)
    normed = rms_scale(rows, table[:1])
    router = jnp.concatenate(
        [table[8:], jnp.zeros((LANES + 8 - table.shape[0], rows.shape[1]), jnp.float32)], axis=0
    ).astype(jnp.bfloat16)
    logits = lax.dot_general(normed, router, NT, preferred_element_type=jnp.float32)
    lane = lax.broadcasted_iota(jnp.int32, logits.shape, 1)
    gate = jax.nn.sigmoid(jnp.sum(jnp.where(lane == column, logits, 0.0), axis=1, keepdims=True))
    stacked = join_rows(returned).astype(jnp.bfloat16)
    mixed = lax.dot_general(pick, stacked, NN, preferred_element_type=jnp.float32)
    return (rows.astype(jnp.float32) + gate * mixed).astype(jnp.bfloat16)


def dispatch(rows, ids, member, experts, capacity, frame_count):
    width = rows.shape[1]

    def kernel(member_ref, rows_ref, ids_ref, *out_refs):
        scatter_rows(
            rows_ref[...], ids_ref[...], member_ref[0], experts, capacity, frame_count, out_refs
        )

    return call(
        kernel,
        tuple(bf16_rows(capacity, width) for _ in range(experts)),
        1 << 27,
        in_specs=[smem_spec()] + [vmem_spec()] * 2,
        out_specs=tuple(vmem_spec() for _ in range(experts)),
    )(member, rows, ids)


def pick_table(pick_ref, tables):
    if len(tables) == 1:
        return tables[0][...]
    return jnp.where(pick_ref[0] == 1, tables[0][...], tables[1][...])


def note_row(first_ref, labels_ref, frames_ref, counts_ref, pairs, width):
    utt_dev, label_max = labels_ref.shape[1:]
    lane = lax.broadcasted_iota(jnp.int32, (1, width), 1)
    row = jnp.zeros((1, width), jnp.int32)
    for pair in range(pairs):
        index = first_ref[0] + pair
        micro, utt = index // utt_dev, index % utt_dev
        values = [labels_ref[micro, utt, c] for c in range(label_max)]
        values += [frames_ref[utt, micro], counts_ref[utt, micro]]
        for c, value in enumerate(values):
            row = jnp.where(lane == pair * COLS + c, value // LANES, row)
            row = jnp.where(lane == LANES + pair * COLS + c, value % LANES, row)
    return row.astype(jnp.float32)


def run_expert(received, tables, own, other, pick_own, spare, note, pairs):
    count = len(received)
    capacity, width = received[0].shape
    others, choices = len(other), len(tables)
    noted = [] if note is None else list(note)

    def kernel(pick_ref, in_ref, out_weight_ref, *refs):
        table_refs, refs = refs[:choices], refs[choices:]
        other_refs, refs = refs[: 2 * others], refs[2 * others :]
        received_refs, refs = refs[:count], refs[count:]
        out_refs = refs[len(noted) :]

        def work(pieces):
            gain = pick_table(pick_ref, table_refs)[:1]
            normed = rms_scale(join_rows(received_refs), gain)
            total = None
            for weight_in, weight_out in pieces:
                hidden = lax.dot_general(
                    normed, weight_in[...], NN, preferred_element_type=jnp.float32
                )
                active = (hidden / (1.0 + jnp.exp(-hidden))).astype(jnp.bfloat16)
                part = lax.dot_general(
                    active, weight_out[...], NN, preferred_element_type=jnp.float32
                )
                total = part if total is None else total + part
            row = note_row(*refs[: len(noted)], pairs, width) if noted else None
            split_rows(total, out_refs, spare, row)

        if others == 0:
            work([(in_ref, out_weight_ref)])
            return

        @pl.when(pick_ref[0] == 1)
        def _():
            work([(in_ref, out_weight_ref)])

        @pl.when(pick_ref[0] != 1)
        def _():
            work([(other_refs[2 * i], other_refs[2 * i + 1]) for i in range(others)])

    flat = [weight for pair in other for weight in pair]
    return call(
        kernel,
        tuple(bf16_rows(capacity, width) for _ in range(count)),
        4 * count * capacity * width * own[0].shape[1],
        in_specs=[smem_spec()] + [vmem_spec()] * (2 + choices + 2 * others + count)
        + [smem_spec()] * len(noted),
        out_specs=tuple(vmem_spec() for _ in range(count)),
    )(pick_own, *own, *tables, *flat, *received, *noted)


def combine_and_dispatch(
    rows, returned, ids, tables, pick_own, next_ids, member, experts, capacity, frame_count
):
    width = rows.shape[1]
    choices = len(tables)

    def kernel(member_ref, pick_ref, rows_ref, ids_ref, next_ref, *refs):
        table_refs, refs = refs[:choices], refs[choices:]
        returned_refs, x_ref, out_refs = refs[:experts], refs[experts], refs[experts + 1 :]
        mixed = combine_rows(
            rows_ref[...],
            returned_refs,
            ids_ref[...],
            pick_table(pick_ref, table_refs),
            member_ref[0],
            experts,
            capacity,
            frame_count,
        )
        x_ref[...] = mixed
        scatter_rows(
            mixed, next_ref[...], member_ref[0], experts, capacity, frame_count, out_refs
        )

    shapes = (bf16_rows(*rows.shape),) + tuple(
        bf16_rows(capacity, width) for _ in range(experts)
    )
    result = call(
        kernel,
        shapes,
        1 << 28,
        in_specs=[smem_spec()] * 2 + [vmem_spec()] * (3 + choices + experts),
        out_specs=tuple(vmem_spec() for _ in shapes),
    )(member, pick_own, rows, ids, next_ids, *tables, *returned)
    return result[0], result[1:]


def combine_and_norm(
    rows, returned, ids, tables, pick_own, head_gain, member, experts, capacity, frame_count
):
    choices = len(tables)

    def kernel(member_ref, pick_ref, rows_ref, ids_ref, head_ref, *refs):
        table_refs, refs = refs[:choices], refs[choices:]
        final = combine_rows(
            rows_ref[...],
            refs[:experts],
            ids_ref[...],
            pick_table(pick_ref, table_refs),
            member_ref[0],
            experts,
            capacity,
            frame_count,
        )
        refs[experts][...] = rms_scale(final, head_ref[...])

    return call(
        kernel,
        bf16_rows(*rows.shape),
        1 << 28,
        in_specs=[smem_spec()] * 2 + [vmem_spec()] * (3 + choices + experts),
        out_specs=vmem_spec(),
    )(member, pick_own, rows, ids, head_gain, *tables, *returned)


def half_weights(core, weight_in, weight_out):
    width, hidden = weight_in.shape
    half = hidden // 2

    def kernel(core_ref, in_ref, out_ref, half_in, half_out, sems):
        start = pl.multiple_of(core_ref[0] * half, half)
        copies = (
            pltpu.make_async_copy(in_ref.at[:, pl.ds(start, half)], half_in, sems.at[0]),
            pltpu.make_async_copy(out_ref.at[pl.ds(start, half)], half_out, sems.at[1]),
        )
        for copy in copies:
            copy.start()
        for copy in copies:
            copy.wait()

    return call(
        kernel,
        (bf16_rows(width, half), bf16_rows(half, width)),
        1 << 20,
        in_specs=[smem_spec()] + [pl.BlockSpec(memory_space=pl.ANY)] * 2,
        out_specs=(vmem_spec(), vmem_spec()),
        scratch_shapes=[pltpu.SemaphoreType.DMA((2,))],
    )(core, weight_in, weight_out)


def block_list(shard):
    return [(i, min(BLOCK_ROWS, shard - i)) for i in range(0, shard, BLOCK_ROWS)]


def label_rows(weight, notes, member, groups, pairs, spare, label_max, line):
    shard, width = weight.shape
    sources = len(notes)
    utterances = sources * groups * pairs
    entries = utterances * COLS

    def kernel(member_ref, weight_ref, *refs):
        note_refs = refs[:sources]
        out_ref, places_ref, names_ref, turned_ref = refs[sources:]
        place = member_ref[0]
        found = []
        for ref in note_refs:
            row = ref[...].astype(jnp.float32)[spare : spare + 1]
            found.append((row[:, :LANES] * LANES + row[:, LANES : 2 * LANES]).astype(jnp.int32))
        if line:
            ends = (place == 0) | (place == 3)
            found = [
                found[0],
                found[1],
                jnp.where(ends, found[2], found[3]),
                jnp.where(ends, found[3], found[2]),
            ]
        names_ref[...] = jnp.zeros(names_ref.shape, jnp.int32)
        for slot in range(sources):
            for pair in range(groups * pairs):
                row = (pair // pairs * sources + slot) * pairs + pair % pairs
                names_ref[row : row + 1, :COLS] = found[slot][:, pair * COLS : (pair + 1) * COLS]
        lane = lax.broadcasted_iota(jnp.int32, (utterances, LANES), 1)
        named = jnp.where(lane < label_max, names_ref[...], jnp.where(lane == label_max, 0, -1))
        local = named - place * shard
        local = jnp.where((named >= 0) & (local >= 0) & (local < shard), local, -1)
        square = jnp.concatenate(
            [
                local.astype(jnp.float32),
                jnp.full((LANES - utterances, LANES), -1.0, jnp.float32),
            ],
            axis=0,
        )
        turned = jnp.transpose(square, (1, 0))
        for utterance in range(utterances):
            turned_ref[utterance * COLS : (utterance + 1) * COLS] = jnp.broadcast_to(
                turned[:COLS, utterance : utterance + 1], (COLS, LANES)
            )
        places = turned_ref[:, :1].astype(jnp.int32)
        places_ref[...] = jnp.transpose(turned_ref[...], (1, 0))[:1].astype(jnp.int32)
        total = jnp.zeros((entries, width), jnp.float32)
        for first, size in block_list(shard):
            entry = first + lax.broadcasted_iota(jnp.int32, (entries, size), 1)
            total = total + lax.dot_general(
                as_mask(entry == places),
                weight_ref[first : first + size],
                NN,
                preferred_element_type=jnp.float32,
            )
        out_ref[...] = total.astype(jnp.bfloat16)

    return call(
        kernel,
        (
            bf16_rows(entries, width),
            jax.ShapeDtypeStruct((1, entries), jnp.int32),
            jax.ShapeDtypeStruct((utterances, LANES), jnp.int32),
        ),
        2 * shard * entries * width,
        LARGE_LIMIT,
        in_specs=[smem_spec()] + [vmem_spec()] * (1 + sources),
        out_specs=tuple(vmem_spec() for _ in range(3)),
        scratch_shapes=[pltpu.VMEM((entries, LANES), jnp.float32)],
    )(member, weight, *notes)


def head_logits(
    fill, first_slot, count, pieces, member, weight, label_weight, frame_count, earlier=None
):
    given = len(pieces)
    span, width = pieces[0].shape
    row_count = count * span
    shard = weight.shape[0]
    height = round_up(shard, BLOCK_ROWS)
    entries = row_count // frame_count * COLS
    first_entry = first_slot * entries // count
    others = [] if earlier is None else [earlier]
    ahead = 0 if earlier is None else earlier.shape[0]

    def kernel(member_ref, weight_ref, label_ref, *refs):
        piece_refs = refs[:given]
        logits_ref, rows_ref, stats_ref = refs[given + len(others) :]

        def put(slot, piece_ref):
            rows_ref[slot * span : (slot + 1) * span] = piece_ref[...]

        def put_if(condition, slot, piece_ref):
            @pl.when(condition)
            def _():
                put(slot, piece_ref)

        fill(member_ref[0], piece_refs, put, put_if)
        peak = jnp.full((1, row_count), LOG_ZERO, jnp.float32)
        total = jnp.zeros((1, row_count), jnp.float32)
        for first, size in block_list(shard):
            logits = lax.dot_general(
                weight_ref[first : first + size],
                rows_ref[...],
                NT,
                preferred_element_type=jnp.float32,
            )
            logits_ref[first : first + size] = logits
            before = peak
            peak = jnp.maximum(before, jnp.max(logits, axis=0, keepdims=True))
            total = total * jnp.exp(before - peak) + jnp.sum(
                jnp.exp(logits - peak), axis=0, keepdims=True
            )
        if height > shard:
            logits_ref[shard:] = jnp.full((height - shard, row_count), LOG_ZERO, jnp.float32)
        crossed = lax.dot_general(
            label_ref[first_entry : first_entry + entries],
            rows_ref[...],
            NT,
            preferred_element_type=jnp.float32,
        )
        owner = lax.broadcasted_iota(jnp.int32, (COLS, row_count), 1) // frame_count
        picked = jnp.zeros((COLS, row_count), jnp.float32)
        for utterance in range(entries // COLS):
            part = crossed[utterance * COLS : (utterance + 1) * COLS]
            picked = picked + jnp.where(owner == utterance, part, 0.0)
        place = lax.broadcasted_iota(jnp.int32, (COLS, row_count), 0)
        stats = jnp.where(place == PEAK, peak, picked)
        stats = jnp.where(place == TOTAL, total, stats)
        for slot in range(ahead):
            stats_ref[slot] = refs[given][slot]
        for slot in range(count):
            stats_ref[ahead + slot] = stats[:, slot * span : (slot + 1) * span]

    return call(
        kernel,
        (
            jax.ShapeDtypeStruct((height, row_count), jnp.float32),
            bf16_rows(row_count, width),
            jax.ShapeDtypeStruct((ahead + count, COLS, span), jnp.float32),
        ),
        2 * height * row_count * width,
        LARGE_LIMIT,
        in_specs=[smem_spec()] + [vmem_spec()] * (2 + given + len(others)),
        out_specs=tuple(vmem_spec() for _ in range(3)),
    )(member, weight, label_weight, *pieces, *others)


def fill_line(place, piece_refs, put, put_if):
    own, beside, middle, outward, far, last = piece_refs
    ends = (place == 0) | (place == 3)
    inner = (place == 1) | (place == 2)
    put(0, own)
    put(1, beside)
    put_if(ends, 2, outward)
    put_if(ends, 3, last)
    put_if(inner, 2, middle)
    put_if(inner, 3, far)


def fill_all(place, piece_refs, put, put_if):
    for slot, piece_ref in enumerate(piece_refs):
        put(slot, piece_ref)


def log_add(first, second):
    peak = jnp.maximum(first, second)
    return peak + jnp.log(jnp.exp(first - peak) + jnp.exp(second - peak))


def log_add3(first, second, third):
    peak = jnp.maximum(jnp.maximum(first, second), third)
    return peak + jnp.log(
        jnp.exp(first - peak) + jnp.exp(second - peak) + jnp.exp(third - peak)
    )


def ctc_pass(stats, slots, notes, frame_count, label_max, parts, kept):
    calls, sources = len(stats), len(stats[0])
    each, _, span = stats[0][0].shape
    count = calls * each
    row_count = count * span
    utterances = notes.shape[0]
    entries = utterances * COLS
    tall = round_up(span, LANES)

    def kernel(slots_ref, notes_ref, *refs):
        (
            out_ref,
            high_ref,
            low_ref,
            loss_ref,
            turn_ref,
            emission_ref,
            emit_blank,
            emit_label,
            blank_fwd,
            label_fwd,
            blank_bwd,
            label_bwd,
            occupancy_ref,
        ) = refs[calls * sources :]
        place = lax.broadcasted_iota(jnp.int32, (COLS, span), 0)
        turn_ref[...] = jnp.zeros(turn_ref.shape, jnp.float32)
        for slot in range(count):
            found = []
            for k in range(sources):
                where = slots_ref[k * count + slot]
                part = refs[k][where % each]
                for other in range(1, calls):
                    later = refs[other * sources + k][where % each]
                    part = jnp.where(where >= other * each, later, part)
                found.append(part)
            joined = found[0]
            peak = found[0][PEAK : PEAK + 1]
            for other in found[1:]:
                joined = joined + other
                peak = jnp.maximum(peak, other[PEAK : PEAK + 1])
            total = jnp.zeros((1, span), jnp.float32)
            for other in found:
                total = total + other[TOTAL : TOTAL + 1] * jnp.exp(other[PEAK : PEAK + 1] - peak)
            log_total = peak + jnp.log(total)
            turn_ref[:COLS, :span] = jnp.where(place == TOTAL, log_total, joined - log_total)
            emission_ref[slot * span : (slot + 1) * span] = jnp.transpose(turn_ref[...], (1, 0))[
                :span
            ]

        lane = lax.broadcasted_iota(jnp.int32, (utterances, LANES), 1)
        is_label = lane < label_max
        is_blank = lane <= label_max
        names = jnp.where(is_label, notes_ref[...], 0)
        earlier = pltpu.roll(names, 1, 1)
        skip = is_label & (lane >= 1) & (names != 0) & (names != earlier)
        later = pltpu.roll(names, LANES - 1, 1)
        skip_next = (lane < label_max - 1) & (later != 0) & (later != names)
        frames = notes_ref[:, label_max : label_max + 1]
        counts = notes_ref[:, label_max + 1 : label_max + 2]
        ends_blank = jnp.where(lane == counts, 0.0, LOG_ZERO)
        ends_label = jnp.where(lane == counts - 1, 0.0, LOG_ZERO)

        def spread(step, carry):
            row = emission_ref[pl.ds(step, utterances, stride=frame_count), :]
            blank = jnp.sum(jnp.where(lane == label_max, row, 0.0), axis=1, keepdims=True)
            emit_blank[step] = jnp.where(is_blank, blank, LOG_ZERO)
            emit_label[step] = jnp.where(is_label, row, LOG_ZERO)
            return carry

        lax.fori_loop(0, frame_count, spread, 0, unroll=16)

        def advance(step, carry):
            fwd_blank, fwd_label, bwd_blank, bwd_label = carry
            moved = jnp.where(lane == 0, LOG_ZERO, pltpu.roll(fwd_label, 1, 1))
            new_blank = log_add(fwd_blank, moved) + emit_blank[step]
            new_label = (
                log_add3(fwd_label, fwd_blank, jnp.where(skip, moved, LOG_ZERO))
                + emit_label[step]
            )
            alive = step < frames
            fwd_blank = jnp.where(alive, new_blank, fwd_blank)
            fwd_label = jnp.where(alive, new_label, fwd_label)
            blank_fwd[step] = fwd_blank
            label_fwd[step] = fwd_label

            back = frame_count - 1 - step
            out_blank = bwd_blank + emit_blank[back + 1]
            out_label = bwd_label + emit_label[back + 1]
            next_blank = pltpu.roll(out_blank, LANES - 1, 1)
            next_label = jnp.where(skip_next, pltpu.roll(out_label, LANES - 1, 1), LOG_ZERO)
            ended = back >= frames - 1
            bwd_blank = jnp.where(ended, ends_blank, log_add(out_blank, out_label))
            bwd_label = jnp.where(
                ended, ends_label, log_add3(out_label, next_blank, next_label)
            )
            blank_bwd[back] = bwd_blank
            label_bwd[back] = bwd_label
            return (fwd_blank, fwd_label, bwd_blank, bwd_label)

        first_blank = jnp.where(lane == 0, emit_blank[0], LOG_ZERO)
        first_label = jnp.where(lane == 0, emit_label[0], LOG_ZERO)
        blank_fwd[0] = first_blank
        label_fwd[0] = first_label
        blank_bwd[frame_count - 1] = ends_blank
        label_bwd[frame_count - 1] = ends_label
        fwd_blank, fwd_label, _, _ = lax.fori_loop(
            1, frame_count, advance, (first_blank, first_label, ends_blank, ends_label), unroll=frame_count - 1
        )
        end_state = jnp.sum(jnp.where(lane == counts, fwd_blank, 0.0), axis=1, keepdims=True)
        near_state = jnp.sum(jnp.where(lane == counts - 1, fwd_label, 0.0), axis=1, keepdims=True)
        log_like = log_add(end_state, near_state)
        turned_losses = jnp.transpose(jnp.broadcast_to(-log_like, (utterances, LANES)), (1, 0))
        for part in range(parts):
            first = part * utterances // parts
            loss_ref[:, part * kept : (part + 1) * kept] = turned_losses[:1, first : first + kept]

        def occupy(step, carry):
            blank = jnp.exp(blank_fwd[step] + blank_bwd[step] - log_like)
            label = jnp.exp(label_fwd[step] + label_bwd[step] - log_like)
            blank = jnp.sum(jnp.where(is_blank, blank, 0.0), axis=1, keepdims=True)
            label = jnp.where(is_label, label, 0.0)
            whole = blank + jnp.sum(label, axis=1, keepdims=True)
            filled = jnp.where(lane == label_max, blank, label)
            filled = jnp.where(lane == WHOLE, whole, filled)
            filled = jnp.where(step < frames, -filled, 0.0)
            row = emission_ref[pl.ds(step, utterances, stride=frame_count), :]
            occupancy_ref[pl.ds(step, utterances, stride=frame_count), :] = jnp.where(
                lane == TOTAL, row, filled
            )
            return carry

        lax.fori_loop(0, frame_count, occupy, 0, unroll=16)
        turned = jnp.transpose(occupancy_ref[...], (1, 0))[:COLS]
        out_ref[...] = turned
        row_place = lax.broadcasted_iota(jnp.int32, (COLS, row_count), 0)
        owner = lax.broadcasted_iota(jnp.int32, (COLS, row_count), 1) // frame_count
        source = jnp.where(row_place < WHOLE, turned, 0.0)
        for utterance in range(utterances):
            part = jnp.where(owner == utterance, source, 0.0)
            high = part.astype(jnp.bfloat16)
            high_ref[utterance * COLS : (utterance + 1) * COLS] = high
            low_ref[utterance * COLS : (utterance + 1) * COLS] = (
                part - high.astype(jnp.float32)
            ).astype(jnp.bfloat16)

    held = pltpu.VMEM((frame_count, utterances, LANES), jnp.float32)
    table = pltpu.VMEM((row_count, LANES), jnp.float32)
    return call(
        kernel,
        (
            jax.ShapeDtypeStruct((COLS, row_count), jnp.float32),
            bf16_rows(entries, row_count),
            bf16_rows(entries, row_count),
            jax.ShapeDtypeStruct((1, parts * kept), jnp.float32),
        ),
        1 << 26,
        in_specs=[smem_spec()] + [vmem_spec()] * (1 + calls * sources),
        out_specs=tuple(vmem_spec() for _ in range(4)),
        scratch_shapes=[pltpu.VMEM((LANES, tall), jnp.float32), table]
        + [held] * 6
        + [table],
    )(slots, notes, *[value for group in stats for value in group])


def head_gradient(logits, rows, occupancy, high, low, places, order, outputs, each):
    count = len(logits)
    row_count, width = rows[0].shape
    entries = places.shape[1]
    blocks = outputs * each

    def kernel(order_ref, *refs):
        logits_refs, rows_refs = refs[:count], refs[count : 2 * count]
        occupancy_ref, high_ref, low_ref, places_ref = refs[2 * count : 2 * count + 4]
        out_refs = refs[2 * count + 4 :]
        for block in range(blocks):
            start = pl.multiple_of(order_ref[block] * BLOCK_ROWS, BLOCK_ROWS)
            entry = start + lax.broadcasted_iota(jnp.int32, (BLOCK_ROWS, entries), 0)
            select = as_mask(entry == places_ref[...])
            total = None
            for g in range(count):
                lanes = slice(g * row_count, (g + 1) * row_count)
                scattered = lax.dot_general(
                    select, high_ref[:, lanes], NN, preferred_element_type=jnp.float32
                ) + lax.dot_general(
                    select, low_ref[:, lanes], NN, preferred_element_type=jnp.float32
                )
                whole = occupancy_ref[WHOLE : WHOLE + 1, lanes]
                log_total = occupancy_ref[TOTAL : TOTAL + 1, lanes]
                values = logits_refs[g][pl.ds(start, BLOCK_ROWS), :]
                grad = (scattered - jnp.exp(values - log_total) * whole).astype(jnp.bfloat16)
                part = lax.dot_general(
                    grad, rows_refs[g][...], NN, preferred_element_type=jnp.float32
                )
                total = part if total is None else total + part
            out_refs[block // each][
                block % each * BLOCK_ROWS : (block % each + 1) * BLOCK_ROWS
            ] = total.astype(jnp.bfloat16)

    return call(
        kernel,
        tuple(bf16_rows(each * BLOCK_ROWS, width) for _ in range(outputs)),
        2 * blocks * BLOCK_ROWS * count * row_count * (width + 2 * entries),
        LARGE_LIMIT,
        in_specs=[smem_spec()] + [vmem_spec()] * (2 * count + 4),
        out_specs=tuple(vmem_spec() for _ in range(outputs)),
    )(order, *logits, *rows, occupancy, high, low, places)


def assemble(pieces, offsets, height, whole=None):
    count = len(pieces)
    part, width = pieces[0].shape
    short = height % part
    started = [] if whole is None else [whole]

    def kernel(offsets_ref, *refs):
        out_ref, sems = refs[count + len(started) :]

        def each(act):
            for index in range(count):
                offset = pl.multiple_of(offsets_ref[index], part)

                @pl.when(offset + part <= height)
                def _():
                    act(
                        pltpu.make_async_copy(
                            refs[index], out_ref.at[pl.ds(offset, part)], sems.at[index]
                        )
                    )

                if short:

                    @pl.when(offset + part > height)
                    def _():
                        act(
                            pltpu.make_async_copy(
                                refs[index].at[pl.ds(0, short)],
                                out_ref.at[pl.ds(height - short, short)],
                                sems.at[index],
                            )
                        )

        each(lambda copy: copy.start())
        each(lambda copy: copy.wait())

    anywhere = pl.BlockSpec(memory_space=pl.ANY)
    return call(
        kernel,
        bf16_rows(height, width),
        in_specs=[smem_spec()] + [vmem_spec()] * count + [anywhere] * len(started),
        out_specs=anywhere,
        scratch_shapes=[pltpu.SemaphoreType.DMA((count,))],
        input_output_aliases={} if whole is None else {1 + count: 0},
    )(offsets, *pieces, *started)


def swap(value, axis):
    return lax.ppermute(value, axis, [(0, 1), (1, 0)])


def crossed(value, axis, by):
    count = lax.axis_size(axis)
    return lax.ppermute(value, axis, [(i, i ^ by) for i in range(count)])


def after(value, *others):
    return lax.optimization_barrier((value,) + others)[0]


LINE_ORDER = np.array([[0, 1, 2, 3], [1, 0, 2, 3], [2, 3, 1, 0], [3, 2, 1, 0]])
MIDDLE = [(1, 2), (2, 1)]
OUTWARD = [(1, 0), (2, 3)]


def slot_orders(count):
    return LINE_ORDER if count == 4 else np.tile(np.arange(count), (count, 1))


def slot_tables(count, groups):
    orders = slot_orders(count)
    tables = np.zeros((count, count, count), np.int32)
    for member in range(count):
        for k in range(count):
            source = member ^ k
            for slot in range(count):
                tables[member, k, slot] = list(orders[source]).index(orders[member][slot])
    tables = np.concatenate([tables + g * count for g in range(groups)], axis=2)
    return tables.reshape(count, groups * count * count)


def wide(ref, start, size):
    return ref[pl.ds(start, size), :].astype(jnp.float32)


def sum_sent(own, came, places):
    height, width = own.shape
    part = height // 4

    def kernel(places_ref, own_ref, came_ref, *out_refs):
        section, outer = places_ref[0], places_ref[1]
        starts = (
            (1 - outer) * part,
            outer * part,
            (2 + 1 - section) * part,
            (2 + section) * part,
        )
        for start, out_ref in zip(starts, out_refs):
            start = pl.multiple_of(start, part)
            out_ref[...] = (wide(own_ref, start, part) + wide(came_ref, start, part)).astype(
                jnp.bfloat16
            )

    return call(
        kernel,
        tuple(bf16_rows(part, width) for _ in range(4)),
        1 << 20,
        in_specs=[smem_spec()] + [vmem_spec()] * 2,
        out_specs=tuple(vmem_spec() for _ in range(4)),
    )(places, own, came)


def sum_kept(own, came, arrived, places, keep):
    height, width = own.shape
    part = height // 4
    count = len(arrived) // 2

    def kernel(places_ref, own_ref, came_ref, *refs):
        section, outer = places_ref[0], places_ref[1]
        if not keep:
            section, outer = 1 - section, 1 - outer
        for side, start in enumerate((outer * part, (2 + section) * part)):
            start = pl.multiple_of(start, part)
            total = wide(own_ref, start, part) + wide(came_ref, start, part)
            for ref in refs[side * count : (side + 1) * count]:
                total = total + ref[...].astype(jnp.float32)
            refs[2 * count + side][...] = total.astype(jnp.bfloat16)

    return call(
        kernel,
        (bf16_rows(part, width), bf16_rows(part, width)),
        1 << 20,
        in_specs=[smem_spec()] + [vmem_spec()] * (2 + 2 * count),
        out_specs=(vmem_spec(), vmem_spec()),
    )(places, own, came, *arrived)


def per_device(
    frames,
    norm_gain,
    router,
    w_in,
    w_out,
    routing,
    head_gain,
    head_weight,
    frame_lengths,
    labels,
    label_lengths,
):
    sections = lax.axis_size("section")
    section_id = lax.axis_index("section")
    group_size = lax.axis_size("expert")
    member = lax.axis_index("expert")
    outer_size = lax.axis_size("dpo")
    inner_size = lax.axis_size("dpi")
    core = lax.axis_index("dpi")
    micro, utt_dev, frame_count, width = frames.shape
    label_max = labels.shape[2]
    experts = w_in.shape[1] * group_size
    pair_count = micro * utt_dev
    per_section = pair_count // sections
    first_pair = section_id * per_section
    share = (utt_dev * frame_count * 9 + 8 * experts - 1) // (8 * experts)
    group_count = 2 if per_section % (2 * utt_dev) == 0 else 1
    group_pairs = per_section // group_count
    filled = share * -(-group_pairs // utt_dev)
    capacity = round_up(filled + 1, 8)
    span = group_pairs * frame_count
    member_ref = member.astype(jnp.int32).reshape(1)

    def mine_of(value):
        return lax.dynamic_slice_in_dim(value, first_pair, per_section, 0)

    def exchange(blocks):
        return [blocks[0]] + [crossed(blocks[k], "expert", k) for k in range(1, group_size)]

    def lanes_of(ids):
        ids = jnp.pad(mine_of(ids), ((0, 0), (0, LANES - frame_count)), constant_values=-1)
        return [ids[g * group_pairs : (g + 1) * group_pairs] for g in range(group_count)]

    flat_frames = frames.reshape(pair_count * frame_count, width)
    current = [
        lax.dynamic_slice_in_dim(flat_frames, first_pair * frame_count + g * span, span, 0)
        for g in range(group_count)
    ]
    own_ids = routing.reshape(pair_count, frame_count)
    paired = sections == 2 and inner_size == 2
    if paired:
        other_ids = swap(own_ids, "section")
        all_ids = [
            jnp.where(section_id == layer, own_ids, other_ids) for layer in range(sections)
        ]
    else:
        all_ids = lax.all_gather(own_ids, "section")
    layer_ids = [lanes_of(all_ids[layer]) for layer in range(sections)]
    own_table = jnp.concatenate(
        [
            norm_gain,
            jnp.zeros((7, width), jnp.float32),
            jnp.transpose(router[0]).astype(jnp.float32),
            jnp.zeros((round_up(experts, 8) - experts, width), jnp.float32),
        ],
        axis=0,
    )
    own = (w_in[0, 0], w_out[0, 0])
    layers = []
    if paired:
        other_table = swap(own_table, "section")
    else:
        all_tables = lax.all_gather(own_table, "section")
        all_in = lax.all_gather(own[0], "section")
        all_out = lax.all_gather(own[1], "section")
        for layer in range(sections):
            chosen = (all_in[layer], all_out[layer])
            layers.append(((all_tables[layer],), chosen, [], jnp.ones((1,), jnp.int32)))

    outgoing = [
        dispatch(current[g], layer_ids[0][g], member_ref, experts, capacity, frame_count)
        for g in range(group_count)
    ]
    received = [exchange(blocks) for blocks in outgoing]
    if paired:
        sent_in, sent_out = half_weights(
            after(core.astype(jnp.int32).reshape(1), outgoing[0][0]), *own
        )
        came_in = swap(sent_in, "section")
        came_out = swap(sent_out, "section")
        came_in, came_out = lax.optimization_barrier((came_in, came_out, received))[:2]
        other = [(came_in, came_out), (swap(came_in, "dpi"), swap(came_out, "dpi"))]
        for layer in range(sections):
            mine = (section_id == layer).astype(jnp.int32).reshape(1)
            layers.append(((own_table, other_table), own, other, mine))

    notes = (
        first_pair.astype(jnp.int32).reshape(1),
        labels,
        jnp.transpose(frame_lengths),
        jnp.transpose(label_lengths),
    )
    shard = head_weight.shape[1]
    weight_rows = jnp.transpose(head_weight)
    line = group_size == 4
    tables = jnp.asarray(slot_tables(group_size, group_count))
    slots = lax.dynamic_index_in_dim(tables, member, 0, keepdims=False)
    outer = lax.axis_index("dpo")
    blocks = -(-shard // BLOCK_ROWS)
    tree = paired and outer_size == 2 and blocks == 8

    def pair_of(side, first, second):
        return [side * 4 + first, side * 4 + 2 + second]

    def offset_of(side, s, y):
        base = side * 4 * BLOCK_ROWS
        part = BLOCK_ROWS // 2
        return [
            base + s * BLOCK_ROWS + y * part,
            base + 2 * BLOCK_ROWS + y * BLOCK_ROWS + s * part,
        ]

    def whole_numbers(values):
        return jnp.stack([jnp.asarray(value, jnp.int32) for value in values])

    here, there = (section_id, outer), (1 - section_id, 1 - outer)
    sibling_order = whole_numbers(pair_of(1 - core, *there) + pair_of(1 - core, *here))
    sent_order = whole_numbers(pair_of(core, *there))
    kept_order = whole_numbers(pair_of(core, *here))
    chip_place = whole_numbers(here)
    first_offsets, last_offsets = [], offset_of(core, *there) + offset_of(1 - core, *there)
    for side in (core, 1 - core):
        for s, y in (here, (section_id, 1 - outer), (1 - section_id, outer)):
            first_offsets += offset_of(side, s, y)
    first_offsets, last_offsets = whole_numbers(first_offsets), whole_numbers(last_offsets)
    early = (
        slots,
        head_gain.reshape(1, width),
        layer_ids[1:],
        sibling_order,
        sent_order,
        kept_order,
        chip_place,
        first_offsets,
        last_offsets,
    )
    early, received = lax.optimization_barrier((early, received))
    slots, head_row, later_ids, sibling_order, sent_order, kept_order = early[:6]
    chip_place, first_offsets, last_offsets = early[6:]
    layer_ids = [layer_ids[0]] + list(later_ids)

    def tied(value, others, g):
        marks = [other for i, other in enumerate(others) if i != g]
        return after(value, *marks) if marks else value

    normed, marks = [], []
    for layer in range(sections):
        choices, weights, others, pick_own = layers[layer]
        done = [
            run_expert(
                received[g],
                choices,
                weights,
                others,
                tied(pick_own, marks, g),
                filled,
                notes if layer == 0 and g == 0 else None,
                per_section,
            )
            for g in range(group_count)
        ]
        returned = [exchange(parts) for parts in done]
        marks = [parts[0] for parts in done]
        tokens = [tied(member_ref, marks, g) for g in range(group_count)]
        if layer == sections - 1 and group_count > 1:
            tokens[-1] = after(tokens[-1], label_weight)
        sizes = (experts, capacity, frame_count)
        if layer < sections - 1:
            made = [
                combine_and_dispatch(
                    current[g],
                    returned[g],
                    layer_ids[layer][g],
                    choices,
                    pick_own,
                    layer_ids[layer + 1][g],
                    tokens[g],
                    *sizes,
                )
                for g in range(group_count)
            ]
            current = [pair[0] for pair in made]
            received = [exchange(pair[1]) for pair in made]
            marks = current
        else:
            normed = [
                combine_and_norm(
                    current[g],
                    returned[g],
                    layer_ids[layer][g],
                    choices,
                    pick_own,
                    head_row,
                    tokens[g],
                    *sizes,
                )
                for g in range(group_count)
            ]
        if layer == 0:
            found = list(returned[0])
            if not line:
                stacked = jnp.stack(found)
                found = [
                    lax.dynamic_index_in_dim(stacked, member ^ k, 0, keepdims=False)
                    for k in range(group_size)
                ]
            label_weight, places, names = label_rows(
                weight_rows, found, member_ref, group_count, group_pairs, filled, label_max, line
            )

    def logits_of(fill, first, count, pieces, earlier=None):
        return head_logits(
            fill, first, count, pieces, member_ref, weight_rows, label_weight, frame_count, earlier
        )

    def stats_of(stats):
        first = crossed(stats, "expert", 1)
        return [stats, first, crossed(stats, "expert", 2), crossed(first, "expert", 2)]

    heads, found = [], []
    for g in range(group_count):
        if line:
            beside = crossed(normed[g], "expert", 1)
            middle = lax.ppermute(normed[g], "expert", MIDDLE)
            beside, middle = lax.optimization_barrier((beside, middle, normed[-1]))[:2]
            far = lax.ppermute(beside, "expert", MIDDLE)
            outward = lax.ppermute(middle, "expert", OUTWARD)
            if g > 0:
                far = after(far, heads[0][2])
            last = lax.ppermute(far, "expert", OUTWARD)
            pieces = [normed[g], beside, middle, outward, far, last]
            earlier = heads[-1][2] if heads else None
            heads.append(logits_of(fill_line, g * group_size, group_size, pieces, earlier))
        else:
            gathered = lax.all_gather(normed[g], "expert")
            pieces = [gathered[k] for k in range(group_size)]
            heads.append(logits_of(fill_all, g * group_size, group_size, pieces))
            gathered = lax.all_gather(heads[g][2], "expert")
            found.append(
                [
                    lax.dynamic_index_in_dim(gathered, member ^ k, 0, keepdims=False)
                    for k in range(group_size)
                ]
            )
    if line:
        found = [stats_of(heads[-1][2])]
    kept_losses = group_pairs if line else group_size * group_pairs
    occupancy, high, low, losses = ctc_pass(
        found, slots, names, frame_count, label_max, group_count, kept_losses
    )
    if not line:
        pairs = losses.reshape(group_count, group_size, group_pairs)
        losses = lax.dynamic_index_in_dim(pairs, member, 1).reshape(1, per_section)
    losses = jnp.transpose(losses)

    def gradient(order, outputs, each):
        return head_gradient(
            [head[0] for head in heads],
            [head[1] for head in heads],
            occupancy,
            high,
            low,
            places,
            order,
            outputs,
            each,
        )

    if tree:
        sibling_sent, sibling_kept = gradient(sibling_order, 2, 2)
        came_sent, came_kept = swap(sibling_sent, "dpi"), swap(sibling_kept, "dpi")
        own_sent = gradient(after(sent_order, sibling_sent), 1, 2)[0]
        a_far, a_near, b_far, b_near = sum_sent(own_sent, came_sent, chip_place)
        kept_order = after(kept_order, a_far)
        a_far, b_far = swap(a_far, "section"), swap(b_far, "dpo")
        a_near, b_near = swap(a_near, "section"), swap(b_near, "dpo")
        own_kept = gradient(kept_order, 1, 2)[0]
        a_on, b_on = sum_kept(own_kept, came_kept, [a_far, b_far], chip_place, False)
        a_in, b_in = swap(a_on, "dpo"), swap(b_on, "section")
        a, b = sum_kept(own_kept, came_kept, [a_near, a_in, b_near, b_in], chip_place, True)
        a_y, b_x = swap(a, "dpo"), swap(b, "section")
        b_y, a_x = swap(b, "dpo"), swap(a, "section")
        a_xy, b_xy = swap(a_y, "section"), swap(b_x, "dpo")
        b_y, a_x = lax.optimization_barrier((b_y, a_x, a_xy, b_xy))[:2]
        mine = [a, b, a_y, b_y, a_x, b_x]
        theirs = [swap(value, "dpi") for value in mine]
        whole = assemble(mine + theirs, first_offsets, shard)
        last = [a_xy, b_xy, swap(a_xy, "dpi"), swap(b_xy, "dpi")]
        whole = assemble(last, last_offsets, shard, whole)
    else:
        partial = gradient(jnp.arange(blocks, dtype=jnp.int32), 1, blocks)[0][:shard]
        whole = lax.psum(partial.astype(jnp.float32), ("section", "dpo", "dpi")).astype(
            jnp.bfloat16
        )
    return (losses, jnp.transpose(whole))


def solution(mesh):
    sections, group_size, spread = (mesh.shape[name] for name in ("section", "expert", "dp"))
    inner = 2 if spread % 2 == 0 else 1
    split = Mesh(
        mesh.devices.reshape(sections, group_size, spread // inner, inner),
        ("section", "expert", "dpo", "dpi"),
    )
    block = ("expert", "dpo", "dpi")
    placed = (
        P(None, block, None, None),
        P("section", None),
        P("section", None, None),
        P("section", "expert", None, None),
        P("section", "expert", None, None),
        P("section", None, block, None, None),
        P(),
        P(None, "expert"),
        P(None, block),
        P(None, block, None),
        P(None, block),
    )
    return jax.shard_map(
        per_device,
        mesh=split,
        in_specs=placed,
        out_specs=(P("section", block), P(None, "expert")),
        check_vma=False,
    )
```
